32 devices in a mesh: row: 4 (over y, core), sample: 8 (over z, x).
Axes of the slice: x: 2, y: 2, z: 4, core: 2. Of those that a mesh axis runs over, the one named last changes fastest.
Arguments:
- atom_feat: bfloat16 [16, 4608, 128], P('sample', 'row'), may hold values from -24 to 24
- atom_token: int32 [4608], P('row'), may hold values from 0 to 287, as said below
- pair_cond: bfloat16 [288, 288, 128], P('row', 'sample'), may hold values from -24 to 24
- token_mask: int32 [288], P('sample'), may hold values 0 or 1
- atom_wq: bfloat16 [128, 128], replicated, may hold values from -3 to 3
- atom_wk: bfloat16 [128, 128], replicated, may hold values from -3 to 3
- atom_wv: bfloat16 [128, 128], replicated, may hold values from -0.5 to 0.5
- atom_wo: bfloat16 [128, 128], replicated, may hold values from -0.5 to 0.5
- agg_weight: bfloat16 [128, 768], replicated, may hold values from -0.5 to 0.5
- pair_weight: bfloat16 [128, 16], replicated, may hold values from -64 to 64
- token_gain: float32 [768], replicated, may hold values from 0.5 to 1.5
- query_weight: bfloat16 [768, 768], replicated, may hold values from -0.21875 to 0.21875
- key_weight: bfloat16 [768, 768], replicated, may hold values from -0.21875 to 0.21875
- value_weight: bfloat16 [768, 768], replicated, may hold values from -0.21875 to 0.21875
- gate_weight: bfloat16 [768, 768], replicated, may hold values from -0.21875 to 0.21875
- out_weight: bfloat16 [768, 768], replicated, may hold values from -0.21875 to 0.21875
Outputs:
- token_out: bfloat16 [16, 288, 768], P('sample', 'row')
The draws below stay inside these ranges and needn't reach their ends.
Inputs may be any that keep to these rules, and one draw needn't show every extreme that they name: atom_token never falls along the atoms; atoms 1152 r to 1152 (r + 1) - 1 belong to tokens 72 r to 72 (r + 1) - 1, and every token has at least one atom.
All inputs are finite; a program needn't handle non-finite values. No bound on the sum of `token_mask` on one device may be relied on, other than what follows from the above.
Results may differ from the reference program's by a relative error of at most 0.008.
The reference program's roundings to bfloat16 on the way count: a program that leaves them out, or rounds other values in their place, can miss the bound.
Values may be sent and summed in bfloat16 or wider, within the bound.
No kernel may reach another device: no remote copies, remote signals or barrier semaphores. Data moves between devices by JAX's collectives and lax.ppermute only.
A program may use at most 128 MiB of HBM per device.

```python
import jax
import jax.numpy as jnp
from jax import lax

D = 768
HEADS = 16
HEAD_DIM = 48
CZ = 128
CA = 128
AHEADS = 4
AHEAD_DIM = 32
QWIN = 32
KWIN = 128
TOK_ROW = 72
ATOM_DEV = 1152
SAMPLES = 16
NTOK = 288
NATOM = 4608


def draw_atom_token(key, part):
    key = jax.random.fold_in(key, 11)
    blocks = NATOM // ATOM_DEV
    extra = jax.random.randint(key, (blocks, ATOM_DEV - TOK_ROW), 0, TOK_ROW, dtype=jnp.int32)
    first = jnp.broadcast_to(jnp.arange(TOK_ROW, dtype=jnp.int32)[None, :], (blocks, TOK_ROW))
    local = jnp.sort(jnp.concatenate([first, extra], axis=1), axis=1)
    offset = (jnp.arange(blocks, dtype=jnp.int32) * TOK_ROW)[:, None]
    return (local + offset).reshape(-1).astype(jnp.int32)


def draw_atom_feat(key, part):
    key = jax.random.fold_in(key, 21)
    noise_key = jax.random.fold_in(key, 0)
    base_noise = jnp.clip(jax.random.normal(noise_key, (SAMPLES, NATOM, CA), jnp.float32), -6.0, 6.0)
    return base_noise.astype(jnp.bfloat16)


def draw_atom_wq(key, part):
    key = jax.random.fold_in(key, 22)
    drawn_part = jnp.clip(jax.random.normal(key, (CA, CA), jnp.float32), -6.0, 6.0) / CA ** 0.5
    return drawn_part.astype(jnp.bfloat16)


def draw_atom_wk(key, part):
    key = jax.random.fold_in(key, 23)
    drawn_part = jnp.clip(jax.random.normal(key, (CA, CA), jnp.float32), -6.0, 6.0) / CA ** 0.5
    return drawn_part.astype(jnp.bfloat16)


def draw_pair_cond(key, part):
    key = jax.random.fold_in(key, 24)
    noise_key = jax.random.fold_in(key, 0)
    base_noise = jnp.clip(jax.random.normal(noise_key, (NTOK, NTOK, CZ), jnp.float32), -6.0, 6.0)
    return base_noise.astype(jnp.bfloat16)


def draw_pair_weight(key, part):
    key = jax.random.fold_in(key, 25)
    drawn_part = jnp.clip(jax.random.normal(key, (CZ, HEADS), jnp.float32), -6.0, 6.0) / CZ ** 0.5
    return drawn_part.astype(jnp.bfloat16)


def plant(drawn, stream_key, low, largest):
    index_at = [jax.random.randint(jax.random.fold_in(stream_key, axis), (), 0, length) for axis, length in enumerate(drawn.shape)]
    main_axis = drawn.shape.index(max(drawn.shape))
    next_to = index_at[:main_axis] + [(index_at[main_axis] + 1) % drawn.shape[main_axis]] + index_at[main_axis + 1:]
    return drawn.at[tuple(index_at)].set(low).at[tuple(next_to)].set(largest)


def scatter_about(key, dims, scale, bound, kind=jnp.bfloat16):
    result = jax.random.normal(key, dims, jnp.float32) * scale
    return jnp.minimum(jnp.maximum(result, -bound), bound).astype(kind)


def setup_inputs(seed: int = 0) -> dict:
    streams_of = jax.random.split(jax.random.key(seed), 17)
    return {
        "atom_feat": draw_atom_feat(jax.random.fold_in(streams_of[16], 71), 0),
        "atom_token": draw_atom_token(jax.random.fold_in(streams_of[16], 71), 0),
        "pair_cond": draw_pair_cond(jax.random.fold_in(streams_of[16], 71), 0),
        "token_mask": plant((jax.random.randint(streams_of[3], (NTOK,), 0, 8) < 7).astype(jnp.int32), jax.random.fold_in(streams_of[3], 1), 0, 1),
        "atom_wq": draw_atom_wq(jax.random.fold_in(streams_of[16], 71), 0),
        "atom_wk": draw_atom_wk(jax.random.fold_in(streams_of[16], 71), 0),
        "atom_wv": scatter_about(streams_of[6], (CA, CA), CA ** -0.5, 0.5),
        "atom_wo": scatter_about(streams_of[7], (CA, CA), CA ** -0.5, 0.5),
        "agg_weight": scatter_about(streams_of[8], (CA, D), CA ** -0.5, 0.5),
        "pair_weight": draw_pair_weight(jax.random.fold_in(streams_of[16], 71), 0),
        "token_gain": jnp.clip(1.0 + 0.1 * jax.random.normal(streams_of[10], (D,), jnp.float32), 0.5, 1.5),
        "query_weight": scatter_about(streams_of[11], (D, D), D ** -0.5, 0.21875),
        "key_weight": scatter_about(streams_of[12], (D, D), D ** -0.5, 0.21875),
        "value_weight": scatter_about(streams_of[13], (D, D), D ** -0.5, 0.21875),
        "gate_weight": scatter_about(streams_of[14], (D, D), D ** -0.5, 0.21875),
        "out_weight": scatter_about(streams_of[15], (D, D), D ** -0.5, 0.21875),
    }


def layer_norm(x):
    mean = lax.optimization_barrier(jnp.mean(x, -1, keepdims=True))
    centre = x - mean
    var = lax.optimization_barrier(jnp.mean(centre * centre, -1, keepdims=True))
    return centre * lax.rsqrt(var + 1e-05)

def reference(atom_feat, atom_token, pair_cond, token_mask, atom_wq, atom_wk, atom_wv, atom_wo, agg_weight, pair_weight, token_gain, query_weight, key_weight, value_weight, gate_weight, out_weight):
    rim = (KWIN - QWIN) // 2
    windows = NATOM // QWIN
    ascale = 1.0 / AHEAD_DIM ** 0.5
    tscale = 1.0 / HEAD_DIM ** 0.5

    def bias_row(pair_row):
        normed = layer_norm(pair_row.astype(jnp.float32)).astype(jnp.bfloat16)
        return jnp.dot(normed, pair_weight, preferred_element_type=jnp.float32)
    bias_raw = lax.map(bias_row, pair_cond)
    qidx = jnp.arange(NTOK, dtype=jnp.int32)
    allowed = (token_mask[None, :] == 1) | (qidx[:, None] == qidx[None, :])
    bias = jnp.where(allowed[:, :, None], bias_raw, -30000.0).astype(jnp.bfloat16)
    bias = jnp.transpose(bias, (2, 0, 1))
    counts = jax.ops.segment_sum(jnp.ones((NATOM,), jnp.float32), atom_token, NTOK)
    wid = jnp.arange(windows, dtype=jnp.int32)
    tid = jnp.arange(KWIN, dtype=jnp.int32)
    gidx = wid[:, None] * QWIN - rim + tid[None, :]
    valid = (gidx >= 0) & (gidx < NATOM)

    def one_sample(feat):
        normed = layer_norm(feat.astype(jnp.float32)).astype(jnp.bfloat16)
        atom_q = jnp.dot(normed, atom_wq, preferred_element_type=jnp.float32).astype(jnp.bfloat16)
        atom_k = jnp.dot(normed, atom_wk, preferred_element_type=jnp.float32).astype(jnp.bfloat16)
        atom_v = jnp.dot(normed, atom_wv, preferred_element_type=jnp.float32).astype(jnp.bfloat16)
        atom_k = jnp.pad(atom_k, ((rim, rim), (0, 0))).reshape(windows + 3, QWIN, CA)
        atom_v = jnp.pad(atom_v, ((rim, rim), (0, 0))).reshape(windows + 3, QWIN, CA)
        atom_k = jnp.concatenate([atom_k[k:k + windows] for k in range(4)], axis=1).reshape(windows, KWIN, AHEADS, AHEAD_DIM)
        atom_v = jnp.concatenate([atom_v[k:k + windows] for k in range(4)], axis=1).reshape(windows, KWIN, AHEADS, AHEAD_DIM)
        atom_q = atom_q.reshape(windows, QWIN, AHEADS, AHEAD_DIM)
        scores = jnp.einsum('wqhd,wkhd->whqk', atom_q.astype(jnp.float32), atom_k.astype(jnp.float32)) * ascale
        scores = jnp.where(valid[:, None, None, :], scores, -jnp.inf)
        atom_e = jnp.exp(scores - lax.optimization_barrier(jnp.max(scores, -1, keepdims=True)))
        atom_l = lax.optimization_barrier(jnp.sum(atom_e, -1))
        mixed = jnp.einsum('whqk,wkhd->whqd', atom_e.astype(jnp.bfloat16).astype(jnp.float32), atom_v.astype(jnp.float32)) / atom_l[..., None]
        mixed = jnp.transpose(mixed, (0, 2, 1, 3)).reshape(NATOM, CA).astype(jnp.bfloat16)
        atom_out = (feat.astype(jnp.float32) + jnp.dot(mixed, atom_wo, preferred_element_type=jnp.float32)).astype(jnp.bfloat16)
        hidden = jax.nn.relu(jnp.dot(atom_out, agg_weight, preferred_element_type=jnp.float32)).astype(jnp.bfloat16)
        token_in = jax.ops.segment_sum(hidden.astype(jnp.float32), atom_token, NTOK) / counts[:, None]
        tnorm = (layer_norm(token_in) * token_gain).astype(jnp.bfloat16)
        tq = jnp.dot(tnorm, query_weight, preferred_element_type=jnp.float32).astype(jnp.bfloat16).reshape(NTOK, HEADS, HEAD_DIM)
        tk = jnp.dot(tnorm, key_weight, preferred_element_type=jnp.float32).astype(jnp.bfloat16).reshape(NTOK, HEADS, HEAD_DIM)
        tv = jnp.dot(tnorm, value_weight, preferred_element_type=jnp.float32).astype(jnp.bfloat16).reshape(NTOK, HEADS, HEAD_DIM)
        gate = jnp.dot(tnorm, gate_weight, preferred_element_type=jnp.float32)
        tscores = jnp.einsum('qhd,khd->hqk', tq.astype(jnp.float32), tk.astype(jnp.float32)) * tscale + bias.astype(jnp.float32)
        tok_e = jnp.exp(tscores - lax.optimization_barrier(jnp.max(tscores, -1, keepdims=True)))
        tok_l = lax.optimization_barrier(jnp.sum(tok_e, -1))
        tmix = jnp.einsum('hqk,khd->hqd', tok_e.astype(jnp.bfloat16).astype(jnp.float32), tv.astype(jnp.float32)) / tok_l[..., None]
        tmix = jnp.transpose(tmix, (1, 0, 2)).reshape(NTOK, D)
        gated = (tmix * jax.nn.sigmoid(gate)).astype(jnp.bfloat16)
        return (token_in + jnp.dot(gated, out_weight, preferred_element_type=jnp.float32)).astype(jnp.bfloat16)
    return lax.map(one_sample, atom_feat)
```

```python
import functools
import math

import jax
import jax.numpy as jnp
from jax import lax
from jax.experimental import pallas as pl
from jax.experimental.pallas import tpu as pltpu
from jax.sharding import PartitionSpec as P

HEADS = 16
HEAD_DIM = 48
AHEADS = 4
AHEAD_DIM = 32
QWIN = 32
KWIN = 128
RIM = (KWIN - QWIN) // 2
LANES = 128
SUB = 8
F32 = jnp.float32
BF16 = jnp.bfloat16
VMEM_LIMIT = 48 * 1024 * 1024
NT = (((1,), (1,)), ((), ()))


def layer_norm(x):
    mean = jnp.mean(x, -1, keepdims=True)
    centre = x - mean
    var = jnp.mean(centre * centre, -1, keepdims=True)
    return centre * lax.rsqrt(var + 1e-05)


def dot(a, b):
    return jnp.dot(a, b, preferred_element_type=F32)


def dot_nt(a, b):
    return lax.dot_general(a, b, NT, preferred_element_type=F32)


def iota(shape, dim):
    return lax.broadcasted_iota(jnp.int32, shape, dim)


def skewed(items, stages):
    held = list(items)
    for t in range(len(held) + len(stages) - 1):
        for k in reversed(range(len(stages))):
            if 0 <= t - k < len(held):
                held[t - k] = stages[k](held[t - k])
    return held


def bias_kernel(offs, pair, mask, weight, out, normed):
    cols, rows, chans = pair.shape
    for k in range(cols):
        normed[k] = layer_norm(pair[k].astype(F32))
    spread = (iota((HEADS, LANES), 1) // SUB == iota((HEADS, LANES), 0)).astype(BF16)
    wide = lax.dot_general(weight[...], spread, (((0,), (0,)), ((), ())), preferred_element_type=F32).astype(BF16)
    tall = cols * SUB
    key_of = iota((tall, cols), 0) // SUB == iota((tall, cols), 1)
    open_key = dot_nt(key_of.astype(BF16), jnp.broadcast_to(mask[...], (LANES, cols)).astype(BF16)) > 0.5
    picked = (iota((cols, tall), 1) // SUB == iota((cols, tall), 0)).astype(BF16)
    row = iota((tall, LANES), 0)
    mine = iota((tall, LANES), 1) % SUB == row % SUB
    apart = offs[1] + row // SUB - offs[0] - row % SUB
    for g in range(rows // SUB):
        x = normed[:, g * SUB : (g + 1) * SUB].reshape(tall, chans).astype(BF16)
        raw = jnp.where(open_key | (apart == g * SUB), dot(x, wide), -30000.0)
        raw = jnp.where(mine, raw, 0.0).astype(BF16)
        out[:, g * LANES : (g + 1) * LANES] = dot(picked, raw).astype(BF16)


def pair_bias(offs, pair_cond, token_mask, pair_weight):
    rows, cols, chans = pair_cond.shape
    vmem = pl.BlockSpec(memory_space=pltpu.VMEM)
    return pl.pallas_call(
        bias_kernel,
        out_shape=jax.ShapeDtypeStruct((cols, rows * HEADS), BF16),
        in_specs=[pl.BlockSpec(memory_space=pltpu.SMEM), vmem, vmem, vmem],
        out_specs=vmem,
        scratch_shapes=[pltpu.VMEM((cols, rows, chans), F32)],
        compiler_params=pltpu.CompilerParams(vmem_limit_bytes=VMEM_LIMIT),
        cost_estimate=pl.CostEstimate(flops=200_000_000, bytes_accessed=800_000, transcendentals=0),
        name="pair_bias",
    )(offs, jnp.transpose(pair_cond, (1, 0, 2)), token_mask.reshape(1, cols), pair_weight.T)


def exchange_all(block, axis):
    devices = lax.axis_size(axis)
    held = block[None]
    far = devices // 2
    while far > 1:
        got = lax.ppermute(held, axis, [(i, i ^ far) for i in range(devices)])
        held = jnp.concatenate([held, got], axis=0)
        far //= 2
    return held, lax.ppermute(held, axis, [(i, i ^ 1) for i in range(devices)])


def atom_kernel(
    offs, feat, before, after, token, wq, wk, wv, wo, agg, gain, token_in, token_norm, qs, ks, vs, mixed
):
    atoms, chans = feat.shape[1:]
    rows = token_in.shape[1]
    wqkv = jnp.concatenate([wq[...], wk[...], wv[...]], axis=1)
    wkv = wqkv[:, chans:]
    for ref, at in ((before, 0), (after, RIM + atoms)):
        kv = dot(layer_norm(ref[0].astype(F32)).astype(BF16), wkv).astype(BF16)
        ks[at : at + RIM] = kv[:, :chans]
        vs[at : at + RIM] = kv[:, chans:]
    for c in range(0, atoms, 128):
        qkv = dot(layer_norm(feat[0, c : c + 128].astype(F32)).astype(BF16), wqkv).astype(BF16)
        qs[c : c + 128] = qkv[:, :chans]
        ks[RIM + c : RIM + c + 128] = qkv[:, chans : 2 * chans]
        vs[RIM + c : RIM + c + 128] = qkv[:, 2 * chans :]
    rate = math.log2(math.e) / AHEAD_DIM**0.5
    head_of = iota((QWIN, chans), 1) // AHEAD_DIM
    windows = atoms // QWIN
    keyat = iota((AHEADS * QWIN, KWIN), 1)
    batch = 2

    def score(first):
        out = []
        for at in range(first * QWIN, (first + batch) * QWIN, QWIN):
            q = qs[at : at + QWIN]
            q = jnp.concatenate([jnp.where(head_of == h, q, jnp.zeros_like(q)) for h in range(AHEADS)], axis=0)
            s = dot_nt(q, ks[at : at + KWIN])
            if at < RIM:
                s = jnp.where((offs[2] == 1) & (keyat < RIM - at), -jnp.inf, s)
            if at + KWIN > RIM + atoms:
                s = jnp.where((offs[3] == 1) & (keyat >= RIM + atoms - at), -jnp.inf, s)
            out.append(s)
        return first, jnp.concatenate(out, axis=0)

    def soften(item):
        first, s = item
        e = jnp.exp2((s - jnp.max(s, -1, keepdims=True)) * rate)
        return first, e.astype(BF16), 1.0 / jnp.sum(e, -1, keepdims=True)

    def mix(item):
        first, e, share = item
        tall = AHEADS * QWIN
        for i in range(batch):
            at = (first + i) * QWIN
            o = dot(e[i * tall : (i + 1) * tall], vs[at : at + KWIN]) * share[i * tall : (i + 1) * tall]
            acc = o[:QWIN]
            for h in range(1, AHEADS):
                acc = jnp.where(head_of == h, o[h * QWIN : (h + 1) * QWIN], acc)
            mixed[at : at + QWIN] = acc.astype(BF16)

    skewed(range(0, windows, batch), [score, soften, mix])
    local = token[...] - offs[0]
    step = 384
    tsum = jnp.zeros((rows, agg.shape[1]), F32)
    count = jnp.zeros((rows, 1), F32)
    for c in range(0, atoms, step):
        out = (feat[0, c : c + step].astype(F32) + dot(mixed[c : c + step], wo[...])).astype(BF16)
        hidden = jnp.maximum(dot(out, agg[...]), 0.0).astype(BF16)
        onehot = (iota((rows, step), 0) == local[:, c : c + step]).astype(F32)
        count = count + jnp.sum(onehot, -1, keepdims=True)
        tsum = tsum + dot(onehot.astype(BF16), hidden)
    tin = tsum / count
    token_in[0] = tin
    token_norm[0] = (layer_norm(tin) * gain[...]).astype(BF16)


def atom_stage(offs, feat, before, after, token, wq, wk, wv, wo, agg, gain, rows):
    samples, atoms, chans = feat.shape
    width = agg.shape[1]

    def per_sample(*tail):
        return pl.BlockSpec((1, *tail), lambda s: (s, 0, 0))

    def whole(*shape):
        return pl.BlockSpec(shape, lambda s: (0,) * len(shape))

    return pl.pallas_call(
        atom_kernel,
        grid=(samples,),
        out_shape=[
            jax.ShapeDtypeStruct((samples, rows, width), F32),
            jax.ShapeDtypeStruct((samples, rows, width), BF16),
        ],
        in_specs=[
            pl.BlockSpec(memory_space=pltpu.SMEM),
            per_sample(atoms, chans),
            per_sample(RIM, chans),
            per_sample(RIM, chans),
            whole(1, atoms),
            whole(chans, chans),
            whole(chans, chans),
            whole(chans, chans),
            whole(chans, chans),
            whole(chans, width),
            whole(1, width),
        ],
        out_specs=[per_sample(rows, width), per_sample(rows, width)],
        scratch_shapes=[
            pltpu.VMEM((atoms, chans), BF16),
            pltpu.VMEM((atoms + 2 * RIM, chans), BF16),
            pltpu.VMEM((atoms + 2 * RIM, chans), BF16),
            pltpu.VMEM((atoms, chans), BF16),
        ],
        compiler_params=pltpu.CompilerParams(vmem_limit_bytes=VMEM_LIMIT),
        cost_estimate=pl.CostEstimate(flops=8_000_000_000, bytes_accessed=2_000_000, transcendentals=1_200_000),
        name="atom_stage",
    )(offs, feat, before, after, token.reshape(1, atoms), wq, wk, wv, wo, agg, gain.reshape(1, width))


def head_groups(width):
    groups = []
    for base in range(0, width, 8 * HEAD_DIM):
        first = base // HEAD_DIM
        groups.append((base, range(first, first + 5)))
        groups.append((base + LANES, range(first + 5, first + 8)))
    return groups


def token_kernel(offs, norm_all, norm_own, token_in, near, far, wq, wk, wv, wg, wo, out, bt, bs, ks, vs, wbuf, sems):
    blocks, samples, rows, width = norm_all.shape
    keys = blocks * rows
    copies = [pltpu.make_async_copy(w, wbuf.at[i], sems.at[i]) for i, w in enumerate((wk, wv, wq, wg, wo))]
    for copy in copies:
        copy.start()
    half, cols, _ = near.shape
    for j in range(2 * half):
        apart = offs[4] ^ j
        place = sum(((apart // (half >> i)) % 2) * 2**i for i in range(half.bit_length() - 1))
        block = jnp.where(apart % 2 == 0, near[place], far[place])
        bt[j * cols : (j + 1) * cols] = block.astype(F32)
    for g in range(rows // SUB):
        turned = bt[:, g * LANES : (g + 1) * LANES].T
        for h in range(HEADS):
            bs[h * rows + g * SUB : h * rows + (g + 1) * SUB] = turned[h * SUB : (h + 1) * SUB]
    x_all = jnp.concatenate(
        [norm_all[j, s].astype(F32) for s in range(samples) for j in range(blocks)], axis=0
    ).astype(BF16)
    copies[0].wait()
    ks[...] = dot(x_all, wbuf[0]).astype(BF16)
    copies[1].wait()
    vs[...] = dot(x_all, wbuf[1]).astype(BF16)
    x_own = jnp.concatenate([norm_own[s].astype(F32) for s in range(samples)], axis=0).astype(BF16)
    copies[2].wait()
    q_own = dot(x_own, wbuf[2]).astype(BF16).astype(F32)
    copies[3].wait()
    gate = jax.nn.sigmoid(dot(x_own, wbuf[3]))
    scale = 1.0 / HEAD_DIM**0.5
    lane = iota((rows, 2 * LANES), 1)
    gated = []
    work = [(s, base, h) for s in range(samples) for base, heads in head_groups(width) for h in heads]

    def score(item):
        s, base, h = item
        low = h * HEAD_DIM - base
        mine = (lane >= low) & (lane < low + HEAD_DIM)
        q = q_own[s * rows : (s + 1) * rows, base : base + 2 * LANES]
        k = ks[s * keys : (s + 1) * keys, base : base + 2 * LANES]
        sc = dot_nt(jnp.where(mine, q, 0.0).astype(BF16), k)
        return item, sc * scale + bs[h * rows : (h + 1) * rows]

    def soften(item):
        place, sc = item
        e = jnp.exp(sc - jnp.max(sc, -1, keepdims=True))
        return place, e.astype(BF16), 1.0 / jnp.sum(e, -1, keepdims=True)

    mixes = {}

    def mix(item):
        (s, base, h), e, share = item
        low = h * HEAD_DIM - base
        mine = (lane >= low) & (lane < low + HEAD_DIM)
        o = dot(e, vs[s * keys : (s + 1) * keys, base : base + 2 * LANES]) * share
        mixes[s, base] = jnp.where(mine, o, mixes.get((s, base), 0.0))

    skewed(work, [score, soften, mix])
    gated = []
    for s in range(samples):
        tiles = {}
        for base, _ in head_groups(width):
            for t in range(2):
                at = base + t * LANES
                part = mixes[s, base][:, t * LANES : (t + 1) * LANES]
                tiles[at] = tiles[at] + part if at in tiles else part
        whole = jnp.concatenate([tiles[at] for at in range(0, width, LANES)], axis=1)
        gated.append(whole * gate[s * rows : (s + 1) * rows])
    copies[4].wait()
    res = dot(jnp.concatenate(gated, axis=0).astype(BF16), wbuf[4])
    for s in range(samples):
        out[s] = (token_in[s] + res[s * rows : (s + 1) * rows]).astype(BF16)


def token_stage(offs, norm_all, norm_own, token_in, near, far, wq, wk, wv, wg, wo):
    blocks, samples, rows, width = norm_all.shape
    keys = blocks * rows
    vmem = pl.BlockSpec(memory_space=pltpu.VMEM)
    hbm = pl.BlockSpec(memory_space=pl.ANY)
    return pl.pallas_call(
        token_kernel,
        out_shape=jax.ShapeDtypeStruct((samples, rows, width), BF16),
        in_specs=[pl.BlockSpec(memory_space=pltpu.SMEM)] + [vmem] * 5 + [hbm] * 5,
        out_specs=vmem,
        scratch_shapes=[
            pltpu.VMEM((keys, rows * HEADS), F32),
            pltpu.VMEM((rows * HEADS, keys), F32),
            pltpu.VMEM((samples * keys, width), BF16),
            pltpu.VMEM((samples * keys, width), BF16),
            pltpu.VMEM((5, width, width), BF16),
            pltpu.SemaphoreType.DMA((5,)),
        ],
        compiler_params=pltpu.CompilerParams(vmem_limit_bytes=VMEM_LIMIT),
        cost_estimate=pl.CostEstimate(flops=5_000_000_000, bytes_accessed=9_000_000, transcendentals=700_000),
        name="token_stage",
    )(offs, norm_all, norm_own, token_in, near, far, wq, wk, wv, wg, wo)


def shards(
    atom_feat,
    atom_token,
    pair_cond,
    token_mask,
    atom_wq,
    atom_wk,
    atom_wv,
    atom_wo,
    agg_weight,
    pair_weight,
    token_gain,
    query_weight,
    key_weight,
    value_weight,
    gate_weight,
    out_weight,
):
    rows, cols, _ = pair_cond.shape
    atoms = atom_feat.shape[1]
    ranks = lax.axis_size("row")
    rank = lax.axis_index("row")
    offs = jnp.stack(
        [
            rank * rows,
            lax.axis_index("sample") * cols,
            (rank == 0).astype(jnp.int32),
            (rank == ranks - 1).astype(jnp.int32),
            lax.axis_index("sample"),
        ]
    ).astype(jnp.int32)
    up = [(i, i + 1) for i in range(ranks - 1)]
    down = [(j, i) for i, j in up]
    before = lax.ppermute(atom_feat[:, atoms - RIM :], "row", up)
    after = lax.ppermute(atom_feat[:, :RIM], "row", down)
    bias = pair_bias(offs, pair_cond, token_mask, pair_weight)
    near, far = exchange_all(bias, "sample")
    token_in, token_norm = atom_stage(
        offs, atom_feat, before, after, atom_token, atom_wq, atom_wk, atom_wv, atom_wo, agg_weight, token_gain, rows
    )
    norm_all = lax.all_gather(token_norm, "row", axis=0)
    return token_stage(
        offs, norm_all, token_norm, token_in, near, far, query_weight, key_weight, value_weight, gate_weight, out_weight
    )


def solution(mesh):
    placed = (
        P("sample", "row", None),
        P("row"),
        P("row", "sample", None),
        P("sample"),
    ) + (P(),) * 12
    return jax.shard_map(
        shards, mesh=mesh, in_specs=placed, out_specs=P("sample", "row", None), check_vma=False
    )
```

```python
import functools
import math

import jax
import jax.numpy as jnp
from jax import lax
from jax.experimental import pallas as pl
from jax.experimental.pallas import tpu as pltpu
from jax.sharding import PartitionSpec as P

HEADS = 16
HEAD_DIM = 48
AHEADS = 4
AHEAD_DIM = 32
QWIN = 32
KWIN = 128
RIM = (KWIN - QWIN) // 2
LANES = 128
SUB = 8
F32 = jnp.float32
BF16 = jnp.bfloat16
MIB = 1024 * 1024
NT = (((1,), (1,)), ((), ()))


def layer_norm(x):
    mean = jnp.mean(x, -1, keepdims=True)
    centre = x - mean
    var = jnp.mean(centre * centre, -1, keepdims=True)
    return centre * lax.rsqrt(var + 1e-05)


def dot(a, b):
    return jnp.dot(a, b, preferred_element_type=F32)


def dot_nt(a, b):
    return lax.dot_general(a, b, NT, preferred_element_type=F32)


def iota(shape, dim):
    return lax.broadcasted_iota(jnp.int32, shape, dim)


def cost(micros):
    return pl.CostEstimate(flops=micros * 1_100_000_000, bytes_accessed=1_000_000, transcendentals=0)


def inverse(total):
    guess = pl.reciprocal(total, approx=True)
    return guess * (2.0 - total * guess)


def skewed(items, stages):
    held = list(items)
    for t in range(len(held) + len(stages) - 1):
        for k in reversed(range(len(stages))):
            if 0 <= t - k < len(held):
                held[t - k] = stages[k](held[t - k])
    return held


def bias_kernel(pair, mask, weight, out, other, normed):
    cols, rows, chans = pair.shape
    for k in range(cols):
        normed[k] = layer_norm(pair[k].astype(F32))
    spread = (iota((HEADS, LANES), 1) // SUB == iota((HEADS, LANES), 0)).astype(BF16)
    wide = lax.dot_general(weight[...], spread, (((0,), (0,)), ((), ())), preferred_element_type=F32).astype(BF16)
    tall = cols * SUB
    key_of = iota((tall, cols), 0) // SUB == iota((tall, cols), 1)
    open_row = jnp.broadcast_to(mask[...].reshape(1, cols), (LANES, cols)).astype(BF16)
    open_key = dot_nt(key_of.astype(BF16), open_row) > 0.5
    picked = (iota((cols, tall), 1) // SUB == iota((cols, tall), 0)).astype(BF16)
    row = iota((tall, LANES), 0)
    mine = iota((tall, LANES), 1) % SUB == row % SUB
    apart = lax.axis_index("sample") * cols + row // SUB - lax.axis_index("row") * rows - row % SUB
    for g in range(rows // SUB):
        x = normed[:, g * SUB : (g + 1) * SUB].reshape(tall, chans).astype(BF16)
        raw = jnp.where(open_key | (apart == g * SUB), dot(x, wide), -30000.0)
        raw = jnp.where(mine, raw, 0.0).astype(BF16)
        at = g * LANES
        ref, at = (out, at) if at < out.shape[1] else (other, at - out.shape[1])
        ref[:, at : at + LANES] = dot(picked, raw).astype(BF16)


def pair_bias(pair_cond, token_mask, pair_weight):
    rows, cols, chans = pair_cond.shape
    wide = rows * HEADS
    first = (wide // LANES + 1) // 2 * LANES
    vmem = pl.BlockSpec(memory_space=pltpu.VMEM)
    return pl.pallas_call(
        bias_kernel,
        out_shape=[jax.ShapeDtypeStruct((cols, first), BF16), jax.ShapeDtypeStruct((cols, wide - first), BF16)],
        in_specs=[vmem] * 3,
        out_specs=[vmem] * 2,
        scratch_shapes=[pltpu.VMEM((cols, rows, chans), F32)],
        compiler_params=pltpu.CompilerParams(vmem_limit_bytes=16 * MIB),
        cost_estimate=cost(3),
        name="pair_bias",
    )(jnp.transpose(pair_cond, (1, 0, 2)), token_mask, pair_weight.T)


def after(value, *others):
    return lax.optimization_barrier((value, *others))[0]


def swap(held, axis, far):
    return lax.ppermute(held, axis, [(i, i ^ far) for i in range(lax.axis_size(axis))])


def block_of(near, far, bits, me, j):
    apart = me ^ j
    place = sum((apart // bit) % 2 * 2**i for i, bit in enumerate(bits[:-1]))
    return jnp.where((apart // bits[-1]) % 2 == 0, near[place], far[place])


def bits_of(devices):
    return [devices >> i for i in range(1, devices.bit_length())]


def atom_kernel(sample, feat, before, after, wq, wk, wv, mixed, ns, ks, qt, vt):
    atoms, chans = feat.shape[1:]
    rank = lax.axis_index("row")
    at_start = rank == 0
    at_end = rank == lax.axis_size("row") - 1
    ns[:RIM] = layer_norm(before[sample].astype(F32)).astype(BF16)
    for c in range(0, atoms, LANES):
        ns[RIM + c : RIM + c + LANES] = layer_norm(feat[sample, c : c + LANES].astype(F32)).astype(BF16)
    ns[RIM + atoms : 2 * RIM + atoms] = layer_norm(after[sample].astype(F32)).astype(BF16)
    padded = ns.shape[0]
    ns[atoms + 2 * RIM :] = jnp.zeros((padded - atoms - 2 * RIM, chans), BF16)
    wqv = jnp.concatenate([wq[...].astype(F32).T, wv[...].astype(F32).T], axis=0).astype(BF16)
    for c in range(0, padded, LANES):
        normed = ns[c : c + LANES]
        ks[c : c + LANES] = dot(normed, wk[...]).astype(BF16)
        qv = dot(wqv, normed.astype(F32).T.astype(BF16)).astype(BF16)
        qt[:, c : c + LANES] = qv[:chans]
        vt[:, c : c + LANES] = qv[chans:]
    rate = math.log2(math.e) / AHEAD_DIM**0.5
    tall = AHEADS * QWIN
    group = LANES // QWIN
    wide = group * tall
    batch = 2
    keyat = iota((KWIN, tall), 0)
    col = iota((2 * LANES, wide), 1)
    spread = (iota((2 * LANES, wide), 0) == RIM + col // tall * QWIN + col % QWIN).astype(BF16)
    row = iota((wide, LANES), 0)
    fold = (iota((wide, LANES), 1) == row // tall * QWIN + row % QWIN).astype(BF16)
    own_head = iota((chans, wide), 0) // AHEAD_DIM == iota((chans, wide), 1) % tall // QWIN
    queries, sums = {}, {}

    def score(first):
        base = first // LANES * LANES
        if base not in queries:
            queries[base] = jnp.where(own_head, dot(qt[:, base : base + 2 * LANES], spread), 0.0).astype(BF16)
        out = []
        for at in range(first, first + batch * QWIN, QWIN):
            col = (at - base) // QWIN * tall
            s = dot(ks[at : at + KWIN], queries[base][:, col : col + tall])
            if at < RIM:
                s = jnp.where(at_start & (keyat < RIM - at), -jnp.inf, s)
            if at + KWIN > RIM + atoms:
                s = jnp.where(at_end & (keyat >= RIM + atoms - at), -jnp.inf, s)
            out.append(s)
        return first, out

    def soften(item):
        first, scores = item
        out = []
        for s in scores:
            e = jnp.exp2((s - jnp.max(s, 0, keepdims=True)) * rate)
            out.append((e.astype(BF16), 1.0 / jnp.sum(e, 0, keepdims=True)))
        return first, out

    def mix(item):
        first, parts = item
        base = first // LANES * LANES
        for i, (e, share) in enumerate(parts):
            skip = first + i * QWIN - base
            pads = [jnp.zeros((n, tall), BF16) for n in (skip, 2 * LANES - KWIN - skip)]
            e = jnp.concatenate([p for p in (pads[0], e, pads[1]) if p.shape[0]], axis=0)
            o = dot(vt[:, base : base + 2 * LANES], e) * share
            sums.setdefault(base, []).append(jnp.where(own_head[:, :tall], o, 0.0).astype(BF16))
        if len(sums[base]) == group:
            mixed[:, base : base + LANES] = dot(jnp.concatenate(sums[base], axis=1), fold).astype(BF16)

    skewed(range(0, atoms, batch * QWIN), [score, soften, mix])


def atom_attention(sample, feat, before, after, wq, wk, wv):
    atoms, chans = feat.shape[1:]
    padded = pl.cdiv(atoms + 2 * RIM, LANES) * LANES
    vmem = pl.BlockSpec(memory_space=pltpu.VMEM)
    return pl.pallas_call(
        functools.partial(atom_kernel, sample),
        out_shape=jax.ShapeDtypeStruct((chans, atoms), BF16),
        in_specs=[vmem] * 6,
        out_specs=vmem,
        scratch_shapes=[
            pltpu.VMEM((padded, chans), BF16),
            pltpu.VMEM((padded, chans), BF16),
            pltpu.VMEM((chans, padded), BF16),
            pltpu.VMEM((chans, padded), BF16),
        ],
        compiler_params=pltpu.CompilerParams(vmem_limit_bytes=16 * MIB),
        cost_estimate=cost(4),
        name="atom_attention",
    )(feat, before, after, wq, wk, wv)


def gather_kernel(sample, mixed, feat, token, wo, agg, gain, token_in, token_norm):
    atoms = feat.shape[1]
    rows = token_in.shape[0]
    wo_turned = wo[...].astype(F32).T.astype(BF16)
    local = token[...].reshape(1, atoms) - lax.axis_index("row") * rows
    step = 384
    tsum = jnp.zeros((rows, agg.shape[1]), F32)
    count = jnp.zeros((rows, 1), F32)
    for c in range(0, atoms, step):
        out = (feat[sample, c : c + step].astype(F32) + dot(wo_turned, mixed[:, c : c + step]).T).astype(BF16)
        hidden = jnp.maximum(dot(out, agg[...]), 0.0).astype(BF16)
        onehot = (iota((rows, step), 0) == local[:, c : c + step]).astype(F32)
        count = count + jnp.sum(onehot, -1, keepdims=True)
        tsum = tsum + dot(onehot.astype(BF16), hidden)
    tin = tsum / count
    token_in[...] = tin
    token_norm[...] = (layer_norm(tin) * gain[...].reshape(1, -1)).astype(BF16)


def gather_tokens(sample, mixed, feat, token, wo, agg, gain, rows):
    width = agg.shape[1]
    vmem = pl.BlockSpec(memory_space=pltpu.VMEM)
    return pl.pallas_call(
        functools.partial(gather_kernel, sample),
        out_shape=[jax.ShapeDtypeStruct((rows, width), F32), jax.ShapeDtypeStruct((rows, width), BF16)],
        in_specs=[vmem] * 6,
        out_specs=[vmem, vmem],
        compiler_params=pltpu.CompilerParams(vmem_limit_bytes=16 * MIB),
        cost_estimate=cost(1),
        name="gather_tokens",
    )(mixed, feat, token, wo, agg, gain)


def turn_kernel(orders, *refs):
    *halves, out, tall = refs
    rows = out.shape[0] // HEADS
    me = lax.axis_index("sample")
    at = 0
    for near, far, bits in zip(halves[::2], halves[1::2], orders):
        half, cols, wide = near.shape
        for j in range(2 * half):
            tall[j * cols : (j + 1) * cols, at : at + wide] = block_of(near, far, bits, me, j).astype(F32)
        at += wide
    for g in range(rows // SUB):
        turned = tall[:, g * LANES : (g + 1) * LANES].T
        for h in range(HEADS):
            out[h * rows + g * SUB : h * rows + (g + 1) * SUB] = turned[h * SUB : (h + 1) * SUB]


def turn_bias(orders, halves):
    half, cols, _ = halves[0].shape
    keys = 2 * half * cols
    wide = sum(near.shape[2] for near in halves[::2])
    vmem = pl.BlockSpec(memory_space=pltpu.VMEM)
    return pl.pallas_call(
        functools.partial(turn_kernel, orders),
        out_shape=jax.ShapeDtypeStruct((wide, keys), F32),
        in_specs=[vmem] * len(halves),
        out_specs=vmem,
        scratch_shapes=[pltpu.VMEM((keys, wide), F32)],
        compiler_params=pltpu.CompilerParams(vmem_limit_bytes=24 * MIB),
        cost_estimate=cost(1),
        name="turn_bias",
    )(*halves)


def head_groups(width):
    groups = []
    for base in range(0, width, 8 * HEAD_DIM):
        first = base // HEAD_DIM
        groups.append((base, range(first, first + 5)))
        groups.append((base + LANES, range(first + 5, first + 8)))
    return groups


def project_kernel(near, far, wq, wk, wv, wg, q, kt, v, gate):
    half, rows, width = near.shape
    me = lax.axis_index("row")
    x = jnp.concatenate([block_of(near, far, bits_of(2 * half), me, j).astype(F32) for j in range(2 * half)], axis=0).astype(BF16)
    own = near[0]
    q[...] = dot(own, wq[...]).astype(BF16)
    gate[...] = jax.nn.sigmoid(dot(own, wg[...]))
    for c in range(0, width, 2 * LANES):
        kt[c : c + 2 * LANES] = dot(x, wk[:, c : c + 2 * LANES]).T.astype(BF16)
    v[...] = dot(x, wv[...]).astype(BF16)


def project(near, far, wq, wk, wv, wg):
    half, rows, width = near.shape
    keys = 2 * half * rows
    vmem = pl.BlockSpec(memory_space=pltpu.VMEM)
    return pl.pallas_call(
        project_kernel,
        out_shape=[
            jax.ShapeDtypeStruct((rows, width), BF16),
            jax.ShapeDtypeStruct((width, keys), BF16),
            jax.ShapeDtypeStruct((keys, width), BF16),
            jax.ShapeDtypeStruct((rows, width), F32),
        ],
        in_specs=[vmem] * 6,
        out_specs=[vmem] * 4,
        compiler_params=pltpu.CompilerParams(vmem_limit_bytes=24 * MIB),
        cost_estimate=cost(2),
        name="project",
    )(near, far, wq, wk, wv, wg)


def attend_kernel(q, kt, v, gate, token_in, bias, wo, *rest):
    *earlier, out = rest
    rows, width = token_in.shape
    scale = 1.0 / HEAD_DIM**0.5
    lane = iota((rows, 2 * LANES), 1)
    work = [(base, h) for base, heads in head_groups(width) for h in heads]

    def channels(base, h):
        low = h * HEAD_DIM - base
        return (lane >= low) & (lane < low + HEAD_DIM)

    def score(item):
        base, h = item
        mine = q[:, base : base + 2 * LANES]
        mine = jnp.where(channels(base, h), mine, jnp.zeros_like(mine))
        return item, dot(mine, kt[base : base + 2 * LANES]) * scale + bias[h * rows : (h + 1) * rows]

    def soften(item):
        place, sc = item
        e = jnp.exp(sc - jnp.max(sc, -1, keepdims=True))
        return place, e.astype(BF16), inverse(jnp.sum(e, -1, keepdims=True))

    mixes = {}

    def mix(item):
        (base, h), e, share = item
        o = dot(e, v[:, base : base + 2 * LANES]) * share
        mixes[base] = jnp.where(channels(base, h), o, mixes.get(base, 0.0))

    skewed(work, [score, soften, mix])
    tiles = {}
    for base, _ in head_groups(width):
        for t in range(2):
            at = base + t * LANES
            part = mixes[base][:, t * LANES : (t + 1) * LANES]
            tiles[at] = tiles[at] + part if at in tiles else part
    gated = jnp.concatenate([tiles[at] for at in range(0, width, LANES)], axis=1) * gate[...]
    res = (token_in[...] + dot(gated.astype(BF16), wo[...])).astype(BF16)
    if earlier:
        for s, ref in enumerate(earlier):
            out[s] = ref[...]
        out[len(earlier)] = res
    else:
        out[...] = res


def attend(q, kt, v, gate, token_in, bias, wo, earlier):
    rows, width = token_in.shape
    vmem = pl.BlockSpec(memory_space=pltpu.VMEM)
    shape = (len(earlier) + 1, rows, width) if earlier else (rows, width)
    return pl.pallas_call(
        attend_kernel,
        out_shape=jax.ShapeDtypeStruct(shape, BF16),
        in_specs=[vmem] * (7 + len(earlier)),
        out_specs=vmem,
        compiler_params=pltpu.CompilerParams(vmem_limit_bytes=24 * MIB),
        cost_estimate=cost(3),
        name="attend",
    )(q, kt, v, gate, token_in, bias, wo, *earlier)


def shards(
    atom_feat,
    atom_token,
    pair_cond,
    token_mask,
    atom_wq,
    atom_wk,
    atom_wv,
    atom_wo,
    agg_weight,
    pair_weight,
    token_gain,
    query_weight,
    key_weight,
    value_weight,
    gate_weight,
    out_weight,
):
    samples, atoms, _ = atom_feat.shape
    rows = pair_cond.shape[0]
    ranks = lax.axis_size("row")
    up = [(i, i + 1) for i in range(ranks - 1)]
    down = [(j, i) for i, j in up]
    before = lax.ppermute(atom_feat[:, atoms - RIM :], "row", up)
    behind = lax.ppermute(atom_feat[:, :RIM], "row", down)
    bits = bits_of(lax.axis_size("sample"))
    orders = [bits, bits[-1:] + bits[:-1]]
    held = [part[None] for part in pair_bias(pair_cond, token_mask, pair_weight)]

    def wider(step, *others):
        got = after([swap(h, "sample", order[step]) for h, order in zip(held, orders)], *others)
        return [jnp.concatenate([h, g], axis=0) for h, g in zip(held, got)]

    row_bits = bits_of(ranks)
    norms, inputs = [], []
    step = 0
    for s in range(samples):
        mixed = atom_attention(s, atom_feat, before, behind, atom_wq, atom_wk, atom_wv)
        if step < len(bits) - 1:
            held = wider(step, mixed)
            step += 1
            mixed = after(mixed, held)
        if s:
            norms[-1] = jnp.concatenate([norms[-1], after(swap(norms[-1], "row", row_bits[0]), mixed)], axis=0)
            mixed = after(mixed, norms[-1])
        token_in, token_norm = gather_tokens(s, mixed, atom_feat, atom_token, atom_wo, agg_weight, token_gain, rows)
        inputs.append(token_in)
        norms.append(token_norm[None])
        before = after(before, token_norm)
    while step < len(bits) - 1:
        held = wider(step)
        step += 1
    halves = []
    for h, order in zip(held, orders):
        halves += [h, swap(h, "sample", order[-1])]
    parts = []
    for s in range(samples):
        near = norms[s]
        for i, far in enumerate(row_bits[:-1]):
            if near.shape[0] == 1 << i:
                got = swap(near, "row", far)
                near = jnp.concatenate([near, after(got, *parts[-1]) if parts else got], axis=0)
        norms[s] = near
        if s == samples - 1:
            halves = after(halves, near)
            bias = turn_bias(orders, halves)
        parts.append(project(near, swap(near, "row", row_bits[-1]), query_weight, key_weight, value_weight, gate_weight))
    done = []
    for s, part in enumerate(parts):
        earlier = done if s == samples - 1 else []
        done.append(attend(*part, inputs[s], bias, out_weight, earlier))
    return done[-1]


def solution(mesh):
    placed = (
        P("sample", "row", None),
        P("row"),
        P("row", "sample", None),
        P("sample"),
    ) + (P(),) * 12
    return jax.shard_map(
        shards, mesh=mesh, in_specs=placed, out_specs=P("sample", "row", None), check_vma=False
    )
```

```python
import functools
import math

import jax
import jax.numpy as jnp
from jax import lax
from jax.experimental import pallas as pl
from jax.experimental.pallas import tpu as pltpu
from jax.sharding import PartitionSpec as P

HEADS = 16
HEAD_DIM = 48
AHEADS = 4
AHEAD_DIM = 32
QWIN = 32
KWIN = 128
RIM = (KWIN - QWIN) // 2
LANES = 128
SUB = 8
F32 = jnp.float32
BF16 = jnp.bfloat16
MIB = 1024 * 1024
NT = (((1,), (1,)), ((), ()))


def layer_norm(x):
    mean = jnp.mean(x, -1, keepdims=True)
    centre = x - mean
    var = jnp.mean(centre * centre, -1, keepdims=True)
    return centre * lax.rsqrt(var + 1e-05)


def dot(a, b):
    return jnp.dot(a, b, preferred_element_type=F32)


def dot_nt(a, b):
    return lax.dot_general(a, b, NT, preferred_element_type=F32)


def iota(shape, dim):
    return lax.broadcasted_iota(jnp.int32, shape, dim)


def cost(micros):
    return pl.CostEstimate(flops=micros * 1_100_000_000, bytes_accessed=1_000_000, transcendentals=0)


def inverse(total):
    guess = pl.reciprocal(total, approx=True)
    return guess * (2.0 - total * guess)


def skewed(items, stages):
    held = list(items)
    for t in range(len(held) + len(stages) - 1):
        for k in reversed(range(len(stages))):
            if 0 <= t - k < len(held):
                held[t - k] = stages[k](held[t - k])
    return held


def bias_kernel(feat, pair_hbm, mask_hbm, weight_hbm, out, first, last, pair, mask, weight, normed, sems):
    cols, rows, chans = pair.shape
    atoms = feat.shape[1]
    moves = [
        (weight_hbm, weight),
        (mask_hbm, mask),
        (feat.at[:, :RIM], first),
        (feat.at[:, atoms - RIM :], last),
    ]
    step = cols // 4
    moves += [(pair_hbm.at[k : k + step], pair.at[k : k + step]) for k in range(0, cols, step)]
    copies = [pltpu.make_async_copy(src, dst, sems.at[i]) for i, (src, dst) in enumerate(moves)]
    for copy in copies:
        copy.start()
    for i, copy in enumerate(copies[4:]):
        copy.wait()
        for k in range(i * step, (i + 1) * step):
            normed[k] = layer_norm(pair[k].astype(F32))
    for copy in copies[:4]:
        copy.wait()
    spread = (iota((HEADS, LANES), 1) // SUB == iota((HEADS, LANES), 0)).astype(BF16)
    wide = lax.dot_general(weight[...], spread, (((0,), (0,)), ((), ())), preferred_element_type=F32).astype(BF16)
    tall = cols * SUB
    key_of = iota((tall, cols), 0) // SUB == iota((tall, cols), 1)
    open_row = jnp.broadcast_to(mask[...].reshape(1, cols), (LANES, cols)).astype(BF16)
    open_key = dot_nt(key_of.astype(BF16), open_row) > 0.5
    picked = (iota((cols, tall), 1) // SUB == iota((cols, tall), 0)).astype(BF16)
    row = iota((tall, LANES), 0)
    mine = iota((tall, LANES), 1) % SUB == row % SUB
    apart = lax.axis_index("sample") * cols + row // SUB - lax.axis_index("row") * rows - row % SUB
    for g in range(rows // SUB):
        x = normed[:, g * SUB : (g + 1) * SUB].reshape(tall, chans).astype(BF16)
        raw = jnp.where(open_key | (apart == g * SUB), dot(x, wide), -30000.0)
        raw = jnp.where(mine, raw, 0.0).astype(BF16)
        out[:, g * LANES : (g + 1) * LANES] = dot(picked, raw).astype(BF16)


def pair_bias(feat, pair_cond, token_mask, pair_weight):
    rows, cols, chans = pair_cond.shape
    edge = (feat.shape[0], RIM, feat.shape[2])
    hbm = pl.BlockSpec(memory_space=pltpu.HBM)
    return pl.pallas_call(
        bias_kernel,
        out_shape=[
            jax.ShapeDtypeStruct((cols, rows * HEADS), BF16),
            jax.ShapeDtypeStruct(edge, BF16),
            jax.ShapeDtypeStruct(edge, BF16),
        ],
        in_specs=[hbm] * 4,
        out_specs=[pl.BlockSpec(memory_space=pltpu.VMEM)] * 3,
        scratch_shapes=[
            pltpu.VMEM((cols, rows, chans), BF16),
            pltpu.VMEM((cols,), jnp.int32),
            pltpu.VMEM((HEADS, chans), BF16),
            pltpu.VMEM((cols, rows, chans), F32),
            pltpu.SemaphoreType.DMA((8,)),
        ],
        compiler_params=pltpu.CompilerParams(vmem_limit_bytes=60 * MIB),
        cost_estimate=cost(3),
        name="pair_bias",
    )(feat, jnp.transpose(pair_cond, (1, 0, 2)), token_mask, pair_weight.T)


def after(value, *others):
    return lax.optimization_barrier((value, *others))[0]


def swap(held, axis, far):
    return lax.ppermute(held, axis, [(i, i ^ far) for i in range(lax.axis_size(axis))])


def block_of(near, far, bits, me, j):
    apart = me ^ j
    place = sum((apart // bit) % 2 * 2**i for i, bit in enumerate(bits[:-1]))
    return jnp.where((apart // bits[-1]) % 2 == 0, near[place], far[place])


def bits_of(devices):
    return [devices >> i for i in range(1, devices.bit_length())]


def atom_kernel(sample, feat, before, after, wq, wk, wv, mixed, qs, ks, vs):
    atoms, chans = feat.shape[1:]
    rank = lax.axis_index("row")
    at_start = rank == 0
    at_end = rank == lax.axis_size("row") - 1
    wqkv = jnp.concatenate([wq[...], wk[...], wv[...]], axis=1)
    for ref, at in ((before, 0), (after, RIM + atoms)):
        kv = dot(layer_norm(ref[sample].astype(F32)).astype(BF16), wqkv[:, chans:]).astype(BF16)
        ks[at : at + RIM] = kv[:, :chans]
        vs[at : at + RIM] = kv[:, chans:]
    for c in range(0, atoms, LANES):
        qkv = dot(layer_norm(feat[sample, c : c + LANES].astype(F32)).astype(BF16), wqkv).astype(BF16)
        qs[c : c + LANES] = qkv[:, :chans]
        ks[RIM + c : RIM + c + LANES] = qkv[:, chans : 2 * chans]
        vs[RIM + c : RIM + c + LANES] = qkv[:, 2 * chans :]
    rate = math.log2(math.e) / AHEAD_DIM**0.5
    tall = AHEADS * QWIN
    head_of = iota((QWIN, chans), 1) // AHEAD_DIM
    keyat = iota((tall, KWIN), 1)
    batch = 2

    def score(first):
        out = []
        for at in range(first, first + batch * QWIN, QWIN):
            q = qs[at : at + QWIN]
            q = jnp.concatenate([jnp.where(head_of == h, q, jnp.zeros_like(q)) for h in range(AHEADS)], axis=0)
            s = dot_nt(q, ks[at : at + KWIN])
            if at < RIM:
                s = jnp.where(at_start & (keyat < RIM - at), -jnp.inf, s)
            if at + KWIN > RIM + atoms:
                s = jnp.where(at_end & (keyat >= RIM + atoms - at), -jnp.inf, s)
            out.append(s)
        return first, jnp.concatenate(out, axis=0)

    def soften(item):
        first, s = item
        e = jnp.exp2((s - jnp.max(s, -1, keepdims=True)) * rate)
        return first, e.astype(BF16), inverse(jnp.sum(e, -1, keepdims=True))

    def mix(item):
        first, e, share = item
        for i in range(batch):
            at = first + i * QWIN
            o = dot(e[i * tall : (i + 1) * tall], vs[at : at + KWIN]) * share[i * tall : (i + 1) * tall]
            acc = o[:QWIN]
            for h in range(1, AHEADS):
                acc = jnp.where(head_of == h, o[h * QWIN : (h + 1) * QWIN], acc)
            mixed[at : at + QWIN] = acc.astype(BF16)

    skewed(range(0, atoms, batch * QWIN), [score, soften, mix])


def atom_attention(sample, feat, before, after, wq, wk, wv):
    atoms, chans = feat.shape[1:]
    vmem = pl.BlockSpec(memory_space=pltpu.VMEM)
    return pl.pallas_call(
        functools.partial(atom_kernel, sample),
        out_shape=jax.ShapeDtypeStruct((atoms, chans), BF16),
        in_specs=[vmem] * 6,
        out_specs=vmem,
        scratch_shapes=[
            pltpu.VMEM((atoms, chans), BF16),
            pltpu.VMEM((atoms + 2 * RIM, chans), BF16),
            pltpu.VMEM((atoms + 2 * RIM, chans), BF16),
        ],
        compiler_params=pltpu.CompilerParams(vmem_limit_bytes=16 * MIB),
        cost_estimate=cost(4),
        name="atom_attention",
    )(feat, before, after, wq, wk, wv)


def gather_kernel(sample, mixed, feat, token, wo, agg, gain, token_in, token_norm):
    atoms = feat.shape[1]
    rows = token_in.shape[0]
    local = token[...].reshape(1, atoms) - lax.axis_index("row") * rows
    step = 384
    tsum = jnp.zeros((rows, agg.shape[1]), F32)
    count = jnp.zeros((rows, 1), F32)
    for c in range(0, atoms, step):
        out = (feat[sample, c : c + step].astype(F32) + dot(mixed[c : c + step], wo[...])).astype(BF16)
        hidden = jnp.maximum(dot(out, agg[...]), 0.0).astype(BF16)
        onehot = (iota((rows, step), 0) == local[:, c : c + step]).astype(F32)
        count = count + jnp.sum(onehot, -1, keepdims=True)
        tsum = tsum + dot(onehot.astype(BF16), hidden)
    tin = tsum / count
    token_in[...] = tin
    token_norm[...] = (layer_norm(tin) * gain[...].reshape(1, -1)).astype(BF16)


def gather_tokens(sample, mixed, feat, token, wo, agg, gain, rows):
    width = agg.shape[1]
    vmem = pl.BlockSpec(memory_space=pltpu.VMEM)
    return pl.pallas_call(
        functools.partial(gather_kernel, sample),
        out_shape=[jax.ShapeDtypeStruct((rows, width), F32), jax.ShapeDtypeStruct((rows, width), BF16)],
        in_specs=[vmem] * 6,
        out_specs=[vmem, vmem],
        compiler_params=pltpu.CompilerParams(vmem_limit_bytes=16 * MIB),
        cost_estimate=cost(1),
        name="gather_tokens",
    )(mixed, feat, token, wo, agg, gain)


def turn_kernel(orders, *refs):
    *halves, out, tall = refs
    rows = out.shape[0] // HEADS
    me = lax.axis_index("sample")
    at = 0
    for near, far, bits in zip(halves[::2], halves[1::2], orders):
        half, cols, wide = near.shape
        for j in range(2 * half):
            tall[j * cols : (j + 1) * cols, at : at + wide] = block_of(near, far, bits, me, j).astype(F32)
        at += wide
    for g in range(rows // SUB):
        turned = tall[:, g * LANES : (g + 1) * LANES].T
        for h in range(HEADS):
            out[h * rows + g * SUB : h * rows + (g + 1) * SUB] = turned[h * SUB : (h + 1) * SUB]


def turn_bias(orders, halves):
    half, cols, _ = halves[0].shape
    keys = 2 * half * cols
    wide = sum(near.shape[2] for near in halves[::2])
    vmem = pl.BlockSpec(memory_space=pltpu.VMEM)
    return pl.pallas_call(
        functools.partial(turn_kernel, orders),
        out_shape=jax.ShapeDtypeStruct((wide, keys), F32),
        in_specs=[vmem] * len(halves),
        out_specs=vmem,
        scratch_shapes=[pltpu.VMEM((keys, wide), F32)],
        compiler_params=pltpu.CompilerParams(vmem_limit_bytes=24 * MIB),
        cost_estimate=cost(1),
        name="turn_bias",
    )(*halves)


def head_groups(width):
    groups = []
    for base in range(0, width, 8 * HEAD_DIM):
        first = base // HEAD_DIM
        groups.append((base, range(first, first + 5)))
        groups.append((base + LANES, range(first + 5, first + 8)))
    return groups


def project_kernel(near, far, wq, wk, wv, wg, q, kt, v, gate):
    half, rows, width = near.shape
    me = lax.axis_index("row")
    x = jnp.concatenate([block_of(near, far, bits_of(2 * half), me, j).astype(F32) for j in range(2 * half)], axis=0).astype(BF16)
    own = near[0]
    q[...] = dot(own, wq[...]).astype(BF16)
    gate[...] = jax.nn.sigmoid(dot(own, wg[...]))
    for c in range(0, width, 2 * LANES):
        kt[c : c + 2 * LANES] = dot(x, wk[:, c : c + 2 * LANES]).T.astype(BF16)
    v[...] = dot(x, wv[...]).astype(BF16)


def project(near, far, wq, wk, wv, wg):
    half, rows, width = near.shape
    keys = 2 * half * rows
    vmem = pl.BlockSpec(memory_space=pltpu.VMEM)
    return pl.pallas_call(
        project_kernel,
        out_shape=[
            jax.ShapeDtypeStruct((rows, width), BF16),
            jax.ShapeDtypeStruct((width, keys), BF16),
            jax.ShapeDtypeStruct((keys, width), BF16),
            jax.ShapeDtypeStruct((rows, width), F32),
        ],
        in_specs=[vmem] * 6,
        out_specs=[vmem] * 4,
        compiler_params=pltpu.CompilerParams(vmem_limit_bytes=24 * MIB),
        cost_estimate=cost(2),
        name="project",
    )(near, far, wq, wk, wv, wg)


def attend_kernel(q, kt, v, gate, token_in, bias, wo, *rest):
    *earlier, out = rest
    rows, width = token_in.shape
    scale = 1.0 / HEAD_DIM**0.5
    lane = iota((rows, 2 * LANES), 1)
    work = [(base, h) for base, heads in head_groups(width) for h in heads]

    def channels(base, h):
        low = h * HEAD_DIM - base
        return (lane >= low) & (lane < low + HEAD_DIM)

    def score(item):
        base, h = item
        mine = q[:, base : base + 2 * LANES]
        mine = jnp.where(channels(base, h), mine, jnp.zeros_like(mine))
        return item, dot(mine, kt[base : base + 2 * LANES]) * scale + bias[h * rows : (h + 1) * rows]

    def soften(item):
        place, sc = item
        e = jnp.exp(sc - jnp.max(sc, -1, keepdims=True))
        return place, e.astype(BF16), inverse(jnp.sum(e, -1, keepdims=True))

    mixes = {}

    def mix(item):
        (base, h), e, share = item
        o = dot(e, v[:, base : base + 2 * LANES]) * share
        mixes[base] = jnp.where(channels(base, h), o, mixes.get(base, 0.0))

    skewed(work, [score, soften, mix])
    tiles = {}
    for base, _ in head_groups(width):
        for t in range(2):
            at = base + t * LANES
            part = mixes[base][:, t * LANES : (t + 1) * LANES]
            tiles[at] = tiles[at] + part if at in tiles else part
    gated = jnp.concatenate([tiles[at] for at in range(0, width, LANES)], axis=1) * gate[...]
    res = (token_in[...] + dot(gated.astype(BF16), wo[...])).astype(BF16)
    if earlier:
        for s, ref in enumerate(earlier):
            out[s] = ref[...]
        out[len(earlier)] = res
    else:
        out[...] = res


def attend(q, kt, v, gate, token_in, bias, wo, earlier):
    rows, width = token_in.shape
    vmem = pl.BlockSpec(memory_space=pltpu.VMEM)
    shape = (len(earlier) + 1, rows, width) if earlier else (rows, width)
    return pl.pallas_call(
        attend_kernel,
        out_shape=jax.ShapeDtypeStruct(shape, BF16),
        in_specs=[vmem] * (7 + len(earlier)),
        out_specs=vmem,
        compiler_params=pltpu.CompilerParams(vmem_limit_bytes=24 * MIB),
        cost_estimate=cost(3),
        name="attend",
    )(q, kt, v, gate, token_in, bias, wo, *earlier)


def shards(
    atom_feat,
    atom_token,
    pair_cond,
    token_mask,
    atom_wq,
    atom_wk,
    atom_wv,
    atom_wo,
    agg_weight,
    pair_weight,
    token_gain,
    query_weight,
    key_weight,
    value_weight,
    gate_weight,
    out_weight,
):
    samples, atoms, _ = atom_feat.shape
    rows = pair_cond.shape[0]
    ranks = lax.axis_size("row")
    up = [(i, i + 1) for i in range(ranks - 1)]
    down = [(j, i) for i, j in up]
    bias, first, last = pair_bias(atom_feat, pair_cond, token_mask, pair_weight)
    before = lax.ppermute(last, "row", up)
    behind = lax.ppermute(first, "row", down)
    bits = bits_of(lax.axis_size("sample"))
    orders = [bits]
    held = [bias[None]]

    def wider(step, *others):
        got = after([swap(h, "sample", order[step]) for h, order in zip(held, orders)], *others)
        return [jnp.concatenate([h, g], axis=0) for h, g in zip(held, got)]

    row_bits = bits_of(ranks)
    norms, inputs = [], []
    step = 0
    for s in range(samples):
        mixed = atom_attention(s, atom_feat, before, behind, atom_wq, atom_wk, atom_wv)
        if step < len(bits) - 1:
            held = wider(step, mixed)
            step += 1
            mixed = after(mixed, held)
        if s:
            norms[-1] = jnp.concatenate([norms[-1], after(swap(norms[-1], "row", row_bits[0]), mixed)], axis=0)
            mixed = after(mixed, norms[-1])
        token_in, token_norm = gather_tokens(s, mixed, atom_feat, atom_token, atom_wo, agg_weight, token_gain, rows)
        inputs.append(token_in)
        norms.append(token_norm[None])
        before = after(before, token_norm)
    while step < len(bits) - 1:
        held = wider(step)
        step += 1
    halves = []
    for h, order in zip(held, orders):
        halves += [h, swap(h, "sample", order[-1])]
    parts = []
    for s in range(samples):
        near = norms[s]
        for i, far in enumerate(row_bits[:-1]):
            if near.shape[0] == 1 << i:
                got = swap(near, "row", far)
                near = jnp.concatenate([near, after(got, *parts[-1]) if parts else got], axis=0)
        norms[s] = near
        if s == samples - 1:
            halves = after(halves, near)
            bias = turn_bias(orders, halves)
        parts.append(project(near, swap(near, "row", row_bits[-1]), query_weight, key_weight, value_weight, gate_weight))
    done = []
    for s, part in enumerate(parts):
        earlier = done if s == samples - 1 else []
        done.append(attend(*part, inputs[s], bias, out_weight, earlier))
    return done[-1]


def solution(mesh):
    placed = (
        P("sample", "row", None),
        P("row"),
        P("row", "sample", None),
        P("sample"),
    ) + (P(),) * 12
    return jax.shard_map(
        shards, mesh=mesh, in_specs=placed, out_specs=P("sample", "row", None), check_vma=False
    )
```

```python
import functools
import math

import jax
import jax.numpy as jnp
from jax import lax
from jax.experimental import pallas as pl
from jax.experimental.pallas import tpu as pltpu
from jax.sharding import PartitionSpec as P

HEADS = 16
HEAD_DIM = 48
AHEADS = 4
AHEAD_DIM = 32
QWIN = 32
KWIN = 128
RIM = (KWIN - QWIN) // 2
LANES = 128
SUB = 8
F32 = jnp.float32
BF16 = jnp.bfloat16
MIB = 1024 * 1024
NT = (((1,), (1,)), ((), ()))


def layer_norm(x):
    mean = jnp.mean(x, -1, keepdims=True)
    centre = x - mean
    var = jnp.mean(centre * centre, -1, keepdims=True)
    return centre * lax.rsqrt(var + 1e-05)


def dot(a, b):
    return jnp.dot(a, b, preferred_element_type=F32)


def dot_nt(a, b):
    return lax.dot_general(a, b, NT, preferred_element_type=F32)


def iota(shape, dim):
    return lax.broadcasted_iota(jnp.int32, shape, dim)


def cost(micros):
    return pl.CostEstimate(flops=micros * 20_000_000, bytes_accessed=1_000, transcendentals=0)


def inverse(total):
    guess = pl.reciprocal(total, approx=True)
    return guess * (2.0 - total * guess)


def skewed(items, stages):
    held = list(items)
    for t in range(len(held) + len(stages) - 1):
        for k in reversed(range(len(stages))):
            if 0 <= t - k < len(held):
                held[t - k] = stages[k](held[t - k])
    return held


def bias_kernel(head, tail, pair, mask, weight, out, inner, outer, normed):
    odd = lax.axis_index("row") % 2 == 1
    inner[...] = jnp.where(odd, head[...], tail[...])
    outer[...] = jnp.where(odd, tail[...], head[...])
    cols, rows, chans = pair.shape
    for k in range(cols):
        normed[k] = layer_norm(pair[k].astype(F32))
    spread = (iota((HEADS, LANES), 1) // SUB == iota((HEADS, LANES), 0)).astype(BF16)
    wide = lax.dot_general(weight[...], spread, (((0,), (0,)), ((), ())), preferred_element_type=F32).astype(BF16)
    tall = cols * SUB
    key_of = iota((tall, cols), 0) // SUB == iota((tall, cols), 1)
    open_row = jnp.broadcast_to(mask[...].reshape(1, cols), (LANES, cols)).astype(BF16)
    open_key = dot_nt(key_of.astype(BF16), open_row) > 0.5
    picked = (iota((cols, tall), 1) // SUB == iota((cols, tall), 0)).astype(BF16)
    row = iota((tall, LANES), 0)
    mine = iota((tall, LANES), 1) % SUB == row % SUB
    apart = lax.axis_index("sample") * cols + row // SUB - lax.axis_index("row") * rows - row % SUB
    for g in range(rows // SUB):
        x = normed[:, g * SUB : (g + 1) * SUB].reshape(tall, chans).astype(BF16)
        raw = jnp.where(open_key | (apart == g * SUB), dot(x, wide), -30000.0)
        raw = jnp.where(mine, raw, 0.0).astype(BF16)
        out[:, g * LANES : (g + 1) * LANES] = dot(picked, raw).astype(BF16)


def pair_bias(feat, pair_cond, token_mask, pair_weight):
    rows, cols, chans = pair_cond.shape
    samples, atoms, width = feat.shape
    edge = (samples, RIM, width)

    def whole(*shape):
        return pl.BlockSpec(shape, lambda i: (0,) * len(shape))

    return pl.pallas_call(
        bias_kernel,
        grid=(1,),
        out_shape=[
            jax.ShapeDtypeStruct((cols, rows * HEADS), BF16),
            jax.ShapeDtypeStruct(edge, BF16),
            jax.ShapeDtypeStruct(edge, BF16),
        ],
        in_specs=[
            pl.BlockSpec(edge, lambda i: (0, 0, 0)),
            pl.BlockSpec(edge, lambda i: (0, atoms // RIM - 1, 0)),
            whole(cols, rows, chans),
            whole(cols),
            whole(HEADS, chans),
        ],
        out_specs=[whole(cols, rows * HEADS), whole(*edge), whole(*edge)],
        scratch_shapes=[pltpu.VMEM((cols, rows, chans), F32)],
        compiler_params=pltpu.CompilerParams(vmem_limit_bytes=60 * MIB),
        cost_estimate=cost(3),
        name="pair_bias",
    )(feat, feat, jnp.transpose(pair_cond, (1, 0, 2)), token_mask, pair_weight.T)


def after(value, *others):
    return lax.optimization_barrier((value, *others))[0]


def swap(held, axis, far):
    return lax.ppermute(held, axis, [(i, i ^ far) for i in range(lax.axis_size(axis))])


def bits_of(devices):
    return [devices >> i for i in range(1, devices.bit_length())]


def block_of(near, far, me, j):
    apart = me ^ j
    place = sum((apart // bit) % 2 * 2**i for i, bit in enumerate(bits_of(2 * near.shape[0])[:-1]))
    return jnp.where(apart % 2 == 0, near[place], far[place])


def atom_kernel(sample, feat, inner, outer, wq, wk, wv, mixed, qs, ks, vs):
    atoms, chans = feat.shape[1:]
    rank = lax.axis_index("row")
    at_start = rank == 0
    at_end = rank == lax.axis_size("row") - 1
    wqkv = jnp.concatenate([wq[...], wk[...], wv[...]], axis=1)
    odd = rank % 2 == 1
    before = jnp.where(odd, inner[sample], outer[sample])
    behind = jnp.where(odd, outer[sample], inner[sample])
    for part, at in ((before, 0), (behind, RIM + atoms)):
        kv = dot(layer_norm(part.astype(F32)).astype(BF16), wqkv[:, chans:]).astype(BF16)
        ks[at : at + RIM] = kv[:, :chans]
        vs[at : at + RIM] = kv[:, chans:]
    for c in range(0, atoms, LANES):
        qkv = dot(layer_norm(feat[sample, c : c + LANES].astype(F32)).astype(BF16), wqkv).astype(BF16)
        qs[c : c + LANES] = qkv[:, :chans]
        ks[RIM + c : RIM + c + LANES] = qkv[:, chans : 2 * chans]
        vs[RIM + c : RIM + c + LANES] = qkv[:, 2 * chans :]
    rate = math.log2(math.e) / AHEAD_DIM**0.5
    tall = AHEADS * QWIN
    head_of = iota((QWIN, chans), 1) // AHEAD_DIM
    keyat = iota((tall, KWIN), 1)
    batch = 2

    def score(first):
        out = []
        for at in range(first, first + batch * QWIN, QWIN):
            q = qs[at : at + QWIN]
            q = jnp.concatenate([jnp.where(head_of == h, q, jnp.zeros_like(q)) for h in range(AHEADS)], axis=0)
            s = dot_nt(q, ks[at : at + KWIN])
            if at < RIM:
                s = jnp.where(at_start & (keyat < RIM - at), -jnp.inf, s)
            if at + KWIN > RIM + atoms:
                s = jnp.where(at_end & (keyat >= RIM + atoms - at), -jnp.inf, s)
            out.append(s)
        return first, jnp.concatenate(out, axis=0)

    def soften(item):
        first, s = item
        e = jnp.exp2((s - jnp.max(s, -1, keepdims=True)) * rate)
        return first, e.astype(BF16), inverse(jnp.sum(e, -1, keepdims=True))

    def mix(item):
        first, e, share = item
        for i in range(batch):
            at = first + i * QWIN
            o = dot(e[i * tall : (i + 1) * tall], vs[at : at + KWIN]) * share[i * tall : (i + 1) * tall]
            acc = o[:QWIN]
            for h in range(1, AHEADS):
                acc = jnp.where(head_of == h, o[h * QWIN : (h + 1) * QWIN], acc)
            mixed[at : at + QWIN] = acc.astype(BF16)

    skewed(range(0, atoms, batch * QWIN), [score, soften, mix])


def atom_attention(sample, feat, inner, outer, wq, wk, wv):
    atoms, chans = feat.shape[1:]
    vmem = pl.BlockSpec(memory_space=pltpu.VMEM)
    return pl.pallas_call(
        functools.partial(atom_kernel, sample),
        out_shape=jax.ShapeDtypeStruct((atoms, chans), BF16),
        in_specs=[vmem] * 6,
        out_specs=vmem,
        scratch_shapes=[
            pltpu.VMEM((atoms, chans), BF16),
            pltpu.VMEM((atoms + 2 * RIM, chans), BF16),
            pltpu.VMEM((atoms + 2 * RIM, chans), BF16),
        ],
        compiler_params=pltpu.CompilerParams(vmem_limit_bytes=16 * MIB),
        cost_estimate=cost(4),
        name="atom_attention",
    )(feat, inner, outer, wq, wk, wv)


def gather_kernel(sample, mixed, feat, token, wo, agg, gain, token_in, token_norm):
    atoms = feat.shape[1]
    rows = token_in.shape[0]
    local = token[...].reshape(1, atoms) - lax.axis_index("row") * rows
    step = 384
    tsum = jnp.zeros((rows, agg.shape[1]), F32)
    count = jnp.zeros((rows, 1), F32)
    for c in range(0, atoms, step):
        out = (feat[sample, c : c + step].astype(F32) + dot(mixed[c : c + step], wo[...])).astype(BF16)
        hidden = jnp.maximum(dot(out, agg[...]), 0.0).astype(BF16)
        onehot = (iota((rows, step), 0) == local[:, c : c + step]).astype(F32)
        count = count + jnp.sum(onehot, -1, keepdims=True)
        tsum = tsum + dot(onehot.astype(BF16), hidden)
    tin = tsum / count
    token_in[...] = tin
    token_norm[...] = (layer_norm(tin) * gain[...].reshape(1, -1)).astype(BF16)


def gather_tokens(sample, mixed, feat, token, wo, agg, gain, rows):
    width = agg.shape[1]
    vmem = pl.BlockSpec(memory_space=pltpu.VMEM)
    return pl.pallas_call(
        functools.partial(gather_kernel, sample),
        out_shape=[jax.ShapeDtypeStruct((rows, width), F32), jax.ShapeDtypeStruct((rows, width), BF16)],
        in_specs=[vmem] * 6,
        out_specs=[vmem, vmem],
        compiler_params=pltpu.CompilerParams(vmem_limit_bytes=16 * MIB),
        cost_estimate=cost(1),
        name="gather_tokens",
    )(mixed, feat, token, wo, agg, gain)


def turn_kernel(near, far, out, tall):
    half, cols, _ = near.shape
    rows = out.shape[0] // HEADS
    me = lax.axis_index("sample")
    for j in range(2 * half):
        tall[j * cols : (j + 1) * cols] = block_of(near, far, me, j).astype(F32)
    for g in range(rows // SUB):
        turned = tall[:, g * LANES : (g + 1) * LANES].T
        for h in range(HEADS):
            out[h * rows + g * SUB : h * rows + (g + 1) * SUB] = turned[h * SUB : (h + 1) * SUB]


def turn_bias(near, far):
    half, cols, wide = near.shape
    keys = 2 * half * cols
    vmem = pl.BlockSpec(memory_space=pltpu.VMEM)
    return pl.pallas_call(
        turn_kernel,
        out_shape=jax.ShapeDtypeStruct((wide, keys), F32),
        in_specs=[vmem, vmem],
        out_specs=vmem,
        scratch_shapes=[pltpu.VMEM((keys, wide), F32)],
        compiler_params=pltpu.CompilerParams(vmem_limit_bytes=24 * MIB),
        cost_estimate=cost(1),
        name="turn_bias",
    )(near, far)


def head_groups(width):
    groups = []
    for base in range(0, width, 8 * HEAD_DIM):
        first = base // HEAD_DIM
        groups.append((base, range(first, first + 5)))
        groups.append((base + LANES, range(first + 5, first + 8)))
    return groups


def project_kernel(near, far, wq, wk, wv, wg, q, kt, v, gate):
    half, rows, width = near.shape
    me = lax.axis_index("row")
    x = jnp.concatenate([block_of(near, far, me, j).astype(F32) for j in range(2 * half)], axis=0).astype(BF16)
    own = near[0]
    q[...] = dot(own, wq[...]).astype(BF16)
    gate[...] = jax.nn.sigmoid(dot(own, wg[...]))
    for c in range(0, width, 2 * LANES):
        kt[c : c + 2 * LANES] = dot(x, wk[:, c : c + 2 * LANES]).T.astype(BF16)
    v[...] = dot(x, wv[...]).astype(BF16)


def project(near, far, wq, wk, wv, wg):
    half, rows, width = near.shape
    keys = 2 * half * rows
    vmem = pl.BlockSpec(memory_space=pltpu.VMEM)
    return pl.pallas_call(
        project_kernel,
        out_shape=[
            jax.ShapeDtypeStruct((rows, width), BF16),
            jax.ShapeDtypeStruct((width, keys), BF16),
            jax.ShapeDtypeStruct((keys, width), BF16),
            jax.ShapeDtypeStruct((rows, width), F32),
        ],
        in_specs=[vmem] * 6,
        out_specs=[vmem] * 4,
        compiler_params=pltpu.CompilerParams(vmem_limit_bytes=24 * MIB),
        cost_estimate=cost(2),
        name="project",
    )(near, far, wq, wk, wv, wg)


def attend_kernel(q, kt, v, gate, token_in, bias, wo, *rest):
    *earlier, out = rest
    rows, width = token_in.shape
    scale = 1.0 / HEAD_DIM**0.5
    lane = iota((rows, 2 * LANES), 1)
    work = [(base, h) for base, heads in head_groups(width) for h in heads]

    def channels(base, h):
        low = h * HEAD_DIM - base
        return (lane >= low) & (lane < low + HEAD_DIM)

    def score(item):
        base, h = item
        mine = q[:, base : base + 2 * LANES]
        mine = jnp.where(channels(base, h), mine, jnp.zeros_like(mine))
        return item, dot(mine, kt[base : base + 2 * LANES]) * scale + bias[h * rows : (h + 1) * rows]

    def soften(item):
        place, sc = item
        e = jnp.exp(sc - jnp.max(sc, -1, keepdims=True))
        return place, e.astype(BF16), inverse(jnp.sum(e, -1, keepdims=True))

    mixes = {}

    def mix(item):
        (base, h), e, share = item
        o = dot(e, v[:, base : base + 2 * LANES]) * share
        mixes[base] = jnp.where(channels(base, h), o, mixes.get(base, 0.0))

    skewed(work, [score, soften, mix])
    tiles = {}
    for base, _ in head_groups(width):
        for t in range(2):
            at = base + t * LANES
            part = mixes[base][:, t * LANES : (t + 1) * LANES]
            tiles[at] = tiles[at] + part if at in tiles else part
    gated = jnp.concatenate([tiles[at] for at in range(0, width, LANES)], axis=1) * gate[...]
    res = (token_in[...] + dot(gated.astype(BF16), wo[...])).astype(BF16)
    if earlier:
        for s, ref in enumerate(earlier):
            out[s] = ref[...]
        out[len(earlier)] = res
    else:
        out[...] = res


def attend(q, kt, v, gate, token_in, bias, wo, earlier):
    rows, width = token_in.shape
    vmem = pl.BlockSpec(memory_space=pltpu.VMEM)
    shape = (len(earlier) + 1, rows, width) if earlier else (rows, width)
    return pl.pallas_call(
        attend_kernel,
        out_shape=jax.ShapeDtypeStruct(shape, BF16),
        in_specs=[vmem] * (7 + len(earlier)),
        out_specs=vmem,
        compiler_params=pltpu.CompilerParams(vmem_limit_bytes=24 * MIB),
        cost_estimate=cost(3),
        name="attend",
    )(q, kt, v, gate, token_in, bias, wo, *earlier)


def shards(
    atom_feat,
    atom_token,
    pair_cond,
    token_mask,
    atom_wq,
    atom_wk,
    atom_wv,
    atom_wo,
    agg_weight,
    pair_weight,
    token_gain,
    query_weight,
    key_weight,
    value_weight,
    gate_weight,
    out_weight,
):
    samples = atom_feat.shape[0]
    rows = pair_cond.shape[0]
    ranks = lax.axis_size("row")
    bias, inner, outer = pair_bias(atom_feat, pair_cond, token_mask, pair_weight)
    inner = swap(inner, "row", 1)
    odd_pairs = [(i, i + 1) for i in range(1, ranks - 1, 2)]
    outer = lax.ppermute(outer, "row", odd_pairs + [(j, i) for i, j in odd_pairs])

    def widen(held, axis, bit, *others):
        return jnp.concatenate([held, after(swap(held, axis, bit), *others)], axis=0)

    bits, row_bits = bits_of(lax.axis_size("sample")), bits_of(ranks)
    held, norms, inputs = bias[None], [], []
    for s in range(samples):
        if s < len(bits) - 1:
            held = widen(held, "sample", bits[s], inner, outer, *norms[-1:])
        inner = after(inner, held, *norms[-1:])
        mixed = atom_attention(s, atom_feat, inner, outer, atom_wq, atom_wk, atom_wv)
        if s:
            norms[-1] = widen(norms[-1], "row", row_bits[0], mixed)
            mixed = after(mixed, norms[-1])
        token_in, token_norm = gather_tokens(s, mixed, atom_feat, atom_token, atom_wo, agg_weight, token_gain, rows)
        inputs.append(token_in)
        norms.append(token_norm[None])
    for bit in bits[samples:-1]:
        held = widen(held, "sample", bit)
    far_bias = swap(held, "sample", bits[-1])
    done = []
    for s in range(samples):
        near = norms[s]
        for bit in row_bits[near.shape[0].bit_length() - 1 : -1]:
            near = widen(near, "row", bit, *done)
        far = swap(near, "row", row_bits[-1])
        part = project(near, far, query_weight, key_weight, value_weight, gate_weight)
        if s == 0:
            bias = turn_bias(held, after(far_bias, part))
        earlier = done if s == samples - 1 else []
        done.append(attend(*part, inputs[s], bias, out_weight, earlier))
    return done[-1]


def solution(mesh):
    placed = (
        P("sample", "row", None),
        P("row"),
        P("row", "sample", None),
        P("sample"),
    ) + (P(),) * 12
    return jax.shard_map(
        shards, mesh=mesh, in_specs=placed, out_specs=P("sample", "row", None), check_vma=False
    )
```

```python
import functools
import math

import jax
import jax.numpy as jnp
from jax import lax
from jax.experimental import pallas as pl
from jax.experimental.pallas import tpu as pltpu
from jax.sharding import PartitionSpec as P

HEADS = 16
HEAD_DIM = 48
AHEADS = 4
AHEAD_DIM = 32
QWIN = 32
KWIN = 128
RIM = (KWIN - QWIN) // 2
LANES = 128
SUB = 8
F32 = jnp.float32
BF16 = jnp.bfloat16
MIB = 1024 * 1024
NT = (((1,), (1,)), ((), ()))


def layer_norm(x):
    mean = jnp.mean(x, -1, keepdims=True)
    centre = x - mean
    var = jnp.mean(centre * centre, -1, keepdims=True)
    return centre * lax.rsqrt(var + 1e-05)


def dot(a, b):
    return jnp.dot(a, b, preferred_element_type=F32)


def dot_nt(a, b):
    return lax.dot_general(a, b, NT, preferred_element_type=F32)


def iota(shape, dim):
    return lax.broadcasted_iota(jnp.int32, shape, dim)


def cost(micros):
    return pl.CostEstimate(flops=micros * 20_000_000, bytes_accessed=1_000, transcendentals=0)


def inverse(total):
    guess = pl.reciprocal(total, approx=True)
    return guess * (2.0 - total * guess)


def skewed(items, stages):
    held = list(items)
    for t in range(len(held) + len(stages) - 1):
        for k in reversed(range(len(stages))):
            if 0 <= t - k < len(held):
                held[t - k] = stages[k](held[t - k])
    return held


def bias_kernel(head, tail, pair, mask, weight, out, inner, outer, normed):
    odd = lax.axis_index("row") % 2 == 1
    inner[...] = jnp.where(odd, head[...], tail[...])
    outer[...] = jnp.where(odd, tail[...], head[...])
    cols, rows, chans = pair.shape
    for k in range(cols):
        normed[k] = layer_norm(pair[k].astype(F32))
    spread = (iota((HEADS, LANES), 1) // SUB == iota((HEADS, LANES), 0)).astype(BF16)
    wide = lax.dot_general(weight[...], spread, (((0,), (0,)), ((), ())), preferred_element_type=F32).astype(BF16)
    tall = cols * SUB
    key_of = iota((tall, cols), 0) // SUB == iota((tall, cols), 1)
    open_row = jnp.broadcast_to(mask[...].reshape(1, cols), (LANES, cols)).astype(BF16)
    open_key = dot_nt(key_of.astype(BF16), open_row) > 0.5
    picked = (iota((cols, tall), 1) // SUB == iota((cols, tall), 0)).astype(BF16)
    row = iota((tall, LANES), 0)
    mine = iota((tall, LANES), 1) % SUB == row % SUB
    apart = lax.axis_index("sample") * cols + row // SUB - lax.axis_index("row") * rows - row % SUB
    for g in range(rows // SUB):
        x = normed[:, g * SUB : (g + 1) * SUB].reshape(tall, chans).astype(BF16)
        raw = jnp.where(open_key | (apart == g * SUB), dot(x, wide), -30000.0)
        raw = jnp.where(mine, raw, 0.0).astype(BF16)
        out[:, g * LANES : (g + 1) * LANES] = dot(picked, raw).astype(BF16)


def pair_bias(feat, pair_cond, token_mask, pair_weight):
    rows, cols, chans = pair_cond.shape
    samples, atoms, width = feat.shape
    edge = (samples, RIM, width)

    def whole(*shape):
        return pl.BlockSpec(shape, lambda i: (0,) * len(shape))

    return pl.pallas_call(
        bias_kernel,
        grid=(1,),
        out_shape=[
            jax.ShapeDtypeStruct((cols, rows * HEADS), BF16),
            jax.ShapeDtypeStruct(edge, BF16),
            jax.ShapeDtypeStruct(edge, BF16),
        ],
        in_specs=[
            pl.BlockSpec(edge, lambda i: (0, 0, 0)),
            pl.BlockSpec(edge, lambda i: (0, atoms // RIM - 1, 0)),
            whole(cols, rows, chans),
            whole(cols),
            whole(HEADS, chans),
        ],
        out_specs=[whole(cols, rows * HEADS), whole(*edge), whole(*edge)],
        scratch_shapes=[pltpu.VMEM((cols, rows, chans), F32)],
        compiler_params=pltpu.CompilerParams(vmem_limit_bytes=60 * MIB),
        cost_estimate=cost(3),
        name="pair_bias",
    )(feat, feat, jnp.transpose(pair_cond, (1, 0, 2)), token_mask, pair_weight.T)


def after(value, *others):
    return lax.optimization_barrier((value, *others))[0]


def swap(held, axis, far):
    return lax.ppermute(held, axis, [(i, i ^ far) for i in range(lax.axis_size(axis))])


def bits_of(devices):
    return [devices >> i for i in range(1, devices.bit_length())]


def block_of(near, far, me, j):
    apart = me ^ j
    place = sum((apart // bit) % 2 * 2**i for i, bit in enumerate(bits_of(2 * near.shape[0])[:-1]))
    return jnp.where(apart % 2 == 0, near[place], far[place])


def atom_kernel(sample, feat, inner, outer, wq, wk, wv, mixed, qs, ks, vs):
    atoms, chans = feat.shape[1:]
    rank = lax.axis_index("row")
    at_start = rank == 0
    at_end = rank == lax.axis_size("row") - 1
    wqkv = jnp.concatenate([wq[...], wk[...], wv[...]], axis=1)
    odd = rank % 2 == 1
    before = jnp.where(odd, inner[sample], outer[sample])
    behind = jnp.where(odd, outer[sample], inner[sample])

    def normalise(at):
        if isinstance(at, int):
            part = feat[sample, at : at + LANES]
        else:
            at, part = at
        return at, layer_norm(part.astype(F32)).astype(BF16)

    def project_atoms(item):
        at, normed = item
        count = normed.shape[0]
        if count == RIM:
            kv = dot(normed, wqkv[:, chans:]).astype(BF16)
        else:
            qkv = dot(normed, wqkv).astype(BF16)
            qs[at : at + count] = qkv[:, :chans]
            kv = qkv[:, chans:]
        ks[RIM + at : RIM + at + count] = kv[:, :chans]
        vs[RIM + at : RIM + at + count] = kv[:, chans:]

    skewed([*range(0, atoms, LANES), (-RIM, before), (atoms, behind)], [normalise, project_atoms])
    rate = math.log2(math.e) / AHEAD_DIM**0.5
    tall = AHEADS * QWIN
    head_of = iota((QWIN, chans), 1) // AHEAD_DIM
    keyat = iota((tall, KWIN), 1)
    batch = 4

    def score(first):
        out = []
        for at in range(first, first + batch * QWIN, QWIN):
            q = qs[at : at + QWIN]
            q = jnp.concatenate([jnp.where(head_of == h, q, jnp.zeros_like(q)) for h in range(AHEADS)], axis=0)
            s = dot_nt(q, ks[at : at + KWIN])
            if at < RIM:
                s = jnp.where(at_start & (keyat < RIM - at), -jnp.inf, s)
            if at + KWIN > RIM + atoms:
                s = jnp.where(at_end & (keyat >= RIM + atoms - at), -jnp.inf, s)
            out.append(s)
        return first, jnp.concatenate(out, axis=0)

    def soften(item):
        first, s = item
        e = jnp.exp2((s - jnp.max(s, -1, keepdims=True)) * rate)
        return first, e.astype(BF16), inverse(jnp.sum(e, -1, keepdims=True))

    def mix(item):
        first, e, share = item
        for i in range(batch):
            at = first + i * QWIN
            o = dot(e[i * tall : (i + 1) * tall], vs[at : at + KWIN]) * share[i * tall : (i + 1) * tall]
            acc = o[:QWIN]
            for h in range(1, AHEADS):
                acc = jnp.where(head_of == h, o[h * QWIN : (h + 1) * QWIN], acc)
            mixed[at : at + QWIN] = acc.astype(BF16)

    skewed(range(0, atoms, batch * QWIN), [score, soften, mix])


def atom_attention(sample, feat, inner, outer, wq, wk, wv):
    atoms, chans = feat.shape[1:]
    vmem = pl.BlockSpec(memory_space=pltpu.VMEM)
    return pl.pallas_call(
        functools.partial(atom_kernel, sample),
        out_shape=jax.ShapeDtypeStruct((atoms, chans), BF16),
        in_specs=[vmem] * 6,
        out_specs=vmem,
        scratch_shapes=[
            pltpu.VMEM((atoms, chans), BF16),
            pltpu.VMEM((atoms + 2 * RIM, chans), BF16),
            pltpu.VMEM((atoms + 2 * RIM, chans), BF16),
        ],
        compiler_params=pltpu.CompilerParams(vmem_limit_bytes=16 * MIB),
        cost_estimate=cost(4),
        name="atom_attention",
    )(feat, inner, outer, wq, wk, wv)


def gather_kernel(sample, mixed, feat, token, wo, agg, gain, token_in, token_norm):
    atoms = feat.shape[1]
    rows = token_in.shape[0]
    local = token[...].reshape(1, atoms) - lax.axis_index("row") * rows
    step = 192

    def finish(c):
        return c, (feat[sample, c : c + step].astype(F32) + dot(mixed[c : c + step], wo[...])).astype(BF16)

    def hide(item):
        c, out = item
        return c, jnp.maximum(dot(out, agg[...]), 0.0).astype(BF16)

    hidden = jnp.concatenate([h for _, h in skewed(range(0, atoms, step), [finish, hide])], axis=0)
    onehot = (iota((rows, atoms), 0) == local).astype(F32)
    tin = dot(onehot.astype(BF16), hidden) / jnp.sum(onehot, -1, keepdims=True)
    token_in[...] = tin
    token_norm[...] = (layer_norm(tin) * gain[...].reshape(1, -1)).astype(BF16)


def gather_tokens(sample, mixed, feat, token, wo, agg, gain, rows):
    width = agg.shape[1]
    vmem = pl.BlockSpec(memory_space=pltpu.VMEM)
    return pl.pallas_call(
        functools.partial(gather_kernel, sample),
        out_shape=[jax.ShapeDtypeStruct((rows, width), F32), jax.ShapeDtypeStruct((rows, width), BF16)],
        in_specs=[vmem] * 6,
        out_specs=[vmem, vmem],
        compiler_params=pltpu.CompilerParams(vmem_limit_bytes=16 * MIB),
        cost_estimate=cost(1),
        name="gather_tokens",
    )(mixed, feat, token, wo, agg, gain)


def turn_kernel(near, far, out, tall):
    half, cols, _ = near.shape
    rows = out.shape[0] // HEADS
    me = lax.axis_index("sample")
    for j in range(2 * half):
        tall[j * cols : (j + 1) * cols] = block_of(near, far, me, j).astype(F32)
    for g in range(rows // SUB):
        turned = tall[:, g * LANES : (g + 1) * LANES].T
        for h in range(HEADS):
            out[h * rows + g * SUB : h * rows + (g + 1) * SUB] = turned[h * SUB : (h + 1) * SUB]


def turn_bias(near, far):
    half, cols, wide = near.shape
    keys = 2 * half * cols
    vmem = pl.BlockSpec(memory_space=pltpu.VMEM)
    return pl.pallas_call(
        turn_kernel,
        out_shape=jax.ShapeDtypeStruct((wide, keys), F32),
        in_specs=[vmem, vmem],
        out_specs=vmem,
        scratch_shapes=[pltpu.VMEM((keys, wide), F32)],
        compiler_params=pltpu.CompilerParams(vmem_limit_bytes=24 * MIB),
        cost_estimate=cost(1),
        name="turn_bias",
    )(near, far)


def head_groups(width):
    groups = []
    for base in range(0, width, 8 * HEAD_DIM):
        first = base // HEAD_DIM
        groups.append((base, range(first, first + 5)))
        groups.append((base + LANES, range(first + 5, first + 8)))
    return groups


def project_kernel(near, far, wq, wk, wv, wg, q, kt, v, gate):
    half, rows, width = near.shape
    me = lax.axis_index("row")
    x = jnp.concatenate([block_of(near, far, me, j).astype(F32) for j in range(2 * half)], axis=0).astype(BF16)
    own = near[0]
    q[...] = dot(own, wq[...]).astype(BF16)
    gate[...] = jax.nn.sigmoid(dot(own, wg[...]))
    for c in range(0, width, 2 * LANES):
        kt[c : c + 2 * LANES] = dot(x, wk[:, c : c + 2 * LANES]).T.astype(BF16)
    v[...] = dot(x, wv[...]).astype(BF16)


def project(near, far, wq, wk, wv, wg):
    half, rows, width = near.shape
    keys = 2 * half * rows
    vmem = pl.BlockSpec(memory_space=pltpu.VMEM)
    return pl.pallas_call(
        project_kernel,
        out_shape=[
            jax.ShapeDtypeStruct((rows, width), BF16),
            jax.ShapeDtypeStruct((width, keys), BF16),
            jax.ShapeDtypeStruct((keys, width), BF16),
            jax.ShapeDtypeStruct((rows, width), F32),
        ],
        in_specs=[vmem] * 6,
        out_specs=[vmem] * 4,
        compiler_params=pltpu.CompilerParams(vmem_limit_bytes=24 * MIB),
        cost_estimate=cost(2),
        name="project",
    )(near, far, wq, wk, wv, wg)


def attend_kernel(q, kt, v, gate, token_in, bias, wo, *rest):
    *earlier, out = rest
    rows, width = token_in.shape
    scale = 1.0 / HEAD_DIM**0.5
    lane = iota((rows, 2 * LANES), 1)
    work = [(base, heads[i : i + 2]) for base, heads in head_groups(width) for i in range(0, len(heads), 2)]

    def channels(base, h):
        low = h * HEAD_DIM - base
        return (lane >= low) & (lane < low + HEAD_DIM)

    def score(item):
        base, heads = item
        mine = q[:, base : base + 2 * LANES].astype(F32)
        mine = jnp.concatenate([jnp.where(channels(base, h), mine, 0.0) for h in heads], axis=0).astype(BF16)
        some = bias[heads[0] * rows : (heads[-1] + 1) * rows]
        return item, dot(mine, kt[base : base + 2 * LANES]) * scale + some

    def soften(item):
        place, sc = item
        e = jnp.exp(sc - jnp.max(sc, -1, keepdims=True))
        return place, e.astype(BF16), inverse(jnp.sum(e, -1, keepdims=True))

    mixes = {}

    def mix(item):
        (base, heads), e, share = item
        o = dot(e, v[:, base : base + 2 * LANES]) * share
        for i, h in enumerate(heads):
            mixes[base] = jnp.where(channels(base, h), o[i * rows : (i + 1) * rows], mixes.get(base, 0.0))

    skewed(work, [score, soften, mix])
    tiles = {}
    for base, _ in head_groups(width):
        for t in range(2):
            at = base + t * LANES
            part = mixes[base][:, t * LANES : (t + 1) * LANES]
            tiles[at] = tiles[at] + part if at in tiles else part
    gated = jnp.concatenate([tiles[at] for at in range(0, width, LANES)], axis=1) * gate[...]
    res = (token_in[...] + dot(gated.astype(BF16), wo[...])).astype(BF16)
    if earlier:
        for s, ref in enumerate(earlier):
            out[s] = ref[...]
        out[len(earlier)] = res
    else:
        out[...] = res


def attend(q, kt, v, gate, token_in, bias, wo, earlier):
    rows, width = token_in.shape
    vmem = pl.BlockSpec(memory_space=pltpu.VMEM)
    shape = (len(earlier) + 1, rows, width) if earlier else (rows, width)
    return pl.pallas_call(
        attend_kernel,
        out_shape=jax.ShapeDtypeStruct(shape, BF16),
        in_specs=[vmem] * (7 + len(earlier)),
        out_specs=vmem,
        compiler_params=pltpu.CompilerParams(vmem_limit_bytes=24 * MIB),
        cost_estimate=cost(3),
        name="attend",
    )(q, kt, v, gate, token_in, bias, wo, *earlier)


def shards(
    atom_feat,
    atom_token,
    pair_cond,
    token_mask,
    atom_wq,
    atom_wk,
    atom_wv,
    atom_wo,
    agg_weight,
    pair_weight,
    token_gain,
    query_weight,
    key_weight,
    value_weight,
    gate_weight,
    out_weight,
):
    samples = atom_feat.shape[0]
    rows = pair_cond.shape[0]
    ranks = lax.axis_size("row")
    bias, inner, outer = pair_bias(atom_feat, pair_cond, token_mask, pair_weight)
    inner = swap(inner, "row", 1)
    odd_pairs = [(i, (i + 1) % ranks) for i in range(1, ranks, 2)]
    outer = lax.ppermute(outer, "row", odd_pairs + [(j, i) for i, j in odd_pairs])

    def widen(held, axis, bit, *others):
        return jnp.concatenate([held, after(swap(held, axis, bit), *others)], axis=0)

    bits, row_bits = bits_of(lax.axis_size("sample")), bits_of(ranks)
    held, norms, inputs = bias[None], [], []
    for s in range(samples):
        if s < len(bits) - 1:
            held = widen(held, "sample", bits[s], inner, outer, *norms[-1:])
        inner = after(inner, held, *norms[-1:])
        mixed = atom_attention(s, atom_feat, inner, outer, atom_wq, atom_wk, atom_wv)
        if s:
            norms[-1] = widen(norms[-1], "row", row_bits[0], mixed)
            mixed = after(mixed, norms[-1])
        token_in, token_norm = gather_tokens(s, mixed, atom_feat, atom_token, atom_wo, agg_weight, token_gain, rows)
        inputs.append(token_in)
        norms.append(token_norm[None])
    for bit in bits[samples:-1]:
        held = widen(held, "sample", bit)
    far_bias = swap(held, "sample", bits[-1])
    done = []
    for s in range(samples):
        near = norms[s]
        for bit in row_bits[near.shape[0].bit_length() - 1 : -1]:
            near = widen(near, "row", bit, *done)
        far = swap(near, "row", row_bits[-1])
        part = project(near, far, query_weight, key_weight, value_weight, gate_weight)
        if s == 0:
            bias = turn_bias(held, after(far_bias, part))
        earlier = done if s == samples - 1 else []
        done.append(attend(*part, inputs[s], bias, out_weight, earlier))
    return done[-1]


def solution(mesh):
    placed = (
        P("sample", "row", None),
        P("row"),
        P("row", "sample", None),
        P("sample"),
    ) + (P(),) * 12
    return jax.shard_map(
        shards, mesh=mesh, in_specs=placed, out_specs=P("sample", "row", None), check_vma=False
    )
```

```python
import functools
import math

import jax
import jax.numpy as jnp
from jax import lax
from jax.experimental import pallas as pl
from jax.experimental.pallas import tpu as pltpu
from jax.sharding import PartitionSpec as P

HEADS = 16
HEAD_DIM = 48
AHEADS = 4
AHEAD_DIM = 32
QWIN = 32
KWIN = 128
RIM = (KWIN - QWIN) // 2
LANES = 128
SUB = 8
F32 = jnp.float32
BF16 = jnp.bfloat16
MIB = 1024 * 1024
NT = (((1,), (1,)), ((), ()))


def layer_norm(x):
    mean = jnp.mean(x, -1, keepdims=True)
    centre = x - mean
    var = jnp.mean(centre * centre, -1, keepdims=True)
    return centre * lax.rsqrt(var + 1e-05)


def dot(a, b):
    return jnp.dot(a, b, preferred_element_type=F32)


def dot_nt(a, b):
    return lax.dot_general(a, b, NT, preferred_element_type=F32)


def iota(shape, dim):
    return lax.broadcasted_iota(jnp.int32, shape, dim)


def cost(micros):
    return pl.CostEstimate(flops=micros * 20_000_000, bytes_accessed=1_000, transcendentals=0)


def inverse(total):
    guess = pl.reciprocal(total, approx=True)
    return guess * (2.0 - total * guess)


def skewed(items, stages):
    held = list(items)
    for t in range(len(held) + len(stages) - 1):
        for k in reversed(range(len(stages))):
            if 0 <= t - k < len(held):
                held[t - k] = stages[k](held[t - k])
    return held


def bias_kernel(head, tail, pair, mask, weight, out, inner, outer, normed):
    odd = lax.axis_index("row") % 2 == 1
    inner[...] = jnp.where(odd, head[...], tail[...])
    outer[...] = jnp.where(odd, tail[...], head[...])
    cols, rows, chans = pair.shape
    for k in range(cols):
        normed[k] = layer_norm(pair[k].astype(F32))
    spread = (iota((HEADS, LANES), 1) // SUB == iota((HEADS, LANES), 0)).astype(BF16)
    wide = lax.dot_general(weight[...], spread, (((0,), (0,)), ((), ())), preferred_element_type=F32).astype(BF16)
    tall = cols * SUB
    key_of = iota((tall, cols), 0) // SUB == iota((tall, cols), 1)
    open_row = jnp.broadcast_to(mask[...].reshape(1, cols), (LANES, cols)).astype(BF16)
    open_key = dot_nt(key_of.astype(BF16), open_row) > 0.5
    picked = (iota((cols, tall), 1) // SUB == iota((cols, tall), 0)).astype(BF16)
    row = iota((tall, LANES), 0)
    mine = iota((tall, LANES), 1) % SUB == row % SUB
    apart = lax.axis_index("sample") * cols + row // SUB - lax.axis_index("row") * rows - row % SUB
    for g in range(rows // SUB):
        x = normed[:, g * SUB : (g + 1) * SUB].reshape(tall, chans).astype(BF16)
        raw = jnp.where(open_key | (apart == g * SUB), dot(x, wide), -30000.0)
        raw = jnp.where(mine, raw, 0.0).astype(BF16)
        out[:, g * LANES : (g + 1) * LANES] = dot(picked, raw).astype(BF16)


def pair_bias(feat, pair_cond, token_mask, pair_weight):
    rows, cols, chans = pair_cond.shape
    samples, atoms, width = feat.shape
    edge = (samples, RIM, width)

    def whole(*shape):
        return pl.BlockSpec(shape, lambda i: (0,) * len(shape))

    return pl.pallas_call(
        bias_kernel,
        grid=(1,),
        out_shape=[
            jax.ShapeDtypeStruct((cols, rows * HEADS), BF16),
            jax.ShapeDtypeStruct(edge, BF16),
            jax.ShapeDtypeStruct(edge, BF16),
        ],
        in_specs=[
            pl.BlockSpec(edge, lambda i: (0, 0, 0)),
            pl.BlockSpec(edge, lambda i: (0, atoms // RIM - 1, 0)),
            whole(cols, rows, chans),
            whole(cols),
            whole(HEADS, chans),
        ],
        out_specs=[whole(cols, rows * HEADS), whole(*edge), whole(*edge)],
        scratch_shapes=[pltpu.VMEM((cols, rows, chans), F32)],
        compiler_params=pltpu.CompilerParams(vmem_limit_bytes=60 * MIB),
        cost_estimate=cost(3),
        name="pair_bias",
    )(feat, feat, jnp.transpose(pair_cond, (1, 0, 2)), token_mask, pair_weight.T)


def after(value, *others):
    return lax.optimization_barrier((value, *others))[0]


def swap(held, axis, far):
    return lax.ppermute(held, axis, [(i, i ^ far) for i in range(lax.axis_size(axis))])


def bits_of(devices):
    return [devices >> i for i in range(1, devices.bit_length())]


def places_of(bits):
    places = [0]
    for bit in bits:
        places += [p ^ bit for p in places]
    return places


def atom_kernel(sample, feat, inner, outer, wq, wk, wv, mixed, qs, ks, vs):
    atoms, chans = feat.shape[1:]
    rank = lax.axis_index("row")
    at_start = rank == 0
    at_end = rank == lax.axis_size("row") - 1
    wqkv = jnp.concatenate([wq[...], wk[...], wv[...]], axis=1)
    odd = rank % 2 == 1
    before = jnp.where(odd, inner[sample], outer[sample])
    behind = jnp.where(odd, outer[sample], inner[sample])

    def normalise(at):
        if isinstance(at, int):
            part = feat[sample, at : at + LANES]
        else:
            at, part = at
        return at, layer_norm(part.astype(F32)).astype(BF16)

    def project_atoms(item):
        at, normed = item
        count = normed.shape[0]
        if count == RIM:
            kv = dot(normed, wqkv[:, chans:]).astype(BF16)
        else:
            qkv = dot(normed, wqkv).astype(BF16)
            qs[at : at + count] = qkv[:, :chans]
            kv = qkv[:, chans:]
        ks[RIM + at : RIM + at + count] = kv[:, :chans]
        vs[RIM + at : RIM + at + count] = kv[:, chans:]

    skewed([*range(0, atoms, LANES), (-RIM, before), (atoms, behind)], [normalise, project_atoms])
    rate = math.log2(math.e) / AHEAD_DIM**0.5
    tall = AHEADS * QWIN
    head_of = iota((QWIN, chans), 1) // AHEAD_DIM
    keyat = iota((tall, KWIN), 1)
    batch = 6

    def score(first):
        out = []
        for at in range(first, first + batch * QWIN, QWIN):
            q = qs[at : at + QWIN]
            q = jnp.concatenate([jnp.where(head_of == h, q, jnp.zeros_like(q)) for h in range(AHEADS)], axis=0)
            s = dot_nt(q, ks[at : at + KWIN])
            if at < RIM:
                s = jnp.where(at_start & (keyat < RIM - at), -jnp.inf, s)
            if at + KWIN > RIM + atoms:
                s = jnp.where(at_end & (keyat >= RIM + atoms - at), -jnp.inf, s)
            out.append(s)
        return first, jnp.concatenate(out, axis=0)

    def soften(item):
        first, s = item
        e = jnp.exp2((s - jnp.max(s, -1, keepdims=True)) * rate)
        return first, e.astype(BF16), inverse(jnp.sum(e, -1, keepdims=True))

    def mix(item):
        first, e, share = item
        for i in range(batch):
            at = first + i * QWIN
            o = dot(e[i * tall : (i + 1) * tall], vs[at : at + KWIN]) * share[i * tall : (i + 1) * tall]
            acc = o[:QWIN]
            for h in range(1, AHEADS):
                acc = jnp.where(head_of == h, o[h * QWIN : (h + 1) * QWIN], acc)
            mixed[at : at + QWIN] = acc.astype(BF16)

    skewed(range(0, atoms, batch * QWIN), [score, soften, mix])


def atom_attention(sample, feat, inner, outer, wq, wk, wv):
    atoms, chans = feat.shape[1:]
    vmem = pl.BlockSpec(memory_space=pltpu.VMEM)
    return pl.pallas_call(
        functools.partial(atom_kernel, sample),
        out_shape=jax.ShapeDtypeStruct((atoms, chans), BF16),
        in_specs=[vmem] * 6,
        out_specs=vmem,
        scratch_shapes=[
            pltpu.VMEM((atoms, chans), BF16),
            pltpu.VMEM((atoms + 2 * RIM, chans), BF16),
            pltpu.VMEM((atoms + 2 * RIM, chans), BF16),
        ],
        compiler_params=pltpu.CompilerParams(vmem_limit_bytes=16 * MIB),
        cost_estimate=cost(4),
        name="atom_attention",
    )(feat, inner, outer, wq, wk, wv)


def gather_kernel(sample, mixed, feat, token, wo, agg, gain, token_in, token_norm):
    atoms = feat.shape[1]
    rows = token_in.shape[0]
    local = token[...].reshape(1, atoms) - lax.axis_index("row") * rows
    step = 384
    sums = []

    def finish(c):
        return c, (feat[sample, c : c + step].astype(F32) + dot(mixed[c : c + step], wo[...])).astype(BF16)

    def hide(item):
        c, out = item
        return c, jnp.maximum(dot(out, agg[...]), 0.0).astype(BF16)

    def add(item):
        c, hidden = item
        onehot = (iota((rows, step), 0) == local[:, c : c + step]).astype(F32)
        part = dot(onehot.astype(BF16), hidden), jnp.sum(onehot, -1, keepdims=True)
        sums[:] = [a + b for a, b in zip(sums, part)] if sums else part

    skewed(range(0, atoms, step), [finish, hide, add])
    tin = sums[0] / sums[1]
    token_in[...] = tin
    token_norm[...] = (layer_norm(tin) * gain[...].reshape(1, -1)).astype(BF16)


def gather_tokens(sample, mixed, feat, token, wo, agg, gain, rows):
    width = agg.shape[1]
    vmem = pl.BlockSpec(memory_space=pltpu.VMEM)
    return pl.pallas_call(
        functools.partial(gather_kernel, sample),
        out_shape=[jax.ShapeDtypeStruct((rows, width), F32), jax.ShapeDtypeStruct((rows, width), BF16)],
        in_specs=[vmem] * 6,
        out_specs=[vmem, vmem],
        compiler_params=pltpu.CompilerParams(vmem_limit_bytes=16 * MIB),
        cost_estimate=cost(1),
        name="gather_tokens",
    )(mixed, feat, token, wo, agg, gain)


def turn_kernel(orders, row_bits, *refs):
    *halves, out, tall = refs
    rows = out.shape[0] // HEADS
    me = lax.axis_index("sample")
    at = 0
    for near, far, bits in zip(halves[::2], halves[1::2], orders):
        half, cols, wide = near.shape
        places = places_of(bits)
        for j in range(2 * half):
            place = sum(jnp.where(me ^ j == p, i, 0) for i, p in enumerate(places))
            block = jnp.where(place < half, near[place % half], far[place % half])
            tall[j * cols : (j + 1) * cols, at : at + wide] = block.astype(F32)
        at += wide
    starts = [pl.multiple_of((lax.axis_index("row") ^ p) * rows, SUB) for p in places_of(row_bits)]
    for g in range(rows // SUB):
        lanes = slice(g * LANES, (g + 1) * LANES)
        turned = jnp.concatenate([tall[pl.ds(start, rows), lanes] for start in starts], axis=0).T
        for h in range(HEADS):
            out[h * rows + g * SUB : h * rows + (g + 1) * SUB] = turned[h * SUB : (h + 1) * SUB]


def turn_bias(orders, row_bits, halves):
    half, cols, _ = halves[0].shape
    keys = 2 * half * cols
    wide = sum(near.shape[2] for near in halves[::2])
    vmem = pl.BlockSpec(memory_space=pltpu.VMEM)
    return pl.pallas_call(
        functools.partial(turn_kernel, orders, row_bits),
        out_shape=jax.ShapeDtypeStruct((wide, keys), F32),
        in_specs=[vmem] * len(halves),
        out_specs=vmem,
        scratch_shapes=[pltpu.VMEM((keys, wide), F32)],
        compiler_params=pltpu.CompilerParams(vmem_limit_bytes=24 * MIB),
        cost_estimate=cost(1),
        name="turn_bias",
    )(*halves)


def head_groups(width):
    groups = []
    for base in range(0, width, 8 * HEAD_DIM):
        first = base // HEAD_DIM
        groups.append((base, range(first, first + 5)))
        groups.append((base + LANES, range(first + 5, first + 8)))
    return groups


def stack(blocks):
    return jnp.concatenate([blocks[j].astype(F32) for j in range(blocks.shape[0])], axis=0).astype(BF16)


def project_kernel(near, wq, wk, wv, wg, wo, q, k, v, gate):
    x = stack(near)
    q[...] = dot(near[0], wq[...]).astype(BF16)
    gate[...] = jax.nn.sigmoid(dot(near[0], wg[...]))
    k[...] = dot(x, wk[...]).astype(BF16)
    v[...] = dot(x, wv[...]).astype(BF16)


def project(near, wq, wk, wv, wg, wo):
    half, rows, width = near.shape
    vmem = pl.BlockSpec(memory_space=pltpu.VMEM)
    return pl.pallas_call(
        project_kernel,
        out_shape=[
            jax.ShapeDtypeStruct((rows, width), BF16),
            jax.ShapeDtypeStruct((half * rows, width), BF16),
            jax.ShapeDtypeStruct((half * rows, width), BF16),
            jax.ShapeDtypeStruct((rows, width), F32),
        ],
        in_specs=[vmem] * 6,
        out_specs=[vmem] * 4,
        compiler_params=pltpu.CompilerParams(vmem_limit_bytes=24 * MIB),
        cost_estimate=cost(2),
        name="project",
    )(near, wq, wk, wv, wg, wo)


def attend_kernel(far, q, k_near, v_near, gate, token_in, bias, wk, wv, wo, *rest):
    *earlier, out, kt, v = rest
    rows, width = token_in.shape
    x = stack(far)
    for c in range(0, width, 2 * LANES):
        lanes = slice(c, c + 2 * LANES)
        k = jnp.concatenate([k_near[:, lanes].astype(F32), dot(x, wk[:, lanes])], axis=0)
        kt[lanes] = k.T.astype(BF16)
    v[: v_near.shape[0]] = v_near[...]
    v[v_near.shape[0] :] = dot(x, wv[...]).astype(BF16)
    scale = 1.0 / HEAD_DIM**0.5
    lane = iota((rows, 2 * LANES), 1)
    work = [(base, heads[i : i + 2]) for base, heads in head_groups(width) for i in range(0, len(heads), 2)]

    def channels(base, h):
        low = h * HEAD_DIM - base
        return (lane >= low) & (lane < low + HEAD_DIM)

    def score(item):
        base, heads = item
        mine = q[:, base : base + 2 * LANES].astype(F32)
        mine = jnp.concatenate([jnp.where(channels(base, h), mine, 0.0) for h in heads], axis=0).astype(BF16)
        some = bias[heads[0] * rows : (heads[-1] + 1) * rows]
        return item, dot(mine, kt[base : base + 2 * LANES]) * scale + some

    def soften(item):
        place, sc = item
        e = jnp.exp(sc - jnp.max(sc, -1, keepdims=True))
        return place, e.astype(BF16), inverse(jnp.sum(e, -1, keepdims=True))

    mixes = {}

    def mix(item):
        (base, heads), e, share = item
        o = dot(e, v[:, base : base + 2 * LANES]) * share
        for i, h in enumerate(heads):
            mixes[base] = jnp.where(channels(base, h), o[i * rows : (i + 1) * rows], mixes.get(base, 0.0))

    skewed(work, [score, soften, mix])
    tiles = {}
    for base, _ in head_groups(width):
        for t in range(2):
            at = base + t * LANES
            part = mixes[base][:, t * LANES : (t + 1) * LANES]
            tiles[at] = tiles[at] + part if at in tiles else part
    gated = jnp.concatenate([tiles[at] for at in range(0, width, LANES)], axis=1) * gate[...]
    res = (token_in[...] + dot(gated.astype(BF16), wo[...])).astype(BF16)
    if earlier:
        for s, ref in enumerate(earlier):
            out[s] = ref[...]
        out[len(earlier)] = res
    else:
        out[...] = res


def attend(far, q, k, v, gate, token_in, bias, wk, wv, wo, earlier):
    rows, width = token_in.shape
    keys = 2 * k.shape[0]
    vmem = pl.BlockSpec(memory_space=pltpu.VMEM)
    shape = (len(earlier) + 1, rows, width) if earlier else (rows, width)
    return pl.pallas_call(
        attend_kernel,
        out_shape=jax.ShapeDtypeStruct(shape, BF16),
        in_specs=[vmem] * (10 + len(earlier)),
        out_specs=vmem,
        scratch_shapes=[pltpu.VMEM((width, keys), BF16), pltpu.VMEM((keys, width), BF16)],
        compiler_params=pltpu.CompilerParams(vmem_limit_bytes=24 * MIB),
        cost_estimate=cost(3),
        name="attend",
    )(far, q, k, v, gate, token_in, bias, wk, wv, wo, *earlier)


def shards(
    atom_feat,
    atom_token,
    pair_cond,
    token_mask,
    atom_wq,
    atom_wk,
    atom_wv,
    atom_wo,
    agg_weight,
    pair_weight,
    token_gain,
    query_weight,
    key_weight,
    value_weight,
    gate_weight,
    out_weight,
):
    samples = atom_feat.shape[0]
    rows = pair_cond.shape[0]
    ranks = lax.axis_size("row")
    bias, inner, outer = pair_bias(atom_feat, pair_cond, token_mask, pair_weight)
    inner = swap(inner, "row", 1)
    odd_pairs = [(i, (i + 1) % ranks) for i in range(1, ranks, 2)]
    outer = lax.ppermute(outer, "row", odd_pairs + [(j, i) for i, j in odd_pairs])

    def widen(held, axis, bit, *others):
        return jnp.concatenate([held, after(swap(held, axis, bit), *others)], axis=0)

    bits, row_bits = bits_of(lax.axis_size("sample")), bits_of(ranks)
    orders = [bits, bits[:1] + bits[-1:] + bits[1:-1]]
    split = (bias.shape[1] // LANES + 1) // 2 * LANES
    mixed = atom_attention(0, atom_feat, inner, outer, atom_wq, atom_wk, atom_wv)
    got = after(swap(bias, "sample", bits[0]), mixed)
    held = [jnp.stack([bias[:, lanes], got[:, lanes]]) for lanes in (slice(0, split), slice(split, None))]
    mixed = after(mixed, held)
    norms, inputs = [], []
    for s in range(samples):
        if s:
            mixed = atom_attention(s, atom_feat, inner, outer, atom_wq, atom_wk, atom_wv)
            norms[-1] = widen(norms[-1], "row", row_bits[0], mixed)
            mixed = after(mixed, norms[-1])
        token_in, token_norm = gather_tokens(s, mixed, atom_feat, atom_token, atom_wo, agg_weight, token_gain, rows)
        inputs.append(token_in)
        norms.append(token_norm[None])
        if s == 0:
            for i in range(1, len(bits) - 1):
                held = [widen(h, "sample", order[i], token_norm) for h, order in zip(held, orders)]
            inner = after(inner, held, token_norm)
    halves = []
    for h, order in zip(held, orders):
        halves += [h, swap(h, "sample", order[-1])]
    done = []
    for s in range(samples):
        near = norms[s]
        for bit in row_bits[near.shape[0].bit_length() - 1 : -1]:
            near = widen(near, "row", bit, *done)
        far = swap(near, "row", row_bits[-1])
        part = project(near, query_weight, key_weight, value_weight, gate_weight, out_weight)
        if s == 0:
            bias = turn_bias(orders, row_bits, after(halves, part))
        earlier = done if s == samples - 1 else []
        done.append(attend(far, *part, inputs[s], bias, key_weight, value_weight, out_weight, earlier))
    return done[-1]


def solution(mesh):
    placed = (
        P("sample", "row", None),
        P("row"),
        P("row", "sample", None),
        P("sample"),
    ) + (P(),) * 12
    return jax.shard_map(
        shards, mesh=mesh, in_specs=placed, out_specs=P("sample", "row", None), check_vma=False
    )
```

```python
import functools
import math

import jax
import jax.numpy as jnp
from jax import lax
from jax.experimental import pallas as pl
from jax.experimental.pallas import tpu as pltpu
from jax.sharding import PartitionSpec as P

HEADS = 16
HEAD_DIM = 48
AHEADS = 4
AHEAD_DIM = 32
QWIN = 32
KWIN = 128
RIM = (KWIN - QWIN) // 2
LANES = 128
SUB = 8
F32 = jnp.float32
BF16 = jnp.bfloat16
MIB = 1024 * 1024
LOG2E = math.log2(math.e)
NT = (((1,), (1,)), ((), ()))


def layer_norm(x):
    mean = jnp.mean(x, -1, keepdims=True)
    centre = x - mean
    var = jnp.mean(centre * centre, -1, keepdims=True)
    return centre * lax.rsqrt(var + 1e-05)


def dot(a, b):
    return jnp.dot(a, b, preferred_element_type=F32)


def dot_nt(a, b):
    return lax.dot_general(a, b, NT, preferred_element_type=F32)


def iota(shape, dim):
    return lax.broadcasted_iota(jnp.int32, shape, dim)


def cost(micros):
    return pl.CostEstimate(flops=micros * 20_000_000, bytes_accessed=1_000, transcendentals=0)


def inverse(total):
    guess = pl.reciprocal(total, approx=True)
    return guess * (2.0 - total * guess)


def skewed(items, stages):
    held = list(items)
    for t in range(len(held) + len(stages) - 1):
        for k in reversed(range(len(stages))):
            if 0 <= t - k < len(held):
                held[t - k] = stages[k](held[t - k])
    return held


def bias_kernel(head, tail, pair, mask, weight, out, inner, outer, normed):
    odd = lax.axis_index("row") % 2 == 1
    inner[...] = jnp.where(odd, head[...], tail[...])
    outer[...] = jnp.where(odd, tail[...], head[...])
    cols, rows, chans = pair.shape
    for k in range(0, cols, 6):
        normed[k : k + 6] = layer_norm(pair[k : k + 6].astype(F32))
    spread = (iota((HEADS, LANES), 1) // SUB == iota((HEADS, LANES), 0)).astype(BF16)
    wide = lax.dot_general(weight[...], spread, (((0,), (0,)), ((), ())), preferred_element_type=F32).astype(BF16)
    tall = cols * SUB
    key_of = iota((tall, cols), 0) // SUB == iota((tall, cols), 1)
    open_row = jnp.broadcast_to(mask[...].reshape(1, cols), (LANES, cols)).astype(BF16)
    open_key = dot_nt(key_of.astype(BF16), open_row) > 0.5
    picked = (iota((cols, tall), 1) // SUB == iota((cols, tall), 0)).astype(BF16)
    row = iota((tall, LANES), 0)
    mine = iota((tall, LANES), 1) % SUB == row % SUB
    apart = lax.axis_index("sample") * cols + row // SUB - lax.axis_index("row") * rows - row % SUB

    def weigh(g):
        x = normed[:, g * SUB : (g + 1) * SUB].reshape(tall, chans).astype(BF16)
        raw = jnp.where(open_key | (apart == g * SUB), dot(x, wide), -30000.0)
        return g, jnp.where(mine, raw, 0.0).astype(BF16)

    def pick(item):
        g, raw = item
        out[:, g * LANES : (g + 1) * LANES] = dot(picked, raw).astype(BF16)

    skewed(range(rows // SUB), [weigh, pick])


def pair_bias(feat, pair_cond, token_mask, pair_weight):
    rows, cols, chans = pair_cond.shape
    samples, atoms, width = feat.shape
    edge = (samples, RIM, width)

    def whole(*shape):
        return pl.BlockSpec(shape, lambda i: (0,) * len(shape))

    return pl.pallas_call(
        bias_kernel,
        grid=(1,),
        out_shape=[
            jax.ShapeDtypeStruct((cols, rows * HEADS), BF16),
            jax.ShapeDtypeStruct(edge, BF16),
            jax.ShapeDtypeStruct(edge, BF16),
        ],
        in_specs=[
            pl.BlockSpec(edge, lambda i: (0, 0, 0)),
            pl.BlockSpec(edge, lambda i: (0, atoms // RIM - 1, 0)),
            whole(cols, rows, chans),
            whole(cols),
            whole(HEADS, chans),
        ],
        out_specs=[whole(cols, rows * HEADS), whole(*edge), whole(*edge)],
        scratch_shapes=[pltpu.VMEM((cols, rows, chans), F32)],
        compiler_params=pltpu.CompilerParams(vmem_limit_bytes=60 * MIB),
        cost_estimate=cost(3),
        name="pair_bias",
    )(feat, feat, jnp.transpose(pair_cond, (1, 0, 2)), token_mask, pair_weight.T)


def after(value, *others):
    return lax.optimization_barrier((value, *others))[0]


def swap(held, axis, far):
    return lax.ppermute(held, axis, [(i, i ^ far) for i in range(lax.axis_size(axis))])


def bits_of(devices):
    return [devices >> i for i in range(1, devices.bit_length())]


def places_of(bits):
    places = [0]
    for bit in bits:
        places += [p ^ bit for p in places]
    return places


def atom_kernel(sample, feat, inner, outer, wq, wk, wv, mixed, qs, ks, vs):
    atoms, chans = feat.shape[1:]
    rank = lax.axis_index("row")
    at_start = rank == 0
    at_end = rank == lax.axis_size("row") - 1
    wqkv = jnp.concatenate([wq[...], wk[...], wv[...]], axis=1)
    odd = rank % 2 == 1
    before = jnp.where(odd, inner[sample], outer[sample])
    behind = jnp.where(odd, outer[sample], inner[sample])

    def normalise(at):
        if isinstance(at, int):
            part = feat[sample, at : at + LANES]
        else:
            at, part = at
        return at, layer_norm(part.astype(F32)).astype(BF16)

    def project_atoms(item):
        at, normed = item
        count = normed.shape[0]
        if count == RIM:
            kv = dot(normed, wqkv[:, chans:]).astype(BF16)
        else:
            qkv = dot(normed, wqkv).astype(BF16)
            qs[at : at + count] = qkv[:, :chans]
            kv = qkv[:, chans:]
        ks[RIM + at : RIM + at + count] = kv[:, :chans]
        vs[RIM + at : RIM + at + count] = kv[:, chans:]

    skewed([*range(0, atoms, LANES), (-RIM, before), (atoms, behind)], [normalise, project_atoms])
    rate = LOG2E / AHEAD_DIM**0.5
    tall = AHEADS * QWIN
    head_of = iota((QWIN, chans), 1) // AHEAD_DIM
    keyat = iota((tall, KWIN), 1)
    batch = 6

    def score(first):
        out = []
        for at in range(first, first + batch * QWIN, QWIN):
            q = qs[at : at + QWIN]
            q = jnp.concatenate([jnp.where(head_of == h, q, jnp.zeros_like(q)) for h in range(AHEADS)], axis=0)
            s = dot_nt(q, ks[at : at + KWIN])
            if at < RIM:
                s = jnp.where(at_start & (keyat < RIM - at), -jnp.inf, s)
            if at + KWIN > RIM + atoms:
                s = jnp.where(at_end & (keyat >= RIM + atoms - at), -jnp.inf, s)
            out.append(s)
        return first, jnp.concatenate(out, axis=0)

    def soften(item):
        first, s = item
        e = jnp.exp2((s - jnp.max(s, -1, keepdims=True)) * rate)
        return first, e.astype(BF16), jnp.sum(e, -1, keepdims=True)

    def own_head(parts):
        acc = parts[:QWIN]
        for h in range(1, AHEADS):
            acc = jnp.where(head_of == h, parts[h * QWIN : (h + 1) * QWIN], acc)
        return acc

    def mix(item):
        first, e, total = item
        for i in range(batch):
            at = first + i * QWIN
            part = slice(i * tall, (i + 1) * tall)
            o = own_head(dot(e[part], vs[at : at + KWIN])) * inverse(own_head(total[part]))
            mixed[at : at + QWIN] = o.astype(BF16)

    skewed(range(0, atoms, batch * QWIN), [score, soften, mix])


def atom_attention(sample, feat, inner, outer, wq, wk, wv):
    atoms, chans = feat.shape[1:]
    vmem = pl.BlockSpec(memory_space=pltpu.VMEM)
    return pl.pallas_call(
        functools.partial(atom_kernel, sample),
        out_shape=jax.ShapeDtypeStruct((atoms, chans), BF16),
        in_specs=[vmem] * 6,
        out_specs=vmem,
        scratch_shapes=[
            pltpu.VMEM((atoms, chans), BF16),
            pltpu.VMEM((atoms + 2 * RIM, chans), BF16),
            pltpu.VMEM((atoms + 2 * RIM, chans), BF16),
        ],
        compiler_params=pltpu.CompilerParams(vmem_limit_bytes=16 * MIB),
        cost_estimate=cost(4),
        name="atom_attention",
    )(feat, inner, outer, wq, wk, wv)


def gather_kernel(sample, mixed, feat, token, wo, agg, gain, token_in, token_norm):
    atoms = feat.shape[1]
    rows = token_in.shape[0]
    local = token[...].reshape(1, atoms) - lax.axis_index("row") * rows
    step = 384
    sums = []

    def finish(c):
        return c, (feat[sample, c : c + step].astype(F32) + dot(mixed[c : c + step], wo[...])).astype(BF16)

    def hide(item):
        c, out = item
        return c, jnp.maximum(dot(out, agg[...]), 0.0).astype(BF16)

    def add(item):
        c, hidden = item
        onehot = (iota((rows, step), 0) == local[:, c : c + step]).astype(F32)
        part = dot(onehot.astype(BF16), hidden), jnp.sum(onehot, -1, keepdims=True)
        sums[:] = [a + b for a, b in zip(sums, part)] if sums else part

    skewed(range(0, atoms, step), [finish, hide, add])
    tin = sums[0] / sums[1]
    token_in[...] = tin
    token_norm[...] = (layer_norm(tin) * gain[...].reshape(1, -1)).astype(BF16)


def gather_tokens(sample, mixed, feat, token, wo, agg, gain, rows):
    width = agg.shape[1]
    vmem = pl.BlockSpec(memory_space=pltpu.VMEM)
    return pl.pallas_call(
        functools.partial(gather_kernel, sample),
        out_shape=[jax.ShapeDtypeStruct((rows, width), F32), jax.ShapeDtypeStruct((rows, width), BF16)],
        in_specs=[vmem] * 6,
        out_specs=[vmem, vmem],
        compiler_params=pltpu.CompilerParams(vmem_limit_bytes=16 * MIB),
        cost_estimate=cost(1),
        name="gather_tokens",
    )(mixed, feat, token, wo, agg, gain)


def turn_kernel(orders, row_bits, *refs):
    *halves, out, tall = refs
    rows = out.shape[0] // HEADS
    me = lax.axis_index("sample")
    at = 0
    for near, far, bits in zip(halves[::2], halves[1::2], orders):
        half, cols, wide = near.shape
        places = places_of(bits)
        for j in range(2 * half):
            place = sum(jnp.where(me ^ j == p, i, 0) for i, p in enumerate(places))
            block = jnp.where(place < half, near[place % half], far[place % half])
            tall[j * cols : (j + 1) * cols, at : at + wide] = block.astype(F32)
        at += wide
    starts = [pl.multiple_of((lax.axis_index("row") ^ p) * rows, SUB) for p in places_of(row_bits)]
    for g in range(rows // SUB):
        lanes = slice(g * LANES, (g + 1) * LANES)
        turned = jnp.concatenate([tall[pl.ds(start, rows), lanes] for start in starts], axis=0).T
        for h in range(HEADS):
            out[h * rows + g * SUB : h * rows + (g + 1) * SUB] = turned[h * SUB : (h + 1) * SUB] * LOG2E


def turn_bias(orders, row_bits, halves):
    half, cols, _ = halves[0].shape
    keys = 2 * half * cols
    wide = sum(near.shape[2] for near in halves[::2])
    vmem = pl.BlockSpec(memory_space=pltpu.VMEM)
    return pl.pallas_call(
        functools.partial(turn_kernel, orders, row_bits),
        out_shape=jax.ShapeDtypeStruct((wide, keys), F32),
        in_specs=[vmem] * len(halves),
        out_specs=vmem,
        scratch_shapes=[pltpu.VMEM((keys, wide), F32)],
        compiler_params=pltpu.CompilerParams(vmem_limit_bytes=24 * MIB),
        cost_estimate=cost(1),
        name="turn_bias",
    )(*halves)


def head_groups(width):
    groups = []
    for base in range(0, width, 8 * HEAD_DIM):
        first = base // HEAD_DIM
        groups.append((base, range(first, first + 5)))
        groups.append((base + LANES, range(first + 5, first + 8)))
    return groups


def stack(blocks):
    return jnp.concatenate([blocks[j].astype(F32) for j in range(blocks.shape[0])], axis=0).astype(BF16)


def project_kernel(near, wq, wk, wv, wg, wo, q, k, v, gate):
    x = stack(near)
    q[...] = dot(near[0], wq[...]).astype(BF16)
    gate[...] = jax.nn.sigmoid(dot(near[0], wg[...]))
    k[...] = dot(x, wk[...]).astype(BF16)
    v[...] = dot(x, wv[...]).astype(BF16)


def project(near, wq, wk, wv, wg, wo):
    half, rows, width = near.shape
    vmem = pl.BlockSpec(memory_space=pltpu.VMEM)
    return pl.pallas_call(
        project_kernel,
        out_shape=[
            jax.ShapeDtypeStruct((rows, width), BF16),
            jax.ShapeDtypeStruct((half * rows, width), BF16),
            jax.ShapeDtypeStruct((half * rows, width), BF16),
            jax.ShapeDtypeStruct((rows, width), F32),
        ],
        in_specs=[vmem] * 6,
        out_specs=[vmem] * 4,
        compiler_params=pltpu.CompilerParams(vmem_limit_bytes=24 * MIB),
        cost_estimate=cost(2),
        name="project",
    )(near, wq, wk, wv, wg, wo)


def attend_kernel(far, q, k_near, v_near, gate, token_in, bias, wk, wv, wo, *rest):
    *earlier, out, kt, v = rest
    rows, width = token_in.shape
    x = stack(far)
    for c in range(0, width, 2 * LANES):
        lanes = slice(c, c + 2 * LANES)
        k = jnp.concatenate([k_near[:, lanes].astype(F32), dot(x, wk[:, lanes])], axis=0)
        kt[lanes] = k.T.astype(BF16)
    v[: v_near.shape[0]] = v_near[...]
    v[v_near.shape[0] :] = dot(x, wv[...]).astype(BF16)
    scale = LOG2E / HEAD_DIM**0.5
    lane = iota((rows, 2 * LANES), 1)
    work = [(base, heads[i : i + 2]) for base, heads in head_groups(width) for i in range(0, len(heads), 2)]

    def channels(base, h):
        low = h * HEAD_DIM - base
        return (lane >= low) & (lane < low + HEAD_DIM)

    def score(item):
        base, heads = item
        mine = q[:, base : base + 2 * LANES].astype(F32)
        mine = jnp.concatenate([jnp.where(channels(base, h), mine, 0.0) for h in heads], axis=0).astype(BF16)
        some = bias[heads[0] * rows : (heads[-1] + 1) * rows]
        return item, dot(mine, kt[base : base + 2 * LANES]) * scale + some

    def soften(item):
        place, sc = item
        e = jnp.exp2(sc - jnp.max(sc, -1, keepdims=True))
        return place, e.astype(BF16), inverse(jnp.sum(e, -1, keepdims=True))

    mixes = {}

    def mix(item):
        (base, heads), e, share = item
        o = dot(e, v[:, base : base + 2 * LANES]) * share
        for i, h in enumerate(heads):
            mixes[base] = jnp.where(channels(base, h), o[i * rows : (i + 1) * rows], mixes.get(base, 0.0))

    skewed(work, [score, soften, mix])
    tiles = {}
    for base, _ in head_groups(width):
        for t in range(2):
            at = base + t * LANES
            part = mixes[base][:, t * LANES : (t + 1) * LANES]
            tiles[at] = tiles[at] + part if at in tiles else part
    gated = jnp.concatenate([tiles[at] for at in range(0, width, LANES)], axis=1) * gate[...]
    res = (token_in[...] + dot(gated.astype(BF16), wo[...])).astype(BF16)
    if earlier:
        for s, ref in enumerate(earlier):
            out[s] = ref[...]
        out[len(earlier)] = res
    else:
        out[...] = res


def attend(far, q, k, v, gate, token_in, bias, wk, wv, wo, earlier):
    rows, width = token_in.shape
    keys = 2 * k.shape[0]
    vmem = pl.BlockSpec(memory_space=pltpu.VMEM)
    shape = (len(earlier) + 1, rows, width) if earlier else (rows, width)
    return pl.pallas_call(
        attend_kernel,
        out_shape=jax.ShapeDtypeStruct(shape, BF16),
        in_specs=[vmem] * (10 + len(earlier)),
        out_specs=vmem,
        scratch_shapes=[pltpu.VMEM((width, keys), BF16), pltpu.VMEM((keys, width), BF16)],
        compiler_params=pltpu.CompilerParams(vmem_limit_bytes=24 * MIB),
        cost_estimate=cost(3),
        name="attend",
    )(far, q, k, v, gate, token_in, bias, wk, wv, wo, *earlier)


def shards(
    atom_feat,
    atom_token,
    pair_cond,
    token_mask,
    atom_wq,
    atom_wk,
    atom_wv,
    atom_wo,
    agg_weight,
    pair_weight,
    token_gain,
    query_weight,
    key_weight,
    value_weight,
    gate_weight,
    out_weight,
):
    samples = atom_feat.shape[0]
    rows = pair_cond.shape[0]
    ranks = lax.axis_size("row")
    bias, inner, outer = pair_bias(atom_feat, pair_cond, token_mask, pair_weight)
    inner = swap(inner, "row", 1)
    odd_pairs = [(i, (i + 1) % ranks) for i in range(1, ranks, 2)]
    outer = lax.ppermute(outer, "row", odd_pairs + [(j, i) for i, j in odd_pairs])

    def widen(held, axis, bit, *others):
        return jnp.concatenate([held, after(swap(held, axis, bit), *others)], axis=0)

    bits, row_bits = bits_of(lax.axis_size("sample")), bits_of(ranks)
    orders = [bits, bits[:1] + bits[-1:] + bits[1:-1]]
    split = (bias.shape[1] // LANES + 1) // 2 * LANES
    got = swap(bias, "sample", bits[0])
    norms, inputs = [], []
    for s in range(samples):
        mixed = atom_attention(s, atom_feat, inner, outer, atom_wq, atom_wk, atom_wv)
        if s:
            norms[-1] = widen(norms[-1], "row", row_bits[0], mixed)
            if s == 1:
                for i in range(1, len(bits) - 1):
                    held = [widen(h, "sample", order[i], mixed) for h, order in zip(held, orders)]
                mixed = after(mixed, held)
            mixed = after(mixed, norms[-1])
        token_in, token_norm = gather_tokens(s, mixed, atom_feat, atom_token, atom_wo, agg_weight, token_gain, rows)
        inputs.append(token_in)
        norms.append(token_norm[None])
        if s == 0:
            bias, got, _ = lax.optimization_barrier((bias, got, token_norm))
            held = [jnp.stack([bias[:, lanes], got[:, lanes]]) for lanes in (slice(0, split), slice(split, None))]
            inner = after(inner, held, token_norm)
    halves = []
    for h, order in zip(held, orders):
        halves += [h, swap(h, "sample", order[-1])]
    done = []
    for s in range(samples):
        near = norms[s]
        for bit in row_bits[near.shape[0].bit_length() - 1 : -1]:
            near = widen(near, "row", bit, *done)
        far = swap(near, "row", row_bits[-1])
        part = project(near, query_weight, key_weight, value_weight, gate_weight, out_weight)
        if s == 0:
            bias = turn_bias(orders, row_bits, after(halves, part))
        earlier = done if s == samples - 1 else []
        done.append(attend(far, *part, inputs[s], bias, key_weight, value_weight, out_weight, earlier))
    return done[-1]


def solution(mesh):
    placed = (
        P("sample", "row", None),
        P("row"),
        P("row", "sample", None),
        P("sample"),
    ) + (P(),) * 12
    return jax.shard_map(
        shards, mesh=mesh, in_specs=placed, out_specs=P("sample", "row", None), check_vma=False
    )
```

```python
import functools
import math

import jax
import jax.numpy as jnp
from jax import lax
from jax.experimental import pallas as pl
from jax.experimental.pallas import tpu as pltpu
from jax.sharding import PartitionSpec as P

HEADS = 16
HEAD_DIM = 48
AHEADS = 4
AHEAD_DIM = 32
QWIN = 32
KWIN = 128
RIM = (KWIN - QWIN) // 2
LANES = 128
SUB = 8
F32 = jnp.float32
BF16 = jnp.bfloat16
MIB = 1024 * 1024
LOG2E = math.log2(math.e)
NT = (((1,), (1,)), ((), ()))


def layer_norm(x):
    mean = jnp.mean(x, -1, keepdims=True)
    centre = x - mean
    var = jnp.mean(centre * centre, -1, keepdims=True)
    return centre * lax.rsqrt(var + 1e-05)


def dot(a, b):
    return jnp.dot(a, b, preferred_element_type=F32)


def dot_nt(a, b):
    return lax.dot_general(a, b, NT, preferred_element_type=F32)


def iota(shape, dim):
    return lax.broadcasted_iota(jnp.int32, shape, dim)


def cost(micros):
    return pl.CostEstimate(flops=micros * 20_000_000, bytes_accessed=1_000, transcendentals=0)


def inverse(total):
    guess = pl.reciprocal(total, approx=True)
    return guess * (2.0 - total * guess)


def skewed(items, stages):
    held = list(items)
    for t in range(len(held) + len(stages) - 1):
        for k in reversed(range(len(stages))):
            if 0 <= t - k < len(held):
                held[t - k] = stages[k](held[t - k])
    return held


def bias_kernel(head, tail, pair, mask, weight, out, inner, outer, normed):
    odd = lax.axis_index("row") % 2 == 1
    inner[...] = jnp.where(odd, head[...], tail[...])
    outer[...] = jnp.where(odd, tail[...], head[...])
    cols, rows, chans = pair.shape
    for k in range(0, cols, 6):
        normed[k : k + 6] = layer_norm(pair[k : k + 6].astype(F32))
    spread = (iota((HEADS, LANES), 1) // SUB == iota((HEADS, LANES), 0)).astype(BF16)
    wide = lax.dot_general(weight[...], spread, (((0,), (0,)), ((), ())), preferred_element_type=F32).astype(BF16)
    tall = cols * SUB
    key_of = iota((tall, cols), 0) // SUB == iota((tall, cols), 1)
    open_row = jnp.broadcast_to(mask[...].reshape(1, cols), (LANES, cols)).astype(BF16)
    open_key = dot_nt(key_of.astype(BF16), open_row) > 0.5
    picked = (iota((cols, tall), 1) // SUB == iota((cols, tall), 0)).astype(BF16)
    row = iota((tall, LANES), 0)
    mine = iota((tall, LANES), 1) % SUB == row % SUB
    apart = lax.axis_index("sample") * cols + row // SUB - lax.axis_index("row") * rows - row % SUB

    def weigh(g):
        x = normed[:, g * SUB : (g + 1) * SUB].reshape(tall, chans).astype(BF16)
        raw = jnp.where(open_key | (apart == g * SUB), dot(x, wide), -30000.0)
        return g, jnp.where(mine, raw, 0.0).astype(BF16)

    def pick(item):
        g, raw = item
        out[:, g * LANES : (g + 1) * LANES] = dot(picked, raw).astype(BF16)

    skewed(range(rows // SUB), [weigh, pick])


def pair_bias(feat, pair_cond, token_mask, pair_weight):
    rows, cols, chans = pair_cond.shape
    samples, atoms, width = feat.shape
    edge = (samples, RIM, width)

    def whole(*shape):
        return pl.BlockSpec(shape, lambda i: (0,) * len(shape))

    return pl.pallas_call(
        bias_kernel,
        grid=(1,),
        out_shape=[
            jax.ShapeDtypeStruct((cols, rows * HEADS), BF16),
            jax.ShapeDtypeStruct(edge, BF16),
            jax.ShapeDtypeStruct(edge, BF16),
        ],
        in_specs=[
            pl.BlockSpec(edge, lambda i: (0, 0, 0)),
            pl.BlockSpec(edge, lambda i: (0, atoms // RIM - 1, 0)),
            whole(cols, rows, chans),
            whole(cols),
            whole(HEADS, chans),
        ],
        out_specs=[whole(cols, rows * HEADS), whole(*edge), whole(*edge)],
        scratch_shapes=[pltpu.VMEM((cols, rows, chans), F32)],
        compiler_params=pltpu.CompilerParams(vmem_limit_bytes=60 * MIB),
        cost_estimate=cost(3),
        name="pair_bias",
    )(feat, feat, jnp.transpose(pair_cond, (1, 0, 2)), token_mask, pair_weight.T)


def after(value, *others):
    return lax.optimization_barrier((value, *others))[0]


def swap(held, axis, far):
    return lax.ppermute(held, axis, [(i, i ^ far) for i in range(lax.axis_size(axis))])


def bits_of(devices):
    return [devices >> i for i in range(1, devices.bit_length())]


def places_of(bits):
    places = [0]
    for bit in bits:
        places += [p ^ bit for p in places]
    return places


def windows_attend(starts, qs, ks, vs, mixed, shift, hide):
    rate = LOG2E / AHEAD_DIM**0.5
    tall = AHEADS * QWIN
    head_of = iota((QWIN, qs.shape[1]), 1) // AHEAD_DIM

    def score(batch):
        out = []
        for at in batch:
            q = qs[at - shift : at - shift + QWIN]
            q = jnp.concatenate([jnp.where(head_of == h, q, jnp.zeros_like(q)) for h in range(AHEADS)], axis=0)
            out.append(hide(at, dot_nt(q, ks[at : at + KWIN])))
        return batch, jnp.concatenate(out, axis=0)

    def soften(item):
        batch, s = item
        e = jnp.exp2((s - jnp.max(s, -1, keepdims=True)) * rate)
        return batch, e.astype(BF16), jnp.sum(e, -1, keepdims=True)

    def own_head(parts):
        acc = parts[:QWIN]
        for h in range(1, AHEADS):
            acc = jnp.where(head_of == h, parts[h * QWIN : (h + 1) * QWIN], acc)
        return acc

    def mix(item):
        batch, e, total = item
        for i, at in enumerate(batch):
            part = slice(i * tall, (i + 1) * tall)
            o = own_head(dot(e[part], vs[at : at + KWIN])) * inverse(own_head(total[part]))
            mixed[at - shift : at - shift + QWIN] = o.astype(BF16)

    skewed(starts, [score, soften, mix])


def halo_of(sample, inner, outer):
    odd = lax.axis_index("row") % 2 == 1
    return jnp.where(odd, inner[sample], outer[sample]), jnp.where(odd, outer[sample], inner[sample])


def hide_outside(atoms):
    rank = lax.axis_index("row")
    at_start = rank == 0
    at_end = rank == lax.axis_size("row") - 1
    keyat = iota((AHEADS * QWIN, KWIN), 1)

    def hide(at, s):
        if at < RIM:
            s = jnp.where(at_start & (keyat < RIM - at), -jnp.inf, s)
        if at + KWIN > RIM + atoms:
            s = jnp.where(at_end & (keyat >= RIM + atoms - at), -jnp.inf, s)
        return s

    return hide


def atom_kernel(sample, feat, *refs):
    *halo, wq, wk, wv, mixed, qs, ks, vs = refs
    atoms, chans = feat.shape[1:]
    wqkv = jnp.concatenate([wq[...], wk[...], wv[...]], axis=1)

    def normalise(at):
        if isinstance(at, int):
            part = feat[sample, at : at + LANES]
        else:
            at, part = at
        return at, layer_norm(part.astype(F32)).astype(BF16)

    def project_atoms(item):
        at, normed = item
        count = normed.shape[0]
        if count == RIM:
            kv = dot(normed, wqkv[:, chans:]).astype(BF16)
        else:
            qkv = dot(normed, wqkv).astype(BF16)
            qs[at : at + count] = qkv[:, :chans]
            kv = qkv[:, chans:]
        ks[RIM + at : RIM + at + count] = kv[:, :chans]
        vs[RIM + at : RIM + at + count] = kv[:, chans:]

    parts = list(range(0, atoms, LANES))
    if halo:
        before, behind = halo_of(sample, *halo)
        parts += [(-RIM, before), (atoms, behind)]
    skewed(parts, [normalise, project_atoms])
    starts = list(range(0, atoms, QWIN))
    if not halo:
        starts = [at for at in starts if RIM <= at <= atoms + RIM - KWIN]
    batch = 8 if len(starts) % 8 == 0 else 6
    batches = [starts[i : i + batch] for i in range(0, len(starts), batch)]
    windows_attend(batches, qs, ks, vs, mixed, 0, hide_outside(atoms))


def atom_attention(sample, feat, halo, wq, wk, wv):
    atoms, chans = feat.shape[1:]
    vmem = pl.BlockSpec(memory_space=pltpu.VMEM)
    return pl.pallas_call(
        functools.partial(atom_kernel, sample),
        out_shape=jax.ShapeDtypeStruct((atoms, chans), BF16),
        in_specs=[vmem] * (4 + len(halo)),
        out_specs=vmem,
        scratch_shapes=[
            pltpu.VMEM((atoms, chans), BF16),
            pltpu.VMEM((atoms + 2 * RIM, chans), BF16),
            pltpu.VMEM((atoms + 2 * RIM, chans), BF16),
        ],
        compiler_params=pltpu.CompilerParams(vmem_limit_bytes=16 * MIB),
        cost_estimate=cost(4),
        name="atom_attention",
    )(feat, *halo, wq, wk, wv)


def gather_kernel(sample, mixed, feat, token, wo, agg, gain, *refs):
    *outside, token_in, token_norm, qs, ks, vs, ends = refs
    atoms, chans = feat.shape[1:]
    rows = token_in.shape[0]
    local = token[...].reshape(1, atoms) - lax.axis_index("row") * rows
    step = 384
    sums = []
    edge = 2 * QWIN
    if outside:
        inner, outer, wq, wk, wv = outside
        before, behind = halo_of(sample, inner, outer)
        wqkv = jnp.concatenate([wq[...], wk[...], wv[...]], axis=1)
        near = edge + KWIN - QWIN - RIM
        both = [before, feat[sample, :near], feat[sample, atoms - near :], behind]
        qkv = dot(layer_norm(jnp.concatenate([p.astype(F32) for p in both], axis=0)).astype(BF16), wqkv).astype(BF16)
        qs[...] = qkv[:, :chans]
        ks[...] = qkv[:, chans : 2 * chans]
        vs[...] = qkv[:, 2 * chans :]
        apart = atoms - 2 * near
        starts = [0, QWIN, RIM + near, RIM + near + QWIN]
        hide = hide_outside(atoms)
        windows_attend([starts], qs, ks, vs, ends, -RIM, lambda at, s: hide(at if at < RIM else at + apart, s))

    def finish(c):
        part = mixed[c : c + step]
        if outside and c == 0:
            part = jnp.concatenate([ends[RIM : RIM + edge], part[edge:]], axis=0)
        if outside and c + step == atoms:
            at = ends.shape[0] - RIM - edge
            part = jnp.concatenate([part[: step - edge], ends[at : at + edge]], axis=0)
        return c, (feat[sample, c : c + step].astype(F32) + dot(part, wo[...])).astype(BF16)

    def hide_below(item):
        c, out = item
        return c, jnp.maximum(dot(out, agg[...]), 0.0).astype(BF16)

    def add(item):
        c, hidden = item
        onehot = (iota((rows, step), 0) == local[:, c : c + step]).astype(F32)
        part = dot(onehot.astype(BF16), hidden), jnp.sum(onehot, -1, keepdims=True)
        sums[:] = [a + b for a, b in zip(sums, part)] if sums else part

    chunks = list(range(0, atoms, step))
    skewed(chunks[1:-1] + [chunks[0], chunks[-1]], [finish, hide_below, add])
    tin = sums[0] / sums[1]
    token_in[...] = tin
    token_norm[...] = (layer_norm(tin) * gain[...].reshape(1, -1)).astype(BF16)


def gather_tokens(sample, mixed, feat, token, wo, agg, gain, outside, rows):
    width = agg.shape[1]
    chans = feat.shape[2]
    reach = 2 * (KWIN + QWIN)
    vmem = pl.BlockSpec(memory_space=pltpu.VMEM)
    return pl.pallas_call(
        functools.partial(gather_kernel, sample),
        out_shape=[jax.ShapeDtypeStruct((rows, width), F32), jax.ShapeDtypeStruct((rows, width), BF16)],
        in_specs=[vmem] * (6 + len(outside)),
        out_specs=[vmem, vmem],
        scratch_shapes=[pltpu.VMEM((reach, chans), BF16)] * 4,
        compiler_params=pltpu.CompilerParams(vmem_limit_bytes=16 * MIB),
        cost_estimate=cost(1),
        name="gather_tokens",
    )(mixed, feat, token, wo, agg, gain, *outside)


def turn_kernel(orders, row_bits, *refs):
    *halves, out, tall = refs
    rows = out.shape[0] // HEADS
    me = lax.axis_index("sample")
    at = 0
    for near, far, bits in zip(halves[::2], halves[1::2], orders):
        half, cols, wide = near.shape
        places = places_of(bits)
        for j in range(2 * half):
            place = sum(jnp.where(me ^ j == p, i, 0) for i, p in enumerate(places))
            block = jnp.where(place < half, near[place % half], far[place % half])
            tall[j * cols : (j + 1) * cols, at : at + wide] = block.astype(F32)
        at += wide
    starts = [pl.multiple_of((lax.axis_index("row") ^ p) * rows, SUB) for p in places_of(row_bits)]
    for g in range(rows // SUB):
        lanes = slice(g * LANES, (g + 1) * LANES)
        turned = jnp.concatenate([tall[pl.ds(start, rows), lanes] for start in starts], axis=0).T
        for h in range(HEADS):
            out[h * rows + g * SUB : h * rows + (g + 1) * SUB] = turned[h * SUB : (h + 1) * SUB] * LOG2E


def turn_bias(orders, row_bits, halves):
    half, cols, _ = halves[0].shape
    keys = 2 * half * cols
    wide = sum(near.shape[2] for near in halves[::2])
    vmem = pl.BlockSpec(memory_space=pltpu.VMEM)
    return pl.pallas_call(
        functools.partial(turn_kernel, orders, row_bits),
        out_shape=jax.ShapeDtypeStruct((wide, keys), F32),
        in_specs=[vmem] * len(halves),
        out_specs=vmem,
        scratch_shapes=[pltpu.VMEM((keys, wide), F32)],
        compiler_params=pltpu.CompilerParams(vmem_limit_bytes=24 * MIB),
        cost_estimate=cost(1),
        name="turn_bias",
    )(*halves)


def head_groups(width):
    groups = []
    for base in range(0, width, 8 * HEAD_DIM):
        first = base // HEAD_DIM
        groups.append((base, range(first, first + 5)))
        groups.append((base + LANES, range(first + 5, first + 8)))
    return groups


def stack(blocks):
    return jnp.concatenate([blocks[j].astype(F32) for j in range(blocks.shape[0])], axis=0).astype(BF16)


def project_kernel(near, wq, wk, wv, wg, wo, q, k, v, gate):
    x = stack(near)
    q[...] = dot(near[0], wq[...]).astype(BF16)
    gate[...] = jax.nn.sigmoid(dot(near[0], wg[...]))
    k[...] = dot(x, wk[...]).astype(BF16)
    v[...] = dot(x, wv[...]).astype(BF16)


def project(near, wq, wk, wv, wg, wo):
    half, rows, width = near.shape
    vmem = pl.BlockSpec(memory_space=pltpu.VMEM)
    return pl.pallas_call(
        project_kernel,
        out_shape=[
            jax.ShapeDtypeStruct((rows, width), BF16),
            jax.ShapeDtypeStruct((half * rows, width), BF16),
            jax.ShapeDtypeStruct((half * rows, width), BF16),
            jax.ShapeDtypeStruct((rows, width), F32),
        ],
        in_specs=[vmem] * 6,
        out_specs=[vmem] * 4,
        compiler_params=pltpu.CompilerParams(vmem_limit_bytes=24 * MIB),
        cost_estimate=cost(2),
        name="project",
    )(near, wq, wk, wv, wg, wo)


def attend_kernel(far, q, k_near, v_near, gate, token_in, bias, wk, wv, wo, *rest):
    *earlier, out, kt, v = rest
    rows, width = token_in.shape
    x = stack(far)
    for c in range(0, width, 2 * LANES):
        lanes = slice(c, c + 2 * LANES)
        k = jnp.concatenate([k_near[:, lanes].astype(F32), dot(x, wk[:, lanes])], axis=0)
        kt[lanes] = k.T.astype(BF16)
    v[: v_near.shape[0]] = v_near[...]
    v[v_near.shape[0] :] = dot(x, wv[...]).astype(BF16)
    scale = LOG2E / HEAD_DIM**0.5
    lane = iota((rows, 2 * LANES), 1)
    work = [(base, heads[i : i + 2]) for base, heads in head_groups(width) for i in range(0, len(heads), 2)]

    def channels(base, h):
        low = h * HEAD_DIM - base
        return (lane >= low) & (lane < low + HEAD_DIM)

    def score(item):
        base, heads = item
        mine = q[:, base : base + 2 * LANES].astype(F32)
        mine = jnp.concatenate([jnp.where(channels(base, h), mine, 0.0) for h in heads], axis=0).astype(BF16)
        some = bias[heads[0] * rows : (heads[-1] + 1) * rows]
        return item, dot(mine, kt[base : base + 2 * LANES]) * scale + some

    def soften(item):
        place, sc = item
        e = jnp.exp2(sc - jnp.max(sc, -1, keepdims=True))
        return place, e.astype(BF16), inverse(jnp.sum(e, -1, keepdims=True))

    mixes = {}

    def mix(item):
        (base, heads), e, share = item
        o = dot(e, v[:, base : base + 2 * LANES]) * share
        for i, h in enumerate(heads):
            mixes[base] = jnp.where(channels(base, h), o[i * rows : (i + 1) * rows], mixes.get(base, 0.0))

    skewed(work, [score, soften, mix])
    tiles = {}
    for base, _ in head_groups(width):
        for t in range(2):
            at = base + t * LANES
            part = mixes[base][:, t * LANES : (t + 1) * LANES]
            tiles[at] = tiles[at] + part if at in tiles else part
    gated = jnp.concatenate([tiles[at] for at in range(0, width, LANES)], axis=1) * gate[...]
    res = (token_in[...] + dot(gated.astype(BF16), wo[...])).astype(BF16)
    if earlier:
        for s, ref in enumerate(earlier):
            out[s] = ref[...]
        out[len(earlier)] = res
    else:
        out[...] = res


def attend(far, q, k, v, gate, token_in, bias, wk, wv, wo, earlier):
    rows, width = token_in.shape
    keys = 2 * k.shape[0]
    vmem = pl.BlockSpec(memory_space=pltpu.VMEM)
    shape = (len(earlier) + 1, rows, width) if earlier else (rows, width)
    return pl.pallas_call(
        attend_kernel,
        out_shape=jax.ShapeDtypeStruct(shape, BF16),
        in_specs=[vmem] * (10 + len(earlier)),
        out_specs=vmem,
        scratch_shapes=[pltpu.VMEM((width, keys), BF16), pltpu.VMEM((keys, width), BF16)],
        compiler_params=pltpu.CompilerParams(vmem_limit_bytes=24 * MIB),
        cost_estimate=cost(3),
        name="attend",
    )(far, q, k, v, gate, token_in, bias, wk, wv, wo, *earlier)


def shards(
    atom_feat,
    atom_token,
    pair_cond,
    token_mask,
    atom_wq,
    atom_wk,
    atom_wv,
    atom_wo,
    agg_weight,
    pair_weight,
    token_gain,
    query_weight,
    key_weight,
    value_weight,
    gate_weight,
    out_weight,
):
    samples = atom_feat.shape[0]
    rows = pair_cond.shape[0]
    ranks = lax.axis_size("row")
    bias, inner, outer = pair_bias(atom_feat, pair_cond, token_mask, pair_weight)
    inner = swap(inner, "row", 1)
    odd_pairs = [(i, (i + 1) % ranks) for i in range(1, ranks, 2)]
    outer = lax.ppermute(outer, "row", odd_pairs + [(j, i) for i, j in odd_pairs])

    def widen(held, axis, bit, *others):
        return jnp.concatenate([held, after(swap(held, axis, bit), *others)], axis=0)

    bits, row_bits = bits_of(lax.axis_size("sample")), bits_of(ranks)
    orders = [bits, bits[:1] + bits[-1:] + bits[1:-1]]
    split = (bias.shape[1] // LANES + 1) // 2 * LANES
    got = swap(bias, "sample", bits[0])
    norms, inputs = [], []
    for s in range(samples):
        halo = (inner, outer)
        mixed = atom_attention(s, atom_feat, halo if s else (), atom_wq, atom_wk, atom_wv)
        if s:
            norms[-1] = widen(norms[-1], "row", row_bits[0], mixed)
            if s == 1:
                for i in range(1, len(bits) - 1):
                    held = [widen(h, "sample", order[i], mixed) for h, order in zip(held, orders)]
                mixed = after(mixed, held)
            mixed = after(mixed, norms[-1])
        outside = () if s else (*halo, atom_wq, atom_wk, atom_wv)
        token_in, token_norm = gather_tokens(
            s, mixed, atom_feat, atom_token, atom_wo, agg_weight, token_gain, outside, rows
        )
        inputs.append(token_in)
        norms.append(token_norm[None])
        if s == 0:
            bias, got, _ = lax.optimization_barrier((bias, got, token_norm))
            held = [jnp.stack([bias[:, lanes], got[:, lanes]]) for lanes in (slice(0, split), slice(split, None))]
            inner = after(inner, held, token_norm)
    halves = []
    for h, order in zip(held, orders):
        halves += [h, swap(h, "sample", order[-1])]
    done = []
    for s in range(samples):
        near = norms[s]
        for bit in row_bits[near.shape[0].bit_length() - 1 : -1]:
            near = widen(near, "row", bit, *done)
        far = swap(near, "row", row_bits[-1])
        part = project(near, query_weight, key_weight, value_weight, gate_weight, out_weight)
        if s == 0:
            bias = turn_bias(orders, row_bits, after(halves, part))
        earlier = done if s == samples - 1 else []
        done.append(attend(far, *part, inputs[s], bias, key_weight, value_weight, out_weight, earlier))
    return done[-1]


def solution(mesh):
    placed = (
        P("sample", "row", None),
        P("row"),
        P("row", "sample", None),
        P("sample"),
    ) + (P(),) * 12
    return jax.shard_map(
        shards, mesh=mesh, in_specs=placed, out_specs=P("sample", "row", None), check_vma=False
    )
```

```python
import functools
import math

import jax
import jax.numpy as jnp
from jax import lax
from jax.experimental import pallas as pl
from jax.experimental.pallas import tpu as pltpu
from jax.sharding import PartitionSpec as P

HEADS = 16
HEAD_DIM = 48
AHEADS = 4
AHEAD_DIM = 32
QWIN = 32
KWIN = 128
RIM = (KWIN - QWIN) // 2
LANES = 128
SUB = 8
F32 = jnp.float32
BF16 = jnp.bfloat16
MIB = 1024 * 1024
LOG2E = math.log2(math.e)
NT = (((1,), (1,)), ((), ()))


def layer_norm(x):
    mean = jnp.mean(x, -1, keepdims=True)
    centre = x - mean
    var = jnp.mean(centre * centre, -1, keepdims=True)
    return centre * lax.rsqrt(var + 1e-05)


def dot(a, b):
    return jnp.dot(a, b, preferred_element_type=F32)


def dot_nt(a, b):
    return lax.dot_general(a, b, NT, preferred_element_type=F32)


def iota(shape, dim):
    return lax.broadcasted_iota(jnp.int32, shape, dim)


def cost(micros):
    return pl.CostEstimate(flops=micros * 20_000_000, bytes_accessed=1_000, transcendentals=0)


def inverse(total):
    guess = pl.reciprocal(total, approx=True)
    return guess * (2.0 - total * guess)


def skewed(items, stages):
    held = list(items)
    for t in range(len(held) + len(stages) - 1):
        for k in reversed(range(len(stages))):
            if 0 <= t - k < len(held):
                held[t - k] = stages[k](held[t - k])
    return held


def bias_kernel(head, tail, pair, mask, weight, out, inner, outer, normed):
    odd = lax.axis_index("row") % 2 == 1
    inner[...] = jnp.where(odd, head[...], tail[...])
    outer[...] = jnp.where(odd, tail[...], head[...])
    cols, rows, chans = pair.shape
    for k in range(0, cols, 6):
        normed[k : k + 6] = layer_norm(pair[k : k + 6].astype(F32))
    spread = (iota((HEADS, LANES), 1) // SUB == iota((HEADS, LANES), 0)).astype(BF16)
    wide = lax.dot_general(weight[...], spread, (((0,), (0,)), ((), ())), preferred_element_type=F32).astype(BF16)
    tall = cols * SUB
    key_of = iota((tall, cols), 0) // SUB == iota((tall, cols), 1)
    open_row = jnp.broadcast_to(mask[...].reshape(1, cols), (LANES, cols)).astype(BF16)
    open_key = dot_nt(key_of.astype(BF16), open_row) > 0.5
    picked = (iota((cols, tall), 1) // SUB == iota((cols, tall), 0)).astype(BF16)
    row = iota((tall, LANES), 0)
    mine = iota((tall, LANES), 1) % SUB == row % SUB
    apart = lax.axis_index("sample") * cols + row // SUB - lax.axis_index("row") * rows - row % SUB

    def weigh(g):
        x = normed[:, g * SUB : (g + 1) * SUB].reshape(tall, chans).astype(BF16)
        raw = jnp.where(open_key | (apart == g * SUB), dot(x, wide), -30000.0)
        return g, jnp.where(mine, raw, 0.0).astype(BF16)

    def pick(item):
        g, raw = item
        out[:, g * LANES : (g + 1) * LANES] = dot(picked, raw).astype(BF16)

    skewed(range(rows // SUB), [weigh, pick])


def pair_bias(feat, pair_cond, token_mask, pair_weight):
    rows, cols, chans = pair_cond.shape
    samples, atoms, width = feat.shape
    edge = (samples, RIM, width)

    def whole(*shape):
        return pl.BlockSpec(shape, lambda i: (0,) * len(shape))

    return pl.pallas_call(
        bias_kernel,
        grid=(1,),
        out_shape=[
            jax.ShapeDtypeStruct((cols, rows * HEADS), BF16),
            jax.ShapeDtypeStruct(edge, BF16),
            jax.ShapeDtypeStruct(edge, BF16),
        ],
        in_specs=[
            pl.BlockSpec(edge, lambda i: (0, 0, 0)),
            pl.BlockSpec(edge, lambda i: (0, atoms // RIM - 1, 0)),
            whole(cols, rows, chans),
            whole(cols),
            whole(HEADS, chans),
        ],
        out_specs=[whole(cols, rows * HEADS), whole(*edge), whole(*edge)],
        scratch_shapes=[pltpu.VMEM((cols, rows, chans), F32)],
        compiler_params=pltpu.CompilerParams(vmem_limit_bytes=60 * MIB),
        cost_estimate=cost(3),
        name="pair_bias",
    )(feat, feat, jnp.transpose(pair_cond, (1, 0, 2)), token_mask, pair_weight.T)


def after(value, *others):
    return lax.optimization_barrier((value, *others))[0]


def swap(held, axis, far):
    return lax.ppermute(held, axis, [(i, i ^ far) for i in range(lax.axis_size(axis))])


def bits_of(devices):
    return [devices >> i for i in range(1, devices.bit_length())]


def places_of(bits):
    places = [0]
    for bit in bits:
        places += [p ^ bit for p in places]
    return places


def windows_attend(starts, qs, ks, vs, mixed, shift, hide):
    rate = LOG2E / AHEAD_DIM**0.5
    tall = AHEADS * QWIN
    head_of = iota((QWIN, qs.shape[1]), 1) // AHEAD_DIM

    def score(batch):
        out = []
        for at in batch:
            q = qs[at - shift : at - shift + QWIN]
            q = jnp.concatenate([jnp.where(head_of == h, q, jnp.zeros_like(q)) for h in range(AHEADS)], axis=0)
            out.append(hide(at, dot_nt(q, ks[at : at + KWIN])))
        return batch, jnp.concatenate(out, axis=0)

    def soften(item):
        batch, s = item
        e = jnp.exp2((s - jnp.max(s, -1, keepdims=True)) * rate)
        return batch, e.astype(BF16), jnp.sum(e, -1, keepdims=True)

    def own_head(parts):
        acc = parts[:QWIN]
        for h in range(1, AHEADS):
            acc = jnp.where(head_of == h, parts[h * QWIN : (h + 1) * QWIN], acc)
        return acc

    def mix(item):
        batch, e, total = item
        for i, at in enumerate(batch):
            part = slice(i * tall, (i + 1) * tall)
            o = own_head(dot(e[part], vs[at : at + KWIN])) * inverse(own_head(total[part]))
            mixed[at - shift : at - shift + QWIN] = o.astype(BF16)

    skewed(starts, [score, soften, mix])


def halo_of(sample, inner, outer):
    odd = lax.axis_index("row") % 2 == 1
    return jnp.where(odd, inner[sample], outer[sample]), jnp.where(odd, outer[sample], inner[sample])


def hide_outside(atoms):
    rank = lax.axis_index("row")
    at_start = rank == 0
    at_end = rank == lax.axis_size("row") - 1
    keyat = iota((AHEADS * QWIN, KWIN), 1)

    def hide(at, s):
        if at < RIM:
            s = jnp.where(at_start & (keyat < RIM - at), -jnp.inf, s)
        if at + KWIN > RIM + atoms:
            s = jnp.where(at_end & (keyat >= RIM + atoms - at), -jnp.inf, s)
        return s

    return hide


def atom_kernel(sample, feat, *refs):
    *halo, wq, wk, wv, mixed, qs, ks, vs = refs
    atoms, chans = feat.shape[1:]
    wqkv = jnp.concatenate([wq[...], wk[...], wv[...]], axis=1)

    def normalise(at):
        if isinstance(at, int):
            part = feat[sample, at : at + LANES]
        else:
            at, part = at
        return at, layer_norm(part.astype(F32)).astype(BF16)

    def project_atoms(item):
        at, normed = item
        count = normed.shape[0]
        if count == RIM:
            kv = dot(normed, wqkv[:, chans:]).astype(BF16)
        else:
            qkv = dot(normed, wqkv).astype(BF16)
            qs[at : at + count] = qkv[:, :chans]
            kv = qkv[:, chans:]
        ks[RIM + at : RIM + at + count] = kv[:, :chans]
        vs[RIM + at : RIM + at + count] = kv[:, chans:]

    parts = list(range(0, atoms, LANES))
    if halo:
        before, behind = halo_of(sample, *halo)
        parts += [(-RIM, before), (atoms, behind)]
    skewed(parts, [normalise, project_atoms])
    starts = list(range(0, atoms, QWIN))
    if not halo:
        starts = [at for at in starts if RIM <= at <= atoms + RIM - KWIN]
    batch = 6
    batches = [starts[i : i + batch] for i in range(0, len(starts), batch)]
    windows_attend(batches, qs, ks, vs, mixed, 0, hide_outside(atoms))


def atom_attention(sample, feat, halo, wq, wk, wv):
    atoms, chans = feat.shape[1:]
    vmem = pl.BlockSpec(memory_space=pltpu.VMEM)
    return pl.pallas_call(
        functools.partial(atom_kernel, sample),
        out_shape=jax.ShapeDtypeStruct((atoms, chans), BF16),
        in_specs=[vmem] * (4 + len(halo)),
        out_specs=vmem,
        scratch_shapes=[
            pltpu.VMEM((atoms, chans), BF16),
            pltpu.VMEM((atoms + 2 * RIM, chans), BF16),
            pltpu.VMEM((atoms + 2 * RIM, chans), BF16),
        ],
        compiler_params=pltpu.CompilerParams(vmem_limit_bytes=16 * MIB),
        cost_estimate=cost(4),
        name="atom_attention",
    )(feat, *halo, wq, wk, wv)


def gather_kernel(sample, mixed, feat, token, wo, agg, gain, *refs):
    *outside, token_in, token_norm, qs, ks, vs, ends = refs
    atoms, chans = feat.shape[1:]
    rows = token_in.shape[0]
    local = token[...].reshape(1, atoms) - lax.axis_index("row") * rows
    step = 384
    sums = []
    edge = 2 * QWIN
    if outside:
        inner, outer, wq, wk, wv = outside
        before, behind = halo_of(sample, inner, outer)
        wqkv = jnp.concatenate([wq[...], wk[...], wv[...]], axis=1)
        near = edge + KWIN - QWIN - RIM
        both = [before, feat[sample, :near], feat[sample, atoms - near :], behind]
        qkv = dot(layer_norm(jnp.concatenate([p.astype(F32) for p in both], axis=0)).astype(BF16), wqkv).astype(BF16)
        qs[...] = qkv[:, :chans]
        ks[...] = qkv[:, chans : 2 * chans]
        vs[...] = qkv[:, 2 * chans :]
        apart = atoms - 2 * near
        starts = [0, QWIN, RIM + near, RIM + near + QWIN]
        hide = hide_outside(atoms)
        windows_attend([starts], qs, ks, vs, ends, -RIM, lambda at, s: hide(at if at < RIM else at + apart, s))

    def finish(c):
        part = mixed[c : c + step]
        if outside and c == 0:
            part = jnp.concatenate([ends[RIM : RIM + edge], part[edge:]], axis=0)
        if outside and c + step == atoms:
            at = ends.shape[0] - RIM - edge
            part = jnp.concatenate([part[: step - edge], ends[at : at + edge]], axis=0)
        return c, (feat[sample, c : c + step].astype(F32) + dot(part, wo[...])).astype(BF16)

    def hide_below(item):
        c, out = item
        return c, jnp.maximum(dot(out, agg[...]), 0.0).astype(BF16)

    def add(item):
        c, hidden = item
        onehot = (iota((rows, step), 0) == local[:, c : c + step]).astype(F32)
        part = dot(onehot.astype(BF16), hidden), jnp.sum(onehot, -1, keepdims=True)
        sums[:] = [a + b for a, b in zip(sums, part)] if sums else part

    chunks = list(range(0, atoms, step))
    skewed(chunks[1:-1] + [chunks[0], chunks[-1]], [finish, hide_below, add])
    tin = sums[0] / sums[1]
    token_in[...] = tin
    token_norm[...] = (layer_norm(tin) * gain[...].reshape(1, -1)).astype(BF16)


def gather_tokens(sample, mixed, feat, token, wo, agg, gain, outside, rows):
    width = agg.shape[1]
    chans = feat.shape[2]
    reach = 2 * (KWIN + QWIN)
    vmem = pl.BlockSpec(memory_space=pltpu.VMEM)
    return pl.pallas_call(
        functools.partial(gather_kernel, sample),
        out_shape=[jax.ShapeDtypeStruct((rows, width), F32), jax.ShapeDtypeStruct((rows, width), BF16)],
        in_specs=[vmem] * (6 + len(outside)),
        out_specs=[vmem, vmem],
        scratch_shapes=[pltpu.VMEM((reach, chans), BF16)] * 4,
        compiler_params=pltpu.CompilerParams(vmem_limit_bytes=16 * MIB),
        cost_estimate=cost(1),
        name="gather_tokens",
    )(mixed, feat, token, wo, agg, gain, *outside)


def head_groups(width):
    groups = []
    for base in range(0, width, 8 * HEAD_DIM):
        first = base // HEAD_DIM
        groups.append((base, range(first, first + 5)))
        groups.append((base + LANES, range(first + 5, first + 8)))
    return groups


def stack(blocks):
    return jnp.concatenate([blocks[j].astype(F32) for j in range(blocks.shape[0])], axis=0).astype(BF16)


def project_kernel(near, *refs):
    *far, wq, wk, wv, wg, wo, q, k, v, gate = refs
    x = jnp.concatenate([stack(blocks) for blocks in (near, *far)], axis=0)
    q[...] = dot(near[0], wq[...]).astype(BF16)
    gate[...] = jax.nn.sigmoid(dot(near[0], wg[...]))
    if far:
        for c in range(0, x.shape[1], 2 * LANES):
            k[c : c + 2 * LANES] = dot(x, wk[:, c : c + 2 * LANES]).T.astype(BF16)
    else:
        k[...] = dot(x, wk[...]).astype(BF16)
    v[...] = dot(x, wv[...]).astype(BF16)


def project(blocks, wq, wk, wv, wg, wo):
    half, rows, width = blocks[0].shape
    keys = len(blocks) * half * rows
    vmem = pl.BlockSpec(memory_space=pltpu.VMEM)
    return pl.pallas_call(
        project_kernel,
        out_shape=[
            jax.ShapeDtypeStruct((rows, width), BF16),
            jax.ShapeDtypeStruct((width, keys) if len(blocks) > 1 else (keys, width), BF16),
            jax.ShapeDtypeStruct((keys, width), BF16),
            jax.ShapeDtypeStruct((rows, width), F32),
        ],
        in_specs=[vmem] * (5 + len(blocks)),
        out_specs=[vmem] * 4,
        compiler_params=pltpu.CompilerParams(vmem_limit_bytes=24 * MIB),
        cost_estimate=cost(2),
        name="project",
    )(*blocks, wq, wk, wv, wg, wo)


def turn_kernel(orders, row_bits, *refs):
    *halves, out, tall = refs
    rows = out.shape[0] // HEADS
    me = lax.axis_index("sample")
    at = 0
    for near, far, bits in zip(halves[::2], halves[1::2], orders):
        half, cols, wide = near.shape
        places = places_of(bits)
        for j in range(2 * half):
            place = sum(jnp.where(me ^ j == p, i, 0) for i, p in enumerate(places))
            block = jnp.where(place < half, near[place % half], far[place % half])
            tall[j * cols : (j + 1) * cols, at : at + wide] = block.astype(F32)
        at += wide
    starts = [pl.multiple_of((lax.axis_index("row") ^ p) * rows, SUB) for p in places_of(row_bits)]
    for g in range(rows // SUB):
        lanes = slice(g * LANES, (g + 1) * LANES)
        turned = jnp.concatenate([tall[pl.ds(start, rows), lanes] for start in starts], axis=0).T
        for h in range(HEADS):
            out[h * rows + g * SUB : h * rows + (g + 1) * SUB] = turned[h * SUB : (h + 1) * SUB] * LOG2E


def turn_bias(orders, row_bits, halves):
    half, cols, _ = halves[0].shape
    keys = 2 * half * cols
    wide = sum(near.shape[2] for near in halves[::2])
    vmem = pl.BlockSpec(memory_space=pltpu.VMEM)
    return pl.pallas_call(
        functools.partial(turn_kernel, orders, row_bits),
        out_shape=jax.ShapeDtypeStruct((wide, keys), F32),
        in_specs=[vmem] * len(halves),
        out_specs=vmem,
        scratch_shapes=[pltpu.VMEM((keys, wide), F32)],
        compiler_params=pltpu.CompilerParams(vmem_limit_bytes=24 * MIB),
        cost_estimate=cost(1),
        name="turn_bias",
    )(*halves)


def attend_kernel(samples, bias, *refs):
    parts, refs = [refs[5 * s : 5 * s + 5] for s in range(samples)], refs[5 * samples :]
    far, wk, wv, wo, out, kt, v = refs
    _, k_near, v_near, _, _ = parts[-1]
    rows, width = parts[-1][4].shape
    x = stack(far)
    for c in range(0, width, 2 * LANES):
        lanes = slice(c, c + 2 * LANES)
        k = jnp.concatenate([k_near[:, lanes].astype(F32), dot(x, wk[:, lanes])], axis=0)
        kt[lanes] = k.T.astype(BF16)
    v[: v_near.shape[0]] = v_near[...]
    v[v_near.shape[0] :] = dot(x, wv[...]).astype(BF16)
    scale = LOG2E / HEAD_DIM**0.5
    lane = iota((rows, 2 * LANES), 1)
    work = [
        (s, base, heads[i : i + 2])
        for s in range(samples)
        for base, heads in head_groups(width)
        for i in range(0, len(heads), 2)
    ]

    def channels(base, h):
        low = h * HEAD_DIM - base
        return (lane >= low) & (lane < low + HEAD_DIM)

    def score(item):
        s, base, heads = item
        q, keys = parts[s][0], parts[s][1] if s < samples - 1 else kt
        mine = q[:, base : base + 2 * LANES].astype(F32)
        mine = jnp.concatenate([jnp.where(channels(base, h), mine, 0.0) for h in heads], axis=0).astype(BF16)
        some = bias[heads[0] * rows : (heads[-1] + 1) * rows]
        return item, dot(mine, keys[base : base + 2 * LANES]) * scale + some

    def soften(item):
        place, sc = item
        e = jnp.exp2(sc - jnp.max(sc, -1, keepdims=True))
        return place, e.astype(BF16), inverse(jnp.sum(e, -1, keepdims=True))

    mixes = {}

    def mix(item):
        (s, base, heads), e, share = item
        values = parts[s][2] if s < samples - 1 else v
        o = dot(e, values[:, base : base + 2 * LANES]) * share
        for i, h in enumerate(heads):
            mixes[s, base] = jnp.where(channels(base, h), o[i * rows : (i + 1) * rows], mixes.get((s, base), 0.0))
        if h == HEADS - 1:
            close(s)

    def close(s):
        tiles = {}
        for base, _ in head_groups(width):
            for t in range(2):
                at = base + t * LANES
                part = mixes[s, base][:, t * LANES : (t + 1) * LANES]
                tiles[at] = tiles[at] + part if at in tiles else part
        gate, token_in = parts[s][3:]
        gated = jnp.concatenate([tiles[at] for at in range(0, width, LANES)], axis=1) * gate[...]
        out[s] = (token_in[...] + dot(gated.astype(BF16), wo[...])).astype(BF16)

    skewed(work, [score, soften, mix])


def attend(bias, parts, far, wk, wv, wo):
    rows, width = parts[-1][4].shape
    keys = 2 * parts[-1][1].shape[0]
    vmem = pl.BlockSpec(memory_space=pltpu.VMEM)
    operands = [bias, *(ref for part in parts for ref in part), far, wk, wv, wo]
    return pl.pallas_call(
        functools.partial(attend_kernel, len(parts)),
        out_shape=jax.ShapeDtypeStruct((len(parts), rows, width), BF16),
        in_specs=[vmem] * len(operands),
        out_specs=vmem,
        scratch_shapes=[pltpu.VMEM((width, keys), BF16), pltpu.VMEM((keys, width), BF16)],
        compiler_params=pltpu.CompilerParams(vmem_limit_bytes=32 * MIB),
        cost_estimate=cost(3),
        name="attend",
    )(*operands)


def shards(
    atom_feat,
    atom_token,
    pair_cond,
    token_mask,
    atom_wq,
    atom_wk,
    atom_wv,
    atom_wo,
    agg_weight,
    pair_weight,
    token_gain,
    query_weight,
    key_weight,
    value_weight,
    gate_weight,
    out_weight,
):
    samples = atom_feat.shape[0]
    rows = pair_cond.shape[0]
    ranks = lax.axis_size("row")
    bias, inner, outer = pair_bias(atom_feat, pair_cond, token_mask, pair_weight)
    inner = swap(inner, "row", 1)
    odd_pairs = [(i, (i + 1) % ranks) for i in range(1, ranks, 2)]
    outer = lax.ppermute(outer, "row", odd_pairs + [(j, i) for i, j in odd_pairs])

    def widen(held, axis, bit, *others):
        return jnp.concatenate([held, after(swap(held, axis, bit), *others)], axis=0)

    bits, row_bits = bits_of(lax.axis_size("sample")), bits_of(ranks)
    orders = [bits, bits[:1] + bits[-1:] + bits[1:-1]]
    split = (bias.shape[1] // LANES + 1) // 2 * LANES
    got = swap(bias, "sample", bits[0])
    norms, inputs = [], []
    for s in range(samples):
        halo = (inner, outer)
        mixed = atom_attention(s, atom_feat, halo if s else (), atom_wq, atom_wk, atom_wv)
        outside = () if s else (*halo, atom_wq, atom_wk, atom_wv)
        token_in, token_norm = gather_tokens(
            s, mixed, atom_feat, atom_token, atom_wo, agg_weight, token_gain, outside, rows
        )
        inputs.append(token_in)
        norms.append(token_norm[None])
        if s == 0:
            bias, got, _ = lax.optimization_barrier((bias, got, token_norm))
            held = [jnp.stack([bias[:, lanes], got[:, lanes]]) for lanes in (slice(0, split), slice(split, None))]
            inner = after(inner, held, token_norm)
    for i in range(1, len(bits) - 1):
        held = [widen(h, "sample", order[i], token_norm) for h, order in zip(held, orders)]
    halves = []
    for h, order in zip(held, orders):
        halves += [h, swap(h, "sample", order[-1])]
    parts = []
    weights = (query_weight, key_weight, value_weight, gate_weight, out_weight)
    for s in range(samples):
        near = norms[s]
        for bit in row_bits[:-1]:
            near = widen(near, "row", bit, mixed, *((parts, halves) if s == samples - 1 else parts))
        far = swap(near, "row", row_bits[-1])
        near = after(near, held)
        blocks = (near, far) if s < samples - 1 else (near,)
        parts.append((*project(blocks, *weights), inputs[s]))
    bias = turn_bias(orders, row_bits, after(halves, near))
    return attend(bias, parts, far, key_weight, value_weight, out_weight)


def solution(mesh):
    placed = (
        P("sample", "row", None),
        P("row"),
        P("row", "sample", None),
        P("sample"),
    ) + (P(),) * 12
    return jax.shard_map(
        shards, mesh=mesh, in_specs=placed, out_specs=P("sample", "row", None), check_vma=False
    )
```

```python
import functools
import math

import jax
import jax.numpy as jnp
from jax import lax
from jax.experimental import pallas as pl
from jax.experimental.pallas import tpu as pltpu
from jax.sharding import PartitionSpec as P

HEADS = 16
HEAD_DIM = 48
AHEADS = 4
AHEAD_DIM = 32
QWIN = 32
KWIN = 128
RIM = (KWIN - QWIN) // 2
LANES = 128
SUB = 8
F32 = jnp.float32
BF16 = jnp.bfloat16
MIB = 1024 * 1024
LOG2E = math.log2(math.e)
NT = (((1,), (1,)), ((), ()))


def layer_norm(x):
    mean = jnp.mean(x, -1, keepdims=True)
    centre = x - mean
    var = jnp.mean(centre * centre, -1, keepdims=True)
    return centre * lax.rsqrt(var + 1e-05)


def dot(a, b):
    return jnp.dot(a, b, preferred_element_type=F32)


def dot_nt(a, b):
    return lax.dot_general(a, b, NT, preferred_element_type=F32)


def iota(shape, dim):
    return lax.broadcasted_iota(jnp.int32, shape, dim)


def cost(micros):
    return pl.CostEstimate(flops=micros * 20_000_000, bytes_accessed=1_000, transcendentals=0)


def inverse(total):
    guess = pl.reciprocal(total, approx=True)
    return guess * (2.0 - total * guess)


def skewed(items, stages):
    held = list(items)
    for t in range(len(held) + len(stages) - 1):
        for k in reversed(range(len(stages))):
            if 0 <= t - k < len(held):
                held[t - k] = stages[k](held[t - k])
    return held


def bias_kernel(head, tail, pair, mask, weight, out, inner, outer, normed):
    odd = lax.axis_index("row") % 2 == 1
    inner[...] = jnp.where(odd, head[...], tail[...])
    outer[...] = jnp.where(odd, tail[...], head[...])
    cols, rows, chans = pair.shape
    for k in range(0, cols, 6):
        normed[k : k + 6] = layer_norm(pair[k : k + 6].astype(F32))
    spread = (iota((HEADS, LANES), 1) // SUB == iota((HEADS, LANES), 0)).astype(BF16)
    wide = lax.dot_general(weight[...], spread, (((0,), (0,)), ((), ())), preferred_element_type=F32).astype(BF16)
    tall = cols * SUB
    key_of = iota((tall, cols), 0) // SUB == iota((tall, cols), 1)
    open_row = jnp.broadcast_to(mask[...].reshape(1, cols), (LANES, cols)).astype(BF16)
    open_key = dot_nt(key_of.astype(BF16), open_row) > 0.5
    picked = (iota((cols, tall), 1) // SUB == iota((cols, tall), 0)).astype(BF16)
    row = iota((tall, LANES), 0)
    mine = iota((tall, LANES), 1) % SUB == row % SUB
    apart = lax.axis_index("sample") * cols + row // SUB - lax.axis_index("row") * rows - row % SUB

    def weigh(g):
        x = normed[:, g * SUB : (g + 1) * SUB].reshape(tall, chans).astype(BF16)
        raw = jnp.where(open_key | (apart == g * SUB), dot(x, wide), -30000.0)
        return g, jnp.where(mine, raw, 0.0).astype(BF16)

    def pick(item):
        g, raw = item
        out[:, g * LANES : (g + 1) * LANES] = dot(picked, raw).astype(BF16)

    skewed(range(rows // SUB), [weigh, pick])


def pair_bias(feat, pair_cond, token_mask, pair_weight):
    rows, cols, chans = pair_cond.shape
    samples, atoms, width = feat.shape
    edge = (samples, RIM, width)

    def whole(*shape):
        return pl.BlockSpec(shape, lambda i: (0,) * len(shape))

    return pl.pallas_call(
        bias_kernel,
        grid=(1,),
        out_shape=[
            jax.ShapeDtypeStruct((cols, rows * HEADS), BF16),
            jax.ShapeDtypeStruct(edge, BF16),
            jax.ShapeDtypeStruct(edge, BF16),
        ],
        in_specs=[
            pl.BlockSpec(edge, lambda i: (0, 0, 0)),
            pl.BlockSpec(edge, lambda i: (0, atoms // RIM - 1, 0)),
            whole(cols, rows, chans),
            whole(cols),
            whole(HEADS, chans),
        ],
        out_specs=[whole(cols, rows * HEADS), whole(*edge), whole(*edge)],
        scratch_shapes=[pltpu.VMEM((cols, rows, chans), F32)],
        compiler_params=pltpu.CompilerParams(vmem_limit_bytes=60 * MIB),
        cost_estimate=cost(3),
        name="pair_bias",
    )(feat, feat, jnp.transpose(pair_cond, (1, 0, 2)), token_mask, pair_weight.T)


def after(value, *others):
    return lax.optimization_barrier((value, *others))[0]


def swap(held, axis, far):
    return lax.ppermute(held, axis, [(i, i ^ far) for i in range(lax.axis_size(axis))])


def bits_of(devices):
    return [devices >> i for i in range(1, devices.bit_length())]


def places_of(bits):
    places = [0]
    for bit in bits:
        places += [p ^ bit for p in places]
    return places


def windows_attend(starts, qs, ks, vs, mixed, shift, hide):
    rate = LOG2E / AHEAD_DIM**0.5
    tall = AHEADS * QWIN
    head_of = iota((QWIN, qs.shape[1]), 1) // AHEAD_DIM

    def score(batch):
        out = []
        for at in batch:
            q = qs[at - shift : at - shift + QWIN]
            q = jnp.concatenate([jnp.where(head_of == h, q, jnp.zeros_like(q)) for h in range(AHEADS)], axis=0)
            out.append(hide(at, dot_nt(q, ks[at : at + KWIN])))
        return batch, jnp.concatenate(out, axis=0)

    def soften(item):
        batch, s = item
        e = jnp.exp2((s - jnp.max(s, -1, keepdims=True)) * rate)
        return batch, e.astype(BF16), jnp.sum(e, -1, keepdims=True)

    def own_head(parts):
        acc = parts[:QWIN]
        for h in range(1, AHEADS):
            acc = jnp.where(head_of == h, parts[h * QWIN : (h + 1) * QWIN], acc)
        return acc

    def mix(item):
        batch, e, total = item
        for i, at in enumerate(batch):
            part = slice(i * tall, (i + 1) * tall)
            o = own_head(dot(e[part], vs[at : at + KWIN])) * inverse(own_head(total[part]))
            mixed[at - shift : at - shift + QWIN] = o.astype(BF16)

    skewed(starts, [score, soften, mix])


def halo_of(sample, inner, outer):
    odd = lax.axis_index("row") % 2 == 1
    return jnp.where(odd, inner[sample], outer[sample]), jnp.where(odd, outer[sample], inner[sample])


def hide_outside(atoms):
    rank = lax.axis_index("row")
    at_start = rank == 0
    at_end = rank == lax.axis_size("row") - 1
    keyat = iota((AHEADS * QWIN, KWIN), 1)

    def hide(at, s):
        if at < RIM:
            s = jnp.where(at_start & (keyat < RIM - at), -jnp.inf, s)
        if at + KWIN > RIM + atoms:
            s = jnp.where(at_end & (keyat >= RIM + atoms - at), -jnp.inf, s)
        return s

    return hide


def atom_kernel(sample, feat, *refs):
    *halo, wq, wk, wv, mixed, qs, ks, vs = refs
    atoms, chans = feat.shape[1:]
    wqkv = jnp.concatenate([wq[...], wk[...], wv[...]], axis=1)

    def normalise(at):
        if isinstance(at, int):
            part = feat[sample, at : at + LANES]
        else:
            at, part = at
        return at, layer_norm(part.astype(F32)).astype(BF16)

    def project_atoms(item):
        at, normed = item
        count = normed.shape[0]
        if count == RIM:
            kv = dot(normed, wqkv[:, chans:]).astype(BF16)
        else:
            qkv = dot(normed, wqkv).astype(BF16)
            qs[at : at + count] = qkv[:, :chans]
            kv = qkv[:, chans:]
        ks[RIM + at : RIM + at + count] = kv[:, :chans]
        vs[RIM + at : RIM + at + count] = kv[:, chans:]

    parts = list(range(0, atoms, LANES))
    if halo:
        before, behind = halo_of(sample, *halo)
        parts += [(-RIM, before), (atoms, behind)]
    skewed(parts, [normalise, project_atoms])
    starts = list(range(0, atoms, QWIN))
    if not halo:
        starts = [at for at in starts if RIM <= at <= atoms + RIM - KWIN]
    batch = 6
    batches = [starts[i : i + batch] for i in range(0, len(starts), batch)]
    windows_attend(batches, qs, ks, vs, mixed, 0, hide_outside(atoms))


def atom_attention(sample, feat, halo, wq, wk, wv):
    atoms, chans = feat.shape[1:]
    vmem = pl.BlockSpec(memory_space=pltpu.VMEM)
    return pl.pallas_call(
        functools.partial(atom_kernel, sample),
        out_shape=jax.ShapeDtypeStruct((atoms, chans), BF16),
        in_specs=[vmem] * (4 + len(halo)),
        out_specs=vmem,
        scratch_shapes=[
            pltpu.VMEM((atoms, chans), BF16),
            pltpu.VMEM((atoms + 2 * RIM, chans), BF16),
            pltpu.VMEM((atoms + 2 * RIM, chans), BF16),
        ],
        compiler_params=pltpu.CompilerParams(vmem_limit_bytes=16 * MIB),
        cost_estimate=cost(4),
        name="atom_attention",
    )(feat, *halo, wq, wk, wv)


def gather_kernel(sample, mixed, feat, token, wo, agg, gain, *refs):
    *outside, token_in, token_norm, qs, ks, vs, ends = refs
    atoms, chans = feat.shape[1:]
    rows = token_in.shape[0]
    local = token[...].reshape(1, atoms) - lax.axis_index("row") * rows
    step = 384
    sums = []
    edge = 2 * QWIN
    if outside:
        inner, outer, wq, wk, wv = outside
        before, behind = halo_of(sample, inner, outer)
        wqkv = jnp.concatenate([wq[...], wk[...], wv[...]], axis=1)
        near = edge + KWIN - QWIN - RIM
        both = [before, feat[sample, :near], feat[sample, atoms - near :], behind]
        qkv = dot(layer_norm(jnp.concatenate([p.astype(F32) for p in both], axis=0)).astype(BF16), wqkv).astype(BF16)
        qs[...] = qkv[:, :chans]
        ks[...] = qkv[:, chans : 2 * chans]
        vs[...] = qkv[:, 2 * chans :]
        apart = atoms - 2 * near
        starts = [0, QWIN, RIM + near, RIM + near + QWIN]
        hide = hide_outside(atoms)
        windows_attend([starts], qs, ks, vs, ends, -RIM, lambda at, s: hide(at if at < RIM else at + apart, s))

    def finish(c):
        part = mixed[c : c + step]
        if outside and c == 0:
            part = jnp.concatenate([ends[RIM : RIM + edge], part[edge:]], axis=0)
        if outside and c + step == atoms:
            at = ends.shape[0] - RIM - edge
            part = jnp.concatenate([part[: step - edge], ends[at : at + edge]], axis=0)
        return c, (feat[sample, c : c + step].astype(F32) + dot(part, wo[...])).astype(BF16)

    def hide_below(item):
        c, out = item
        return c, jnp.maximum(dot(out, agg[...]), 0.0).astype(BF16)

    def add(item):
        c, hidden = item
        onehot = (iota((rows, step), 0) == local[:, c : c + step]).astype(F32)
        part = dot(onehot.astype(BF16), hidden), jnp.sum(onehot, -1, keepdims=True)
        sums[:] = [a + b for a, b in zip(sums, part)] if sums else part

    chunks = list(range(0, atoms, step))
    skewed(chunks[1:-1] + [chunks[0], chunks[-1]], [finish, hide_below, add])
    tin = sums[0] / sums[1]
    token_in[...] = tin
    token_norm[...] = (layer_norm(tin) * gain[...].reshape(1, -1)).astype(BF16)


def gather_tokens(sample, mixed, feat, token, wo, agg, gain, outside, rows):
    width = agg.shape[1]
    chans = feat.shape[2]
    reach = 2 * (KWIN + QWIN)
    vmem = pl.BlockSpec(memory_space=pltpu.VMEM)
    return pl.pallas_call(
        functools.partial(gather_kernel, sample),
        out_shape=[jax.ShapeDtypeStruct((rows, width), F32), jax.ShapeDtypeStruct((rows, width), BF16)],
        in_specs=[vmem] * (6 + len(outside)),
        out_specs=[vmem, vmem],
        scratch_shapes=[pltpu.VMEM((reach, chans), BF16)] * 4,
        compiler_params=pltpu.CompilerParams(vmem_limit_bytes=16 * MIB),
        cost_estimate=cost(1),
        name="gather_tokens",
    )(mixed, feat, token, wo, agg, gain, *outside)


def head_groups(width):
    groups = []
    for base in range(0, width, 8 * HEAD_DIM):
        first = base // HEAD_DIM
        groups.append((base, range(first, first + 5)))
        groups.append((base + LANES, range(first + 5, first + 8)))
    return groups


def stack(blocks):
    return jnp.concatenate([blocks[j].astype(F32) for j in range(blocks.shape[0])], axis=0).astype(BF16)


def project_kernel(near, *refs):
    *far, wq, wk, wv, wg, wo, q, k, v, gate = refs
    x = jnp.concatenate([stack(blocks) for blocks in (near, *far)], axis=0)
    q[...] = dot(near[0], wq[...]).astype(BF16)
    gate[...] = jax.nn.sigmoid(dot(near[0], wg[...]))
    if far:
        for c in range(0, x.shape[1], 2 * LANES):
            k[c : c + 2 * LANES] = dot(x, wk[:, c : c + 2 * LANES]).T.astype(BF16)
    else:
        k[...] = dot(x, wk[...]).astype(BF16)
    v[...] = dot(x, wv[...]).astype(BF16)


def project(blocks, wq, wk, wv, wg, wo):
    half, rows, width = blocks[0].shape
    keys = len(blocks) * half * rows
    vmem = pl.BlockSpec(memory_space=pltpu.VMEM)
    return pl.pallas_call(
        project_kernel,
        out_shape=[
            jax.ShapeDtypeStruct((rows, width), BF16),
            jax.ShapeDtypeStruct((width, keys) if len(blocks) > 1 else (keys, width), BF16),
            jax.ShapeDtypeStruct((keys, width), BF16),
            jax.ShapeDtypeStruct((rows, width), F32),
        ],
        in_specs=[vmem] * (5 + len(blocks)),
        out_specs=[vmem] * 4,
        compiler_params=pltpu.CompilerParams(vmem_limit_bytes=24 * MIB),
        cost_estimate=cost(2),
        name="project",
    )(*blocks, wq, wk, wv, wg, wo)


def turn_kernel(orders, row_bits, *refs):
    *halves, out, tall = refs
    rows = out.shape[0] // HEADS
    me = lax.axis_index("sample")
    at = 0
    for near, far, bits in zip(halves[::2], halves[1::2], orders):
        half, cols, wide = near.shape
        places = places_of(bits)
        for j in range(2 * half):
            place = sum(jnp.where(me ^ j == p, i, 0) for i, p in enumerate(places))
            block = jnp.where(place < half, near[place % half], far[place % half])
            tall[j * cols : (j + 1) * cols, at : at + wide] = block.astype(F32)
        at += wide
    starts = [pl.multiple_of((lax.axis_index("row") ^ p) * rows, SUB) for p in places_of(row_bits)]
    for g in range(rows // SUB):
        lanes = slice(g * LANES, (g + 1) * LANES)
        turned = jnp.concatenate([tall[pl.ds(start, rows), lanes] for start in starts], axis=0).T
        for h in range(HEADS):
            out[h * rows + g * SUB : h * rows + (g + 1) * SUB] = turned[h * SUB : (h + 1) * SUB] * LOG2E


def turn_bias(orders, row_bits, halves):
    half, cols, _ = halves[0].shape
    keys = 2 * half * cols
    wide = sum(near.shape[2] for near in halves[::2])
    vmem = pl.BlockSpec(memory_space=pltpu.VMEM)
    return pl.pallas_call(
        functools.partial(turn_kernel, orders, row_bits),
        out_shape=jax.ShapeDtypeStruct((wide, keys), F32),
        in_specs=[vmem] * len(halves),
        out_specs=vmem,
        scratch_shapes=[pltpu.VMEM((keys, wide), F32)],
        compiler_params=pltpu.CompilerParams(vmem_limit_bytes=24 * MIB),
        cost_estimate=cost(1),
        name="turn_bias",
    )(*halves)


def attend_kernel(samples, bias, *refs):
    parts, refs = [refs[5 * s : 5 * s + 5] for s in range(samples)], refs[5 * samples :]
    far, wk, wv, wo, out, kt, v = refs
    _, k_near, v_near, _, _ = parts[-1]
    rows, width = parts[-1][4].shape
    x = stack(far)
    scale = LOG2E / HEAD_DIM**0.5
    lane = iota((rows, 2 * LANES), 1)
    groups = head_groups(width)
    work = [(s, base, heads) for s in range(samples) for base, heads in groups]
    chunks = list(range(0, width, 2 * LANES))
    for i, c in enumerate(chunks):
        work.insert(min(2 * i + 1, (samples - 1) * len(groups) + i), c)

    def fill(c):
        lanes = slice(c, c + 2 * LANES)
        k = jnp.concatenate([k_near[:, lanes].astype(F32), dot(x, wk[:, lanes])], axis=0)
        kt[lanes] = k.T.astype(BF16)
        v[: v_near.shape[0], lanes] = v_near[:, lanes]
        v[v_near.shape[0] :, lanes] = dot(x, wv[:, lanes]).astype(BF16)

    def channels(base, h):
        low = h * HEAD_DIM - base
        return (lane >= low) & (lane < low + HEAD_DIM)

    def score(item):
        if isinstance(item, int):
            return fill(item)
        s, base, heads = item
        q, keys = parts[s][0], parts[s][1] if s < samples - 1 else kt
        mine = q[:, base : base + 2 * LANES].astype(F32)
        mine = jnp.concatenate([jnp.where(channels(base, h), mine, 0.0) for h in heads], axis=0).astype(BF16)
        some = bias[heads[0] * rows : (heads[-1] + 1) * rows]
        return item, dot(mine, keys[base : base + 2 * LANES]) * scale + some

    def soften(item):
        if item is None:
            return None
        place, sc = item
        e = jnp.exp2(sc - jnp.max(sc, -1, keepdims=True))
        return place, e.astype(BF16), inverse(jnp.sum(e, -1, keepdims=True))

    mixes = {}

    def mix(item):
        if item is None:
            return
        (s, base, heads), e, share = item
        values = parts[s][2] if s < samples - 1 else v
        o = dot(e, values[:, base : base + 2 * LANES]) * share
        for i, h in enumerate(heads):
            mixes[s, base] = jnp.where(channels(base, h), o[i * rows : (i + 1) * rows], mixes.get((s, base), 0.0))
        if h == HEADS - 1:
            close(s)

    def close(s):
        tiles = {}
        for base, _ in groups:
            for t in range(2):
                at = base + t * LANES
                part = mixes[s, base][:, t * LANES : (t + 1) * LANES]
                tiles[at] = tiles[at] + part if at in tiles else part
        gate, token_in = parts[s][3:]
        gated = jnp.concatenate([tiles[at] for at in range(0, width, LANES)], axis=1) * gate[...]
        out[s] = (token_in[...] + dot(gated.astype(BF16), wo[...])).astype(BF16)

    skewed(work, [score, soften, mix])


def attend(bias, parts, far, wk, wv, wo):
    rows, width = parts[-1][4].shape
    keys = 2 * parts[-1][1].shape[0]
    vmem = pl.BlockSpec(memory_space=pltpu.VMEM)
    operands = [bias, *(ref for part in parts for ref in part), far, wk, wv, wo]
    return pl.pallas_call(
        functools.partial(attend_kernel, len(parts)),
        out_shape=jax.ShapeDtypeStruct((len(parts), rows, width), BF16),
        in_specs=[vmem] * len(operands),
        out_specs=vmem,
        scratch_shapes=[pltpu.VMEM((width, keys), BF16), pltpu.VMEM((keys, width), BF16)],
        compiler_params=pltpu.CompilerParams(vmem_limit_bytes=32 * MIB),
        cost_estimate=cost(3),
        name="attend",
    )(*operands)


def shards(
    atom_feat,
    atom_token,
    pair_cond,
    token_mask,
    atom_wq,
    atom_wk,
    atom_wv,
    atom_wo,
    agg_weight,
    pair_weight,
    token_gain,
    query_weight,
    key_weight,
    value_weight,
    gate_weight,
    out_weight,
):
    samples = atom_feat.shape[0]
    rows = pair_cond.shape[0]
    ranks = lax.axis_size("row")
    bias, inner, outer = pair_bias(atom_feat, pair_cond, token_mask, pair_weight)
    inner = swap(inner, "row", 1)
    odd_pairs = [(i, (i + 1) % ranks) for i in range(1, ranks, 2)]
    outer = lax.ppermute(outer, "row", odd_pairs + [(j, i) for i, j in odd_pairs])

    def widen(held, axis, bit, *others):
        return jnp.concatenate([held, after(swap(held, axis, bit), *others)], axis=0)

    bits, row_bits = bits_of(lax.axis_size("sample")), bits_of(ranks)
    orders = [bits, bits[:1] + bits[-1:] + bits[1:-1]]
    split = (bias.shape[1] // LANES + 1) // 2 * LANES
    got = swap(bias, "sample", bits[0])
    norms, inputs = [], []
    for s in range(samples):
        halo = (inner, outer)
        mixed = atom_attention(s, atom_feat, halo if s else (), atom_wq, atom_wk, atom_wv)
        outside = () if s else (*halo, atom_wq, atom_wk, atom_wv)
        token_in, token_norm = gather_tokens(
            s, mixed, atom_feat, atom_token, atom_wo, agg_weight, token_gain, outside, rows
        )
        inputs.append(token_in)
        norms.append(token_norm[None])
        if s == 0:
            bias, got, _ = lax.optimization_barrier((bias, got, token_norm))
            held = [jnp.stack([bias[:, lanes], got[:, lanes]]) for lanes in (slice(0, split), slice(split, None))]
            inner = after(inner, held, token_norm)
    last = swap(norms[-1], "row", row_bits[0])
    for i in range(1, len(bits) - 1):
        held = [widen(h, "sample", order[i], token_norm) for h, order in zip(held, orders)]
    halves = []
    for h, order in zip(held, orders):
        halves += [h, swap(h, "sample", order[-1])]
    parts = []
    weights = (query_weight, key_weight, value_weight, gate_weight, out_weight)
    for s in range(samples):
        near = norms[s]
        others = (mixed, parts, halves) if s == samples - 1 else (mixed, parts)
        for bit in row_bits[:-1]:
            if s == samples - 1 and bit == row_bits[0]:
                near = jnp.concatenate([near, after(last, *others)], axis=0)
            else:
                near = widen(near, "row", bit, *others)
        far = swap(near, "row", row_bits[-1])
        near = after(near, held)
        blocks = (near, far) if s < samples - 1 else (near,)
        parts.append((*project(blocks, *weights), inputs[s]))
    bias = turn_bias(orders, row_bits, after(halves, near))
    return attend(bias, parts, far, key_weight, value_weight, out_weight)


def solution(mesh):
    placed = (
        P("sample", "row", None),
        P("row"),
        P("row", "sample", None),
        P("sample"),
    ) + (P(),) * 12
    return jax.shard_map(
        shards, mesh=mesh, in_specs=placed, out_specs=P("sample", "row", None), check_vma=False
    )
```

```python
import functools
import math

import jax
import jax.numpy as jnp
from jax import lax
from jax.experimental import pallas as pl
from jax.experimental.pallas import tpu as pltpu
from jax.sharding import PartitionSpec as P

HEADS = 16
HEAD_DIM = 48
AHEADS = 4
AHEAD_DIM = 32
QWIN = 32
KWIN = 128
RIM = (KWIN - QWIN) // 2
LANES = 128
SUB = 8
F32 = jnp.float32
BF16 = jnp.bfloat16
MIB = 1024 * 1024
LOG2E = math.log2(math.e)
NT = (((1,), (1,)), ((), ()))


def layer_norm(x):
    mean = jnp.mean(x, -1, keepdims=True)
    centre = x - mean
    var = jnp.mean(centre * centre, -1, keepdims=True)
    return centre * lax.rsqrt(var + 1e-05)


def dot(a, b):
    return jnp.dot(a, b, preferred_element_type=F32)


def dot_nt(a, b):
    return lax.dot_general(a, b, NT, preferred_element_type=F32)


def iota(shape, dim):
    return lax.broadcasted_iota(jnp.int32, shape, dim)


def cost(micros):
    return pl.CostEstimate(flops=micros * 20_000_000, bytes_accessed=1_000, transcendentals=0)


def inverse(total):
    guess = pl.reciprocal(total, approx=True)
    return guess * (2.0 - total * guess)


def skewed(items, stages):
    held = list(items)
    for t in range(len(held) + len(stages) - 1):
        for k in reversed(range(len(stages))):
            if 0 <= t - k < len(held):
                held[t - k] = stages[k](held[t - k])
    return held


def normalise_kernel(pair, normed):
    for k in range(0, pair.shape[0], 6):
        normed[k : k + 6] = layer_norm(pair[k : k + 6].astype(F32))


def normalise_pairs(pair_cond):
    rows, cols, chans = pair_cond.shape
    vmem = pl.BlockSpec(memory_space=pltpu.VMEM)
    return pl.pallas_call(
        normalise_kernel,
        out_shape=jax.ShapeDtypeStruct((cols, rows, chans), F32),
        in_specs=[vmem],
        out_specs=vmem,
        compiler_params=pltpu.CompilerParams(vmem_limit_bytes=8 * MIB),
        cost_estimate=cost(1),
        name="normalise_pairs",
    )(jnp.transpose(pair_cond, (1, 0, 2)))


def bias_kernel(feat, normed, mask, weight, out, inner, outer):
    odd = lax.axis_index("row") % 2 == 1
    head, tail = feat[:, :RIM], feat[:, feat.shape[1] - RIM :]
    inner[...] = jnp.where(odd, head, tail)
    outer[...] = jnp.where(odd, tail, head)
    cols, rows, chans = normed.shape
    spread = (iota((HEADS, LANES), 1) // SUB == iota((HEADS, LANES), 0)).astype(BF16)
    wide = lax.dot_general(weight[...], spread, (((0,), (0,)), ((), ())), preferred_element_type=F32).astype(BF16)
    tall = cols * SUB
    key_of = iota((tall, cols), 0) // SUB == iota((tall, cols), 1)
    open_row = jnp.broadcast_to(mask[...].reshape(1, cols), (LANES, cols)).astype(BF16)
    open_key = dot_nt(key_of.astype(BF16), open_row) > 0.5
    picked = (iota((cols, tall), 1) // SUB == iota((cols, tall), 0)).astype(BF16)
    row = iota((tall, LANES), 0)
    mine = iota((tall, LANES), 1) % SUB == row % SUB
    apart = lax.axis_index("sample") * cols + row // SUB - lax.axis_index("row") * rows - row % SUB

    def weigh(g):
        x = normed[:, g * SUB : (g + 1) * SUB].reshape(tall, chans).astype(BF16)
        raw = jnp.where(open_key | (apart == g * SUB), dot(x, wide), -30000.0)
        return g, jnp.where(mine, raw, 0.0).astype(BF16)

    def pick(item):
        g, raw = item
        out[:, g * LANES : (g + 1) * LANES] = dot(picked, raw).astype(BF16)

    skewed(range(rows // SUB), [weigh, pick])


def pair_bias(feat, pair_cond, token_mask, pair_weight):
    rows, cols, _ = pair_cond.shape
    edge = (feat.shape[0], RIM, feat.shape[2])
    vmem = pl.BlockSpec(memory_space=pltpu.VMEM)
    return pl.pallas_call(
        bias_kernel,
        out_shape=[
            jax.ShapeDtypeStruct((cols, rows * HEADS), BF16),
            jax.ShapeDtypeStruct(edge, BF16),
            jax.ShapeDtypeStruct(edge, BF16),
        ],
        in_specs=[vmem] * 4,
        out_specs=[vmem] * 3,
        compiler_params=pltpu.CompilerParams(vmem_limit_bytes=8 * MIB),
        cost_estimate=cost(3),
        name="pair_bias",
    )(feat, normalise_pairs(pair_cond), token_mask, pair_weight.T)


def after(value, *others):
    return lax.optimization_barrier((value, *others))[0]


def swap(held, axis, far):
    return lax.ppermute(held, axis, [(i, i ^ far) for i in range(lax.axis_size(axis))])


def bits_of(devices):
    return [devices >> i for i in range(1, devices.bit_length())]


def places_of(bits):
    places = [0]
    for bit in bits:
        places += [p ^ bit for p in places]
    return places


def windows_attend(starts, qs, ks, vs, mixed, shift, hide):
    rate = LOG2E / AHEAD_DIM**0.5
    tall = AHEADS * QWIN
    head_of = iota((QWIN, qs.shape[1]), 1) // AHEAD_DIM

    def score(batch):
        out = []
        for at in batch:
            q = qs[at - shift : at - shift + QWIN]
            q = jnp.concatenate([jnp.where(head_of == h, q, jnp.zeros_like(q)) for h in range(AHEADS)], axis=0)
            out.append(hide(at, dot_nt(q, ks[at : at + KWIN])))
        return batch, jnp.concatenate(out, axis=0)

    def soften(item):
        batch, s = item
        e = jnp.exp2((s - jnp.max(s, -1, keepdims=True)) * rate)
        return batch, e.astype(BF16), jnp.sum(e, -1, keepdims=True)

    def own_head(parts):
        acc = parts[:QWIN]
        for h in range(1, AHEADS):
            acc = jnp.where(head_of == h, parts[h * QWIN : (h + 1) * QWIN], acc)
        return acc

    def mix(item):
        batch, e, total = item
        for i, at in enumerate(batch):
            part = slice(i * tall, (i + 1) * tall)
            o = own_head(dot(e[part], vs[at : at + KWIN])) * inverse(own_head(total[part]))
            mixed[at - shift : at - shift + QWIN] = o.astype(BF16)

    skewed(starts, [score, soften, mix])


def halo_of(sample, inner, outer):
    odd = lax.axis_index("row") % 2 == 1
    return jnp.where(odd, inner[sample], outer[sample]), jnp.where(odd, outer[sample], inner[sample])


def hide_outside(atoms):
    rank = lax.axis_index("row")
    at_start = rank == 0
    at_end = rank == lax.axis_size("row") - 1
    keyat = iota((AHEADS * QWIN, KWIN), 1)

    def hide(at, s):
        if at < RIM:
            s = jnp.where(at_start & (keyat < RIM - at), -jnp.inf, s)
        if at + KWIN > RIM + atoms:
            s = jnp.where(at_end & (keyat >= RIM + atoms - at), -jnp.inf, s)
        return s

    return hide


def atom_kernel(sample, feat, *refs):
    *halo, wq, wk, wv, mixed, qs, ks, vs = refs
    atoms, chans = feat.shape[1:]
    wqkv = jnp.concatenate([wq[...], wk[...], wv[...]], axis=1)

    def normalise(at):
        if isinstance(at, int):
            part = feat[sample, at : at + LANES]
        else:
            at, part = at
        return at, layer_norm(part.astype(F32)).astype(BF16)

    def project_atoms(item):
        at, normed = item
        count = normed.shape[0]
        if count == RIM:
            kv = dot(normed, wqkv[:, chans:]).astype(BF16)
        else:
            qkv = dot(normed, wqkv).astype(BF16)
            qs[at : at + count] = qkv[:, :chans]
            kv = qkv[:, chans:]
        ks[RIM + at : RIM + at + count] = kv[:, :chans]
        vs[RIM + at : RIM + at + count] = kv[:, chans:]

    parts = list(range(0, atoms, LANES))
    if halo:
        before, behind = halo_of(sample, *halo)
        parts += [(-RIM, before), (atoms, behind)]
    skewed(parts, [normalise, project_atoms])
    starts = list(range(0, atoms, QWIN))
    if not halo:
        starts = [at for at in starts if RIM <= at <= atoms + RIM - KWIN]
    batch = 6
    batches = [starts[i : i + batch] for i in range(0, len(starts), batch)]
    windows_attend(batches, qs, ks, vs, mixed, 0, hide_outside(atoms))


def atom_attention(sample, feat, halo, wq, wk, wv):
    atoms, chans = feat.shape[1:]
    vmem = pl.BlockSpec(memory_space=pltpu.VMEM)
    return pl.pallas_call(
        functools.partial(atom_kernel, sample),
        out_shape=jax.ShapeDtypeStruct((atoms, chans), BF16),
        in_specs=[vmem] * (4 + len(halo)),
        out_specs=vmem,
        scratch_shapes=[
            pltpu.VMEM((atoms, chans), BF16),
            pltpu.VMEM((atoms + 2 * RIM, chans), BF16),
            pltpu.VMEM((atoms + 2 * RIM, chans), BF16),
        ],
        compiler_params=pltpu.CompilerParams(vmem_limit_bytes=16 * MIB),
        cost_estimate=cost(4),
        name="atom_attention",
    )(feat, *halo, wq, wk, wv)


def gather_kernel(sample, mixed, feat, token, wo, agg, gain, *refs):
    *outside, token_in, token_norm, qs, ks, vs, ends = refs
    atoms, chans = feat.shape[1:]
    rows = token_in.shape[0]
    local = token[...].reshape(1, atoms) - lax.axis_index("row") * rows
    step = 384
    sums = []
    edge = 2 * QWIN
    if outside:
        inner, outer, wq, wk, wv = outside
        before, behind = halo_of(sample, inner, outer)
        wqkv = jnp.concatenate([wq[...], wk[...], wv[...]], axis=1)
        near = edge + KWIN - QWIN - RIM
        both = [before, feat[sample, :near], feat[sample, atoms - near :], behind]
        qkv = dot(layer_norm(jnp.concatenate([p.astype(F32) for p in both], axis=0)).astype(BF16), wqkv).astype(BF16)
        qs[...] = qkv[:, :chans]
        ks[...] = qkv[:, chans : 2 * chans]
        vs[...] = qkv[:, 2 * chans :]
        apart = atoms - 2 * near
        starts = [0, QWIN, RIM + near, RIM + near + QWIN]
        hide = hide_outside(atoms)
        windows_attend([starts], qs, ks, vs, ends, -RIM, lambda at, s: hide(at if at < RIM else at + apart, s))

    def finish(c):
        part = mixed[c : c + step]
        if outside and c == 0:
            part = jnp.concatenate([ends[RIM : RIM + edge], part[edge:]], axis=0)
        if outside and c + step == atoms:
            at = ends.shape[0] - RIM - edge
            part = jnp.concatenate([part[: step - edge], ends[at : at + edge]], axis=0)
        return c, (feat[sample, c : c + step].astype(F32) + dot(part, wo[...])).astype(BF16)

    def hide_below(item):
        c, out = item
        return c, jnp.maximum(dot(out, agg[...]), 0.0).astype(BF16)

    def add(item):
        c, hidden = item
        onehot = (iota((rows, step), 0) == local[:, c : c + step]).astype(F32)
        part = dot(onehot.astype(BF16), hidden), jnp.sum(onehot, -1, keepdims=True)
        sums[:] = [a + b for a, b in zip(sums, part)] if sums else part

    chunks = list(range(0, atoms, step))
    skewed(chunks[1:-1] + [chunks[0], chunks[-1]], [finish, hide_below, add])
    tin = sums[0] / sums[1]
    token_in[...] = tin
    token_norm[...] = (layer_norm(tin) * gain[...].reshape(1, -1)).astype(BF16)


def gather_tokens(sample, mixed, feat, token, wo, agg, gain, outside, rows):
    width = agg.shape[1]
    chans = feat.shape[2]
    reach = 2 * (KWIN + QWIN)
    vmem = pl.BlockSpec(memory_space=pltpu.VMEM)
    return pl.pallas_call(
        functools.partial(gather_kernel, sample),
        out_shape=[jax.ShapeDtypeStruct((rows, width), F32), jax.ShapeDtypeStruct((rows, width), BF16)],
        in_specs=[vmem] * (6 + len(outside)),
        out_specs=[vmem, vmem],
        scratch_shapes=[pltpu.VMEM((reach, chans), BF16)] * 4,
        compiler_params=pltpu.CompilerParams(vmem_limit_bytes=16 * MIB),
        cost_estimate=cost(1),
        name="gather_tokens",
    )(mixed, feat, token, wo, agg, gain, *outside)


def head_groups(width):
    groups = []
    for base in range(0, width, 8 * HEAD_DIM):
        first = base // HEAD_DIM
        groups.append((base, range(first, first + 5)))
        groups.append((base + LANES, range(first + 5, first + 8)))
    return groups


def stack(blocks):
    return jnp.concatenate([blocks[j].astype(F32) for j in range(blocks.shape[0])], axis=0).astype(BF16)


def project_kernel(near, far, wq, wk, wv, wg, wo, q, kt, v, gate):
    x = jnp.concatenate([stack(near), stack(far)], axis=0)
    q[...] = dot(near[0], wq[...]).astype(BF16)
    gate[...] = jax.nn.sigmoid(dot(near[0], wg[...]))
    for c in range(0, x.shape[1], 2 * LANES):
        kt[c : c + 2 * LANES] = dot(x, wk[:, c : c + 2 * LANES]).T.astype(BF16)
    v[...] = dot(x, wv[...]).astype(BF16)


def project(near, far, wq, wk, wv, wg, wo):
    half, rows, width = near.shape
    keys = 2 * half * rows
    vmem = pl.BlockSpec(memory_space=pltpu.VMEM)
    return pl.pallas_call(
        project_kernel,
        out_shape=[
            jax.ShapeDtypeStruct((rows, width), BF16),
            jax.ShapeDtypeStruct((width, keys), BF16),
            jax.ShapeDtypeStruct((keys, width), BF16),
            jax.ShapeDtypeStruct((rows, width), F32),
        ],
        in_specs=[vmem] * 7,
        out_specs=[vmem] * 4,
        compiler_params=pltpu.CompilerParams(vmem_limit_bytes=24 * MIB),
        cost_estimate=cost(2),
        name="project",
    )(near, far, wq, wk, wv, wg, wo)


def turn_kernel(orders, row_bits, near, wq, wk, wv, wg, *refs):
    *halves, q, k, v, gate, out, tall = refs
    x = stack(near)
    width = x.shape[1]

    def project_columns(c):
        lanes = slice(c, c + 2 * LANES)
        q[:, lanes] = dot(near[0], wq[:, lanes]).astype(BF16)
        k[:, lanes] = dot(x, wk[:, lanes]).astype(BF16)
        v[:, lanes] = dot(x, wv[:, lanes]).astype(BF16)
        gate[:, lanes] = jax.nn.sigmoid(dot(near[0], wg[:, lanes]))

    rows = out.shape[0] // HEADS
    me = lax.axis_index("sample")
    at = 0
    for i, (mine, other, bits) in enumerate(zip(halves[::2], halves[1::2], orders)):
        half, cols, wide = mine.shape
        places = places_of(bits)
        for j in range(2 * half):
            place = sum(jnp.where(me ^ j == p, i, 0) for i, p in enumerate(places))
            block = jnp.where(place < half, mine[place % half], other[place % half])
            tall[j * cols : (j + 1) * cols, at : at + wide] = block.astype(F32)
        at += wide
    starts = [pl.multiple_of((lax.axis_index("row") ^ p) * rows, SUB) for p in places_of(row_bits)]
    for g in range(rows // SUB):
        if g * 2 * LANES < width:
            project_columns(g * 2 * LANES)
        lanes = slice(g * LANES, (g + 1) * LANES)
        turned = jnp.concatenate([tall[pl.ds(start, rows), lanes] for start in starts], axis=0).T
        for h in range(HEADS):
            out[h * rows + g * SUB : h * rows + (g + 1) * SUB] = turned[h * SUB : (h + 1) * SUB] * LOG2E


def turn_bias(orders, row_bits, halves, near, wq, wk, wv, wg):
    half, cols, _ = halves[0].shape
    keys = 2 * half * cols
    wide = sum(part.shape[2] for part in halves[::2])
    blocks, rows, width = near.shape
    vmem = pl.BlockSpec(memory_space=pltpu.VMEM)
    return pl.pallas_call(
        functools.partial(turn_kernel, orders, row_bits),
        out_shape=[
            jax.ShapeDtypeStruct((rows, width), BF16),
            jax.ShapeDtypeStruct((blocks * rows, width), BF16),
            jax.ShapeDtypeStruct((blocks * rows, width), BF16),
            jax.ShapeDtypeStruct((rows, width), F32),
            jax.ShapeDtypeStruct((wide, keys), F32),
        ],
        in_specs=[vmem] * (5 + len(halves)),
        out_specs=[vmem] * 5,
        scratch_shapes=[pltpu.VMEM((keys, wide), F32)],
        compiler_params=pltpu.CompilerParams(vmem_limit_bytes=24 * MIB),
        cost_estimate=cost(1),
        name="turn_bias",
    )(near, wq, wk, wv, wg, *halves)


def attend_kernel(samples, bias, *refs):
    parts, refs = [refs[5 * s : 5 * s + 5] for s in range(samples)], refs[5 * samples :]
    far, wk, wv, wo, out, kt, v = refs
    _, k_near, v_near, _, _ = parts[-1]
    rows, width = parts[-1][4].shape
    x = stack(far)
    scale = LOG2E / HEAD_DIM**0.5
    lane = iota((rows, 2 * LANES), 1)
    groups = head_groups(width)
    work = [(s, base, heads) for s in range(samples) for base, heads in groups]
    chunks = list(range(0, width, 2 * LANES))
    for i, c in enumerate(chunks):
        work.insert(min(2 * i + 1, (samples - 1) * len(groups) + i), c)

    def fill(c):
        lanes = slice(c, c + 2 * LANES)
        k = jnp.concatenate([k_near[:, lanes].astype(F32), dot(x, wk[:, lanes])], axis=0)
        kt[lanes] = k.T.astype(BF16)
        v[: v_near.shape[0], lanes] = v_near[:, lanes]
        v[v_near.shape[0] :, lanes] = dot(x, wv[:, lanes]).astype(BF16)

    def channels(base, h):
        low = h * HEAD_DIM - base
        return (lane >= low) & (lane < low + HEAD_DIM)

    def score(item):
        if isinstance(item, int):
            return fill(item)
        s, base, heads = item
        q, keys = parts[s][0], parts[s][1] if s < samples - 1 else kt
        mine = q[:, base : base + 2 * LANES].astype(F32)
        mine = jnp.concatenate([jnp.where(channels(base, h), mine, 0.0) for h in heads], axis=0).astype(BF16)
        some = bias[heads[0] * rows : (heads[-1] + 1) * rows]
        return item, dot(mine, keys[base : base + 2 * LANES]) * scale + some

    def soften(item):
        if item is None:
            return None
        place, sc = item
        e = jnp.exp2(sc - jnp.max(sc, -1, keepdims=True))
        return place, e.astype(BF16), inverse(jnp.sum(e, -1, keepdims=True))

    mixes = {}

    def mix(item):
        if item is None:
            return
        (s, base, heads), e, share = item
        values = parts[s][2] if s < samples - 1 else v
        o = dot(e, values[:, base : base + 2 * LANES]) * share
        for i, h in enumerate(heads):
            mixes[s, base] = jnp.where(channels(base, h), o[i * rows : (i + 1) * rows], mixes.get((s, base), 0.0))
        if h == HEADS - 1:
            close(s)

    def close(s):
        tiles = {}
        for base, _ in groups:
            for t in range(2):
                at = base + t * LANES
                part = mixes[s, base][:, t * LANES : (t + 1) * LANES]
                tiles[at] = tiles[at] + part if at in tiles else part
        gate, token_in = parts[s][3:]
        gated = jnp.concatenate([tiles[at] for at in range(0, width, LANES)], axis=1) * gate[...]
        out[s] = (token_in[...] + dot(gated.astype(BF16), wo[...])).astype(BF16)

    skewed(work, [score, soften, mix])


def attend(bias, parts, far, wk, wv, wo):
    rows, width = parts[-1][4].shape
    keys = 2 * parts[-1][1].shape[0]
    vmem = pl.BlockSpec(memory_space=pltpu.VMEM)
    operands = [bias, *(ref for part in parts for ref in part), far, wk, wv, wo]
    return pl.pallas_call(
        functools.partial(attend_kernel, len(parts)),
        out_shape=jax.ShapeDtypeStruct((len(parts), rows, width), BF16),
        in_specs=[vmem] * len(operands),
        out_specs=vmem,
        scratch_shapes=[pltpu.VMEM((width, keys), BF16), pltpu.VMEM((keys, width), BF16)],
        compiler_params=pltpu.CompilerParams(vmem_limit_bytes=32 * MIB),
        cost_estimate=cost(3),
        name="attend",
    )(*operands)


def shards(
    atom_feat,
    atom_token,
    pair_cond,
    token_mask,
    atom_wq,
    atom_wk,
    atom_wv,
    atom_wo,
    agg_weight,
    pair_weight,
    token_gain,
    query_weight,
    key_weight,
    value_weight,
    gate_weight,
    out_weight,
):
    samples = atom_feat.shape[0]
    rows = pair_cond.shape[0]
    ranks = lax.axis_size("row")
    bias, inner, outer = pair_bias(atom_feat, pair_cond, token_mask, pair_weight)
    inner = swap(inner, "row", 1)
    odd_pairs = [(i, (i + 1) % ranks) for i in range(1, ranks, 2)]
    outer = lax.ppermute(outer, "row", odd_pairs + [(j, i) for i, j in odd_pairs])

    def widen(held, axis, bit, *others):
        return jnp.concatenate([held, after(swap(held, axis, bit), *others)], axis=0)

    bits, row_bits = bits_of(lax.axis_size("sample")), bits_of(ranks)
    orders = [bits, bits[:1] + bits[-1:] + bits[1:-1]]
    split = (bias.shape[1] // LANES + 1) // 2 * LANES
    got = swap(bias, "sample", bits[0])
    norms, inputs = [], []
    for s in range(samples):
        halo = (inner, outer)
        mixed = atom_attention(s, atom_feat, halo if s else (), atom_wq, atom_wk, atom_wv)
        outside = () if s else (*halo, atom_wq, atom_wk, atom_wv)
        token_in, token_norm = gather_tokens(
            s, mixed, atom_feat, atom_token, atom_wo, agg_weight, token_gain, outside, rows
        )
        inputs.append(token_in)
        norms.append(token_norm[None])
        if s == 0:
            bias, got, _ = lax.optimization_barrier((bias, got, token_norm))
            held = [jnp.stack([bias[:, lanes], got[:, lanes]]) for lanes in (slice(0, split), slice(split, None))]
            inner = after(inner, held, token_norm)
    last = swap(norms[-1], "row", row_bits[0])
    for i in range(1, len(bits) - 1):
        held = [widen(h, "sample", order[i], token_norm) for h, order in zip(held, orders)]
    halves = []
    for h, order in zip(held, orders):
        halves += [h, swap(h, "sample", order[-1])]
    parts = []
    weights = (query_weight, key_weight, value_weight, gate_weight, out_weight)
    for s in range(samples):
        near = norms[s]
        others = (mixed, parts, halves) if s == samples - 1 else (mixed, parts)
        for bit in row_bits[:-1]:
            if s == samples - 1 and bit == row_bits[0]:
                near = jnp.concatenate([near, after(last, *others)], axis=0)
            else:
                near = widen(near, "row", bit, *others)
        far = swap(near, "row", row_bits[-1])
        near = after(near, held)
        if s < samples - 1:
            parts.append((*project(near, far, *weights), inputs[s]))
        else:
            *part, bias = turn_bias(orders, row_bits, halves, near, *weights[:4])
            parts.append((*part, inputs[s]))
    return attend(bias, parts, far, key_weight, value_weight, out_weight)


def solution(mesh):
    placed = (
        P("sample", "row", None),
        P("row"),
        P("row", "sample", None),
        P("sample"),
    ) + (P(),) * 12
    return jax.shard_map(
        shards, mesh=mesh, in_specs=placed, out_specs=P("sample", "row", None), check_vma=False
    )
```

```python
import functools
import math

import jax
import jax.numpy as jnp
from jax import lax
from jax.experimental import pallas as pl
from jax.experimental.pallas import tpu as pltpu
from jax.sharding import PartitionSpec as P

HEADS = 16
HEAD_DIM = 48
AHEADS = 4
AHEAD_DIM = 32
QWIN = 32
KWIN = 128
RIM = (KWIN - QWIN) // 2
LANES = 128
SUB = 8
F32 = jnp.float32
BF16 = jnp.bfloat16
MIB = 1024 * 1024
LOG2E = math.log2(math.e)
NT = (((1,), (1,)), ((), ()))


def layer_norm(x):
    mean = jnp.mean(x, -1, keepdims=True)
    centre = x - mean
    var = jnp.mean(centre * centre, -1, keepdims=True)
    return centre * lax.rsqrt(var + 1e-05)


def dot(a, b):
    return jnp.dot(a, b, preferred_element_type=F32)


def dot_nt(a, b):
    return lax.dot_general(a, b, NT, preferred_element_type=F32)


def iota(shape, dim):
    return lax.broadcasted_iota(jnp.int32, shape, dim)


def cost(micros):
    return pl.CostEstimate(flops=micros * 20_000_000, bytes_accessed=1_000, transcendentals=0)


def inverse(total):
    guess = pl.reciprocal(total, approx=True)
    return guess * (2.0 - total * guess)


def skewed(items, stages):
    held = list(items)
    for t in range(len(held) + len(stages) - 1):
        for k in reversed(range(len(stages))):
            if 0 <= t - k < len(held):
                held[t - k] = stages[k](held[t - k])
    return held


def normalise_kernel(pair, normed):
    for k in range(0, pair.shape[0], 6):
        normed[k : k + 6] = layer_norm(pair[k : k + 6].astype(F32))


def normalise_pairs(pair_cond):
    rows, cols, chans = pair_cond.shape
    vmem = pl.BlockSpec(memory_space=pltpu.VMEM)
    return pl.pallas_call(
        normalise_kernel,
        out_shape=jax.ShapeDtypeStruct((cols, rows, chans), F32),
        in_specs=[vmem],
        out_specs=vmem,
        compiler_params=pltpu.CompilerParams(vmem_limit_bytes=8 * MIB),
        cost_estimate=cost(1),
        name="normalise_pairs",
    )(jnp.transpose(pair_cond, (1, 0, 2)))


def bias_kernel(feat, normed, mask, weight, out, inner, outer, whole):
    odd = lax.axis_index("row") % 2 == 1
    head, tail = feat[:, :RIM], feat[:, feat.shape[1] - RIM :]
    inner[...] = jnp.where(odd, head, tail)
    outer[...] = jnp.where(odd, tail, head)
    cols, rows, chans = normed.shape
    spread = (iota((HEADS, LANES), 1) // SUB == iota((HEADS, LANES), 0)).astype(BF16)
    wide = lax.dot_general(weight[...], spread, (((0,), (0,)), ((), ())), preferred_element_type=F32).astype(BF16)
    tall = cols * SUB
    key_of = iota((tall, cols), 0) // SUB == iota((tall, cols), 1)
    open_row = jnp.broadcast_to(mask[...].reshape(1, cols), (LANES, cols)).astype(BF16)
    open_key = dot_nt(key_of.astype(BF16), open_row) > 0.5
    picked = (iota((cols, tall), 1) // SUB == iota((cols, tall), 0)).astype(BF16)
    batch = 3
    row = iota((batch * tall, LANES), 0)
    mine = iota((batch * tall, LANES), 1) % SUB == row % SUB
    query = row // tall * SUB + row % SUB
    apart = lax.axis_index("sample") * cols + row % tall // SUB - lax.axis_index("row") * rows - query
    open_key = jnp.concatenate([open_key] * batch, axis=0)

    def weigh(first):
        x = [normed[:, g * SUB : (g + 1) * SUB].reshape(tall, chans) for g in range(first, first + batch)]
        raw = dot(jnp.concatenate(x, axis=0).astype(BF16), wide)
        raw = jnp.where(open_key | (apart == first * SUB), raw, -30000.0)
        return first, jnp.where(mine, raw, 0.0).astype(BF16)

    def pick(item):
        first, raw = item
        for i in range(batch):
            whole[(first + i) * cols : (first + i + 1) * cols] = dot(picked, raw[i * tall : (i + 1) * tall])

    skewed(range(0, rows // SUB, batch), [weigh, pick])
    out[...] = whole[...].astype(BF16)


def pair_bias(feat, pair_cond, token_mask, pair_weight):
    rows, cols, _ = pair_cond.shape
    edge = (feat.shape[0], RIM, feat.shape[2])
    vmem = pl.BlockSpec(memory_space=pltpu.VMEM)
    return pl.pallas_call(
        bias_kernel,
        out_shape=[
            jax.ShapeDtypeStruct((rows // SUB * cols, LANES), BF16),
            jax.ShapeDtypeStruct(edge, BF16),
            jax.ShapeDtypeStruct(edge, BF16),
        ],
        in_specs=[vmem] * 4,
        out_specs=[vmem] * 3,
        scratch_shapes=[pltpu.VMEM((rows // SUB * cols, LANES), F32)],
        compiler_params=pltpu.CompilerParams(vmem_limit_bytes=8 * MIB),
        cost_estimate=cost(3),
        name="pair_bias",
    )(feat, normalise_pairs(pair_cond), token_mask, pair_weight.T)


def after(value, *others):
    return lax.optimization_barrier((value, *others))[0]


def swap(held, axis, far):
    return lax.ppermute(held, axis, [(i, i ^ far) for i in range(lax.axis_size(axis))])


def bits_of(devices):
    return [devices >> i for i in range(1, devices.bit_length())]


def places_of(bits):
    places = [0]
    for bit in bits:
        places += [p ^ bit for p in places]
    return places


def windows_attend(starts, qs, ks, vs, mixed, shift, hide):
    rate = LOG2E / AHEAD_DIM**0.5
    tall = AHEADS * QWIN
    head_of = iota((QWIN, qs.shape[1]), 1) // AHEAD_DIM

    def score(batch):
        out = []
        for at in batch:
            q = qs[at - shift : at - shift + QWIN]
            q = jnp.concatenate([jnp.where(head_of == h, q, jnp.zeros_like(q)) for h in range(AHEADS)], axis=0)
            out.append(hide(at, dot_nt(q, ks[at : at + KWIN])))
        return batch, jnp.concatenate(out, axis=0)

    def soften(item):
        batch, s = item
        e = jnp.exp2((s - jnp.max(s, -1, keepdims=True)) * rate)
        return batch, e.astype(BF16), jnp.sum(e, -1, keepdims=True)

    def own_head(parts):
        acc = parts[:QWIN]
        for h in range(1, AHEADS):
            acc = jnp.where(head_of == h, parts[h * QWIN : (h + 1) * QWIN], acc)
        return acc

    def mix(item):
        batch, e, total = item
        for i, at in enumerate(batch):
            part = slice(i * tall, (i + 1) * tall)
            o = own_head(dot(e[part], vs[at : at + KWIN])) * inverse(own_head(total[part]))
            mixed[at - shift : at - shift + QWIN] = o.astype(BF16)

    skewed(starts, [score, soften, mix])


def halo_of(sample, inner, outer):
    odd = lax.axis_index("row") % 2 == 1
    return jnp.where(odd, inner[sample], outer[sample]), jnp.where(odd, outer[sample], inner[sample])


def hide_outside(atoms):
    rank = lax.axis_index("row")
    at_start = rank == 0
    at_end = rank == lax.axis_size("row") - 1
    keyat = iota((AHEADS * QWIN, KWIN), 1)

    def hide(at, s):
        if at < RIM:
            s = jnp.where(at_start & (keyat < RIM - at), -jnp.inf, s)
        if at + KWIN > RIM + atoms:
            s = jnp.where(at_end & (keyat >= RIM + atoms - at), -jnp.inf, s)
        return s

    return hide


def atom_kernel(sample, feat, *refs):
    *halo, wq, wk, wv, mixed, qs, ks, vs = refs
    atoms, chans = feat.shape[1:]
    wqkv = jnp.concatenate([wq[...], wk[...], wv[...]], axis=1)

    def normalise(at):
        if isinstance(at, int):
            part = feat[sample, at : at + LANES]
        else:
            at, part = at
        return at, layer_norm(part.astype(F32)).astype(BF16)

    def project_atoms(item):
        at, normed = item
        count = normed.shape[0]
        if count == RIM:
            kv = dot(normed, wqkv[:, chans:]).astype(BF16)
        else:
            qkv = dot(normed, wqkv).astype(BF16)
            qs[at : at + count] = qkv[:, :chans]
            kv = qkv[:, chans:]
        ks[RIM + at : RIM + at + count] = kv[:, :chans]
        vs[RIM + at : RIM + at + count] = kv[:, chans:]

    parts = list(range(0, atoms, LANES))
    if halo:
        before, behind = halo_of(sample, *halo)
        parts += [(-RIM, before), (atoms, behind)]
    skewed(parts, [normalise, project_atoms])
    starts = list(range(0, atoms, QWIN))
    if not halo:
        starts = [at for at in starts if RIM <= at <= atoms + RIM - KWIN]
    batch = 6
    batches = [starts[i : i + batch] for i in range(0, len(starts), batch)]
    windows_attend(batches, qs, ks, vs, mixed, 0, hide_outside(atoms))


def atom_attention(sample, feat, halo, wq, wk, wv):
    atoms, chans = feat.shape[1:]
    vmem = pl.BlockSpec(memory_space=pltpu.VMEM)
    return pl.pallas_call(
        functools.partial(atom_kernel, sample),
        out_shape=jax.ShapeDtypeStruct((atoms, chans), BF16),
        in_specs=[vmem] * (4 + len(halo)),
        out_specs=vmem,
        scratch_shapes=[
            pltpu.VMEM((atoms, chans), BF16),
            pltpu.VMEM((atoms + 2 * RIM, chans), BF16),
            pltpu.VMEM((atoms + 2 * RIM, chans), BF16),
        ],
        compiler_params=pltpu.CompilerParams(vmem_limit_bytes=16 * MIB),
        cost_estimate=cost(4),
        name="atom_attention",
    )(feat, *halo, wq, wk, wv)


def gather_kernel(sample, mixed, feat, token, wo, agg, gain, *refs):
    *outside, token_in, token_norm, qs, ks, vs, ends = refs
    atoms, chans = feat.shape[1:]
    rows = token_in.shape[0]
    local = token[...].reshape(1, atoms) - lax.axis_index("row") * rows
    step = 384
    sums = []
    edge = 2 * QWIN
    if outside:
        inner, outer, wq, wk, wv = outside
        before, behind = halo_of(sample, inner, outer)
        wqkv = jnp.concatenate([wq[...], wk[...], wv[...]], axis=1)
        near = edge + KWIN - QWIN - RIM
        both = [before, feat[sample, :near], feat[sample, atoms - near :], behind]
        qkv = dot(layer_norm(jnp.concatenate([p.astype(F32) for p in both], axis=0)).astype(BF16), wqkv).astype(BF16)
        qs[...] = qkv[:, :chans]
        ks[...] = qkv[:, chans : 2 * chans]
        vs[...] = qkv[:, 2 * chans :]
        apart = atoms - 2 * near
        starts = [0, QWIN, RIM + near, RIM + near + QWIN]
        hide = hide_outside(atoms)
        windows_attend([starts], qs, ks, vs, ends, -RIM, lambda at, s: hide(at if at < RIM else at + apart, s))

    def finish(c):
        part = mixed[c : c + step]
        if outside and c == 0:
            part = jnp.concatenate([ends[RIM : RIM + edge], part[edge:]], axis=0)
        if outside and c + step == atoms:
            at = ends.shape[0] - RIM - edge
            part = jnp.concatenate([part[: step - edge], ends[at : at + edge]], axis=0)
        return c, (feat[sample, c : c + step].astype(F32) + dot(part, wo[...])).astype(BF16)

    def hide_below(item):
        c, out = item
        return c, jnp.maximum(dot(out, agg[...]), 0.0).astype(BF16)

    def add(item):
        c, hidden = item
        onehot = (iota((rows, step), 0) == local[:, c : c + step]).astype(F32)
        part = dot(onehot.astype(BF16), hidden), jnp.sum(onehot, -1, keepdims=True)
        sums[:] = [a + b for a, b in zip(sums, part)] if sums else part

    chunks = list(range(0, atoms, step))
    skewed(chunks[1:-1] + [chunks[0], chunks[-1]], [finish, hide_below, add])
    tin = sums[0] / sums[1]
    token_in[...] = tin
    token_norm[...] = (layer_norm(tin) * gain[...].reshape(1, -1)).astype(BF16)


def gather_tokens(sample, mixed, feat, token, wo, agg, gain, outside, rows):
    width = agg.shape[1]
    chans = feat.shape[2]
    reach = 2 * (KWIN + QWIN)
    vmem = pl.BlockSpec(memory_space=pltpu.VMEM)
    return pl.pallas_call(
        functools.partial(gather_kernel, sample),
        out_shape=[jax.ShapeDtypeStruct((rows, width), F32), jax.ShapeDtypeStruct((rows, width), BF16)],
        in_specs=[vmem] * (6 + len(outside)),
        out_specs=[vmem, vmem],
        scratch_shapes=[pltpu.VMEM((reach, chans), BF16)] * 4,
        compiler_params=pltpu.CompilerParams(vmem_limit_bytes=16 * MIB),
        cost_estimate=cost(1),
        name="gather_tokens",
    )(mixed, feat, token, wo, agg, gain, *outside)


def head_groups(width):
    groups = []
    for base in range(0, width, 8 * HEAD_DIM):
        first = base // HEAD_DIM
        groups.append((base, range(first, first + 5)))
        groups.append((base + LANES, range(first + 5, first + 8)))
    return groups


def stack(blocks):
    return jnp.concatenate([blocks[j].astype(F32) for j in range(blocks.shape[0])], axis=0).astype(BF16)


def project_kernel(near, far, wq, wk, wv, wg, wo, q, kt, v, gate):
    x = jnp.concatenate([stack(near), stack(far)], axis=0)
    q[...] = dot(near[0], wq[...]).astype(BF16)
    gate[...] = jax.nn.sigmoid(dot(near[0], wg[...]))
    for c in range(0, x.shape[1], 2 * LANES):
        kt[c : c + 2 * LANES] = dot(x, wk[:, c : c + 2 * LANES]).T.astype(BF16)
    v[...] = dot(x, wv[...]).astype(BF16)


def project(near, far, wq, wk, wv, wg, wo):
    half, rows, width = near.shape
    keys = 2 * half * rows
    vmem = pl.BlockSpec(memory_space=pltpu.VMEM)
    return pl.pallas_call(
        project_kernel,
        out_shape=[
            jax.ShapeDtypeStruct((rows, width), BF16),
            jax.ShapeDtypeStruct((width, keys), BF16),
            jax.ShapeDtypeStruct((keys, width), BF16),
            jax.ShapeDtypeStruct((rows, width), F32),
        ],
        in_specs=[vmem] * 7,
        out_specs=[vmem] * 4,
        compiler_params=pltpu.CompilerParams(vmem_limit_bytes=24 * MIB),
        cost_estimate=cost(2),
        name="project",
    )(near, far, wq, wk, wv, wg, wo)


def turn_kernel(orders, row_bits, near, wq, wk, wv, wg, *refs):
    *halves, q, k, v, gate, out, tall, flat = refs
    x = stack(near)
    width = x.shape[1]

    def project_columns(c):
        lanes = slice(c, c + 2 * LANES)
        q[:, lanes] = dot(near[0], wq[:, lanes]).astype(BF16)
        k[:, lanes] = dot(x, wk[:, lanes]).astype(BF16)
        v[:, lanes] = dot(x, wv[:, lanes]).astype(BF16)
        gate[:, lanes] = jax.nn.sigmoid(dot(near[0], wg[:, lanes]))

    rows = out.shape[0] // HEADS
    me = lax.axis_index("sample")
    groups = 0
    for mine, other, bits in zip(halves[::2], halves[1::2], orders):
        half, count, _ = mine.shape
        cols = tall.shape[0] // (2 * half)
        places = places_of(bits)
        for j in range(2 * half):
            place = sum(jnp.where(me ^ j == p, i, 0) for i, p in enumerate(places))
            block = jnp.where(place < half, mine[place % half], other[place % half])
            low = groups * cols
            flat[j, low : low + count] = block.astype(F32)
            for g in range(count // cols):
                lanes = slice((groups + g) * LANES, (groups + g + 1) * LANES)
                tall[j * cols : (j + 1) * cols, lanes] = flat[j, low + g * cols : low + (g + 1) * cols]
        groups += count // cols
    starts = [pl.multiple_of((lax.axis_index("row") ^ p) * rows, SUB) for p in places_of(row_bits)]
    for g in range(rows // SUB):
        if g * 2 * LANES < width:
            project_columns(g * 2 * LANES)
        lanes = slice(g * LANES, (g + 1) * LANES)
        turned = jnp.concatenate([tall[pl.ds(start, rows), lanes] for start in starts], axis=0).T
        for h in range(HEADS):
            out[h * rows + g * SUB : h * rows + (g + 1) * SUB] = turned[h * SUB : (h + 1) * SUB] * LOG2E


def turn_bias(orders, row_bits, halves, near, wq, wk, wv, wg):
    blocks, rows, width = near.shape
    devices = 2 * halves[0].shape[0]
    wide = rows * HEADS
    count = sum(part.shape[1] for part in halves[::2])
    keys = devices * count * LANES // wide
    vmem = pl.BlockSpec(memory_space=pltpu.VMEM)
    return pl.pallas_call(
        functools.partial(turn_kernel, orders, row_bits),
        out_shape=[
            jax.ShapeDtypeStruct((rows, width), BF16),
            jax.ShapeDtypeStruct((blocks * rows, width), BF16),
            jax.ShapeDtypeStruct((blocks * rows, width), BF16),
            jax.ShapeDtypeStruct((rows, width), F32),
            jax.ShapeDtypeStruct((wide, keys), F32),
        ],
        in_specs=[vmem] * (5 + len(halves)),
        out_specs=[vmem] * 5,
        scratch_shapes=[pltpu.VMEM((keys, wide), F32), pltpu.VMEM((devices, count, LANES), F32)],
        compiler_params=pltpu.CompilerParams(vmem_limit_bytes=32 * MIB),
        cost_estimate=cost(1),
        name="turn_bias",
    )(near, wq, wk, wv, wg, *halves)


def attend_kernel(samples, bias, *refs):
    parts, refs = [refs[5 * s : 5 * s + 5] for s in range(samples)], refs[5 * samples :]
    far, wk, wv, wo, out, kt, v = refs
    _, k_near, v_near, _, _ = parts[-1]
    rows, width = parts[-1][4].shape
    x = stack(far)
    scale = LOG2E / HEAD_DIM**0.5
    lane = iota((rows, 2 * LANES), 1)
    groups = head_groups(width)
    work = [(s, base, heads) for s in range(samples) for base, heads in groups]
    chunks = list(range(0, width, 2 * LANES))
    for i, c in enumerate(chunks):
        work.insert(min(2 * i + 1, (samples - 1) * len(groups) + i), c)

    def fill(c):
        lanes = slice(c, c + 2 * LANES)
        k = jnp.concatenate([k_near[:, lanes].astype(F32), dot(x, wk[:, lanes])], axis=0)
        kt[lanes] = k.T.astype(BF16)
        v[: v_near.shape[0], lanes] = v_near[:, lanes]
        v[v_near.shape[0] :, lanes] = dot(x, wv[:, lanes]).astype(BF16)

    def channels(base, h):
        low = h * HEAD_DIM - base
        return (lane >= low) & (lane < low + HEAD_DIM)

    def score(item):
        if isinstance(item, int):
            return fill(item)
        s, base, heads = item
        q, keys = parts[s][0], parts[s][1] if s < samples - 1 else kt
        mine = q[:, base : base + 2 * LANES].astype(F32)
        mine = jnp.concatenate([jnp.where(channels(base, h), mine, 0.0) for h in heads], axis=0).astype(BF16)
        some = bias[heads[0] * rows : (heads[-1] + 1) * rows]
        return item, dot(mine, keys[base : base + 2 * LANES]) * scale + some

    def soften(item):
        if item is None:
            return None
        place, sc = item
        e = jnp.exp2(sc - jnp.max(sc, -1, keepdims=True))
        return place, e.astype(BF16), inverse(jnp.sum(e, -1, keepdims=True))

    mixes = {}

    def mix(item):
        if item is None:
            return
        (s, base, heads), e, share = item
        values = parts[s][2] if s < samples - 1 else v
        o = dot(e, values[:, base : base + 2 * LANES]) * share
        for i, h in enumerate(heads):
            mixes[s, base] = jnp.where(channels(base, h), o[i * rows : (i + 1) * rows], mixes.get((s, base), 0.0))
        if h == HEADS - 1:
            close(s)

    def close(s):
        tiles = {}
        for base, _ in groups:
            for t in range(2):
                at = base + t * LANES
                part = mixes[s, base][:, t * LANES : (t + 1) * LANES]
                tiles[at] = tiles[at] + part if at in tiles else part
        gate, token_in = parts[s][3:]
        gated = jnp.concatenate([tiles[at] for at in range(0, width, LANES)], axis=1) * gate[...]
        out[s] = (token_in[...] + dot(gated.astype(BF16), wo[...])).astype(BF16)

    skewed(work, [score, soften, mix])


def attend(bias, parts, far, wk, wv, wo):
    rows, width = parts[-1][4].shape
    keys = 2 * parts[-1][1].shape[0]
    vmem = pl.BlockSpec(memory_space=pltpu.VMEM)
    operands = [bias, *(ref for part in parts for ref in part), far, wk, wv, wo]
    return pl.pallas_call(
        functools.partial(attend_kernel, len(parts)),
        out_shape=jax.ShapeDtypeStruct((len(parts), rows, width), BF16),
        in_specs=[vmem] * len(operands),
        out_specs=vmem,
        scratch_shapes=[pltpu.VMEM((width, keys), BF16), pltpu.VMEM((keys, width), BF16)],
        compiler_params=pltpu.CompilerParams(vmem_limit_bytes=32 * MIB),
        cost_estimate=cost(3),
        name="attend",
    )(*operands)


def shards(
    atom_feat,
    atom_token,
    pair_cond,
    token_mask,
    atom_wq,
    atom_wk,
    atom_wv,
    atom_wo,
    agg_weight,
    pair_weight,
    token_gain,
    query_weight,
    key_weight,
    value_weight,
    gate_weight,
    out_weight,
):
    samples = atom_feat.shape[0]
    rows = pair_cond.shape[0]
    ranks = lax.axis_size("row")
    bias, inner, outer = pair_bias(atom_feat, pair_cond, token_mask, pair_weight)
    inner = swap(inner, "row", 1)
    odd_pairs = [(i, (i + 1) % ranks) for i in range(1, ranks, 2)]
    outer = lax.ppermute(outer, "row", odd_pairs + [(j, i) for i, j in odd_pairs])

    def widen(held, axis, bit, *others):
        return jnp.concatenate([held, after(swap(held, axis, bit), *others)], axis=0)

    bits, row_bits = bits_of(lax.axis_size("sample")), bits_of(ranks)
    orders = [bits, bits[:1] + bits[-1:] + bits[1:-1]]
    split = rows // SUB // 2 * pair_cond.shape[1]
    got = swap(bias, "sample", bits[0])
    norms, inputs = [], []
    for s in range(samples):
        halo = (inner, outer)
        mixed = atom_attention(s, atom_feat, halo if s else (), atom_wq, atom_wk, atom_wv)
        outside = () if s else (*halo, atom_wq, atom_wk, atom_wv)
        token_in, token_norm = gather_tokens(
            s, mixed, atom_feat, atom_token, atom_wo, agg_weight, token_gain, outside, rows
        )
        inputs.append(token_in)
        norms.append(token_norm[None])
        if s == 0:
            bias, got, _ = lax.optimization_barrier((bias, got, token_norm))
            held = [jnp.stack([bias[part], got[part]]) for part in (slice(0, split), slice(split, None))]
            inner = after(inner, held, token_norm)
    last = swap(norms[-1], "row", row_bits[0])
    for i in range(1, len(bits) - 1):
        held = [widen(h, "sample", order[i], token_norm) for h, order in zip(held, orders)]
    halves = []
    for h, order in zip(held, orders):
        halves += [h, swap(h, "sample", order[-1])]
    parts = []
    weights = (query_weight, key_weight, value_weight, gate_weight, out_weight)
    for s in range(samples):
        near = norms[s]
        others = (mixed, parts, halves) if s == samples - 1 else (mixed, parts)
        for bit in row_bits[:-1]:
            if s == samples - 1 and bit == row_bits[0]:
                near = jnp.concatenate([near, after(last, *others)], axis=0)
            else:
                near = widen(near, "row", bit, *others)
        far = swap(near, "row", row_bits[-1])
        near = after(near, held)
        if s < samples - 1:
            parts.append((*project(near, far, *weights), inputs[s]))
        else:
            *part, bias = turn_bias(orders, row_bits, halves, near, *weights[:4])
            parts.append((*part, inputs[s]))
    return attend(bias, parts, far, key_weight, value_weight, out_weight)


def solution(mesh):
    placed = (
        P("sample", "row", None),
        P("row"),
        P("row", "sample", None),
        P("sample"),
    ) + (P(),) * 12
    return jax.shard_map(
        shards, mesh=mesh, in_specs=placed, out_specs=P("sample", "row", None), check_vma=False
    )
```

```python
import functools
import math

import jax
import jax.numpy as jnp
from jax import lax
from jax.experimental import pallas as pl
from jax.experimental.pallas import tpu as pltpu
from jax.sharding import PartitionSpec as P

HEADS = 16
HEAD_DIM = 48
AHEADS = 4
AHEAD_DIM = 32
QWIN = 32
KWIN = 128
RIM = (KWIN - QWIN) // 2
LANES = 128
SUB = 8
F32 = jnp.float32
BF16 = jnp.bfloat16
MIB = 1024 * 1024
LOG2E = math.log2(math.e)
NT = (((1,), (1,)), ((), ()))


def layer_norm(x):
    mean = jnp.mean(x, -1, keepdims=True)
    centre = x - mean
    var = jnp.mean(centre * centre, -1, keepdims=True)
    return centre * lax.rsqrt(var + 1e-05)


def dot(a, b):
    return jnp.dot(a, b, preferred_element_type=F32)


def dot_nt(a, b):
    return lax.dot_general(a, b, NT, preferred_element_type=F32)


def iota(shape, dim):
    return lax.broadcasted_iota(jnp.int32, shape, dim)


def cost(micros):
    return pl.CostEstimate(flops=micros * 20_000_000, bytes_accessed=1_000, transcendentals=0)


def inverse(total):
    guess = pl.reciprocal(total, approx=True)
    return guess * (2.0 - total * guess)


def skewed(items, stages):
    held = list(items)
    for t in range(len(held) + len(stages) - 1):
        for k in reversed(range(len(stages))):
            if 0 <= t - k < len(held):
                held[t - k] = stages[k](held[t - k])
    return held


def normalise_kernel(pair, normed):
    for k in range(0, pair.shape[0], 6):
        normed[k : k + 6] = layer_norm(pair[k : k + 6].astype(F32))


def normalise_pairs(pair_cond):
    rows, cols, chans = pair_cond.shape
    vmem = pl.BlockSpec(memory_space=pltpu.VMEM)
    return pl.pallas_call(
        normalise_kernel,
        out_shape=jax.ShapeDtypeStruct((cols, rows, chans), F32),
        in_specs=[vmem],
        out_specs=vmem,
        compiler_params=pltpu.CompilerParams(vmem_limit_bytes=8 * MIB),
        cost_estimate=cost(1),
        name="normalise_pairs",
    )(jnp.transpose(pair_cond, (1, 0, 2)))


def bias_kernel(feat, normed, mask, weight, out, inner, outer, whole):
    odd = lax.axis_index("row") % 2 == 1
    head, tail = feat[:, :RIM], feat[:, feat.shape[1] - RIM :]
    inner[...] = jnp.where(odd, head, tail)
    outer[...] = jnp.where(odd, tail, head)
    cols, rows, chans = normed.shape
    spread = (iota((HEADS, LANES), 1) // SUB == iota((HEADS, LANES), 0)).astype(BF16)
    wide = lax.dot_general(weight[...], spread, (((0,), (0,)), ((), ())), preferred_element_type=F32).astype(BF16)
    tall = cols * SUB
    key_of = iota((tall, cols), 0) // SUB == iota((tall, cols), 1)
    open_row = jnp.broadcast_to(mask[...].reshape(1, cols), (LANES, cols)).astype(BF16)
    open_key = dot_nt(key_of.astype(BF16), open_row) > 0.5
    picked = (iota((cols, tall), 1) // SUB == iota((cols, tall), 0)).astype(BF16)
    batch = 3
    row = iota((tall, LANES), 0)
    mine = iota((tall, LANES), 1) % SUB == row % SUB
    own = lax.axis_index("sample") * cols + row // SUB - lax.axis_index("row") * rows - row % SUB
    own = jnp.where(mine, own, -1)
    kept = mine & open_key
    base = jnp.where(mine & ~open_key, -30000.0, 0.0)

    def weigh(first):
        out = []
        for g in range(first, first + batch):
            raw = dot(normed[:, g * SUB : (g + 1) * SUB].reshape(tall, chans).astype(BF16), wide)
            out.append(jnp.where(kept | (own == g * SUB), raw, base).astype(BF16))
        return first, out

    def pick(item):
        first, out = item
        for i, raw in enumerate(out):
            whole[(first + i) * cols : (first + i + 1) * cols] = dot(picked, raw)

    skewed(range(0, rows // SUB, batch), [weigh, pick])
    out[...] = whole[...].astype(BF16)


def pair_bias(feat, pair_cond, token_mask, pair_weight):
    rows, cols, _ = pair_cond.shape
    edge = (feat.shape[0], RIM, feat.shape[2])
    vmem = pl.BlockSpec(memory_space=pltpu.VMEM)
    return pl.pallas_call(
        bias_kernel,
        out_shape=[
            jax.ShapeDtypeStruct((rows // SUB * cols, LANES), BF16),
            jax.ShapeDtypeStruct(edge, BF16),
            jax.ShapeDtypeStruct(edge, BF16),
        ],
        in_specs=[vmem] * 4,
        out_specs=[vmem] * 3,
        scratch_shapes=[pltpu.VMEM((rows // SUB * cols, LANES), F32)],
        compiler_params=pltpu.CompilerParams(vmem_limit_bytes=8 * MIB),
        cost_estimate=cost(3),
        name="pair_bias",
    )(feat, normalise_pairs(pair_cond), token_mask, pair_weight.T)


def after(value, *others):
    return lax.optimization_barrier((value, *others))[0]


def swap(held, axis, far):
    return lax.ppermute(held, axis, [(i, i ^ far) for i in range(lax.axis_size(axis))])


def bits_of(devices):
    return [devices >> i for i in range(1, devices.bit_length())]


def places_of(bits):
    places = [0]
    for bit in bits:
        places += [p ^ bit for p in places]
    return places


def windows_attend(starts, qs, ks, vs, mixed, shift, hide):
    rate = LOG2E / AHEAD_DIM**0.5
    tall = AHEADS * QWIN
    head_of = iota((QWIN, qs.shape[1]), 1) // AHEAD_DIM

    def score(batch):
        out = []
        for at in batch:
            q = qs[at - shift : at - shift + QWIN]
            q = jnp.concatenate([jnp.where(head_of == h, q, jnp.zeros_like(q)) for h in range(AHEADS)], axis=0)
            out.append(hide(at, dot_nt(q, ks[at : at + KWIN])))
        return batch, jnp.concatenate(out, axis=0)

    def soften(item):
        batch, s = item
        e = jnp.exp2((s - jnp.max(s, -1, keepdims=True)) * rate)
        return batch, e.astype(BF16), jnp.sum(e, -1, keepdims=True)

    def own_head(parts):
        acc = parts[:QWIN]
        for h in range(1, AHEADS):
            acc = jnp.where(head_of == h, parts[h * QWIN : (h + 1) * QWIN], acc)
        return acc

    def mix(item):
        batch, e, total = item
        for i, at in enumerate(batch):
            part = slice(i * tall, (i + 1) * tall)
            o = own_head(dot(e[part], vs[at : at + KWIN])) * inverse(own_head(total[part]))
            mixed[at - shift : at - shift + QWIN] = o.astype(BF16)

    skewed(starts, [score, soften, mix])


def halo_of(sample, inner, outer):
    odd = lax.axis_index("row") % 2 == 1
    return jnp.where(odd, inner[sample], outer[sample]), jnp.where(odd, outer[sample], inner[sample])


def hide_outside(atoms):
    rank = lax.axis_index("row")
    at_start = rank == 0
    at_end = rank == lax.axis_size("row") - 1
    keyat = iota((AHEADS * QWIN, KWIN), 1)

    def hide(at, s):
        if at < RIM:
            s = jnp.where(at_start & (keyat < RIM - at), -jnp.inf, s)
        if at + KWIN > RIM + atoms:
            s = jnp.where(at_end & (keyat >= RIM + atoms - at), -jnp.inf, s)
        return s

    return hide


def atom_kernel(sample, feat, *refs):
    *halo, wq, wk, wv, mixed, qs, ks, vs = refs
    atoms, chans = feat.shape[1:]
    wqkv = jnp.concatenate([wq[...], wk[...], wv[...]], axis=1)

    def normalise(at):
        if isinstance(at, int):
            part = feat[sample, at : at + LANES]
        else:
            at, part = at
        return at, layer_norm(part.astype(F32)).astype(BF16)

    def project_atoms(item):
        at, normed = item
        count = normed.shape[0]
        if count == RIM:
            kv = dot(normed, wqkv[:, chans:]).astype(BF16)
        else:
            qkv = dot(normed, wqkv).astype(BF16)
            qs[at : at + count] = qkv[:, :chans]
            kv = qkv[:, chans:]
        ks[RIM + at : RIM + at + count] = kv[:, :chans]
        vs[RIM + at : RIM + at + count] = kv[:, chans:]

    parts = list(range(0, atoms, LANES))
    if halo:
        before, behind = halo_of(sample, *halo)
        parts += [(-RIM, before), (atoms, behind)]
    skewed(parts, [normalise, project_atoms])
    starts = list(range(0, atoms, QWIN))
    if not halo:
        starts = [at for at in starts if RIM <= at <= atoms + RIM - KWIN]
    batch = 6
    batches = [starts[i : i + batch] for i in range(0, len(starts), batch)]
    windows_attend(batches, qs, ks, vs, mixed, 0, hide_outside(atoms))


def atom_attention(sample, feat, halo, wq, wk, wv):
    atoms, chans = feat.shape[1:]
    vmem = pl.BlockSpec(memory_space=pltpu.VMEM)
    return pl.pallas_call(
        functools.partial(atom_kernel, sample),
        out_shape=jax.ShapeDtypeStruct((atoms, chans), BF16),
        in_specs=[vmem] * (4 + len(halo)),
        out_specs=vmem,
        scratch_shapes=[
            pltpu.VMEM((atoms, chans), BF16),
            pltpu.VMEM((atoms + 2 * RIM, chans), BF16),
            pltpu.VMEM((atoms + 2 * RIM, chans), BF16),
        ],
        compiler_params=pltpu.CompilerParams(vmem_limit_bytes=16 * MIB),
        cost_estimate=cost(4),
        name="atom_attention",
    )(feat, *halo, wq, wk, wv)


def gather_kernel(sample, mixed, feat, token, wo, agg, gain, *refs):
    *outside, token_in, token_norm, qs, ks, vs, ends = refs
    atoms, chans = feat.shape[1:]
    rows = token_in.shape[0]
    local = token[...].reshape(1, atoms) - lax.axis_index("row") * rows
    step = 384
    sums = []
    edge = 2 * QWIN
    if outside:
        inner, outer, wq, wk, wv = outside
        before, behind = halo_of(sample, inner, outer)
        wqkv = jnp.concatenate([wq[...], wk[...], wv[...]], axis=1)
        near = edge + KWIN - QWIN - RIM
        both = [before, feat[sample, :near], feat[sample, atoms - near :], behind]
        qkv = dot(layer_norm(jnp.concatenate([p.astype(F32) for p in both], axis=0)).astype(BF16), wqkv).astype(BF16)
        qs[...] = qkv[:, :chans]
        ks[...] = qkv[:, chans : 2 * chans]
        vs[...] = qkv[:, 2 * chans :]
        apart = atoms - 2 * near
        starts = [0, QWIN, RIM + near, RIM + near + QWIN]
        hide = hide_outside(atoms)
        windows_attend([starts], qs, ks, vs, ends, -RIM, lambda at, s: hide(at if at < RIM else at + apart, s))

    def finish(c):
        part = mixed[c : c + step]
        if outside and c == 0:
            part = jnp.concatenate([ends[RIM : RIM + edge], part[edge:]], axis=0)
        if outside and c + step == atoms:
            at = ends.shape[0] - RIM - edge
            part = jnp.concatenate([part[: step - edge], ends[at : at + edge]], axis=0)
        return c, (feat[sample, c : c + step].astype(F32) + dot(part, wo[...])).astype(BF16)

    def hide_below(item):
        c, out = item
        return c, jnp.maximum(dot(out, agg[...]), 0.0).astype(BF16)

    def add(item):
        c, hidden = item
        onehot = (iota((rows, step), 0) == local[:, c : c + step]).astype(F32)
        part = dot(onehot.astype(BF16), hidden), jnp.sum(onehot, -1, keepdims=True)
        sums[:] = [a + b for a, b in zip(sums, part)] if sums else part

    chunks = list(range(0, atoms, step))
    skewed(chunks[1:-1] + [chunks[0], chunks[-1]], [finish, hide_below, add])
    tin = sums[0] / sums[1]
    token_in[...] = tin
    token_norm[...] = (layer_norm(tin) * gain[...].reshape(1, -1)).astype(BF16)


def gather_tokens(sample, mixed, feat, token, wo, agg, gain, outside, rows):
    width = agg.shape[1]
    chans = feat.shape[2]
    reach = 2 * (KWIN + QWIN)
    vmem = pl.BlockSpec(memory_space=pltpu.VMEM)
    return pl.pallas_call(
        functools.partial(gather_kernel, sample),
        out_shape=[jax.ShapeDtypeStruct((rows, width), F32), jax.ShapeDtypeStruct((rows, width), BF16)],
        in_specs=[vmem] * (6 + len(outside)),
        out_specs=[vmem, vmem],
        scratch_shapes=[pltpu.VMEM((reach, chans), BF16)] * 4,
        compiler_params=pltpu.CompilerParams(vmem_limit_bytes=16 * MIB),
        cost_estimate=cost(1),
        name="gather_tokens",
    )(mixed, feat, token, wo, agg, gain, *outside)


def head_groups(width):
    groups = []
    for base in range(0, width, 8 * HEAD_DIM):
        first = base // HEAD_DIM
        groups.append((base, range(first, first + 5)))
        groups.append((base + LANES, range(first + 5, first + 8)))
    return groups


def stack(blocks):
    return jnp.concatenate([blocks[j].astype(F32) for j in range(blocks.shape[0])], axis=0).astype(BF16)


def project_kernel(near, far, wq, wk, wv, wg, wo, q, kt, v, gate):
    x = jnp.concatenate([stack(near), stack(far)], axis=0)
    q[...] = dot(near[0], wq[...]).astype(BF16)
    gate[...] = jax.nn.sigmoid(dot(near[0], wg[...]))
    for c in range(0, x.shape[1], 2 * LANES):
        kt[c : c + 2 * LANES] = dot(x, wk[:, c : c + 2 * LANES]).T.astype(BF16)
    v[...] = dot(x, wv[...]).astype(BF16)


def project(near, far, wq, wk, wv, wg, wo):
    half, rows, width = near.shape
    keys = 2 * half * rows
    vmem = pl.BlockSpec(memory_space=pltpu.VMEM)
    return pl.pallas_call(
        project_kernel,
        out_shape=[
            jax.ShapeDtypeStruct((rows, width), BF16),
            jax.ShapeDtypeStruct((width, keys), BF16),
            jax.ShapeDtypeStruct((keys, width), BF16),
            jax.ShapeDtypeStruct((rows, width), F32),
        ],
        in_specs=[vmem] * 7,
        out_specs=[vmem] * 4,
        compiler_params=pltpu.CompilerParams(vmem_limit_bytes=24 * MIB),
        cost_estimate=cost(2),
        name="project",
    )(near, far, wq, wk, wv, wg, wo)


def turn_kernel(orders, row_bits, near, wq, wk, wv, wg, *refs):
    *halves, q, k, v, gate, out, tall, flat = refs
    x = stack(near)
    width = x.shape[1]

    def project_columns(c):
        lanes = slice(c, c + 2 * LANES)
        q[:, lanes] = dot(near[0], wq[:, lanes]).astype(BF16)
        k[:, lanes] = dot(x, wk[:, lanes]).astype(BF16)
        v[:, lanes] = dot(x, wv[:, lanes]).astype(BF16)
        gate[:, lanes] = jax.nn.sigmoid(dot(near[0], wg[:, lanes]))

    rows = out.shape[0] // HEADS
    me = lax.axis_index("sample")
    groups = 0
    for mine, other, bits in zip(halves[::2], halves[1::2], orders):
        half, count, _ = mine.shape
        cols = tall.shape[0] // (2 * half)
        places = places_of(bits)
        for j in range(2 * half):
            place = sum(jnp.where(me ^ j == p, i, 0) for i, p in enumerate(places))
            block = jnp.where(place < half, mine[place % half], other[place % half])
            low = groups * cols
            flat[j, low : low + count] = block.astype(F32)
            for g in range(count // cols):
                lanes = slice((groups + g) * LANES, (groups + g + 1) * LANES)
                tall[j * cols : (j + 1) * cols, lanes] = flat[j, low + g * cols : low + (g + 1) * cols]
        groups += count // cols
    starts = [pl.multiple_of((lax.axis_index("row") ^ p) * rows, SUB) for p in places_of(row_bits)]
    for g in range(rows // SUB):
        if g * 2 * LANES < width:
            project_columns(g * 2 * LANES)
        lanes = slice(g * LANES, (g + 1) * LANES)
        turned = jnp.concatenate([tall[pl.ds(start, rows), lanes] for start in starts], axis=0).T
        for h in range(HEADS):
            out[h * rows + g * SUB : h * rows + (g + 1) * SUB] = turned[h * SUB : (h + 1) * SUB] * LOG2E


def turn_bias(orders, row_bits, halves, near, wq, wk, wv, wg):
    blocks, rows, width = near.shape
    devices = 2 * halves[0].shape[0]
    wide = rows * HEADS
    count = sum(part.shape[1] for part in halves[::2])
    keys = devices * count * LANES // wide
    vmem = pl.BlockSpec(memory_space=pltpu.VMEM)
    return pl.pallas_call(
        functools.partial(turn_kernel, orders, row_bits),
        out_shape=[
            jax.ShapeDtypeStruct((rows, width), BF16),
            jax.ShapeDtypeStruct((blocks * rows, width), BF16),
            jax.ShapeDtypeStruct((blocks * rows, width), BF16),
            jax.ShapeDtypeStruct((rows, width), F32),
            jax.ShapeDtypeStruct((wide, keys), F32),
        ],
        in_specs=[vmem] * (5 + len(halves)),
        out_specs=[vmem] * 5,
        scratch_shapes=[pltpu.VMEM((keys, wide), F32), pltpu.VMEM((devices, count, LANES), F32)],
        compiler_params=pltpu.CompilerParams(vmem_limit_bytes=32 * MIB),
        cost_estimate=cost(1),
        name="turn_bias",
    )(near, wq, wk, wv, wg, *halves)


def attend_kernel(samples, bias, *refs):
    parts, refs = [refs[5 * s : 5 * s + 5] for s in range(samples)], refs[5 * samples :]
    far, wk, wv, wo, out, kt, v = refs
    _, k_near, v_near, _, _ = parts[-1]
    rows, width = parts[-1][4].shape
    x = stack(far)
    scale = LOG2E / HEAD_DIM**0.5
    lane = iota((rows, LANES), 1)
    groups = head_groups(width)
    work = [(s, base, heads) for s in range(samples) for base, heads in groups]
    chunks = list(range(0, width, 2 * LANES))
    for i, c in enumerate(chunks):
        work.insert(min(2 * i + 1, (samples - 1) * len(groups) + i), c)

    def fill(c):
        lanes = slice(c, c + 2 * LANES)
        k = jnp.concatenate([k_near[:, lanes].astype(F32), dot(x, wk[:, lanes])], axis=0)
        kt[lanes] = k.T.astype(BF16)
        v[: v_near.shape[0], lanes] = v_near[:, lanes]
        v[v_near.shape[0] :, lanes] = dot(x, wv[:, lanes]).astype(BF16)

    def tiles_of(h):
        return range(h * HEAD_DIM // LANES * LANES, (h + 1) * HEAD_DIM, LANES)

    def channels(at, h):
        low = h * HEAD_DIM - at
        return (lane >= low) & (lane < low + HEAD_DIM)

    blank = jnp.zeros((rows, LANES), F32)

    def score(item):
        if isinstance(item, int):
            return fill(item)
        s, base, heads = item
        q, keys = parts[s][0], parts[s][1] if s < samples - 1 else kt
        both = [(at, q[:, at : at + LANES].astype(F32)) for at in (base, base + LANES)]
        mine = [
            [jnp.where(channels(at, h), part, 0.0) if at in tiles_of(h) else blank for at, part in both] for h in heads
        ]
        mine = jnp.concatenate([jnp.concatenate(pair, axis=1) for pair in mine], axis=0).astype(BF16)
        some = bias[heads[0] * rows : (heads[-1] + 1) * rows]
        return item, dot(mine, keys[base : base + 2 * LANES]) * scale + some

    def soften(item):
        if item is None:
            return None
        place, sc = item
        e = jnp.exp2(sc - jnp.max(sc, -1, keepdims=True))
        return place, e.astype(BF16), inverse(jnp.sum(e, -1, keepdims=True))

    mixes = {}

    def mix(item):
        if item is None:
            return
        (s, base, heads), e, share = item
        values = parts[s][2] if s < samples - 1 else v
        o = dot(e, values[:, base : base + 2 * LANES])
        for i, h in enumerate(heads):
            part = slice(i * rows, (i + 1) * rows)
            for at in tiles_of(h):
                one = o[part, at - base : at - base + LANES] * share[part]
                mixes[s, at] = jnp.where(channels(at, h), one, mixes.get((s, at), 0.0))
        if h == HEADS - 1:
            close(s)

    def close(s):
        gate, token_in = parts[s][3:]
        gated = jnp.concatenate([mixes[s, at] for at in range(0, width, LANES)], axis=1) * gate[...]
        out[s] = (token_in[...] + dot(gated.astype(BF16), wo[...])).astype(BF16)

    skewed(work, [score, soften, mix])


def attend(bias, parts, far, wk, wv, wo):
    rows, width = parts[-1][4].shape
    keys = 2 * parts[-1][1].shape[0]
    vmem = pl.BlockSpec(memory_space=pltpu.VMEM)
    operands = [bias, *(ref for part in parts for ref in part), far, wk, wv, wo]
    return pl.pallas_call(
        functools.partial(attend_kernel, len(parts)),
        out_shape=jax.ShapeDtypeStruct((len(parts), rows, width), BF16),
        in_specs=[vmem] * len(operands),
        out_specs=vmem,
        scratch_shapes=[pltpu.VMEM((width, keys), BF16), pltpu.VMEM((keys, width), BF16)],
        compiler_params=pltpu.CompilerParams(vmem_limit_bytes=32 * MIB),
        cost_estimate=cost(3),
        name="attend",
    )(*operands)


def shards(
    atom_feat,
    atom_token,
    pair_cond,
    token_mask,
    atom_wq,
    atom_wk,
    atom_wv,
    atom_wo,
    agg_weight,
    pair_weight,
    token_gain,
    query_weight,
    key_weight,
    value_weight,
    gate_weight,
    out_weight,
):
    samples = atom_feat.shape[0]
    rows = pair_cond.shape[0]
    ranks = lax.axis_size("row")
    bias, inner, outer = pair_bias(atom_feat, pair_cond, token_mask, pair_weight)
    inner = swap(inner, "row", 1)
    odd_pairs = [(i, (i + 1) % ranks) for i in range(1, ranks, 2)]
    outer = lax.ppermute(outer, "row", odd_pairs + [(j, i) for i, j in odd_pairs])

    def widen(held, axis, bit, *others):
        return jnp.concatenate([held, after(swap(held, axis, bit), *others)], axis=0)

    bits, row_bits = bits_of(lax.axis_size("sample")), bits_of(ranks)
    orders = [bits, bits[:1] + bits[-1:] + bits[1:-1]]
    split = rows // SUB // 2 * pair_cond.shape[1]
    got = swap(bias, "sample", bits[0])
    norms, inputs = [], []
    for s in range(samples):
        halo = (inner, outer)
        mixed = atom_attention(s, atom_feat, halo if s else (), atom_wq, atom_wk, atom_wv)
        outside = () if s else (*halo, atom_wq, atom_wk, atom_wv)
        token_in, token_norm = gather_tokens(
            s, mixed, atom_feat, atom_token, atom_wo, agg_weight, token_gain, outside, rows
        )
        inputs.append(token_in)
        norms.append(token_norm[None])
        if s == 0:
            bias, got, _ = lax.optimization_barrier((bias, got, token_norm))
            held = [jnp.stack([bias[part], got[part]]) for part in (slice(0, split), slice(split, None))]
            inner = after(inner, held, token_norm)
    last = swap(norms[-1], "row", row_bits[0])
    for i in range(1, len(bits) - 1):
        held = [widen(h, "sample", order[i], token_norm) for h, order in zip(held, orders)]
    halves = []
    for h, order in zip(held, orders):
        halves += [h, swap(h, "sample", order[-1])]
    parts = []
    weights = (query_weight, key_weight, value_weight, gate_weight, out_weight)
    for s in range(samples):
        near = norms[s]
        others = (mixed, parts, halves) if s == samples - 1 else (mixed, parts)
        for bit in row_bits[:-1]:
            if s == samples - 1 and bit == row_bits[0]:
                near = jnp.concatenate([near, after(last, *others)], axis=0)
            else:
                near = widen(near, "row", bit, *others)
        far = swap(near, "row", row_bits[-1])
        near = after(near, held)
        if s < samples - 1:
            parts.append((*project(near, far, *weights), inputs[s]))
        else:
            *part, bias = turn_bias(orders, row_bits, halves, near, *weights[:4])
            parts.append((*part, inputs[s]))
    return attend(bias, parts, far, key_weight, value_weight, out_weight)


def solution(mesh):
    placed = (
        P("sample", "row", None),
        P("row"),
        P("row", "sample", None),
        P("sample"),
    ) + (P(),) * 12
    return jax.shard_map(
        shards, mesh=mesh, in_specs=placed, out_specs=P("sample", "row", None), check_vma=False
    )
```

```python
import functools
import math

import jax
import jax.numpy as jnp
from jax import lax
from jax.experimental import pallas as pl
from jax.experimental.pallas import tpu as pltpu
from jax.sharding import PartitionSpec as P

HEADS = 16
HEAD_DIM = 48
AHEADS = 4
AHEAD_DIM = 32
QWIN = 32
KWIN = 128
RIM = (KWIN - QWIN) // 2
LANES = 128
SUB = 8
F32 = jnp.float32
BF16 = jnp.bfloat16
MIB = 1024 * 1024
LOG2E = math.log2(math.e)
NT = (((1,), (1,)), ((), ()))


def layer_norm(x):
    mean = jnp.mean(x, -1, keepdims=True)
    centre = x - mean
    var = jnp.mean(centre * centre, -1, keepdims=True)
    return centre * lax.rsqrt(var + 1e-05)


def dot(a, b):
    return jnp.dot(a, b, preferred_element_type=F32)


def dot_nt(a, b):
    return lax.dot_general(a, b, NT, preferred_element_type=F32)


def iota(shape, dim):
    return lax.broadcasted_iota(jnp.int32, shape, dim)


def cost(micros):
    return pl.CostEstimate(flops=micros * 20_000_000, bytes_accessed=1_000, transcendentals=0)


def inverse(total):
    guess = pl.reciprocal(total, approx=True)
    return guess * (2.0 - total * guess)


def skewed(items, stages):
    held = list(items)
    for t in range(len(held) + len(stages) - 1):
        for k in reversed(range(len(stages))):
            if 0 <= t - k < len(held):
                held[t - k] = stages[k](held[t - k])
    return held


def normalise_kernel(pair, normed):
    for k in range(0, pair.shape[0], 6):
        normed[k : k + 6] = layer_norm(pair[k : k + 6].astype(F32))


def normalise_pairs(pair_cond):
    rows, cols, chans = pair_cond.shape
    vmem = pl.BlockSpec(memory_space=pltpu.VMEM)
    return pl.pallas_call(
        normalise_kernel,
        out_shape=jax.ShapeDtypeStruct((cols, rows, chans), F32),
        in_specs=[vmem],
        out_specs=vmem,
        compiler_params=pltpu.CompilerParams(vmem_limit_bytes=8 * MIB),
        cost_estimate=cost(1),
        name="normalise_pairs",
    )(jnp.transpose(pair_cond, (1, 0, 2)))


def bias_kernel(feat, normed, mask, weight, out, inner, outer, whole):
    odd = lax.axis_index("row") % 2 == 1
    head, tail = feat[:, :RIM], feat[:, feat.shape[1] - RIM :]
    inner[...] = jnp.where(odd, head, tail)
    outer[...] = jnp.where(odd, tail, head)
    cols, rows, chans = normed.shape
    spread = (iota((HEADS, LANES), 1) // SUB == iota((HEADS, LANES), 0)).astype(BF16)
    wide = lax.dot_general(weight[...], spread, (((0,), (0,)), ((), ())), preferred_element_type=F32).astype(BF16)
    tall = cols * SUB
    key_of = iota((tall, cols), 0) // SUB == iota((tall, cols), 1)
    open_row = jnp.broadcast_to(mask[...].reshape(1, cols), (LANES, cols)).astype(BF16)
    open_key = dot_nt(key_of.astype(BF16), open_row) > 0.5
    picked = (iota((cols, tall), 1) // SUB == iota((cols, tall), 0)).astype(BF16)
    batch = 3
    row = iota((tall, LANES), 0)
    mine = iota((tall, LANES), 1) % SUB == row % SUB
    own = lax.axis_index("sample") * cols + row // SUB - lax.axis_index("row") * rows - row % SUB
    own = jnp.where(mine, own, -1)
    kept = mine & open_key
    base = jnp.where(mine & ~open_key, -30000.0, 0.0)

    def weigh(first):
        out = []
        for g in range(first, first + batch):
            raw = dot(normed[:, g * SUB : (g + 1) * SUB].reshape(tall, chans).astype(BF16), wide)
            out.append(jnp.where(kept | (own == g * SUB), raw, base).astype(BF16))
        return first, out

    def pick(item):
        first, out = item
        for i, raw in enumerate(out):
            whole[(first + i) * cols : (first + i + 1) * cols] = dot(picked, raw)

    skewed(range(0, rows // SUB, batch), [weigh, pick])
    out[...] = whole[...].astype(BF16)


def pair_bias(feat, pair_cond, token_mask, pair_weight):
    rows, cols, _ = pair_cond.shape
    edge = (feat.shape[0], RIM, feat.shape[2])
    vmem = pl.BlockSpec(memory_space=pltpu.VMEM)
    return pl.pallas_call(
        bias_kernel,
        out_shape=[
            jax.ShapeDtypeStruct((rows // SUB * cols, LANES), BF16),
            jax.ShapeDtypeStruct(edge, BF16),
            jax.ShapeDtypeStruct(edge, BF16),
        ],
        in_specs=[vmem] * 4,
        out_specs=[vmem] * 3,
        scratch_shapes=[pltpu.VMEM((rows // SUB * cols, LANES), F32)],
        compiler_params=pltpu.CompilerParams(vmem_limit_bytes=8 * MIB),
        cost_estimate=cost(3),
        name="pair_bias",
    )(feat, normalise_pairs(pair_cond), token_mask, pair_weight.T)


def after(value, *others):
    return lax.optimization_barrier((value, *others))[0]


def swap(held, axis, far):
    return lax.ppermute(held, axis, [(i, i ^ far) for i in range(lax.axis_size(axis))])


def bits_of(devices):
    return [devices >> i for i in range(1, devices.bit_length())]


def places_of(bits):
    places = [0]
    for bit in bits:
        places += [p ^ bit for p in places]
    return places


def windows_attend(starts, qs, ks, vs, mixed, shift, hide):
    rate = LOG2E / AHEAD_DIM**0.5
    tall = AHEADS * QWIN
    head_of = iota((QWIN, qs.shape[1]), 1) // AHEAD_DIM

    def score(batch):
        out = []
        for at in batch:
            q = qs[at - shift : at - shift + QWIN]
            q = jnp.concatenate([jnp.where(head_of == h, q, jnp.zeros_like(q)) for h in range(AHEADS)], axis=0)
            out.append(hide(at, dot_nt(q, ks[at : at + KWIN])))
        return batch, jnp.concatenate(out, axis=0)

    def soften(item):
        batch, s = item
        e = jnp.exp2((s - jnp.max(s, -1, keepdims=True)) * rate)
        return batch, e.astype(BF16), jnp.sum(e, -1, keepdims=True)

    def own_head(parts):
        acc = parts[:QWIN]
        for h in range(1, AHEADS):
            acc = jnp.where(head_of == h, parts[h * QWIN : (h + 1) * QWIN], acc)
        return acc

    def mix(item):
        batch, e, total = item
        for i, at in enumerate(batch):
            part = slice(i * tall, (i + 1) * tall)
            o = own_head(dot(e[part], vs[at : at + KWIN])) * inverse(own_head(total[part]))
            mixed[at - shift : at - shift + QWIN] = o.astype(BF16)

    skewed(starts, [score, soften, mix])


def halo_of(sample, inner, outer):
    odd = lax.axis_index("row") % 2 == 1
    return jnp.where(odd, inner[sample], outer[sample]), jnp.where(odd, outer[sample], inner[sample])


def hide_outside(atoms):
    rank = lax.axis_index("row")
    at_start = rank == 0
    at_end = rank == lax.axis_size("row") - 1
    keyat = iota((AHEADS * QWIN, KWIN), 1)

    def hide(at, s):
        if at < RIM:
            s = jnp.where(at_start & (keyat < RIM - at), -jnp.inf, s)
        if at + KWIN > RIM + atoms:
            s = jnp.where(at_end & (keyat >= RIM + atoms - at), -jnp.inf, s)
        return s

    return hide


def atom_kernel(sample, feat, *refs):
    *halo, wq, wk, wv, mixed, qs, ks, vs = refs
    atoms, chans = feat.shape[1:]
    wqkv = jnp.concatenate([wq[...], wk[...], wv[...]], axis=1)

    def normalise(at):
        if isinstance(at, int):
            part = feat[sample, at : at + LANES]
        else:
            at, part = at
        return at, layer_norm(part.astype(F32)).astype(BF16)

    def project_atoms(item):
        at, normed = item
        count = normed.shape[0]
        if count == RIM:
            kv = dot(normed, wqkv[:, chans:]).astype(BF16)
        else:
            qkv = dot(normed, wqkv).astype(BF16)
            qs[at : at + count] = qkv[:, :chans]
            kv = qkv[:, chans:]
        ks[RIM + at : RIM + at + count] = kv[:, :chans]
        vs[RIM + at : RIM + at + count] = kv[:, chans:]

    parts = list(range(0, atoms, LANES))
    if halo:
        before, behind = halo_of(sample, *halo)
        parts += [(-RIM, before), (atoms, behind)]
    skewed(parts, [normalise, project_atoms])
    starts = list(range(0, atoms, QWIN))
    if not halo:
        starts = [at for at in starts if RIM <= at <= atoms + RIM - KWIN]
    batch = 6
    batches = [starts[i : i + batch] for i in range(0, len(starts), batch)]
    windows_attend(batches, qs, ks, vs, mixed, 0, hide_outside(atoms))


def atom_attention(sample, feat, halo, wq, wk, wv):
    atoms, chans = feat.shape[1:]
    vmem = pl.BlockSpec(memory_space=pltpu.VMEM)
    return pl.pallas_call(
        functools.partial(atom_kernel, sample),
        out_shape=jax.ShapeDtypeStruct((atoms, chans), BF16),
        in_specs=[vmem] * (4 + len(halo)),
        out_specs=vmem,
        scratch_shapes=[
            pltpu.VMEM((atoms, chans), BF16),
            pltpu.VMEM((atoms + 2 * RIM, chans), BF16),
            pltpu.VMEM((atoms + 2 * RIM, chans), BF16),
        ],
        compiler_params=pltpu.CompilerParams(vmem_limit_bytes=16 * MIB),
        cost_estimate=cost(4),
        name="atom_attention",
    )(feat, *halo, wq, wk, wv)


def gather_kernel(sample, mixed, feat, token, wo, agg, gain, *refs):
    *outside, token_in, token_norm, qs, ks, vs, ends = refs
    atoms, chans = feat.shape[1:]
    rows = token_in.shape[0]
    local = token[...].reshape(1, atoms) - lax.axis_index("row") * rows
    step = 384
    sums = []
    edge = 2 * QWIN
    if outside:
        inner, outer, wq, wk, wv = outside
        before, behind = halo_of(sample, inner, outer)
        wqkv = jnp.concatenate([wq[...], wk[...], wv[...]], axis=1)
        near = edge + KWIN - QWIN - RIM
        both = [before, feat[sample, :near], feat[sample, atoms - near :], behind]
        qkv = dot(layer_norm(jnp.concatenate([p.astype(F32) for p in both], axis=0)).astype(BF16), wqkv).astype(BF16)
        qs[...] = qkv[:, :chans]
        ks[...] = qkv[:, chans : 2 * chans]
        vs[...] = qkv[:, 2 * chans :]
        apart = atoms - 2 * near
        starts = [0, QWIN, RIM + near, RIM + near + QWIN]
        hide = hide_outside(atoms)
        windows_attend([starts], qs, ks, vs, ends, -RIM, lambda at, s: hide(at if at < RIM else at + apart, s))

    def finish(c):
        part = mixed[c : c + step]
        if outside and c == 0:
            part = jnp.concatenate([ends[RIM : RIM + edge], part[edge:]], axis=0)
        if outside and c + step == atoms:
            at = ends.shape[0] - RIM - edge
            part = jnp.concatenate([part[: step - edge], ends[at : at + edge]], axis=0)
        return c, (feat[sample, c : c + step].astype(F32) + dot(part, wo[...])).astype(BF16)

    def hide_below(item):
        c, out = item
        return c, jnp.maximum(dot(out, agg[...]), 0.0).astype(BF16)

    def add(item):
        c, hidden = item
        onehot = (iota((rows, step), 0) == local[:, c : c + step]).astype(F32)
        part = dot(onehot.astype(BF16), hidden), jnp.sum(onehot, -1, keepdims=True)
        sums[:] = [a + b for a, b in zip(sums, part)] if sums else part

    chunks = list(range(0, atoms, step))
    skewed(chunks[1:-1] + [chunks[0], chunks[-1]], [finish, hide_below, add])
    tin = sums[0] / sums[1]
    token_in[...] = tin
    token_norm[...] = (layer_norm(tin) * gain[...].reshape(1, -1)).astype(BF16)


def gather_tokens(sample, mixed, feat, token, wo, agg, gain, outside, rows):
    width = agg.shape[1]
    chans = feat.shape[2]
    reach = 2 * (KWIN + QWIN)
    vmem = pl.BlockSpec(memory_space=pltpu.VMEM)
    return pl.pallas_call(
        functools.partial(gather_kernel, sample),
        out_shape=[jax.ShapeDtypeStruct((rows, width), F32), jax.ShapeDtypeStruct((rows, width), BF16)],
        in_specs=[vmem] * (6 + len(outside)),
        out_specs=[vmem, vmem],
        scratch_shapes=[pltpu.VMEM((reach, chans), BF16)] * 4,
        compiler_params=pltpu.CompilerParams(vmem_limit_bytes=16 * MIB),
        cost_estimate=cost(1),
        name="gather_tokens",
    )(mixed, feat, token, wo, agg, gain, *outside)


def head_groups(width):
    groups = []
    for base in range(0, width, 8 * HEAD_DIM):
        first = base // HEAD_DIM
        groups.append((base, range(first, first + 5)))
        groups.append((base + LANES, range(first + 5, first + 8)))
    return groups


def stack(blocks):
    return jnp.concatenate([blocks[j].astype(F32) for j in range(blocks.shape[0])], axis=0).astype(BF16)


def tiles_of(h):
    return range(h * HEAD_DIM // LANES * LANES, (h + 1) * HEAD_DIM, LANES)


def channels(rows, at, h):
    lane = iota((rows, LANES), 1)
    low = h * HEAD_DIM - at
    return (lane >= low) & (lane < low + HEAD_DIM)


def head_scores(q, kt, base, heads):
    rows = q.shape[0]
    blank = jnp.zeros((rows, LANES), F32)
    both = [(at, q[:, at : at + LANES].astype(F32)) for at in (base, base + LANES)]
    mine = [
        [jnp.where(channels(rows, at, h), part, 0.0) if at in tiles_of(h) else blank for at, part in both]
        for h in heads
    ]
    mine = jnp.concatenate([jnp.concatenate(pair, axis=1) for pair in mine], axis=0).astype(BF16)
    return dot(mine, kt[base : base + 2 * LANES]) * (LOG2E / HEAD_DIM**0.5)


def project_kernel(near, far, wq, wk, wv, wg, wo, scores, v, gate, q, kt):
    x = jnp.concatenate([stack(near), stack(far)], axis=0)
    rows = near.shape[1]
    q[...] = dot(near[0], wq[...]).astype(BF16)
    for c in range(0, x.shape[1], 2 * LANES):
        kt[c : c + 2 * LANES] = dot(x, wk[:, c : c + 2 * LANES]).T.astype(BF16)
    for base, heads in head_groups(x.shape[1]):
        scores[heads[0] * rows : (heads[-1] + 1) * rows] = head_scores(q, kt, base, heads)
    gate[...] = jax.nn.sigmoid(dot(near[0], wg[...]))
    v[...] = dot(x, wv[...]).astype(BF16)


def project(near, far, wq, wk, wv, wg, wo):
    half, rows, width = near.shape
    keys = 2 * half * rows
    vmem = pl.BlockSpec(memory_space=pltpu.VMEM)
    return pl.pallas_call(
        project_kernel,
        out_shape=[
            jax.ShapeDtypeStruct((HEADS * rows, keys), F32),
            jax.ShapeDtypeStruct((keys, width), BF16),
            jax.ShapeDtypeStruct((rows, width), F32),
        ],
        in_specs=[vmem] * 7,
        out_specs=[vmem] * 3,
        scratch_shapes=[pltpu.VMEM((rows, width), BF16), pltpu.VMEM((width, keys), BF16)],
        compiler_params=pltpu.CompilerParams(vmem_limit_bytes=24 * MIB),
        cost_estimate=cost(2),
        name="project",
    )(near, far, wq, wk, wv, wg, wo)


def turn_kernel(orders, row_bits, near, wq, wk, wv, wg, *refs):
    *halves, q, k, v, gate, out, tall, flat = refs
    x = stack(near)
    width = x.shape[1]

    def project_columns(c):
        lanes = slice(c, c + 2 * LANES)
        q[:, lanes] = dot(near[0], wq[:, lanes]).astype(BF16)
        k[:, lanes] = dot(x, wk[:, lanes]).astype(BF16)
        v[:, lanes] = dot(x, wv[:, lanes]).astype(BF16)
        gate[:, lanes] = jax.nn.sigmoid(dot(near[0], wg[:, lanes]))

    rows = out.shape[0] // HEADS
    me = lax.axis_index("sample")
    groups = 0
    for mine, other, bits in zip(halves[::2], halves[1::2], orders):
        half, count, _ = mine.shape
        cols = tall.shape[0] // (2 * half)
        places = places_of(bits)
        for j in range(2 * half):
            place = sum(jnp.where(me ^ j == p, i, 0) for i, p in enumerate(places))
            block = jnp.where(place < half, mine[place % half], other[place % half])
            low = groups * cols
            flat[j, low : low + count] = block.astype(F32)
            for g in range(count // cols):
                lanes = slice((groups + g) * LANES, (groups + g + 1) * LANES)
                tall[j * cols : (j + 1) * cols, lanes] = flat[j, low + g * cols : low + (g + 1) * cols]
        groups += count // cols
    starts = [pl.multiple_of((lax.axis_index("row") ^ p) * rows, SUB) for p in places_of(row_bits)]
    for g in range(rows // SUB):
        if g * 2 * LANES < width:
            project_columns(g * 2 * LANES)
        lanes = slice(g * LANES, (g + 1) * LANES)
        turned = jnp.concatenate([tall[pl.ds(start, rows), lanes] for start in starts], axis=0).T
        for h in range(HEADS):
            out[h * rows + g * SUB : h * rows + (g + 1) * SUB] = turned[h * SUB : (h + 1) * SUB] * LOG2E


def turn_bias(orders, row_bits, halves, near, wq, wk, wv, wg):
    blocks, rows, width = near.shape
    devices = 2 * halves[0].shape[0]
    wide = rows * HEADS
    count = sum(part.shape[1] for part in halves[::2])
    keys = devices * count * LANES // wide
    vmem = pl.BlockSpec(memory_space=pltpu.VMEM)
    return pl.pallas_call(
        functools.partial(turn_kernel, orders, row_bits),
        out_shape=[
            jax.ShapeDtypeStruct((rows, width), BF16),
            jax.ShapeDtypeStruct((blocks * rows, width), BF16),
            jax.ShapeDtypeStruct((blocks * rows, width), BF16),
            jax.ShapeDtypeStruct((rows, width), F32),
            jax.ShapeDtypeStruct((wide, keys), F32),
        ],
        in_specs=[vmem] * (5 + len(halves)),
        out_specs=[vmem] * 5,
        scratch_shapes=[pltpu.VMEM((keys, wide), F32), pltpu.VMEM((devices, count, LANES), F32)],
        compiler_params=pltpu.CompilerParams(vmem_limit_bytes=32 * MIB),
        cost_estimate=cost(1),
        name="turn_bias",
    )(near, wq, wk, wv, wg, *halves)


def attend_kernel(samples, bias, *refs):
    parts, refs = [refs[4 * s : 4 * s + 4] for s in range(samples - 1)], refs[4 * (samples - 1) :]
    q, k_near, v_near, gate_last, token_last, far, wk, wv, wo, out, kt, v = refs
    parts.append((None, v, gate_last, token_last))
    rows, width = token_last.shape
    x = stack(far)
    groups = head_groups(width)
    work = [(s, base, heads) for s in range(samples) for base, heads in groups]
    chunks = list(range(0, width, 2 * LANES))
    for i, c in enumerate(chunks):
        work.insert(min(2 * i + 1, (samples - 1) * len(groups) + i), c)

    def fill(c):
        lanes = slice(c, c + 2 * LANES)
        k = jnp.concatenate([k_near[:, lanes].astype(F32), dot(x, wk[:, lanes])], axis=0)
        kt[lanes] = k.T.astype(BF16)
        v[: v_near.shape[0], lanes] = v_near[:, lanes]
        v[v_near.shape[0] :, lanes] = dot(x, wv[:, lanes]).astype(BF16)

    def score(item):
        if isinstance(item, int):
            return fill(item)
        s, base, heads = item
        part = slice(heads[0] * rows, (heads[-1] + 1) * rows)
        return item, (parts[s][0][part] if s < samples - 1 else head_scores(q, kt, base, heads)) + bias[part]

    def soften(item):
        if item is None:
            return None
        place, sc = item
        e = jnp.exp2(sc - jnp.max(sc, -1, keepdims=True))
        return place, e.astype(BF16), inverse(jnp.sum(e, -1, keepdims=True))

    mixes = {}

    def mix(item):
        if item is None:
            return
        (s, base, heads), e, share = item
        o = dot(e, parts[s][1][:, base : base + 2 * LANES])
        for i, h in enumerate(heads):
            part = slice(i * rows, (i + 1) * rows)
            for at in tiles_of(h):
                one = o[part, at - base : at - base + LANES] * share[part]
                mixes[s, at] = jnp.where(channels(rows, at, h), one, mixes.get((s, at), 0.0))
        if h == HEADS - 1:
            close(s)

    def close(s):
        gate, token_in = parts[s][2:]
        gated = jnp.concatenate([mixes[s, at] for at in range(0, width, LANES)], axis=1) * gate[...]
        out[s] = (token_in[...] + dot(gated.astype(BF16), wo[...])).astype(BF16)

    skewed(work, [score, soften, mix])


def attend(bias, parts, far, wk, wv, wo):
    rows, width = parts[-1][4].shape
    keys = 2 * parts[-1][1].shape[0]
    vmem = pl.BlockSpec(memory_space=pltpu.VMEM)
    operands = [bias, *(ref for part in parts for ref in part), far, wk, wv, wo]
    return pl.pallas_call(
        functools.partial(attend_kernel, len(parts)),
        out_shape=jax.ShapeDtypeStruct((len(parts), rows, width), BF16),
        in_specs=[vmem] * len(operands),
        out_specs=vmem,
        scratch_shapes=[pltpu.VMEM((width, keys), BF16), pltpu.VMEM((keys, width), BF16)],
        compiler_params=pltpu.CompilerParams(vmem_limit_bytes=32 * MIB),
        cost_estimate=cost(3),
        name="attend",
    )(*operands)


def shards(
    atom_feat,
    atom_token,
    pair_cond,
    token_mask,
    atom_wq,
    atom_wk,
    atom_wv,
    atom_wo,
    agg_weight,
    pair_weight,
    token_gain,
    query_weight,
    key_weight,
    value_weight,
    gate_weight,
    out_weight,
):
    samples = atom_feat.shape[0]
    rows = pair_cond.shape[0]
    ranks = lax.axis_size("row")
    bias, inner, outer = pair_bias(atom_feat, pair_cond, token_mask, pair_weight)
    inner = swap(inner, "row", 1)
    odd_pairs = [(i, (i + 1) % ranks) for i in range(1, ranks, 2)]
    outer = lax.ppermute(outer, "row", odd_pairs + [(j, i) for i, j in odd_pairs])

    def widen(held, axis, bit, *others):
        return jnp.concatenate([held, after(swap(held, axis, bit), *others)], axis=0)

    bits, row_bits = bits_of(lax.axis_size("sample")), bits_of(ranks)
    orders = [bits, bits[:1] + bits[-1:] + bits[1:-1]]
    split = rows // SUB // 2 * pair_cond.shape[1]
    got = swap(bias, "sample", bits[0])
    norms, inputs = [], []
    for s in range(samples):
        halo = (inner, outer)
        mixed = atom_attention(s, atom_feat, halo if s else (), atom_wq, atom_wk, atom_wv)
        outside = () if s else (*halo, atom_wq, atom_wk, atom_wv)
        token_in, token_norm = gather_tokens(
            s, mixed, atom_feat, atom_token, atom_wo, agg_weight, token_gain, outside, rows
        )
        inputs.append(token_in)
        norms.append(token_norm[None])
        if s == 0:
            bias, got, _ = lax.optimization_barrier((bias, got, token_norm))
            held = [jnp.stack([bias[part], got[part]]) for part in (slice(0, split), slice(split, None))]
            inner = after(inner, held, token_norm)
    last = swap(norms[-1], "row", row_bits[0])
    for i in range(1, len(bits) - 1):
        held = [widen(h, "sample", order[i], token_norm) for h, order in zip(held, orders)]
    halves = []
    for h, order in zip(held, orders):
        halves += [h, swap(h, "sample", order[-1])]
    parts = []
    weights = (query_weight, key_weight, value_weight, gate_weight, out_weight)
    for s in range(samples):
        near = norms[s]
        others = (mixed, parts, halves) if s == samples - 1 else (mixed, parts)
        for bit in row_bits[:-1]:
            if s == samples - 1 and bit == row_bits[0]:
                near = jnp.concatenate([near, after(last, *others)], axis=0)
            else:
                near = widen(near, "row", bit, *others)
        far = swap(near, "row", row_bits[-1])
        near = after(near, held)
        if s < samples - 1:
            parts.append((*project(near, far, *weights), inputs[s]))
        else:
            *part, bias = turn_bias(orders, row_bits, halves, near, *weights[:4])
            parts.append((*part, inputs[s]))
    return attend(bias, parts, far, key_weight, value_weight, out_weight)


def solution(mesh):
    placed = (
        P("sample", "row", None),
        P("row"),
        P("row", "sample", None),
        P("sample"),
    ) + (P(),) * 12
    return jax.shard_map(
        shards, mesh=mesh, in_specs=placed, out_specs=P("sample", "row", None), check_vma=False
    )
```

```python
import functools
import math

import jax
import jax.numpy as jnp
from jax import lax
from jax.experimental import pallas as pl
from jax.experimental.pallas import tpu as pltpu
from jax.sharding import PartitionSpec as P

HEADS = 16
HEAD_DIM = 48
AHEADS = 4
AHEAD_DIM = 32
QWIN = 32
KWIN = 128
RIM = (KWIN - QWIN) // 2
LANES = 128
SUB = 8
F32 = jnp.float32
BF16 = jnp.bfloat16
MIB = 1024 * 1024
LOG2E = math.log2(math.e)
NT = (((1,), (1,)), ((), ()))


def layer_norm(x):
    mean = jnp.mean(x, -1, keepdims=True)
    centre = x - mean
    var = jnp.mean(centre * centre, -1, keepdims=True)
    return centre * lax.rsqrt(var + 1e-05)


def dot(a, b):
    return jnp.dot(a, b, preferred_element_type=F32)


def dot_nt(a, b):
    return lax.dot_general(a, b, NT, preferred_element_type=F32)


def iota(shape, dim):
    return lax.broadcasted_iota(jnp.int32, shape, dim)


def cost(micros):
    return pl.CostEstimate(flops=micros * 20_000_000, bytes_accessed=1_000, transcendentals=0)


def inverse(total):
    guess = pl.reciprocal(total, approx=True)
    return guess * (2.0 - total * guess)


def skewed(items, stages):
    held = list(items)
    for t in range(len(held) + len(stages) - 1):
        for k in reversed(range(len(stages))):
            if 0 <= t - k < len(held):
                held[t - k] = stages[k](held[t - k])
    return held


def normalise_kernel(pair, normed):
    for k in range(0, pair.shape[0], 6):
        normed[k : k + 6] = layer_norm(pair[k : k + 6].astype(F32))


def normalise_pairs(pair_cond):
    rows, cols, chans = pair_cond.shape
    vmem = pl.BlockSpec(memory_space=pltpu.VMEM)
    return pl.pallas_call(
        normalise_kernel,
        out_shape=jax.ShapeDtypeStruct((cols, rows, chans), F32),
        in_specs=[vmem],
        out_specs=vmem,
        compiler_params=pltpu.CompilerParams(vmem_limit_bytes=8 * MIB),
        cost_estimate=cost(1),
        name="normalise_pairs",
    )(jnp.transpose(pair_cond, (1, 0, 2)))


def bias_kernel(feat, normed, mask, weight, out, inner, outer, whole):
    odd = lax.axis_index("row") % 2 == 1
    head, tail = feat[:, :RIM], feat[:, feat.shape[1] - RIM :]
    inner[...] = jnp.where(odd, head, tail)
    outer[...] = jnp.where(odd, tail, head)
    cols, rows, chans = normed.shape
    spread = (iota((HEADS, LANES), 1) // SUB == iota((HEADS, LANES), 0)).astype(BF16)
    wide = lax.dot_general(weight[...], spread, (((0,), (0,)), ((), ())), preferred_element_type=F32).astype(BF16)
    tall = cols * SUB
    key_of = iota((tall, cols), 0) // SUB == iota((tall, cols), 1)
    open_row = jnp.broadcast_to(mask[...].reshape(1, cols), (LANES, cols)).astype(BF16)
    open_key = dot_nt(key_of.astype(BF16), open_row) > 0.5
    picked = (iota((cols, tall), 1) // SUB == iota((cols, tall), 0)).astype(BF16)
    batch = 3
    row = iota((tall, LANES), 0)
    mine = iota((tall, LANES), 1) % SUB == row % SUB
    own = lax.axis_index("sample") * cols + row // SUB - lax.axis_index("row") * rows - row % SUB
    own = jnp.where(mine, own, -1)
    kept = mine & open_key
    base = jnp.where(mine & ~open_key, -30000.0, 0.0)

    def weigh(first):
        out = []
        for g in range(first, first + batch):
            raw = dot(normed[:, g * SUB : (g + 1) * SUB].reshape(tall, chans).astype(BF16), wide)
            out.append(jnp.where(kept | (own == g * SUB), raw, base).astype(BF16))
        return first, out

    def pick(item):
        first, out = item
        for i, raw in enumerate(out):
            whole[(first + i) * cols : (first + i + 1) * cols] = dot(picked, raw)

    skewed(range(0, rows // SUB, batch), [weigh, pick])
    out[...] = whole[...].astype(BF16)


def pair_bias(feat, pair_cond, token_mask, pair_weight):
    rows, cols, _ = pair_cond.shape
    edge = (feat.shape[0], RIM, feat.shape[2])
    vmem = pl.BlockSpec(memory_space=pltpu.VMEM)
    return pl.pallas_call(
        bias_kernel,
        out_shape=[
            jax.ShapeDtypeStruct((rows // SUB * cols, LANES), BF16),
            jax.ShapeDtypeStruct(edge, BF16),
            jax.ShapeDtypeStruct(edge, BF16),
        ],
        in_specs=[vmem] * 4,
        out_specs=[vmem] * 3,
        scratch_shapes=[pltpu.VMEM((rows // SUB * cols, LANES), F32)],
        compiler_params=pltpu.CompilerParams(vmem_limit_bytes=8 * MIB),
        cost_estimate=cost(3),
        name="pair_bias",
    )(feat, normalise_pairs(pair_cond), token_mask, pair_weight.T)


def after(value, *others):
    return lax.optimization_barrier((value, *others))[0]


def swap(held, axis, far):
    return lax.ppermute(held, axis, [(i, i ^ far) for i in range(lax.axis_size(axis))])


def bits_of(devices):
    return [devices >> i for i in range(1, devices.bit_length())]


def places_of(bits):
    places = [0]
    for bit in bits:
        places += [p ^ bit for p in places]
    return places


def windows_attend(starts, qs, ks, vs, mixed, shift, hide):
    rate = LOG2E / AHEAD_DIM**0.5
    tall = AHEADS * QWIN
    head_of = iota((QWIN, qs.shape[1]), 1) // AHEAD_DIM

    def score(batch):
        out = []
        for at in batch:
            q = qs[at - shift : at - shift + QWIN]
            q = jnp.concatenate([jnp.where(head_of == h, q, jnp.zeros_like(q)) for h in range(AHEADS)], axis=0)
            out.append(hide(at, dot_nt(q, ks[at : at + KWIN])))
        return batch, jnp.concatenate(out, axis=0)

    def soften(item):
        batch, s = item
        e = jnp.exp2((s - jnp.max(s, -1, keepdims=True)) * rate)
        return batch, e.astype(BF16), jnp.sum(e, -1, keepdims=True)

    def own_head(parts):
        acc = parts[:QWIN]
        for h in range(1, AHEADS):
            acc = jnp.where(head_of == h, parts[h * QWIN : (h + 1) * QWIN], acc)
        return acc

    def mix(item):
        batch, e, total = item
        for i, at in enumerate(batch):
            part = slice(i * tall, (i + 1) * tall)
            o = own_head(dot(e[part], vs[at : at + KWIN])) * inverse(own_head(total[part]))
            mixed[at - shift : at - shift + QWIN] = o.astype(BF16)

    skewed(starts, [score, soften, mix])


def halo_of(sample, inner, outer):
    odd = lax.axis_index("row") % 2 == 1
    return jnp.where(odd, inner[sample], outer[sample]), jnp.where(odd, outer[sample], inner[sample])


def hide_outside(atoms):
    rank = lax.axis_index("row")
    at_start = rank == 0
    at_end = rank == lax.axis_size("row") - 1
    keyat = iota((AHEADS * QWIN, KWIN), 1)

    def hide(at, s):
        if at < RIM:
            s = jnp.where(at_start & (keyat < RIM - at), -jnp.inf, s)
        if at + KWIN > RIM + atoms:
            s = jnp.where(at_end & (keyat >= RIM + atoms - at), -jnp.inf, s)
        return s

    return hide


def atom_kernel(sample, feat, *refs):
    *halo, wq, wk, wv, mixed, qs, ks, vs = refs
    atoms, chans = feat.shape[1:]
    wqkv = jnp.concatenate([wq[...], wk[...], wv[...]], axis=1)

    def normalise(at):
        if isinstance(at, int):
            part = feat[sample, at : at + LANES]
        else:
            at, part = at
        return at, layer_norm(part.astype(F32)).astype(BF16)

    def project_atoms(item):
        at, normed = item
        count = normed.shape[0]
        if count == RIM:
            kv = dot(normed, wqkv[:, chans:]).astype(BF16)
        else:
            qkv = dot(normed, wqkv).astype(BF16)
            qs[at : at + count] = qkv[:, :chans]
            kv = qkv[:, chans:]
        ks[RIM + at : RIM + at + count] = kv[:, :chans]
        vs[RIM + at : RIM + at + count] = kv[:, chans:]

    parts = list(range(0, atoms, LANES))
    if halo:
        before, behind = halo_of(sample, *halo)
        parts += [(-RIM, before), (atoms, behind)]
    skewed(parts, [normalise, project_atoms])
    starts = list(range(0, atoms, QWIN))
    if not halo:
        starts = [at for at in starts if RIM <= at <= atoms + RIM - KWIN]
    batch = 6
    batches = [starts[i : i + batch] for i in range(0, len(starts), batch)]
    windows_attend(batches, qs, ks, vs, mixed, 0, hide_outside(atoms))


def atom_attention(sample, feat, halo, wq, wk, wv):
    atoms, chans = feat.shape[1:]
    vmem = pl.BlockSpec(memory_space=pltpu.VMEM)
    return pl.pallas_call(
        functools.partial(atom_kernel, sample),
        out_shape=jax.ShapeDtypeStruct((atoms, chans), BF16),
        in_specs=[vmem] * (4 + len(halo)),
        out_specs=vmem,
        scratch_shapes=[
            pltpu.VMEM((atoms, chans), BF16),
            pltpu.VMEM((atoms + 2 * RIM, chans), BF16),
            pltpu.VMEM((atoms + 2 * RIM, chans), BF16),
        ],
        compiler_params=pltpu.CompilerParams(vmem_limit_bytes=16 * MIB),
        cost_estimate=cost(4),
        name="atom_attention",
    )(feat, *halo, wq, wk, wv)


def gather_kernel(sample, mixed, feat, token, wo, agg, gain, *refs):
    *outside, token_in, token_norm, qs, ks, vs, ends = refs
    atoms, chans = feat.shape[1:]
    rows = token_in.shape[0]
    local = token[...].reshape(1, atoms) - lax.axis_index("row") * rows
    step = 384
    sums = []
    edge = 2 * QWIN
    if outside:
        inner, outer, wq, wk, wv = outside
        before, behind = halo_of(sample, inner, outer)
        wqkv = jnp.concatenate([wq[...], wk[...], wv[...]], axis=1)
        near = edge + KWIN - QWIN - RIM
        both = [before, feat[sample, :near], feat[sample, atoms - near :], behind]
        qkv = dot(layer_norm(jnp.concatenate([p.astype(F32) for p in both], axis=0)).astype(BF16), wqkv).astype(BF16)
        qs[...] = qkv[:, :chans]
        ks[...] = qkv[:, chans : 2 * chans]
        vs[...] = qkv[:, 2 * chans :]
        apart = atoms - 2 * near
        starts = [0, QWIN, RIM + near, RIM + near + QWIN]
        hide = hide_outside(atoms)
        windows_attend([starts], qs, ks, vs, ends, -RIM, lambda at, s: hide(at if at < RIM else at + apart, s))

    def finish(c):
        part = mixed[c : c + step]
        if outside and c == 0:
            part = jnp.concatenate([ends[RIM : RIM + edge], part[edge:]], axis=0)
        if outside and c + step == atoms:
            at = ends.shape[0] - RIM - edge
            part = jnp.concatenate([part[: step - edge], ends[at : at + edge]], axis=0)
        return c, (feat[sample, c : c + step].astype(F32) + dot(part, wo[...])).astype(BF16)

    def hide_below(item):
        c, out = item
        return c, jnp.maximum(dot(out, agg[...]), 0.0).astype(BF16)

    def add(item):
        c, hidden = item
        onehot = (iota((rows, step), 0) == local[:, c : c + step]).astype(F32)
        part = dot(onehot.astype(BF16), hidden), jnp.sum(onehot, -1, keepdims=True)
        sums[:] = [a + b for a, b in zip(sums, part)] if sums else part

    chunks = list(range(0, atoms, step))
    skewed(chunks[1:-1] + [chunks[0], chunks[-1]], [finish, hide_below, add])
    tin = sums[0] / sums[1]
    token_in[...] = tin
    token_norm[...] = (layer_norm(tin) * gain[...].reshape(1, -1)).astype(BF16)


def gather_tokens(sample, mixed, feat, token, wo, agg, gain, outside, rows):
    width = agg.shape[1]
    chans = feat.shape[2]
    reach = 2 * (KWIN + QWIN)
    vmem = pl.BlockSpec(memory_space=pltpu.VMEM)
    return pl.pallas_call(
        functools.partial(gather_kernel, sample),
        out_shape=[jax.ShapeDtypeStruct((rows, width), F32), jax.ShapeDtypeStruct((rows, width), BF16)],
        in_specs=[vmem] * (6 + len(outside)),
        out_specs=[vmem, vmem],
        scratch_shapes=[pltpu.VMEM((reach, chans), BF16)] * 4,
        compiler_params=pltpu.CompilerParams(vmem_limit_bytes=16 * MIB),
        cost_estimate=cost(1),
        name="gather_tokens",
    )(mixed, feat, token, wo, agg, gain, *outside)


def head_groups(width):
    groups = []
    for base in range(0, width, 8 * HEAD_DIM):
        first = base // HEAD_DIM
        groups.append((base, range(first, first + 5)))
        groups.append((base + LANES, range(first + 5, first + 8)))
    return groups


def stack(blocks):
    return jnp.concatenate([blocks[j].astype(F32) for j in range(blocks.shape[0])], axis=0).astype(BF16)


def tiles_of(h):
    return range(h * HEAD_DIM // LANES * LANES, (h + 1) * HEAD_DIM, LANES)


def channels(rows, at, h):
    lane = iota((rows, LANES), 1)
    low = h * HEAD_DIM - at
    return (lane >= low) & (lane < low + HEAD_DIM)


def head_scores(q, kt, base, heads):
    rows = q.shape[0]
    blank = jnp.zeros((rows, LANES), F32)
    both = [(at, q[:, at : at + LANES].astype(F32)) for at in (base, base + LANES)]
    mine = [
        [jnp.where(channels(rows, at, h), part, 0.0) if at in tiles_of(h) else blank for at, part in both]
        for h in heads
    ]
    mine = jnp.concatenate([jnp.concatenate(pair, axis=1) for pair in mine], axis=0).astype(BF16)
    return dot(mine, kt[base : base + 2 * LANES]) * (LOG2E / HEAD_DIM**0.5)


def project_kernel(near, far, wq, wk, wv, wg, wo, scores, v, gate, q, kt):
    x = jnp.concatenate([stack(near), stack(far)], axis=0)
    rows = near.shape[1]
    q[...] = dot(near[0], wq[...]).astype(BF16)
    for c in range(0, x.shape[1], 2 * LANES):
        kt[c : c + 2 * LANES] = dot(x, wk[:, c : c + 2 * LANES]).T.astype(BF16)
    for base, heads in head_groups(x.shape[1]):
        scores[heads[0] * rows : (heads[-1] + 1) * rows] = head_scores(q, kt, base, heads)
    gate[...] = jax.nn.sigmoid(dot(near[0], wg[...]))
    v[...] = dot(x, wv[...]).astype(BF16)


def project(near, far, wq, wk, wv, wg, wo):
    half, rows, width = near.shape
    keys = 2 * half * rows
    vmem = pl.BlockSpec(memory_space=pltpu.VMEM)
    return pl.pallas_call(
        project_kernel,
        out_shape=[
            jax.ShapeDtypeStruct((HEADS * rows, keys), F32),
            jax.ShapeDtypeStruct((keys, width), BF16),
            jax.ShapeDtypeStruct((rows, width), F32),
        ],
        in_specs=[vmem] * 7,
        out_specs=[vmem] * 3,
        scratch_shapes=[pltpu.VMEM((rows, width), BF16), pltpu.VMEM((width, keys), BF16)],
        compiler_params=pltpu.CompilerParams(vmem_limit_bytes=24 * MIB),
        cost_estimate=cost(2),
        name="project",
    )(near, far, wq, wk, wv, wg, wo)


def turn_kernel(orders, row_bits, near, wq, wk, wv, wg, *refs):
    *halves, q, k, v, gate, out, tall, flat = refs
    x = stack(near)
    width = x.shape[1]

    def project_columns(c):
        lanes = slice(c, c + 2 * LANES)
        q[:, lanes] = dot(near[0], wq[:, lanes]).astype(BF16)
        k[:, lanes] = dot(x, wk[:, lanes]).astype(BF16)
        v[:, lanes] = dot(x, wv[:, lanes]).astype(BF16)
        gate[:, lanes] = jax.nn.sigmoid(dot(near[0], wg[:, lanes]))

    rows = out.shape[0] // HEADS
    me = lax.axis_index("sample")
    groups = 0
    for mine, other, bits in zip(halves[::2], halves[1::2], orders):
        half, count, _ = mine.shape
        cols = tall.shape[0] // (2 * half)
        places = places_of(bits)
        for j in range(2 * half):
            place = sum(jnp.where(me ^ j == p, i, 0) for i, p in enumerate(places))
            block = jnp.where(place < half, mine[place % half], other[place % half])
            low = groups * cols
            flat[j, low : low + count] = block.astype(F32)
            for g in range(count // cols):
                lanes = slice((groups + g) * LANES, (groups + g + 1) * LANES)
                tall[j * cols : (j + 1) * cols, lanes] = flat[j, low + g * cols : low + (g + 1) * cols]
        groups += count // cols
    starts = [pl.multiple_of((lax.axis_index("row") ^ p) * rows, SUB) for p in places_of(row_bits)]
    for g in range(rows // SUB):
        if g * 2 * LANES < width:
            project_columns(g * 2 * LANES)
        lanes = slice(g * LANES, (g + 1) * LANES)
        turned = jnp.concatenate([tall[pl.ds(start, rows), lanes] for start in starts], axis=0).T
        for h in range(HEADS):
            out[h * rows + g * SUB : h * rows + (g + 1) * SUB] = turned[h * SUB : (h + 1) * SUB] * LOG2E


def turn_bias(orders, row_bits, halves, near, wq, wk, wv, wg):
    blocks, rows, width = near.shape
    devices = 2 * halves[0].shape[0]
    wide = rows * HEADS
    count = sum(part.shape[1] for part in halves[::2])
    keys = devices * count * LANES // wide
    vmem = pl.BlockSpec(memory_space=pltpu.VMEM)
    return pl.pallas_call(
        functools.partial(turn_kernel, orders, row_bits),
        out_shape=[
            jax.ShapeDtypeStruct((rows, width), BF16),
            jax.ShapeDtypeStruct((blocks * rows, width), BF16),
            jax.ShapeDtypeStruct((blocks * rows, width), BF16),
            jax.ShapeDtypeStruct((rows, width), F32),
            jax.ShapeDtypeStruct((wide, keys), F32),
        ],
        in_specs=[vmem] * (5 + len(halves)),
        out_specs=[vmem] * 5,
        scratch_shapes=[pltpu.VMEM((keys, wide), F32), pltpu.VMEM((devices, count, LANES), F32)],
        compiler_params=pltpu.CompilerParams(vmem_limit_bytes=32 * MIB),
        cost_estimate=cost(1),
        name="turn_bias",
    )(near, wq, wk, wv, wg, *halves)


def attend_kernel(samples, bias, *refs):
    parts, refs = [refs[4 * s : 4 * s + 4] for s in range(samples - 1)], refs[4 * (samples - 1) :]
    q, k_near, v_near, gate_last, token_last, far, wk, wv, wo, out, kt, v = refs
    parts.append((None, v, gate_last, token_last))
    rows, width = token_last.shape
    x = stack(far)
    groups = head_groups(width)
    work = [
        (s, base, heads[i : i + 3]) for s in range(samples) for base, heads in groups for i in range(0, len(heads), 3)
    ]
    chunks = list(range(0, width, 2 * LANES))
    for i, c in enumerate(chunks):
        work.insert(min(2 * i + 1, (samples - 1) * len(work) // samples), c)

    def fill(c):
        lanes = slice(c, c + 2 * LANES)
        k = jnp.concatenate([k_near[:, lanes].astype(F32), dot(x, wk[:, lanes])], axis=0)
        kt[lanes] = k.T.astype(BF16)
        v[: v_near.shape[0], lanes] = v_near[:, lanes]
        v[v_near.shape[0] :, lanes] = dot(x, wv[:, lanes]).astype(BF16)

    def score(item):
        if isinstance(item, int):
            return fill(item)
        s, base, heads = item
        part = slice(heads[0] * rows, (heads[-1] + 1) * rows)
        return item, (parts[s][0][part] if s < samples - 1 else head_scores(q, kt, base, heads)) + bias[part]

    def soften(item):
        if item is None:
            return None
        place, sc = item
        e = jnp.exp2(sc - jnp.max(sc, -1, keepdims=True))
        return place, e.astype(BF16), inverse(jnp.sum(e, -1, keepdims=True))

    mixes = {}

    def mix(item):
        if item is None:
            return
        (s, base, heads), e, share = item
        o = dot(e, parts[s][1][:, base : base + 2 * LANES])
        for i, h in enumerate(heads):
            part = slice(i * rows, (i + 1) * rows)
            for at in tiles_of(h):
                one = o[part, at - base : at - base + LANES] * share[part]
                mixes[s, at] = jnp.where(channels(rows, at, h), one, mixes.get((s, at), 0.0))
        if (h + 1) * HEAD_DIM % LANES == 0:
            close(s, h)

    sums = {}

    def close(s, h):
        _, _, gate, token_in = parts[s]
        lanes = slice((h - 7) * HEAD_DIM, (h + 1) * HEAD_DIM)
        mixed = jnp.concatenate([mixes[s, at] for at in range(lanes.start, lanes.stop, LANES)], axis=1)
        part = dot((mixed * gate[:, lanes]).astype(BF16), wo[lanes])
        sums[s] = sums[s] + part if s in sums else part
        if h == HEADS - 1:
            out[s] = (token_in[...] + sums[s]).astype(BF16)

    skewed(work, [score, soften, mix])


def attend(bias, parts, far, wk, wv, wo):
    rows, width = parts[-1][4].shape
    keys = 2 * parts[-1][1].shape[0]
    vmem = pl.BlockSpec(memory_space=pltpu.VMEM)
    operands = [bias, *(ref for part in parts for ref in part), far, wk, wv, wo]
    return pl.pallas_call(
        functools.partial(attend_kernel, len(parts)),
        out_shape=jax.ShapeDtypeStruct((len(parts), rows, width), BF16),
        in_specs=[vmem] * len(operands),
        out_specs=vmem,
        scratch_shapes=[pltpu.VMEM((width, keys), BF16), pltpu.VMEM((keys, width), BF16)],
        compiler_params=pltpu.CompilerParams(vmem_limit_bytes=32 * MIB),
        cost_estimate=cost(3),
        name="attend",
    )(*operands)


def shards(
    atom_feat,
    atom_token,
    pair_cond,
    token_mask,
    atom_wq,
    atom_wk,
    atom_wv,
    atom_wo,
    agg_weight,
    pair_weight,
    token_gain,
    query_weight,
    key_weight,
    value_weight,
    gate_weight,
    out_weight,
):
    samples = atom_feat.shape[0]
    rows = pair_cond.shape[0]
    ranks = lax.axis_size("row")
    bias, inner, outer = pair_bias(atom_feat, pair_cond, token_mask, pair_weight)
    inner = swap(inner, "row", 1)
    odd_pairs = [(i, (i + 1) % ranks) for i in range(1, ranks, 2)]
    outer = lax.ppermute(outer, "row", odd_pairs + [(j, i) for i, j in odd_pairs])

    def widen(held, axis, bit, *others):
        return jnp.concatenate([held, after(swap(held, axis, bit), *others)], axis=0)

    bits, row_bits = bits_of(lax.axis_size("sample")), bits_of(ranks)
    orders = [bits, bits[:1] + bits[-1:] + bits[1:-1]]
    split = rows // SUB // 2 * pair_cond.shape[1]
    got = swap(bias, "sample", bits[0])
    norms, inputs = [], []
    for s in range(samples):
        halo = (inner, outer)
        mixed = atom_attention(s, atom_feat, halo if s else (), atom_wq, atom_wk, atom_wv)
        outside = () if s else (*halo, atom_wq, atom_wk, atom_wv)
        token_in, token_norm = gather_tokens(
            s, mixed, atom_feat, atom_token, atom_wo, agg_weight, token_gain, outside, rows
        )
        inputs.append(token_in)
        norms.append(token_norm[None])
        if s == 0:
            bias, got, _ = lax.optimization_barrier((bias, got, token_norm))
            held = [jnp.stack([bias[part], got[part]]) for part in (slice(0, split), slice(split, None))]
            inner = after(inner, held, token_norm)
    last = swap(norms[-1], "row", row_bits[0])
    for i in range(1, len(bits) - 1):
        held = [widen(h, "sample", order[i], token_norm) for h, order in zip(held, orders)]
    halves = []
    for h, order in zip(held, orders):
        halves += [h, swap(h, "sample", order[-1])]
    parts = []
    weights = (query_weight, key_weight, value_weight, gate_weight, out_weight)
    for s in range(samples):
        near = norms[s]
        others = (mixed, parts, halves) if s == samples - 1 else (mixed, parts)
        for bit in row_bits[:-1]:
            if s == samples - 1 and bit == row_bits[0]:
                near = jnp.concatenate([near, after(last, *others)], axis=0)
            else:
                near = widen(near, "row", bit, *others)
        far = swap(near, "row", row_bits[-1])
        near = after(near, held)
        if s < samples - 1:
            parts.append((*project(near, far, *weights), inputs[s]))
        else:
            *part, bias = turn_bias(orders, row_bits, halves, near, *weights[:4])
            parts.append((*part, inputs[s]))
    return attend(bias, parts, far, key_weight, value_weight, out_weight)


def solution(mesh):
    placed = (
        P("sample", "row", None),
        P("row"),
        P("row", "sample", None),
        P("sample"),
    ) + (P(),) * 12
    return jax.shard_map(
        shards, mesh=mesh, in_specs=placed, out_specs=P("sample", "row", None), check_vma=False
    )
```

```python
import functools
import math

import jax
import jax.numpy as jnp
from jax import lax
from jax.experimental import pallas as pl
from jax.experimental.pallas import tpu as pltpu
from jax.sharding import PartitionSpec as P

HEADS = 16
HEAD_DIM = 48
AHEADS = 4
AHEAD_DIM = 32
QWIN = 32
KWIN = 128
RIM = (KWIN - QWIN) // 2
LANES = 128
SUB = 8
F32 = jnp.float32
BF16 = jnp.bfloat16
MIB = 1024 * 1024
LOG2E = math.log2(math.e)
NT = (((1,), (1,)), ((), ()))


def layer_norm(x):
    mean = jnp.mean(x, -1, keepdims=True)
    centre = x - mean
    var = jnp.mean(centre * centre, -1, keepdims=True)
    return centre * lax.rsqrt(var + 1e-05)


def dot(a, b):
    return jnp.dot(a, b, preferred_element_type=F32)


def dot_nt(a, b):
    return lax.dot_general(a, b, NT, preferred_element_type=F32)


def iota(shape, dim):
    return lax.broadcasted_iota(jnp.int32, shape, dim)


def cost(micros):
    return pl.CostEstimate(flops=micros * 20_000_000, bytes_accessed=1_000, transcendentals=0)


def inverse(total):
    guess = pl.reciprocal(total, approx=True)
    return guess * (2.0 - total * guess)


def skewed(items, stages):
    held = list(items)
    for t in range(len(held) + len(stages) - 1):
        for k in reversed(range(len(stages))):
            if 0 <= t - k < len(held):
                held[t - k] = stages[k](held[t - k])
    return held


def normalise_kernel(pair, normed):
    for k in range(0, pair.shape[0], 6):
        normed[k : k + 6] = layer_norm(pair[k : k + 6].astype(F32))


def normalise_pairs(pair_cond):
    rows, cols, chans = pair_cond.shape
    vmem = pl.BlockSpec(memory_space=pltpu.VMEM)
    return pl.pallas_call(
        normalise_kernel,
        out_shape=jax.ShapeDtypeStruct((cols, rows, chans), F32),
        in_specs=[vmem],
        out_specs=vmem,
        compiler_params=pltpu.CompilerParams(vmem_limit_bytes=8 * MIB),
        cost_estimate=cost(1),
        name="normalise_pairs",
    )(jnp.transpose(pair_cond, (1, 0, 2)))


def bias_kernel(feat, normed, mask, weight, out, inner, outer, whole):
    odd = lax.axis_index("row") % 2 == 1
    head, tail = feat[:, :RIM], feat[:, feat.shape[1] - RIM :]
    inner[...] = jnp.where(odd, head, tail)
    outer[...] = jnp.where(odd, tail, head)
    cols, rows, chans = normed.shape
    spread = (iota((HEADS, LANES), 1) // SUB == iota((HEADS, LANES), 0)).astype(BF16)
    wide = lax.dot_general(weight[...], spread, (((0,), (0,)), ((), ())), preferred_element_type=F32).astype(BF16)
    tall = cols * SUB
    key_of = iota((tall, cols), 0) // SUB == iota((tall, cols), 1)
    open_row = jnp.broadcast_to(mask[...].reshape(1, cols), (LANES, cols)).astype(BF16)
    open_key = dot_nt(key_of.astype(BF16), open_row) > 0.5
    picked = (iota((cols, tall), 1) // SUB == iota((cols, tall), 0)).astype(BF16)
    batch = 3
    row = iota((tall, LANES), 0)
    mine = iota((tall, LANES), 1) % SUB == row % SUB
    own = lax.axis_index("sample") * cols + row // SUB - lax.axis_index("row") * rows - row % SUB
    own = jnp.where(mine, own, -1)
    kept = mine & open_key
    base = jnp.where(mine & ~open_key, -30000.0, 0.0)

    def weigh(first):
        out = []
        for g in range(first, first + batch):
            raw = dot(normed[:, g * SUB : (g + 1) * SUB].reshape(tall, chans).astype(BF16), wide)
            out.append(jnp.where(kept | (own == g * SUB), raw, base).astype(BF16))
        return first, out

    def pick(item):
        first, out = item
        for i, raw in enumerate(out):
            whole[(first + i) * cols : (first + i + 1) * cols] = dot(picked, raw)

    skewed(range(0, rows // SUB, batch), [weigh, pick])
    out[...] = whole[...].astype(BF16)


def pair_bias(feat, pair_cond, token_mask, pair_weight):
    rows, cols, _ = pair_cond.shape
    edge = (feat.shape[0], RIM, feat.shape[2])
    vmem = pl.BlockSpec(memory_space=pltpu.VMEM)
    return pl.pallas_call(
        bias_kernel,
        out_shape=[
            jax.ShapeDtypeStruct((rows // SUB * cols, LANES), BF16),
            jax.ShapeDtypeStruct(edge, BF16),
            jax.ShapeDtypeStruct(edge, BF16),
        ],
        in_specs=[vmem] * 4,
        out_specs=[vmem] * 3,
        scratch_shapes=[pltpu.VMEM((rows // SUB * cols, LANES), F32)],
        compiler_params=pltpu.CompilerParams(vmem_limit_bytes=8 * MIB),
        cost_estimate=cost(3),
        name="pair_bias",
    )(feat, normalise_pairs(pair_cond), token_mask, pair_weight.T)


def after(value, *others):
    return lax.optimization_barrier((value, *others))[0]


def swap(held, axis, far):
    return lax.ppermute(held, axis, [(i, i ^ far) for i in range(lax.axis_size(axis))])


def bits_of(devices):
    return [devices >> i for i in range(1, devices.bit_length())]


def places_of(bits):
    places = [0]
    for bit in bits:
        places += [p ^ bit for p in places]
    return places


def windows_attend(starts, qs, ks, vs, mixed, shift, hide):
    rate = LOG2E / AHEAD_DIM**0.5
    tall = AHEADS * QWIN
    head_of = iota((QWIN, qs.shape[1]), 1) // AHEAD_DIM

    def score(batch):
        out = []
        for at in batch:
            q = qs[at - shift : at - shift + QWIN]
            q = jnp.concatenate([jnp.where(head_of == h, q, jnp.zeros_like(q)) for h in range(AHEADS)], axis=0)
            out.append(hide(at, dot_nt(q, ks[at : at + KWIN])))
        return batch, jnp.concatenate(out, axis=0)

    def soften(item):
        batch, s = item
        e = jnp.exp2((s - jnp.max(s, -1, keepdims=True)) * rate)
        return batch, e.astype(BF16), jnp.sum(e, -1, keepdims=True)

    def own_head(parts):
        acc = parts[:QWIN]
        for h in range(1, AHEADS):
            acc = jnp.where(head_of == h, parts[h * QWIN : (h + 1) * QWIN], acc)
        return acc

    def mix(item):
        batch, e, total = item
        for i, at in enumerate(batch):
            part = slice(i * tall, (i + 1) * tall)
            o = own_head(dot(e[part], vs[at : at + KWIN])) * inverse(own_head(total[part]))
            mixed[at - shift : at - shift + QWIN] = o.astype(BF16)

    skewed(starts, [score, soften, mix])


def halo_of(sample, inner, outer):
    odd = lax.axis_index("row") % 2 == 1
    return jnp.where(odd, inner[sample], outer[sample]), jnp.where(odd, outer[sample], inner[sample])


def hide_outside(atoms):
    rank = lax.axis_index("row")
    at_start = rank == 0
    at_end = rank == lax.axis_size("row") - 1
    keyat = iota((AHEADS * QWIN, KWIN), 1)

    def hide(at, s):
        if at < RIM:
            s = jnp.where(at_start & (keyat < RIM - at), -jnp.inf, s)
        if at + KWIN > RIM + atoms:
            s = jnp.where(at_end & (keyat >= RIM + atoms - at), -jnp.inf, s)
        return s

    return hide


def atom_kernel(sample, feat, *refs):
    *halo, wq, wk, wv, mixed, qs, ks, vs = refs
    atoms, chans = feat.shape[1:]
    wqkv = jnp.concatenate([wq[...], wk[...], wv[...]], axis=1)

    def normalise(at):
        if isinstance(at, int):
            part = feat[sample, at : at + LANES]
        else:
            at, part = at
        return at, layer_norm(part.astype(F32)).astype(BF16)

    def project_atoms(item):
        at, normed = item
        count = normed.shape[0]
        if count == RIM:
            kv = dot(normed, wqkv[:, chans:]).astype(BF16)
        else:
            qkv = dot(normed, wqkv).astype(BF16)
            qs[at : at + count] = qkv[:, :chans]
            kv = qkv[:, chans:]
        ks[RIM + at : RIM + at + count] = kv[:, :chans]
        vs[RIM + at : RIM + at + count] = kv[:, chans:]

    parts = list(range(0, atoms, LANES))
    if halo:
        before, behind = halo_of(sample, *halo)
        parts += [(-RIM, before), (atoms, behind)]
    skewed(parts, [normalise, project_atoms])
    starts = list(range(0, atoms, QWIN))
    if not halo:
        starts = [at for at in starts if RIM <= at <= atoms + RIM - KWIN]
    batch = 6
    batches = [starts[i : i + batch] for i in range(0, len(starts), batch)]
    windows_attend(batches, qs, ks, vs, mixed, 0, hide_outside(atoms))


def atom_attention(sample, feat, halo, wq, wk, wv):
    atoms, chans = feat.shape[1:]
    vmem = pl.BlockSpec(memory_space=pltpu.VMEM)
    return pl.pallas_call(
        functools.partial(atom_kernel, sample),
        out_shape=jax.ShapeDtypeStruct((atoms, chans), BF16),
        in_specs=[vmem] * (4 + len(halo)),
        out_specs=vmem,
        scratch_shapes=[
            pltpu.VMEM((atoms, chans), BF16),
            pltpu.VMEM((atoms + 2 * RIM, chans), BF16),
            pltpu.VMEM((atoms + 2 * RIM, chans), BF16),
        ],
        compiler_params=pltpu.CompilerParams(vmem_limit_bytes=16 * MIB),
        cost_estimate=cost(4),
        name="atom_attention",
    )(feat, *halo, wq, wk, wv)


def gather_kernel(sample, mixed, feat, token, wo, agg, gain, *refs):
    *outside, token_in, token_norm, qs, ks, vs, ends = refs
    atoms, chans = feat.shape[1:]
    rows = token_in.shape[0]
    local = token[...].reshape(1, atoms) - lax.axis_index("row") * rows
    step = 384
    sums = []
    edge = 2 * QWIN
    if outside:
        inner, outer, wq, wk, wv = outside
        before, behind = halo_of(sample, inner, outer)
        wqkv = jnp.concatenate([wq[...], wk[...], wv[...]], axis=1)
        near = edge + KWIN - QWIN - RIM
        both = [before, feat[sample, :near], feat[sample, atoms - near :], behind]
        qkv = dot(layer_norm(jnp.concatenate([p.astype(F32) for p in both], axis=0)).astype(BF16), wqkv).astype(BF16)
        qs[...] = qkv[:, :chans]
        ks[...] = qkv[:, chans : 2 * chans]
        vs[...] = qkv[:, 2 * chans :]
        apart = atoms - 2 * near
        starts = [0, QWIN, RIM + near, RIM + near + QWIN]
        hide = hide_outside(atoms)
        windows_attend([starts], qs, ks, vs, ends, -RIM, lambda at, s: hide(at if at < RIM else at + apart, s))

    def finish(c):
        part = mixed[c : c + step]
        if outside and c == 0:
            part = jnp.concatenate([ends[RIM : RIM + edge], part[edge:]], axis=0)
        if outside and c + step == atoms:
            at = ends.shape[0] - RIM - edge
            part = jnp.concatenate([part[: step - edge], ends[at : at + edge]], axis=0)
        return c, (feat[sample, c : c + step].astype(F32) + dot(part, wo[...])).astype(BF16)

    def hide_below(item):
        c, out = item
        return c, jnp.maximum(dot(out, agg[...]), 0.0).astype(BF16)

    def add(item):
        c, hidden = item
        onehot = (iota((rows, step), 0) == local[:, c : c + step]).astype(F32)
        part = dot(onehot.astype(BF16), hidden), jnp.sum(onehot, -1, keepdims=True)
        sums[:] = [a + b for a, b in zip(sums, part)] if sums else part

    chunks = list(range(0, atoms, step))
    skewed(chunks[1:-1] + [chunks[0], chunks[-1]], [finish, hide_below, add])
    tin = sums[0] / sums[1]
    token_in[...] = tin
    token_norm[...] = (layer_norm(tin) * gain[...].reshape(1, -1)).astype(BF16)


def gather_tokens(sample, mixed, feat, token, wo, agg, gain, outside, rows):
    width = agg.shape[1]
    chans = feat.shape[2]
    reach = 2 * (KWIN + QWIN)
    vmem = pl.BlockSpec(memory_space=pltpu.VMEM)
    return pl.pallas_call(
        functools.partial(gather_kernel, sample),
        out_shape=[jax.ShapeDtypeStruct((rows, width), F32), jax.ShapeDtypeStruct((rows, width), BF16)],
        in_specs=[vmem] * (6 + len(outside)),
        out_specs=[vmem, vmem],
        scratch_shapes=[pltpu.VMEM((reach, chans), BF16)] * 4,
        compiler_params=pltpu.CompilerParams(vmem_limit_bytes=16 * MIB),
        cost_estimate=cost(1),
        name="gather_tokens",
    )(mixed, feat, token, wo, agg, gain, *outside)


def head_groups(width):
    groups = []
    for base in range(0, width, 8 * HEAD_DIM):
        first = base // HEAD_DIM
        groups.append((base, range(first, first + 5)))
        groups.append((base + LANES, range(first + 5, first + 8)))
    return groups


def stack(blocks):
    return jnp.concatenate([blocks[j].astype(F32) for j in range(blocks.shape[0])], axis=0).astype(BF16)


def tiles_of(h):
    return range(h * HEAD_DIM // LANES * LANES, (h + 1) * HEAD_DIM, LANES)


def channels(rows, at, h):
    lane = iota((rows, LANES), 1)
    low = h * HEAD_DIM - at
    return (lane >= low) & (lane < low + HEAD_DIM)


def head_scores(q, kt, base, heads):
    rows = q.shape[0]
    blank = jnp.zeros((rows, LANES), F32)
    both = [(at, q[:, at : at + LANES].astype(F32)) for at in (base, base + LANES)]
    mine = [
        [jnp.where(channels(rows, at, h), part, 0.0) if at in tiles_of(h) else blank for at, part in both]
        for h in heads
    ]
    mine = jnp.concatenate([jnp.concatenate(pair, axis=1) for pair in mine], axis=0).astype(BF16)
    return dot(mine, kt[base : base + 2 * LANES]) * (LOG2E / HEAD_DIM**0.5)


def project_kernel(near, far, wq, wk, wv, wg, wo, scores, v, gate, q, kt):
    x = jnp.concatenate([stack(near), stack(far)], axis=0)
    rows = near.shape[1]
    q[...] = dot(near[0], wq[...]).astype(BF16)
    for c in range(0, x.shape[1], 2 * LANES):
        kt[c : c + 2 * LANES] = dot(x, wk[:, c : c + 2 * LANES]).T.astype(BF16)
    for base, heads in head_groups(x.shape[1]):
        scores[heads[0] * rows : (heads[-1] + 1) * rows] = head_scores(q, kt, base, heads)
    gate[...] = jax.nn.sigmoid(dot(near[0], wg[...]))
    v[...] = dot(x, wv[...]).astype(BF16)


def project(near, far, wq, wk, wv, wg, wo):
    half, rows, width = near.shape
    keys = 2 * half * rows
    vmem = pl.BlockSpec(memory_space=pltpu.VMEM)
    return pl.pallas_call(
        project_kernel,
        out_shape=[
            jax.ShapeDtypeStruct((HEADS * rows, keys), F32),
            jax.ShapeDtypeStruct((keys, width), BF16),
            jax.ShapeDtypeStruct((rows, width), F32),
        ],
        in_specs=[vmem] * 7,
        out_specs=[vmem] * 3,
        scratch_shapes=[pltpu.VMEM((rows, width), BF16), pltpu.VMEM((width, keys), BF16)],
        compiler_params=pltpu.CompilerParams(vmem_limit_bytes=24 * MIB),
        cost_estimate=cost(2),
        name="project",
    )(near, far, wq, wk, wv, wg, wo)


def turn_kernel(orders, row_bits, near, wq, wk, wv, wg, *refs):
    *halves, q, k, v, gate, out, tall, flat = refs
    x = stack(near)
    width = x.shape[1]

    def project_columns(c):
        lanes = slice(c, c + 2 * LANES)
        q[:, lanes] = dot(near[0], wq[:, lanes]).astype(BF16)
        k[:, lanes] = dot(x, wk[:, lanes]).astype(BF16)
        v[:, lanes] = dot(x, wv[:, lanes]).astype(BF16)
        gate[:, lanes] = jax.nn.sigmoid(dot(near[0], wg[:, lanes]))

    rows = out.shape[0] // HEADS
    me = lax.axis_index("sample")
    groups = 0
    for mine, other, bits in zip(halves[::2], halves[1::2], orders):
        half, count, _ = mine.shape
        cols = tall.shape[0] // (2 * half)
        places = places_of(bits)
        for j in range(2 * half):
            place = sum(jnp.where(me ^ j == p, i, 0) for i, p in enumerate(places))
            block = jnp.where(place < half, mine[place % half], other[place % half])
            low = groups * cols
            flat[j, low : low + count] = block.astype(F32)
            for g in range(count // cols):
                lanes = slice((groups + g) * LANES, (groups + g + 1) * LANES)
                tall[j * cols : (j + 1) * cols, lanes] = flat[j, low + g * cols : low + (g + 1) * cols]
        groups += count // cols
    starts = [pl.multiple_of((lax.axis_index("row") ^ p) * rows, SUB) for p in places_of(row_bits)]
    for g in range(rows // SUB):
        if g * 2 * LANES < width:
            project_columns(g * 2 * LANES)
        lanes = slice(g * LANES, (g + 1) * LANES)
        turned = jnp.concatenate([tall[pl.ds(start, rows), lanes] for start in starts], axis=0).T
        for h in range(HEADS):
            out[h * rows + g * SUB : h * rows + (g + 1) * SUB] = turned[h * SUB : (h + 1) * SUB] * LOG2E


def turn_bias(orders, row_bits, halves, near, wq, wk, wv, wg):
    blocks, rows, width = near.shape
    devices = 2 * halves[0].shape[0]
    wide = rows * HEADS
    count = sum(part.shape[1] for part in halves[::2])
    keys = devices * count * LANES // wide
    vmem = pl.BlockSpec(memory_space=pltpu.VMEM)
    return pl.pallas_call(
        functools.partial(turn_kernel, orders, row_bits),
        out_shape=[
            jax.ShapeDtypeStruct((rows, width), BF16),
            jax.ShapeDtypeStruct((blocks * rows, width), BF16),
            jax.ShapeDtypeStruct((blocks * rows, width), BF16),
            jax.ShapeDtypeStruct((rows, width), F32),
            jax.ShapeDtypeStruct((wide, keys), F32),
        ],
        in_specs=[vmem] * (5 + len(halves)),
        out_specs=[vmem] * 5,
        scratch_shapes=[pltpu.VMEM((keys, wide), F32), pltpu.VMEM((devices, count, LANES), F32)],
        compiler_params=pltpu.CompilerParams(vmem_limit_bytes=32 * MIB),
        cost_estimate=cost(1),
        name="turn_bias",
    )(near, wq, wk, wv, wg, *halves)


def attend_kernel(samples, bias, *refs):
    parts, refs = [refs[4 * s : 4 * s + 4] for s in range(samples - 1)], refs[4 * (samples - 1) :]
    q, k_near, v_near, gate_last, token_last, far, wk, wv, wo, out, kt, v = refs
    parts.append((None, v, gate_last, token_last))
    rows, width = token_last.shape
    x = stack(far)
    groups = head_groups(width)
    work = [(s, groups[i : i + 2]) for s in range(samples) for i in range(0, len(groups), 2)]
    chunks = list(range(0, width, 2 * LANES))
    for i, c in enumerate(chunks):
        work.insert(min(2 * i + 1, (samples - 1) * len(groups) // 2 + i), c)

    def fill(c):
        lanes = slice(c, c + 2 * LANES)
        k = jnp.concatenate([k_near[:, lanes].astype(F32), dot(x, wk[:, lanes])], axis=0)
        kt[lanes] = k.T.astype(BF16)
        v[: v_near.shape[0], lanes] = v_near[:, lanes]
        v[v_near.shape[0] :, lanes] = dot(x, wv[:, lanes]).astype(BF16)

    def score(item):
        if isinstance(item, int):
            return fill(item)
        s, pair = item
        part = slice(pair[0][1][0] * rows, (pair[-1][1][-1] + 1) * rows)
        if s < samples - 1:
            return item, parts[s][0][part] + bias[part]
        return item, jnp.concatenate([head_scores(q, kt, *group) for group in pair], axis=0) + bias[part]

    def soften(item):
        if item is None:
            return None
        place, sc = item
        e = jnp.exp2(sc - jnp.max(sc, -1, keepdims=True))
        return place, e.astype(BF16), inverse(jnp.sum(e, -1, keepdims=True))

    mixes = {}

    def mix(item):
        if item is None:
            return
        (s, pair), e, share = item
        first = pair[0][1][0]
        for base, heads in pair:
            low = (heads[0] - first) * rows
            o = dot(e[low : low + len(heads) * rows], parts[s][1][:, base : base + 2 * LANES])
            for i, h in enumerate(heads):
                part = slice(i * rows, (i + 1) * rows)
                own = share[low + i * rows : low + (i + 1) * rows]
                for at in tiles_of(h):
                    one = o[part, at - base : at - base + LANES] * own
                    mixes[s, at] = jnp.where(channels(rows, at, h), one, mixes.get((s, at), 0.0))
        if h == HEADS - 1:
            close(s)

    def close(s):
        gate, token_in = parts[s][2:]
        gated = jnp.concatenate([mixes[s, at] for at in range(0, width, LANES)], axis=1) * gate[...]
        out[s] = (token_in[...] + dot(gated.astype(BF16), wo[...])).astype(BF16)

    skewed(work, [score, soften, mix])


def attend(bias, parts, far, wk, wv, wo):
    rows, width = parts[-1][4].shape
    keys = 2 * parts[-1][1].shape[0]
    vmem = pl.BlockSpec(memory_space=pltpu.VMEM)
    operands = [bias, *(ref for part in parts for ref in part), far, wk, wv, wo]
    return pl.pallas_call(
        functools.partial(attend_kernel, len(parts)),
        out_shape=jax.ShapeDtypeStruct((len(parts), rows, width), BF16),
        in_specs=[vmem] * len(operands),
        out_specs=vmem,
        scratch_shapes=[pltpu.VMEM((width, keys), BF16), pltpu.VMEM((keys, width), BF16)],
        compiler_params=pltpu.CompilerParams(vmem_limit_bytes=32 * MIB),
        cost_estimate=cost(3),
        name="attend",
    )(*operands)


def shards(
    atom_feat,
    atom_token,
    pair_cond,
    token_mask,
    atom_wq,
    atom_wk,
    atom_wv,
    atom_wo,
    agg_weight,
    pair_weight,
    token_gain,
    query_weight,
    key_weight,
    value_weight,
    gate_weight,
    out_weight,
):
    samples = atom_feat.shape[0]
    rows = pair_cond.shape[0]
    ranks = lax.axis_size("row")
    bias, inner, outer = pair_bias(atom_feat, pair_cond, token_mask, pair_weight)
    inner = swap(inner, "row", 1)
    odd_pairs = [(i, (i + 1) % ranks) for i in range(1, ranks, 2)]
    outer = lax.ppermute(outer, "row", odd_pairs + [(j, i) for i, j in odd_pairs])

    def widen(held, axis, bit, *others):
        return jnp.concatenate([held, after(swap(held, axis, bit), *others)], axis=0)

    bits, row_bits = bits_of(lax.axis_size("sample")), bits_of(ranks)
    orders = [bits, bits[:1] + bits[-1:] + bits[1:-1]]
    split = rows // SUB // 2 * pair_cond.shape[1]
    got = swap(bias, "sample", bits[0])
    norms, inputs = [], []
    for s in range(samples):
        halo = (inner, outer)
        mixed = atom_attention(s, atom_feat, halo if s else (), atom_wq, atom_wk, atom_wv)
        outside = () if s else (*halo, atom_wq, atom_wk, atom_wv)
        token_in, token_norm = gather_tokens(
            s, mixed, atom_feat, atom_token, atom_wo, agg_weight, token_gain, outside, rows
        )
        inputs.append(token_in)
        norms.append(token_norm[None])
        if s == 0:
            bias, got, _ = lax.optimization_barrier((bias, got, token_norm))
            held = [jnp.stack([bias[part], got[part]]) for part in (slice(0, split), slice(split, None))]
            inner = after(inner, held, token_norm)
    last = swap(norms[-1], "row", row_bits[0])
    for i in range(1, len(bits) - 1):
        held = [widen(h, "sample", order[i], token_norm) for h, order in zip(held, orders)]
    halves = []
    for h, order in zip(held, orders):
        halves += [h, swap(h, "sample", order[-1])]
    parts = []
    weights = (query_weight, key_weight, value_weight, gate_weight, out_weight)
    for s in range(samples):
        near = norms[s]
        others = (mixed, parts, halves) if s == samples - 1 else (mixed, parts)
        for bit in row_bits[:-1]:
            if s == samples - 1 and bit == row_bits[0]:
                near = jnp.concatenate([near, after(last, *others)], axis=0)
            else:
                near = widen(near, "row", bit, *others)
        far = swap(near, "row", row_bits[-1])
        near = after(near, held)
        if s < samples - 1:
            parts.append((*project(near, far, *weights), inputs[s]))
        else:
            *part, bias = turn_bias(orders, row_bits, halves, near, *weights[:4])
            parts.append((*part, inputs[s]))
    return attend(bias, parts, far, key_weight, value_weight, out_weight)


def solution(mesh):
    placed = (
        P("sample", "row", None),
        P("row"),
        P("row", "sample", None),
        P("sample"),
    ) + (P(),) * 12
    return jax.shard_map(
        shards, mesh=mesh, in_specs=placed, out_specs=P("sample", "row", None), check_vma=False
    )
```

```python
import functools
import math

import jax
import jax.numpy as jnp
from jax import lax
from jax.experimental import pallas as pl
from jax.experimental.pallas import tpu as pltpu
from jax.sharding import PartitionSpec as P

HEADS = 16
HEAD_DIM = 48
AHEADS = 4
AHEAD_DIM = 32
QWIN = 32
KWIN = 128
RIM = (KWIN - QWIN) // 2
LANES = 128
SUB = 8
F32 = jnp.float32
BF16 = jnp.bfloat16
MIB = 1024 * 1024
LOG2E = math.log2(math.e)
NT = (((1,), (1,)), ((), ()))


def layer_norm(x):
    mean = jnp.mean(x, -1, keepdims=True)
    centre = x - mean
    var = jnp.mean(centre * centre, -1, keepdims=True)
    return centre * lax.rsqrt(var + 1e-05)


def dot(a, b):
    return jnp.dot(a, b, preferred_element_type=F32)


def dot_nt(a, b):
    return lax.dot_general(a, b, NT, preferred_element_type=F32)


def iota(shape, dim):
    return lax.broadcasted_iota(jnp.int32, shape, dim)


def cost(micros):
    return pl.CostEstimate(flops=micros * 20_000_000, bytes_accessed=1_000, transcendentals=0)


def inverse(total):
    guess = pl.reciprocal(total, approx=True)
    return guess * (2.0 - total * guess)


def skewed(items, stages):
    held = list(items)
    for t in range(len(held) + len(stages) - 1):
        for k in reversed(range(len(stages))):
            if 0 <= t - k < len(held):
                held[t - k] = stages[k](held[t - k])
    return held


def normalise_kernel(pair, normed):
    cols, rows, chans = pair.shape
    evenly = jnp.full((chans, chans), 1.0 / chans, BF16)
    step = 6

    def centre(k):
        x = pair[k : k + step].astype(F32).reshape(step * rows, chans)
        return k, x - dot(x.astype(BF16), evenly)

    def scale(item):
        k, x = item
        x = x * lax.rsqrt(jnp.mean(x * x, -1, keepdims=True) + 1e-05)
        normed[k : k + step] = x.reshape(step, rows, chans)

    skewed(range(0, cols, step), [centre, scale])


def normalise_pairs(pair_cond):
    rows, cols, chans = pair_cond.shape
    vmem = pl.BlockSpec(memory_space=pltpu.VMEM)
    return pl.pallas_call(
        normalise_kernel,
        out_shape=jax.ShapeDtypeStruct((cols, rows, chans), F32),
        in_specs=[vmem],
        out_specs=vmem,
        compiler_params=pltpu.CompilerParams(vmem_limit_bytes=8 * MIB),
        cost_estimate=cost(1),
        name="normalise_pairs",
    )(jnp.transpose(pair_cond, (1, 0, 2)))


def bias_kernel(feat, normed, mask, weight, out, inner, outer, whole):
    odd = lax.axis_index("row") % 2 == 1
    head, tail = feat[:, :RIM], feat[:, feat.shape[1] - RIM :]
    inner[...] = jnp.where(odd, head, tail)
    outer[...] = jnp.where(odd, tail, head)
    cols, rows, chans = normed.shape
    spread = (iota((HEADS, LANES), 1) // SUB == iota((HEADS, LANES), 0)).astype(BF16)
    wide = lax.dot_general(weight[...], spread, (((0,), (0,)), ((), ())), preferred_element_type=F32).astype(BF16)
    tall = cols * SUB
    key_of = iota((tall, cols), 0) // SUB == iota((tall, cols), 1)
    open_row = jnp.broadcast_to(mask[...].reshape(1, cols), (LANES, cols)).astype(BF16)
    open_key = dot_nt(key_of.astype(BF16), open_row) > 0.5
    picked = (iota((cols, tall), 1) // SUB == iota((cols, tall), 0)).astype(BF16)
    batch = 3
    row = iota((tall, LANES), 0)
    mine = iota((tall, LANES), 1) % SUB == row % SUB
    own = lax.axis_index("sample") * cols + row // SUB - lax.axis_index("row") * rows - row % SUB
    own = jnp.where(mine, own, -1)
    kept = mine & open_key
    base = jnp.where(mine & ~open_key, -30000.0, 0.0)

    def weigh(first):
        out = []
        for g in range(first, first + batch):
            raw = dot(normed[:, g * SUB : (g + 1) * SUB].reshape(tall, chans).astype(BF16), wide)
            out.append(jnp.where(kept | (own == g * SUB), raw, base).astype(BF16))
        return first, out

    def pick(item):
        first, out = item
        for i, raw in enumerate(out):
            whole[(first + i) * cols : (first + i + 1) * cols] = dot(picked, raw)

    skewed(range(0, rows // SUB, batch), [weigh, pick])
    out[...] = whole[...].astype(BF16)


def pair_bias(feat, pair_cond, token_mask, pair_weight):
    rows, cols, _ = pair_cond.shape
    edge = (feat.shape[0], RIM, feat.shape[2])
    vmem = pl.BlockSpec(memory_space=pltpu.VMEM)
    return pl.pallas_call(
        bias_kernel,
        out_shape=[
            jax.ShapeDtypeStruct((rows // SUB * cols, LANES), BF16),
            jax.ShapeDtypeStruct(edge, BF16),
            jax.ShapeDtypeStruct(edge, BF16),
        ],
        in_specs=[vmem] * 4,
        out_specs=[vmem] * 3,
        scratch_shapes=[pltpu.VMEM((rows // SUB * cols, LANES), F32)],
        compiler_params=pltpu.CompilerParams(vmem_limit_bytes=8 * MIB),
        cost_estimate=cost(3),
        name="pair_bias",
    )(feat, normalise_pairs(pair_cond), token_mask, pair_weight.T)


def after(value, *others):
    return lax.optimization_barrier((value, *others))[0]


def swap(held, axis, far):
    return lax.ppermute(held, axis, [(i, i ^ far) for i in range(lax.axis_size(axis))])


def bits_of(devices):
    return [devices >> i for i in range(1, devices.bit_length())]


def places_of(bits):
    places = [0]
    for bit in bits:
        places += [p ^ bit for p in places]
    return places


def windows_attend(starts, qs, ks, vs, mixed, shift, hide):
    rate = LOG2E / AHEAD_DIM**0.5
    tall = AHEADS * QWIN
    head_of = iota((QWIN, qs.shape[1]), 1) // AHEAD_DIM

    def score(batch):
        out = []
        for at in batch:
            q = qs[at - shift : at - shift + QWIN]
            q = jnp.concatenate([jnp.where(head_of == h, q, jnp.zeros_like(q)) for h in range(AHEADS)], axis=0)
            out.append(hide(at, dot_nt(q, ks[at : at + KWIN])))
        return batch, jnp.concatenate(out, axis=0)

    def soften(item):
        batch, s = item
        e = jnp.exp2((s - jnp.max(s, -1, keepdims=True)) * rate)
        return batch, e.astype(BF16), jnp.sum(e, -1, keepdims=True)

    def own_head(parts):
        acc = parts[:QWIN]
        for h in range(1, AHEADS):
            acc = jnp.where(head_of == h, parts[h * QWIN : (h + 1) * QWIN], acc)
        return acc

    def mix(item):
        batch, e, total = item
        for i, at in enumerate(batch):
            part = slice(i * tall, (i + 1) * tall)
            o = own_head(dot(e[part], vs[at : at + KWIN])) * inverse(own_head(total[part]))
            mixed[at - shift : at - shift + QWIN] = o.astype(BF16)

    skewed(starts, [score, soften, mix])


def halo_of(sample, inner, outer):
    odd = lax.axis_index("row") % 2 == 1
    return jnp.where(odd, inner[sample], outer[sample]), jnp.where(odd, outer[sample], inner[sample])


def hide_outside(atoms):
    rank = lax.axis_index("row")
    at_start = rank == 0
    at_end = rank == lax.axis_size("row") - 1
    keyat = iota((AHEADS * QWIN, KWIN), 1)

    def hide(at, s):
        if at < RIM:
            s = jnp.where(at_start & (keyat < RIM - at), -jnp.inf, s)
        if at + KWIN > RIM + atoms:
            s = jnp.where(at_end & (keyat >= RIM + atoms - at), -jnp.inf, s)
        return s

    return hide


def atom_kernel(sample, feat, *refs):
    *halo, wq, wk, wv, mixed, qs, ks, vs = refs
    atoms, chans = feat.shape[1:]
    wqkv = jnp.concatenate([wq[...], wk[...], wv[...]], axis=1)

    def normalise(at):
        if isinstance(at, int):
            part = feat[sample, at : at + LANES]
        else:
            at, part = at
        return at, layer_norm(part.astype(F32)).astype(BF16)

    def project_atoms(item):
        at, normed = item
        count = normed.shape[0]
        if count == RIM:
            kv = dot(normed, wqkv[:, chans:]).astype(BF16)
        else:
            qkv = dot(normed, wqkv).astype(BF16)
            qs[at : at + count] = qkv[:, :chans]
            kv = qkv[:, chans:]
        ks[RIM + at : RIM + at + count] = kv[:, :chans]
        vs[RIM + at : RIM + at + count] = kv[:, chans:]

    parts = list(range(0, atoms, LANES))
    if halo:
        before, behind = halo_of(sample, *halo)
        parts += [(-RIM, before), (atoms, behind)]
    skewed(parts, [normalise, project_atoms])
    starts = list(range(0, atoms, QWIN))
    if not halo:
        starts = [at for at in starts if RIM <= at <= atoms + RIM - KWIN]
    batch = 6
    batches = [starts[i : i + batch] for i in range(0, len(starts), batch)]
    windows_attend(batches, qs, ks, vs, mixed, 0, hide_outside(atoms))


def atom_attention(sample, feat, halo, wq, wk, wv):
    atoms, chans = feat.shape[1:]
    vmem = pl.BlockSpec(memory_space=pltpu.VMEM)
    return pl.pallas_call(
        functools.partial(atom_kernel, sample),
        out_shape=jax.ShapeDtypeStruct((atoms, chans), BF16),
        in_specs=[vmem] * (4 + len(halo)),
        out_specs=vmem,
        scratch_shapes=[
            pltpu.VMEM((atoms, chans), BF16),
            pltpu.VMEM((atoms + 2 * RIM, chans), BF16),
            pltpu.VMEM((atoms + 2 * RIM, chans), BF16),
        ],
        compiler_params=pltpu.CompilerParams(vmem_limit_bytes=16 * MIB),
        cost_estimate=cost(4),
        name="atom_attention",
    )(feat, *halo, wq, wk, wv)


def gather_kernel(sample, mixed, feat, token, wo, agg, gain, *refs):
    *outside, token_in, token_norm, qs, ks, vs, ends = refs
    atoms, chans = feat.shape[1:]
    rows = token_in.shape[0]
    local = token[...].reshape(1, atoms) - lax.axis_index("row") * rows
    step = 384
    sums = []
    edge = 2 * QWIN
    if outside:
        inner, outer, wq, wk, wv = outside
        before, behind = halo_of(sample, inner, outer)
        wqkv = jnp.concatenate([wq[...], wk[...], wv[...]], axis=1)
        near = edge + KWIN - QWIN - RIM
        both = [before, feat[sample, :near], feat[sample, atoms - near :], behind]
        qkv = dot(layer_norm(jnp.concatenate([p.astype(F32) for p in both], axis=0)).astype(BF16), wqkv).astype(BF16)
        qs[...] = qkv[:, :chans]
        ks[...] = qkv[:, chans : 2 * chans]
        vs[...] = qkv[:, 2 * chans :]
        apart = atoms - 2 * near
        starts = [0, QWIN, RIM + near, RIM + near + QWIN]
        hide = hide_outside(atoms)
        windows_attend([starts], qs, ks, vs, ends, -RIM, lambda at, s: hide(at if at < RIM else at + apart, s))

    def finish(c):
        part = mixed[c : c + step]
        if outside and c == 0:
            part = jnp.concatenate([ends[RIM : RIM + edge], part[edge:]], axis=0)
        if outside and c + step == atoms:
            at = ends.shape[0] - RIM - edge
            part = jnp.concatenate([part[: step - edge], ends[at : at + edge]], axis=0)
        return c, (feat[sample, c : c + step].astype(F32) + dot(part, wo[...])).astype(BF16)

    def hide_below(item):
        c, out = item
        return c, jnp.maximum(dot(out, agg[...]), 0.0).astype(BF16)

    def add(item):
        c, hidden = item
        onehot = (iota((rows, step), 0) == local[:, c : c + step]).astype(F32)
        part = dot(onehot.astype(BF16), hidden), jnp.sum(onehot, -1, keepdims=True)
        sums[:] = [a + b for a, b in zip(sums, part)] if sums else part

    chunks = list(range(0, atoms, step))
    skewed(chunks[1:-1] + [chunks[0], chunks[-1]], [finish, hide_below, add])
    tin = sums[0] / sums[1]
    token_in[...] = tin
    token_norm[...] = (layer_norm(tin) * gain[...].reshape(1, -1)).astype(BF16)


def gather_tokens(sample, mixed, feat, token, wo, agg, gain, outside, rows):
    width = agg.shape[1]
    chans = feat.shape[2]
    reach = 2 * (KWIN + QWIN)
    vmem = pl.BlockSpec(memory_space=pltpu.VMEM)
    return pl.pallas_call(
        functools.partial(gather_kernel, sample),
        out_shape=[jax.ShapeDtypeStruct((rows, width), F32), jax.ShapeDtypeStruct((rows, width), BF16)],
        in_specs=[vmem] * (6 + len(outside)),
        out_specs=[vmem, vmem],
        scratch_shapes=[pltpu.VMEM((reach, chans), BF16)] * 4,
        compiler_params=pltpu.CompilerParams(vmem_limit_bytes=16 * MIB),
        cost_estimate=cost(1),
        name="gather_tokens",
    )(mixed, feat, token, wo, agg, gain, *outside)


def head_groups(width):
    groups = []
    for base in range(0, width, 8 * HEAD_DIM):
        first = base // HEAD_DIM
        groups.append((base, range(first, first + 5)))
        groups.append((base + LANES, range(first + 5, first + 8)))
    return groups


def stack(blocks):
    return jnp.concatenate([blocks[j].astype(F32) for j in range(blocks.shape[0])], axis=0).astype(BF16)


def tiles_of(h):
    return range(h * HEAD_DIM // LANES * LANES, (h + 1) * HEAD_DIM, LANES)


def channels(rows, at, h):
    lane = iota((rows, LANES), 1)
    low = h * HEAD_DIM - at
    return (lane >= low) & (lane < low + HEAD_DIM)


def head_scores(q, kt, base, heads):
    rows = q.shape[0]
    blank = jnp.zeros((rows, LANES), F32)
    both = [(at, q[:, at : at + LANES].astype(F32)) for at in (base, base + LANES)]
    mine = [
        [jnp.where(channels(rows, at, h), part, 0.0) if at in tiles_of(h) else blank for at, part in both]
        for h in heads
    ]
    mine = jnp.concatenate([jnp.concatenate(pair, axis=1) for pair in mine], axis=0).astype(BF16)
    return dot(mine, kt[base : base + 2 * LANES]) * (LOG2E / HEAD_DIM**0.5)


def project_kernel(near, far, wq, wk, wv, wg, wo, scores, v, gate, q, kt):
    x = jnp.concatenate([stack(near), stack(far)], axis=0)
    rows = near.shape[1]
    q[...] = dot(near[0], wq[...]).astype(BF16)
    for c in range(0, x.shape[1], 2 * LANES):
        kt[c : c + 2 * LANES] = dot(x, wk[:, c : c + 2 * LANES]).T.astype(BF16)
    for base, heads in head_groups(x.shape[1]):
        scores[heads[0] * rows : (heads[-1] + 1) * rows] = head_scores(q, kt, base, heads)
    gate[...] = jax.nn.sigmoid(dot(near[0], wg[...]))
    v[...] = dot(x, wv[...]).astype(BF16)


def project(near, far, wq, wk, wv, wg, wo):
    half, rows, width = near.shape
    keys = 2 * half * rows
    vmem = pl.BlockSpec(memory_space=pltpu.VMEM)
    return pl.pallas_call(
        project_kernel,
        out_shape=[
            jax.ShapeDtypeStruct((HEADS * rows, keys), F32),
            jax.ShapeDtypeStruct((keys, width), BF16),
            jax.ShapeDtypeStruct((rows, width), F32),
        ],
        in_specs=[vmem] * 7,
        out_specs=[vmem] * 3,
        scratch_shapes=[pltpu.VMEM((rows, width), BF16), pltpu.VMEM((width, keys), BF16)],
        compiler_params=pltpu.CompilerParams(vmem_limit_bytes=24 * MIB),
        cost_estimate=cost(2),
        name="project",
    )(near, far, wq, wk, wv, wg, wo)


def turn_kernel(orders, row_bits, near, wq, wk, wv, wg, *refs):
    *halves, q, k, v, gate, out, tall, flat = refs
    x = stack(near)
    width = x.shape[1]

    def project_columns(c):
        lanes = slice(c, c + 2 * LANES)
        q[:, lanes] = dot(near[0], wq[:, lanes]).astype(BF16)
        k[:, lanes] = dot(x, wk[:, lanes]).astype(BF16)
        v[:, lanes] = dot(x, wv[:, lanes]).astype(BF16)
        gate[:, lanes] = jax.nn.sigmoid(dot(near[0], wg[:, lanes]))

    rows = out.shape[0] // HEADS
    me = lax.axis_index("sample")
    groups = 0
    for mine, other, bits in zip(halves[::2], halves[1::2], orders):
        half, count, _ = mine.shape
        cols = tall.shape[0] // (2 * half)
        places = places_of(bits)
        for j in range(2 * half):
            place = sum(jnp.where(me ^ j == p, i, 0) for i, p in enumerate(places))
            block = jnp.where(place < half, mine[place % half], other[place % half])
            low = groups * cols
            flat[j, low : low + count] = block.astype(F32)
            for g in range(count // cols):
                lanes = slice((groups + g) * LANES, (groups + g + 1) * LANES)
                tall[j * cols : (j + 1) * cols, lanes] = flat[j, low + g * cols : low + (g + 1) * cols]
        groups += count // cols
    starts = [pl.multiple_of((lax.axis_index("row") ^ p) * rows, SUB) for p in places_of(row_bits)]
    for g in range(rows // SUB):
        if g * 2 * LANES < width:
            project_columns(g * 2 * LANES)
        lanes = slice(g * LANES, (g + 1) * LANES)
        turned = jnp.concatenate([tall[pl.ds(start, rows), lanes] for start in starts], axis=0).T
        for h in range(HEADS):
            out[h * rows + g * SUB : h * rows + (g + 1) * SUB] = turned[h * SUB : (h + 1) * SUB] * LOG2E


def turn_bias(orders, row_bits, halves, near, wq, wk, wv, wg):
    blocks, rows, width = near.shape
    devices = 2 * halves[0].shape[0]
    wide = rows * HEADS
    count = sum(part.shape[1] for part in halves[::2])
    keys = devices * count * LANES // wide
    vmem = pl.BlockSpec(memory_space=pltpu.VMEM)
    return pl.pallas_call(
        functools.partial(turn_kernel, orders, row_bits),
        out_shape=[
            jax.ShapeDtypeStruct((rows, width), BF16),
            jax.ShapeDtypeStruct((blocks * rows, width), BF16),
            jax.ShapeDtypeStruct((blocks * rows, width), BF16),
            jax.ShapeDtypeStruct((rows, width), F32),
            jax.ShapeDtypeStruct((wide, keys), F32),
        ],
        in_specs=[vmem] * (5 + len(halves)),
        out_specs=[vmem] * 5,
        scratch_shapes=[pltpu.VMEM((keys, wide), F32), pltpu.VMEM((devices, count, LANES), F32)],
        compiler_params=pltpu.CompilerParams(vmem_limit_bytes=32 * MIB),
        cost_estimate=cost(1),
        name="turn_bias",
    )(near, wq, wk, wv, wg, *halves)


def attend_kernel(samples, bias, *refs):
    parts, refs = [refs[4 * s : 4 * s + 4] for s in range(samples - 1)], refs[4 * (samples - 1) :]
    q, k_near, v_near, gate_last, token_last, far, wk, wv, wo, out, kt, v = refs
    parts.append((None, v, gate_last, token_last))
    rows, width = token_last.shape
    x = stack(far)
    groups = head_groups(width)
    work = [(s, base, heads) for s in range(samples) for base, heads in groups]
    chunks = list(range(0, width, 2 * LANES))
    for i, c in enumerate(chunks):
        work.insert(min(2 * i + 1, (samples - 1) * len(groups) + i), c)

    def fill(c):
        lanes = slice(c, c + 2 * LANES)
        k = jnp.concatenate([k_near[:, lanes].astype(F32), dot(x, wk[:, lanes])], axis=0)
        kt[lanes] = k.T.astype(BF16)
        v[: v_near.shape[0], lanes] = v_near[:, lanes]
        v[v_near.shape[0] :, lanes] = dot(x, wv[:, lanes]).astype(BF16)

    def score(item):
        if isinstance(item, int):
            return fill(item)
        s, base, heads = item
        part = slice(heads[0] * rows, (heads[-1] + 1) * rows)
        return item, (parts[s][0][part] if s < samples - 1 else head_scores(q, kt, base, heads)) + bias[part]

    def soften(item):
        if item is None:
            return None
        place, sc = item
        e = jnp.exp2(sc - jnp.max(sc, -1, keepdims=True))
        return place, e.astype(BF16), inverse(jnp.sum(e, -1, keepdims=True))

    mixes = {}

    def mix(item):
        if item is None:
            return
        (s, base, heads), e, share = item
        o = dot(e, parts[s][1][:, base : base + 2 * LANES])
        for i, h in enumerate(heads):
            part = slice(i * rows, (i + 1) * rows)
            for at in tiles_of(h):
                one = o[part, at - base : at - base + LANES] * share[part]
                mixes[s, at] = jnp.where(channels(rows, at, h), one, mixes.get((s, at), 0.0))
        if h == HEADS - 1:
            close(s)

    def close(s):
        gate, token_in = parts[s][2:]
        gated = jnp.concatenate([mixes[s, at] for at in range(0, width, LANES)], axis=1) * gate[...]
        out[s] = (token_in[...] + dot(gated.astype(BF16), wo[...])).astype(BF16)

    skewed(work, [score, soften, mix])


def attend(bias, parts, far, wk, wv, wo):
    rows, width = parts[-1][4].shape
    keys = 2 * parts[-1][1].shape[0]
    vmem = pl.BlockSpec(memory_space=pltpu.VMEM)
    operands = [bias, *(ref for part in parts for ref in part), far, wk, wv, wo]
    return pl.pallas_call(
        functools.partial(attend_kernel, len(parts)),
        out_shape=jax.ShapeDtypeStruct((len(parts), rows, width), BF16),
        in_specs=[vmem] * len(operands),
        out_specs=vmem,
        scratch_shapes=[pltpu.VMEM((width, keys), BF16), pltpu.VMEM((keys, width), BF16)],
        compiler_params=pltpu.CompilerParams(vmem_limit_bytes=32 * MIB),
        cost_estimate=cost(3),
        name="attend",
    )(*operands)


def shards(
    atom_feat,
    atom_token,
    pair_cond,
    token_mask,
    atom_wq,
    atom_wk,
    atom_wv,
    atom_wo,
    agg_weight,
    pair_weight,
    token_gain,
    query_weight,
    key_weight,
    value_weight,
    gate_weight,
    out_weight,
):
    samples = atom_feat.shape[0]
    rows = pair_cond.shape[0]
    ranks = lax.axis_size("row")
    bias, inner, outer = pair_bias(atom_feat, pair_cond, token_mask, pair_weight)
    inner = swap(inner, "row", 1)
    odd_pairs = [(i, (i + 1) % ranks) for i in range(1, ranks, 2)]
    outer = lax.ppermute(outer, "row", odd_pairs + [(j, i) for i, j in odd_pairs])

    def widen(held, axis, bit, *others):
        return jnp.concatenate([held, after(swap(held, axis, bit), *others)], axis=0)

    bits, row_bits = bits_of(lax.axis_size("sample")), bits_of(ranks)
    orders = [bits, bits[:1] + bits[-1:] + bits[1:-1]]
    split = rows // SUB // 2 * pair_cond.shape[1]
    got = swap(bias, "sample", bits[0])
    norms, inputs = [], []
    for s in range(samples):
        halo = (inner, outer)
        mixed = atom_attention(s, atom_feat, halo if s else (), atom_wq, atom_wk, atom_wv)
        outside = () if s else (*halo, atom_wq, atom_wk, atom_wv)
        token_in, token_norm = gather_tokens(
            s, mixed, atom_feat, atom_token, atom_wo, agg_weight, token_gain, outside, rows
        )
        inputs.append(token_in)
        norms.append(token_norm[None])
        if s == 0:
            bias, got, _ = lax.optimization_barrier((bias, got, token_norm))
            held = [jnp.stack([bias[part], got[part]]) for part in (slice(0, split), slice(split, None))]
            inner = after(inner, held, token_norm)
    last = swap(norms[-1], "row", row_bits[0])
    for i in range(1, len(bits) - 1):
        held = [widen(h, "sample", order[i], token_norm) for h, order in zip(held, orders)]
    halves = []
    for h, order in zip(held, orders):
        halves += [h, swap(h, "sample", order[-1])]
    parts = []
    weights = (query_weight, key_weight, value_weight, gate_weight, out_weight)
    for s in range(samples):
        near = norms[s]
        others = (mixed, parts, halves) if s == samples - 1 else (mixed, parts)
        for bit in row_bits[:-1]:
            if s == samples - 1 and bit == row_bits[0]:
                near = jnp.concatenate([near, after(last, *others)], axis=0)
            else:
                near = widen(near, "row", bit, *others)
        far = swap(near, "row", row_bits[-1])
        near = after(near, held)
        if s < samples - 1:
            parts.append((*project(near, far, *weights), inputs[s]))
        else:
            *part, bias = turn_bias(orders, row_bits, halves, near, *weights[:4])
            parts.append((*part, inputs[s]))
    return attend(bias, parts, far, key_weight, value_weight, out_weight)


def solution(mesh):
    placed = (
        P("sample", "row", None),
        P("row"),
        P("row", "sample", None),
        P("sample"),
    ) + (P(),) * 12
    return jax.shard_map(
        shards, mesh=mesh, in_specs=placed, out_specs=P("sample", "row", None), check_vma=False
    )
```

```python
import functools
import math

import jax
import jax.numpy as jnp
from jax import lax
from jax.experimental import pallas as pl
from jax.experimental.pallas import tpu as pltpu
from jax.sharding import PartitionSpec as P

HEADS = 16
HEAD_DIM = 48
AHEADS = 4
AHEAD_DIM = 32
QWIN = 32
KWIN = 128
RIM = (KWIN - QWIN) // 2
LANES = 128
SUB = 8
F32 = jnp.float32
BF16 = jnp.bfloat16
MIB = 1024 * 1024
LOG2E = math.log2(math.e)
NT = (((1,), (1,)), ((), ()))


def layer_norm(x):
    mean = jnp.mean(x, -1, keepdims=True)
    centre = x - mean
    var = jnp.mean(centre * centre, -1, keepdims=True)
    return centre * lax.rsqrt(var + 1e-05)


def dot(a, b):
    return jnp.dot(a, b, preferred_element_type=F32)


def dot_nt(a, b):
    return lax.dot_general(a, b, NT, preferred_element_type=F32)


def iota(shape, dim):
    return lax.broadcasted_iota(jnp.int32, shape, dim)


def cost(micros):
    return pl.CostEstimate(flops=micros * 20_000_000, bytes_accessed=1_000, transcendentals=0)


def inverse(total):
    guess = pl.reciprocal(total, approx=True)
    return guess * (2.0 - total * guess)


def skewed(items, stages):
    held = list(items)
    for t in range(len(held) + len(stages) - 1):
        for k in reversed(range(len(stages))):
            if 0 <= t - k < len(held):
                held[t - k] = stages[k](held[t - k])
    return held


def normalise_kernel(pair, normed):
    cols, rows, chans = pair.shape
    evenly = jnp.full((chans, chans), 1.0 / chans, BF16)
    step = 6

    def centre(k):
        x = pair[k : k + step].astype(F32).reshape(step * rows, chans)
        return k, x - dot(x.astype(BF16), evenly)

    def scale(item):
        k, x = item
        x = x * lax.rsqrt(jnp.mean(x * x, -1, keepdims=True) + 1e-05)
        normed[k : k + step] = x.reshape(step, rows, chans)

    skewed(range(0, cols, step), [centre, scale])


def normalise_pairs(pair_cond):
    rows, cols, chans = pair_cond.shape
    vmem = pl.BlockSpec(memory_space=pltpu.VMEM)
    return pl.pallas_call(
        normalise_kernel,
        out_shape=jax.ShapeDtypeStruct((cols, rows, chans), F32),
        in_specs=[vmem],
        out_specs=vmem,
        compiler_params=pltpu.CompilerParams(vmem_limit_bytes=8 * MIB),
        cost_estimate=cost(1),
        name="normalise_pairs",
    )(jnp.transpose(pair_cond, (1, 0, 2)))


def bias_kernel(feat, normed, mask, weight, out, inner, outer, whole):
    odd = lax.axis_index("row") % 2 == 1
    head, tail = feat[:, :RIM], feat[:, feat.shape[1] - RIM :]
    inner[...] = jnp.where(odd, head, tail)
    outer[...] = jnp.where(odd, tail, head)
    cols, rows, chans = normed.shape
    spread = (iota((HEADS, LANES), 1) // SUB == iota((HEADS, LANES), 0)).astype(BF16)
    wide = lax.dot_general(weight[...], spread, (((0,), (0,)), ((), ())), preferred_element_type=F32).astype(BF16)
    tall = cols * SUB
    key_of = iota((tall, cols), 0) // SUB == iota((tall, cols), 1)
    open_row = jnp.broadcast_to(mask[...].reshape(1, cols), (LANES, cols)).astype(BF16)
    open_key = dot_nt(key_of.astype(BF16), open_row) > 0.5
    picked = (iota((cols, tall), 1) // SUB == iota((cols, tall), 0)).astype(BF16)
    batch = 3
    row = iota((tall, LANES), 0)
    mine = iota((tall, LANES), 1) % SUB == row % SUB
    own = lax.axis_index("sample") * cols + row // SUB - lax.axis_index("row") * rows - row % SUB
    own = jnp.where(mine, own, -1)
    kept = mine & open_key
    base = jnp.where(mine & ~open_key, -30000.0, 0.0)

    def weigh(first):
        out = []
        for g in range(first, first + batch):
            raw = dot(normed[:, g * SUB : (g + 1) * SUB].reshape(tall, chans).astype(BF16), wide)
            out.append(jnp.where(kept | (own == g * SUB), raw, base).astype(BF16))
        return first, out

    def pick(item):
        first, out = item
        for i, raw in enumerate(out):
            whole[(first + i) * cols : (first + i + 1) * cols] = dot(picked, raw)

    skewed(range(0, rows // SUB, batch), [weigh, pick])
    out[...] = whole[...].astype(BF16)


def pair_bias(feat, pair_cond, token_mask, pair_weight):
    rows, cols, _ = pair_cond.shape
    edge = (feat.shape[0], RIM, feat.shape[2])
    vmem = pl.BlockSpec(memory_space=pltpu.VMEM)
    return pl.pallas_call(
        bias_kernel,
        out_shape=[
            jax.ShapeDtypeStruct((rows // SUB * cols, LANES), BF16),
            jax.ShapeDtypeStruct(edge, BF16),
            jax.ShapeDtypeStruct(edge, BF16),
        ],
        in_specs=[vmem] * 4,
        out_specs=[vmem] * 3,
        scratch_shapes=[pltpu.VMEM((rows // SUB * cols, LANES), F32)],
        compiler_params=pltpu.CompilerParams(vmem_limit_bytes=8 * MIB),
        cost_estimate=cost(3),
        name="pair_bias",
    )(feat, normalise_pairs(pair_cond), token_mask, pair_weight.T)


def after(value, *others):
    return lax.optimization_barrier((value, *others))[0]


def swap(held, axis, far):
    return lax.ppermute(held, axis, [(i, i ^ far) for i in range(lax.axis_size(axis))])


def bits_of(devices):
    return [devices >> i for i in range(1, devices.bit_length())]


def places_of(bits):
    places = [0]
    for bit in bits:
        places += [p ^ bit for p in places]
    return places


def windows_attend(starts, qs, ks, vs, mixed, shift, hide):
    rate = LOG2E / AHEAD_DIM**0.5
    tall = AHEADS * QWIN
    head_of = iota((QWIN, qs.shape[1]), 1) // AHEAD_DIM

    def score(batch):
        out = []
        for at in batch:
            q = qs[at - shift : at - shift + QWIN]
            q = jnp.concatenate([jnp.where(head_of == h, q, jnp.zeros_like(q)) for h in range(AHEADS)], axis=0)
            out.append(hide(at, dot_nt(q, ks[at : at + KWIN])))
        return batch, jnp.concatenate(out, axis=0)

    def soften(item):
        batch, s = item
        e = jnp.exp2((s - jnp.max(s, -1, keepdims=True)) * rate)
        return batch, e.astype(BF16), jnp.sum(e, -1, keepdims=True)

    def own_head(parts):
        acc = parts[:QWIN]
        for h in range(1, AHEADS):
            acc = jnp.where(head_of == h, parts[h * QWIN : (h + 1) * QWIN], acc)
        return acc

    def mix(item):
        batch, e, total = item
        for i, at in enumerate(batch):
            part = slice(i * tall, (i + 1) * tall)
            o = own_head(dot(e[part], vs[at : at + KWIN])) * inverse(own_head(total[part]))
            mixed[at - shift : at - shift + QWIN] = o.astype(BF16)

    skewed(starts, [score, soften, mix])


def halo_of(sample, inner, outer):
    odd = lax.axis_index("row") % 2 == 1
    return jnp.where(odd, inner[sample], outer[sample]), jnp.where(odd, outer[sample], inner[sample])


def hide_outside(atoms):
    rank = lax.axis_index("row")
    at_start = rank == 0
    at_end = rank == lax.axis_size("row") - 1
    keyat = iota((AHEADS * QWIN, KWIN), 1)

    def hide(at, s):
        if at < RIM:
            s = jnp.where(at_start & (keyat < RIM - at), -jnp.inf, s)
        if at + KWIN > RIM + atoms:
            s = jnp.where(at_end & (keyat >= RIM + atoms - at), -jnp.inf, s)
        return s

    return hide


def atom_kernel(sample, feat, *refs):
    *halo, wq, wk, wv, mixed, qs, ks, vs = refs
    atoms, chans = feat.shape[1:]
    wqkv = jnp.concatenate([wq[...], wk[...], wv[...]], axis=1)
    evenly = jnp.full((chans, chans), 1.0 / chans, BF16)

    def normalise(at):
        if isinstance(at, int):
            part = feat[sample, at : at + LANES]
        else:
            at, part = at
        x = part.astype(F32) - dot(part, evenly)
        return at, (x * lax.rsqrt(jnp.mean(x * x, -1, keepdims=True) + 1e-05)).astype(BF16)

    def project_atoms(item):
        at, normed = item
        count = normed.shape[0]
        if count == RIM:
            kv = dot(normed, wqkv[:, chans:]).astype(BF16)
        else:
            qkv = dot(normed, wqkv).astype(BF16)
            qs[at : at + count] = qkv[:, :chans]
            kv = qkv[:, chans:]
        ks[RIM + at : RIM + at + count] = kv[:, :chans]
        vs[RIM + at : RIM + at + count] = kv[:, chans:]

    parts = list(range(0, atoms, LANES))
    if halo:
        before, behind = halo_of(sample, *halo)
        parts += [(-RIM, before), (atoms, behind)]
    skewed(parts, [normalise, project_atoms])
    starts = list(range(0, atoms, QWIN))
    if not halo:
        starts = [at for at in starts if RIM <= at <= atoms + RIM - KWIN]
    batch = 6
    batches = [starts[i : i + batch] for i in range(0, len(starts), batch)]
    windows_attend(batches, qs, ks, vs, mixed, 0, hide_outside(atoms))


def atom_attention(sample, feat, halo, wq, wk, wv):
    atoms, chans = feat.shape[1:]
    vmem = pl.BlockSpec(memory_space=pltpu.VMEM)
    return pl.pallas_call(
        functools.partial(atom_kernel, sample),
        out_shape=jax.ShapeDtypeStruct((atoms, chans), BF16),
        in_specs=[vmem] * (4 + len(halo)),
        out_specs=vmem,
        scratch_shapes=[
            pltpu.VMEM((atoms, chans), BF16),
            pltpu.VMEM((atoms + 2 * RIM, chans), BF16),
            pltpu.VMEM((atoms + 2 * RIM, chans), BF16),
        ],
        compiler_params=pltpu.CompilerParams(vmem_limit_bytes=16 * MIB),
        cost_estimate=cost(4),
        name="atom_attention",
    )(feat, *halo, wq, wk, wv)


def gather_kernel(sample, mixed, feat, token, wo, agg, gain, *refs):
    *outside, token_in, token_norm, qs, ks, vs, ends = refs
    atoms, chans = feat.shape[1:]
    rows = token_in.shape[0]
    local = token[...].reshape(1, atoms) - lax.axis_index("row") * rows
    step = 384
    sums = []
    edge = 2 * QWIN
    if outside:
        inner, outer, wq, wk, wv = outside
        before, behind = halo_of(sample, inner, outer)
        wqkv = jnp.concatenate([wq[...], wk[...], wv[...]], axis=1)
        near = edge + KWIN - QWIN - RIM
        both = [before, feat[sample, :near], feat[sample, atoms - near :], behind]
        qkv = dot(layer_norm(jnp.concatenate([p.astype(F32) for p in both], axis=0)).astype(BF16), wqkv).astype(BF16)
        qs[...] = qkv[:, :chans]
        ks[...] = qkv[:, chans : 2 * chans]
        vs[...] = qkv[:, 2 * chans :]
        apart = atoms - 2 * near
        starts = [0, QWIN, RIM + near, RIM + near + QWIN]
        hide = hide_outside(atoms)
        windows_attend([starts], qs, ks, vs, ends, -RIM, lambda at, s: hide(at if at < RIM else at + apart, s))

    def finish(c):
        part = mixed[c : c + step]
        if outside and c == 0:
            part = jnp.concatenate([ends[RIM : RIM + edge], part[edge:]], axis=0)
        if outside and c + step == atoms:
            at = ends.shape[0] - RIM - edge
            part = jnp.concatenate([part[: step - edge], ends[at : at + edge]], axis=0)
        return c, (feat[sample, c : c + step].astype(F32) + dot(part, wo[...])).astype(BF16)

    def hide_below(item):
        c, out = item
        return c, jnp.maximum(dot(out, agg[...]), 0.0).astype(BF16)

    def add(item):
        c, hidden = item
        onehot = (iota((rows, step), 0) == local[:, c : c + step]).astype(F32)
        part = dot(onehot.astype(BF16), hidden), jnp.sum(onehot, -1, keepdims=True)
        sums[:] = [a + b for a, b in zip(sums, part)] if sums else part

    chunks = list(range(0, atoms, step))
    skewed(chunks[1:-1] + [chunks[0], chunks[-1]], [finish, hide_below, add])
    tin = sums[0] / sums[1]
    token_in[...] = tin
    token_norm[...] = (layer_norm(tin) * gain[...].reshape(1, -1)).astype(BF16)


def gather_tokens(sample, mixed, feat, token, wo, agg, gain, outside, rows):
    width = agg.shape[1]
    chans = feat.shape[2]
    reach = 2 * (KWIN + QWIN)
    vmem = pl.BlockSpec(memory_space=pltpu.VMEM)
    return pl.pallas_call(
        functools.partial(gather_kernel, sample),
        out_shape=[jax.ShapeDtypeStruct((rows, width), F32), jax.ShapeDtypeStruct((rows, width), BF16)],
        in_specs=[vmem] * (6 + len(outside)),
        out_specs=[vmem, vmem],
        scratch_shapes=[pltpu.VMEM((reach, chans), BF16)] * 4,
        compiler_params=pltpu.CompilerParams(vmem_limit_bytes=16 * MIB),
        cost_estimate=cost(1),
        name="gather_tokens",
    )(mixed, feat, token, wo, agg, gain, *outside)


def head_groups(width):
    groups = []
    for base in range(0, width, 8 * HEAD_DIM):
        first = base // HEAD_DIM
        groups.append((base, range(first, first + 5)))
        groups.append((base + LANES, range(first + 5, first + 8)))
    return groups


def stack(blocks):
    return jnp.concatenate([blocks[j].astype(F32) for j in range(blocks.shape[0])], axis=0).astype(BF16)


def tiles_of(h):
    return range(h * HEAD_DIM // LANES * LANES, (h + 1) * HEAD_DIM, LANES)


def channels(rows, at, h):
    lane = iota((rows, LANES), 1)
    low = h * HEAD_DIM - at
    return (lane >= low) & (lane < low + HEAD_DIM)


def head_scores(q, kt, base, heads):
    rows = q.shape[0]
    blank = jnp.zeros((rows, LANES), F32)
    both = [(at, q[:, at : at + LANES].astype(F32)) for at in (base, base + LANES)]
    mine = [
        [jnp.where(channels(rows, at, h), part, 0.0) if at in tiles_of(h) else blank for at, part in both]
        for h in heads
    ]
    mine = jnp.concatenate([jnp.concatenate(pair, axis=1) for pair in mine], axis=0).astype(BF16)
    return dot(mine, kt[base : base + 2 * LANES]) * (LOG2E / HEAD_DIM**0.5)


def project_kernel(near, far, wq, wk, wv, wg, wo, scores, v, gate, q, kt):
    x = jnp.concatenate([stack(near), stack(far)], axis=0)
    rows = near.shape[1]
    q[...] = dot(near[0], wq[...]).astype(BF16)
    for c in range(0, x.shape[1], 2 * LANES):
        kt[c : c + 2 * LANES] = dot(x, wk[:, c : c + 2 * LANES]).T.astype(BF16)
    for base, heads in head_groups(x.shape[1]):
        scores[heads[0] * rows : (heads[-1] + 1) * rows] = head_scores(q, kt, base, heads)
    gate[...] = jax.nn.sigmoid(dot(near[0], wg[...]))
    v[...] = dot(x, wv[...]).astype(BF16)


def project(near, far, wq, wk, wv, wg, wo):
    half, rows, width = near.shape
    keys = 2 * half * rows
    vmem = pl.BlockSpec(memory_space=pltpu.VMEM)
    return pl.pallas_call(
        project_kernel,
        out_shape=[
            jax.ShapeDtypeStruct((HEADS * rows, keys), F32),
            jax.ShapeDtypeStruct((keys, width), BF16),
            jax.ShapeDtypeStruct((rows, width), F32),
        ],
        in_specs=[vmem] * 7,
        out_specs=[vmem] * 3,
        scratch_shapes=[pltpu.VMEM((rows, width), BF16), pltpu.VMEM((width, keys), BF16)],
        compiler_params=pltpu.CompilerParams(vmem_limit_bytes=24 * MIB),
        cost_estimate=cost(2),
        name="project",
    )(near, far, wq, wk, wv, wg, wo)


def turn_kernel(orders, row_bits, near, wq, wk, wv, wg, *refs):
    *halves, q, k, v, gate, out, tall, flat = refs
    x = stack(near)
    width = x.shape[1]

    def project_columns(c):
        lanes = slice(c, c + 2 * LANES)
        q[:, lanes] = dot(near[0], wq[:, lanes]).astype(BF16)
        k[:, lanes] = dot(x, wk[:, lanes]).astype(BF16)
        v[:, lanes] = dot(x, wv[:, lanes]).astype(BF16)
        gate[:, lanes] = jax.nn.sigmoid(dot(near[0], wg[:, lanes]))

    rows = out.shape[0] // HEADS
    me = lax.axis_index("sample")
    groups = 0
    for mine, other, bits in zip(halves[::2], halves[1::2], orders):
        half, count, _ = mine.shape
        cols = tall.shape[0] // (2 * half)
        places = places_of(bits)
        for j in range(2 * half):
            place = sum(jnp.where(me ^ j == p, i, 0) for i, p in enumerate(places))
            block = jnp.where(place < half, mine[place % half], other[place % half])
            low = groups * cols
            flat[j, low : low + count] = block.astype(F32)
            for g in range(count // cols):
                lanes = slice((groups + g) * LANES, (groups + g + 1) * LANES)
                tall[j * cols : (j + 1) * cols, lanes] = flat[j, low + g * cols : low + (g + 1) * cols]
        groups += count // cols
    starts = [pl.multiple_of((lax.axis_index("row") ^ p) * rows, SUB) for p in places_of(row_bits)]
    for g in range(rows // SUB):
        if g * 2 * LANES < width:
            project_columns(g * 2 * LANES)
        lanes = slice(g * LANES, (g + 1) * LANES)
        turned = jnp.concatenate([tall[pl.ds(start, rows), lanes] for start in starts], axis=0).T
        for h in range(HEADS):
            out[h * rows + g * SUB : h * rows + (g + 1) * SUB] = turned[h * SUB : (h + 1) * SUB] * LOG2E


def turn_bias(orders, row_bits, halves, near, wq, wk, wv, wg):
    blocks, rows, width = near.shape
    devices = 2 * halves[0].shape[0]
    wide = rows * HEADS
    count = sum(part.shape[1] for part in halves[::2])
    keys = devices * count * LANES // wide
    vmem = pl.BlockSpec(memory_space=pltpu.VMEM)
    return pl.pallas_call(
        functools.partial(turn_kernel, orders, row_bits),
        out_shape=[
            jax.ShapeDtypeStruct((rows, width), BF16),
            jax.ShapeDtypeStruct((blocks * rows, width), BF16),
            jax.ShapeDtypeStruct((blocks * rows, width), BF16),
            jax.ShapeDtypeStruct((rows, width), F32),
            jax.ShapeDtypeStruct((wide, keys), F32),
        ],
        in_specs=[vmem] * (5 + len(halves)),
        out_specs=[vmem] * 5,
        scratch_shapes=[pltpu.VMEM((keys, wide), F32), pltpu.VMEM((devices, count, LANES), F32)],
        compiler_params=pltpu.CompilerParams(vmem_limit_bytes=32 * MIB),
        cost_estimate=cost(1),
        name="turn_bias",
    )(near, wq, wk, wv, wg, *halves)


def attend_kernel(samples, bias, *refs):
    parts, refs = [refs[4 * s : 4 * s + 4] for s in range(samples - 1)], refs[4 * (samples - 1) :]
    q, k_near, v_near, gate_last, token_last, far, wk, wv, wo, out, kt, v = refs
    parts.append((None, v, gate_last, token_last))
    rows, width = token_last.shape
    x = stack(far)
    groups = head_groups(width)
    work = [(s, base, heads) for s in range(samples) for base, heads in groups]
    chunks = list(range(0, width, 2 * LANES))
    for i, c in enumerate(chunks):
        work.insert(min(2 * i + 1, (samples - 1) * len(groups) + i), c)

    def fill(c):
        lanes = slice(c, c + 2 * LANES)
        k = jnp.concatenate([k_near[:, lanes].astype(F32), dot(x, wk[:, lanes])], axis=0)
        kt[lanes] = k.T.astype(BF16)
        v[: v_near.shape[0], lanes] = v_near[:, lanes]
        v[v_near.shape[0] :, lanes] = dot(x, wv[:, lanes]).astype(BF16)

    def score(item):
        if isinstance(item, int):
            return fill(item)
        s, base, heads = item
        part = slice(heads[0] * rows, (heads[-1] + 1) * rows)
        return item, (parts[s][0][part] if s < samples - 1 else head_scores(q, kt, base, heads)) + bias[part]

    def soften(item):
        if item is None:
            return None
        place, sc = item
        e = jnp.exp2(sc - jnp.max(sc, -1, keepdims=True))
        return place, e.astype(BF16), inverse(jnp.sum(e, -1, keepdims=True))

    mixes = {}

    def mix(item):
        if item is None:
            return
        (s, base, heads), e, share = item
        o = dot(e, parts[s][1][:, base : base + 2 * LANES])
        for i, h in enumerate(heads):
            part = slice(i * rows, (i + 1) * rows)
            for at in tiles_of(h):
                one = o[part, at - base : at - base + LANES] * share[part]
                mixes[s, at] = jnp.where(channels(rows, at, h), one, mixes.get((s, at), 0.0))
        if h == HEADS - 1:
            close(s)

    def close(s):
        gate, token_in = parts[s][2:]
        gated = jnp.concatenate([mixes[s, at] for at in range(0, width, LANES)], axis=1) * gate[...]
        out[s] = (token_in[...] + dot(gated.astype(BF16), wo[...])).astype(BF16)

    skewed(work, [score, soften, mix])


def attend(bias, parts, far, wk, wv, wo):
    rows, width = parts[-1][4].shape
    keys = 2 * parts[-1][1].shape[0]
    vmem = pl.BlockSpec(memory_space=pltpu.VMEM)
    operands = [bias, *(ref for part in parts for ref in part), far, wk, wv, wo]
    return pl.pallas_call(
        functools.partial(attend_kernel, len(parts)),
        out_shape=jax.ShapeDtypeStruct((len(parts), rows, width), BF16),
        in_specs=[vmem] * len(operands),
        out_specs=vmem,
        scratch_shapes=[pltpu.VMEM((width, keys), BF16), pltpu.VMEM((keys, width), BF16)],
        compiler_params=pltpu.CompilerParams(vmem_limit_bytes=32 * MIB),
        cost_estimate=cost(3),
        name="attend",
    )(*operands)


def shards(
    atom_feat,
    atom_token,
    pair_cond,
    token_mask,
    atom_wq,
    atom_wk,
    atom_wv,
    atom_wo,
    agg_weight,
    pair_weight,
    token_gain,
    query_weight,
    key_weight,
    value_weight,
    gate_weight,
    out_weight,
):
    samples = atom_feat.shape[0]
    rows = pair_cond.shape[0]
    ranks = lax.axis_size("row")
    bias, inner, outer = pair_bias(atom_feat, pair_cond, token_mask, pair_weight)
    inner = swap(inner, "row", 1)
    odd_pairs = [(i, (i + 1) % ranks) for i in range(1, ranks, 2)]
    outer = lax.ppermute(outer, "row", odd_pairs + [(j, i) for i, j in odd_pairs])

    def widen(held, axis, bit, *others):
        return jnp.concatenate([held, after(swap(held, axis, bit), *others)], axis=0)

    bits, row_bits = bits_of(lax.axis_size("sample")), bits_of(ranks)
    orders = [bits, bits[:1] + bits[-1:] + bits[1:-1]]
    split = rows // SUB // 2 * pair_cond.shape[1]
    got = swap(bias, "sample", bits[0])
    norms, inputs = [], []
    for s in range(samples):
        halo = (inner, outer)
        mixed = atom_attention(s, atom_feat, halo if s else (), atom_wq, atom_wk, atom_wv)
        outside = () if s else (*halo, atom_wq, atom_wk, atom_wv)
        token_in, token_norm = gather_tokens(
            s, mixed, atom_feat, atom_token, atom_wo, agg_weight, token_gain, outside, rows
        )
        inputs.append(token_in)
        norms.append(token_norm[None])
        if s == 0:
            bias, got, _ = lax.optimization_barrier((bias, got, token_norm))
            held = [jnp.stack([bias[part], got[part]]) for part in (slice(0, split), slice(split, None))]
            inner = after(inner, held, token_norm)
    last = swap(norms[-1], "row", row_bits[0])
    for i in range(1, len(bits) - 1):
        held = [widen(h, "sample", order[i], token_norm) for h, order in zip(held, orders)]
    halves = []
    for h, order in zip(held, orders):
        halves += [h, swap(h, "sample", order[-1])]
    parts = []
    weights = (query_weight, key_weight, value_weight, gate_weight, out_weight)
    for s in range(samples):
        near = norms[s]
        others = (mixed, parts, halves) if s == samples - 1 else (mixed, parts)
        for bit in row_bits[:-1]:
            if s == samples - 1 and bit == row_bits[0]:
                near = jnp.concatenate([near, after(last, *others)], axis=0)
            else:
                near = widen(near, "row", bit, *others)
        far = swap(near, "row", row_bits[-1])
        near = after(near, held)
        if s < samples - 1:
            parts.append((*project(near, far, *weights), inputs[s]))
        else:
            *part, bias = turn_bias(orders, row_bits, halves, near, *weights[:4])
            parts.append((*part, inputs[s]))
    return attend(bias, parts, far, key_weight, value_weight, out_weight)


def solution(mesh):
    placed = (
        P("sample", "row", None),
        P("row"),
        P("row", "sample", None),
        P("sample"),
    ) + (P(),) * 12
    return jax.shard_map(
        shards, mesh=mesh, in_specs=placed, out_specs=P("sample", "row", None), check_vma=False
    )
```
